32 devices in a mesh: chan: 4 (over z), brow: 2 (over y), bcol: 4 (over x, core).
Axes of the slice: x: 2, y: 2, z: 4, core: 2. Of those that a mesh axis runs over, the one named last changes fastest.
Arguments:
- voltages: int32 [2, 64, 131072], P(None, ('brow', 'bcol'), 'chan'), may hold values from -127 to 127
- antenna_gains: float32 [64, 2, 512], P(('brow', 'bcol'), None, 'chan'), may hold values from -4 to 4
- tile_map: int32 [8, 8], replicated, may hold values from 0 to 1, as said below
Outputs:
- visibilities: float32 [2, 4, 512, 2, 16, 32], P('brow', 'bcol', 'chan')
The draws below stay inside these ranges and needn't reach their ends.
Inputs may be any that keep to these rules, and one draw needn't show every extreme that they name: For two different antenna blocks i and j exactly one of tile_map[i, j] and tile_map[j, i] is 1; every diagonal entry is 1.
All inputs are finite; a program needn't handle non-finite values.
Results may differ from the reference program's by a relative error of at most 0.0029.
Values may be sent and summed in bfloat16 or wider, within the bound.
No kernel may reach another device: no remote copies, remote signals or barrier semaphores. Data moves between devices by JAX's collectives and lax.ppermute only.
A program may use at most 64 MiB of HBM per device.

```python
import math
import jax
import jax.numpy as jnp
from jax import lax

SIG_DEV = 8
NCHAN = 1024
CHANNELS = 512
TAPS = 4
FIRST = 256
BLOCKS = 8
SIGNALS = 64
SPECTRA = 128
SAMPLES = 131072
N_BROW = 2
N_BCOL = 4


def draw_tile_map(key, part):
    key = jax.random.fold_in(key, 11)
    coins = jax.random.randint(key, (BLOCKS, BLOCKS), 0, 2, dtype=jnp.int32)
    first_block = jnp.arange(BLOCKS, dtype=jnp.int32)[:, None]
    second_block = jnp.arange(BLOCKS, dtype=jnp.int32)[None, :]
    lower_coin = jnp.where(first_block > second_block, coins, coins.T)
    owned = jnp.where(first_block > second_block, lower_coin, 1 - lower_coin)
    return jnp.where(first_block == second_block, 1, owned).astype(jnp.int32)


def with_ends(result, own_key, low, high):
    longest = result.shape.index(max(result.shape))
    spots = []
    for shift in (0, 1):
        where = [jax.random.randint(jax.random.fold_in(own_key, axis), (), 0, length) for axis, length in enumerate(result.shape)]
        where[longest] = (where[longest] + shift) % result.shape[longest]
        spots.append(tuple(where))
    return result.at[spots[0]].set(low).at[spots[1]].set(high)


def block_scale(own_key, dims, pieces, least, high):
    gain = 1.0
    for dim, parts in pieces:
        steps = jax.random.uniform(jax.random.fold_in(jax.random.fold_in(own_key, 6), dim), (parts,), jnp.float32, least / len(pieces), high / len(pieces))
        gain = gain * jnp.repeat(jnp.exp(steps), dims[dim] // parts).reshape((-1,) + (1,) * (len(dims) - 1 - dim))
    return gain


def normal_values(own_key, shape, deviation, bound, pieces=(), kind=jnp.bfloat16):
    loudness = block_scale(own_key, shape, pieces, -0.22, 0.18) if pieces else 1.0
    result = jax.random.normal(own_key, shape, jnp.float32) * deviation * loudness
    return jnp.minimum(jnp.maximum(result, -bound), bound).astype(kind)


def setup_inputs(seed: int = 0) -> dict:
    key_list = jax.random.split(jax.random.key(seed), 4)
    voltages = with_ends(jax.random.randint(key_list[0], (2, SIGNALS, SAMPLES), -127, 128), jax.random.fold_in(key_list[0], 1), -127, 127).astype(jnp.int32)
    antenna_gains = normal_values(key_list[1], (SIGNALS, 2, CHANNELS), 1.0, 4.0, ((0, 8), (2, 4)), jnp.float32)
    tile_map = draw_tile_map(jax.random.fold_in(key_list[3], 71), 0)
    return {"voltages": voltages, "antenna_gains": antenna_gains, "tile_map": tile_map}


def fir_coefficients():
    position = jnp.arange(TAPS * NCHAN, dtype=jnp.int32).astype(jnp.float32) + 0.5
    offsets = position / NCHAN - TAPS / 2.0
    window = 0.5 - 0.5 * jnp.cos(2.0 * math.pi * position / (TAPS * NCHAN))
    return (jnp.sinc(offsets) * window).reshape(TAPS, NCHAN)

def make_dft_table():
    sample_index = jnp.arange(NCHAN, dtype=jnp.int32)[:, None]
    channel_index = FIRST + jnp.arange(CHANNELS, dtype=jnp.int32)[None, :]
    angles = (sample_index * channel_index % NCHAN).astype(jnp.float32) * (2.0 * math.pi / NCHAN)
    cosine = jnp.cos(angles)
    sine_part = jnp.sin(angles)
    upper_half = jnp.concatenate([cosine, -sine_part], axis=1)
    lower_half = jnp.concatenate([sine_part, cosine], axis=1)
    return jnp.stack([upper_half, lower_half], axis=0).astype(jnp.bfloat16)

def reference(voltages, antenna_gains, tile_map):
    coefficients = fir_coefficients()
    dft_table = make_dft_table()
    spectrum_scale = 1.0 / (128.0 * jnp.sqrt(jnp.sum(coefficients * coefficients)))

    def analyse(voltage_block):
        frames = voltage_block.astype(jnp.float32).reshape(2, SIG_DEV, SPECTRA, NCHAN)
        frames = jnp.concatenate([jnp.zeros((2, SIG_DEV, TAPS - 1, NCHAN), jnp.float32), frames], axis=2)
        filtered_sum = jnp.zeros((2, SIG_DEV, SPECTRA, NCHAN), jnp.float32)
        for tap_index in range(TAPS):
            filtered_sum = filtered_sum + coefficients[tap_index] * frames[:, :, tap_index:tap_index + SPECTRA, :]
        filtered = filtered_sum.astype(jnp.bfloat16)
        raw = jnp.einsum('psmn,pnc->scm', filtered.astype(jnp.float32), dft_table.astype(jnp.float32), precision=lax.Precision.HIGHEST)
        return (raw * spectrum_scale).reshape(SIG_DEV, 2, CHANNELS, SPECTRA).astype(jnp.bfloat16)
    blocked = jnp.transpose(voltages.reshape(2, BLOCKS, SIG_DEV, SAMPLES), (1, 0, 2, 3))
    spectrum = lax.map(analyse, blocked).reshape(SIGNALS, 2, CHANNELS, SPECTRA)
    real_part = spectrum[:, 0].astype(jnp.float32)
    imag_part = spectrum[:, 1].astype(jnp.float32)
    gain_real = antenna_gains[:, 0, :, None]
    gain_imag = antenna_gains[:, 1, :, None]
    equalized = jnp.stack([real_part * gain_real - imag_part * gain_imag, real_part * gain_imag + imag_part * gain_real], axis=1).astype(jnp.bfloat16)
    by_channel = jnp.transpose(equalized, (2, 0, 1, 3))

    def correlate(channel_data):
        row_data = channel_data.astype(jnp.float32)
        paired = jnp.stack([row_data, jnp.stack([-row_data[:, 1], row_data[:, 0]], axis=1)], axis=1)
        summed = jnp.einsum('apt,bqpt->qba', row_data, paired, precision=lax.Precision.HIGHEST)
        return summed / SPECTRA
    correlation = lax.map(correlate, by_channel)
    correlation = correlation.reshape(CHANNELS, 2, N_BROW, N_BCOL, SIG_DEV, N_BROW, N_BCOL, SIG_DEV)
    arranged = jnp.transpose(correlation, (5, 3, 0, 1, 2, 4, 6, 7))
    owner = jnp.transpose(tile_map.reshape(N_BROW, N_BCOL, N_BROW, N_BCOL), (0, 3, 2, 1))
    kept_mask = owner[:, :, None, None, :, None, :, None] == 1
    masked = jnp.where(kept_mask, arranged, jnp.zeros_like(arranged))
    return masked.reshape(N_BROW, N_BCOL, CHANNELS, 2, N_BROW * SIG_DEV, N_BCOL * SIG_DEV)
```

```python
import functools
import math

import jax
import jax.numpy as jnp
import ml_dtypes
import numpy as np
from jax import lax
from jax.experimental import pallas as pl
from jax.experimental.pallas import tpu as pltpu
from jax.sharding import PartitionSpec as P

NCHAN = 1024
HALF = NCHAN // 2
CHANNELS = 512
TAPS = 4
FIRST = 256
SIG = 8
LANES = 128
GROUP = 4
VMEM_BYTES = 48 * 1024 * 1024


def fir_coefficients():
    position = np.arange(TAPS * NCHAN, dtype=np.float64) + 0.5
    offsets = position / NCHAN - TAPS / 2.0
    window = 0.5 - 0.5 * np.cos(2.0 * math.pi * position / (TAPS * NCHAN))
    return (np.sinc(offsets) * window).reshape(TAPS, NCHAN)


def dft_tables(owners):
    width = CHANNELS // owners // 2
    n = np.arange(HALF, dtype=np.int64)[:, None]
    tables = []
    for parity in range(2):
        j = 2 * np.arange(CHANNELS // 2, dtype=np.int64)[None, :] + parity
        angles = (n * (FIRST + j) % NCHAN) * (2.0 * math.pi / NCHAN)
        cosine = np.cos(angles).reshape(HALF, owners, 1, width)
        sine = np.sin(angles).reshape(HALF, owners, 1, width)
        first = np.concatenate([cosine, -sine], axis=2).reshape(HALF, CHANNELS)
        second = np.concatenate([sine, cosine], axis=2).reshape(HALF, CHANNELS)
        tables.append(np.concatenate([first, second], axis=0))
    return np.stack(tables).astype(np.float32).astype(ml_dtypes.bfloat16)


def channelize_kernel(
    frames, pieces, owners, width, scale, volt_hbm, table_hbm, coef_ref, out_ref, volt, table, filt, sems
):
    per = frames // pieces
    lead = TAPS - 1
    copies = []
    for piece in range(pieces):
        copies.append(
            pltpu.make_async_copy(
                volt_hbm.at[:, :, pl.ds(piece * per * NCHAN, per * NCHAN)],
                volt.at[:, :, pl.ds((lead + piece * per) * NCHAN, per * NCHAN)],
                sems.at[piece],
            )
        )
    table_copy = pltpu.make_async_copy(table_hbm, table, sems.at[pieces])
    for copy in copies:
        copy.start()
    table_copy.start()
    tail = volt.shape[2] - (lead + frames) * NCHAN
    volt[:, :, : lead * NCHAN] = jnp.zeros((2, SIG, lead * NCHAN), jnp.int32)
    volt[:, :, (lead + frames) * NCHAN :] = jnp.zeros((2, SIG, tail), jnp.int32)

    def filter_group(group, _):
        base = pl.multiple_of(group * (GROUP * NCHAN), GROUP * NCHAN)
        rows = pl.ds(pl.multiple_of(group * (GROUP * SIG), GROUP * SIG), GROUP * SIG)
        for column in range(HALF // LANES):
            for part in range(2):
                halves = []
                for half in range(2):
                    lane = half * HALF + column * LANES
                    taps = [coef_ref[k : k + 1, lane : lane + LANES] for k in range(TAPS)]
                    near = [
                        volt[part, :, pl.ds(base + f * NCHAN + lane, LANES)].astype(jnp.float32)
                        for f in range(GROUP + TAPS - 1)
                    ]
                    sums = []
                    for m in range(GROUP):
                        total = taps[0] * near[m]
                        for k in range(1, TAPS):
                            total = total + taps[k] * near[m + k]
                        sums.append(total)
                    halves.append(jnp.concatenate(sums, axis=0))
                where = pl.ds(part * HALF + column * LANES, LANES)
                filt[0, rows, where] = (halves[0] + halves[1]).astype(jnp.bfloat16)
                filt[1, rows, where] = (halves[0] - halves[1]).astype(jnp.bfloat16)
        return 0

    groups = per // GROUP
    for piece in range(pieces):
        copies[piece].wait()
        lax.fori_loop(piece * groups, (piece + 1) * groups, filter_group, 0)
    lax.fori_loop(frames // GROUP, frames // GROUP + 1, filter_group, 0)
    table_copy.wait()
    for parity in range(2):
        spectrum = jnp.dot(filt[parity], table[parity], preferred_element_type=jnp.float32) * scale
        for owner in range(owners):
            out_ref[owner, :, parity * width : (parity + 1) * width] = spectrum[
                :, owner * width : (owner + 1) * width
            ].astype(jnp.bfloat16)


def channelize(voltages, owners):
    frames = voltages.shape[2] // NCHAN
    width = CHANNELS // owners
    coefficients = fir_coefficients()
    scale = float(1.0 / (128.0 * np.sqrt(np.sum(coefficients * coefficients))))
    rows = (frames + GROUP) * SIG
    pieces = 4
    kernel = functools.partial(channelize_kernel, frames, pieces, owners, width, scale)
    return pl.pallas_call(
        kernel,
        out_shape=jax.ShapeDtypeStruct((owners, rows, 2 * width), jnp.bfloat16),
        in_specs=[
            pl.BlockSpec(memory_space=pl.ANY),
            pl.BlockSpec(memory_space=pl.ANY),
            pl.BlockSpec(memory_space=pltpu.VMEM),
        ],
        out_specs=pl.BlockSpec(memory_space=pltpu.VMEM),
        scratch_shapes=[
            pltpu.VMEM((2, SIG, (frames + GROUP + TAPS - 1) * NCHAN), jnp.int32),
            pltpu.VMEM((2, NCHAN, CHANNELS), jnp.bfloat16),
            pltpu.VMEM((2, rows, NCHAN), jnp.bfloat16),
            pltpu.SemaphoreType.DMA((pieces + 1,)),
        ],
        compiler_params=pltpu.CompilerParams(vmem_limit_bytes=VMEM_BYTES),
        name="channelize",
    )(voltages, jnp.asarray(dft_tables(owners)), jnp.asarray(coefficients, jnp.float32))


def half_turn(x):
    h = x.shape[1] // 2
    return pltpu.roll(x, h, axis=1) if x.shape[1] == LANES else jnp.concatenate([x[:, h:], x[:, :h]], axis=1)


def equalize_kernel(owners, frames, width, turned_ref, direct_ref, cross_ref, out_ref, by_time, by_channel):
    own_rows = frames * SIG
    over = GROUP * SIG
    times = owners * frames
    tiles = times // LANES
    h = width // 2
    for parity in range(2):
        lanes = slice(parity * width, (parity + 1) * width)
        for source in range(owners):
            by_time[source * own_rows : (source + 1) * own_rows, :width] = turned_ref[source, :own_rows, lanes].astype(
                jnp.float32
            )
            if source > 0:
                start = source * own_rows
                by_time[start : start + over, :width] += turned_ref[source - 1, own_rows:, lanes].astype(jnp.float32)
        for s in range(SIG):
            x = by_time[pl.ds(s, times, stride=SIG), :][:, :width]
            y = x * direct_ref[parity, s : s + 1, :] + half_turn(x) * cross_ref[parity, s : s + 1, :]
            y = y.T
            for q in range(2):
                for tile in range(tiles):
                    by_channel[q * tiles + tile, pl.ds(s, h, stride=SIG), :] = y[
                        q * h : (q + 1) * h, tile * LANES : (tile + 1) * LANES
                    ]
        for tile in range(2 * tiles):
            out_ref[parity, :, tile * LANES : (tile + 1) * LANES] = by_channel[tile].astype(jnp.bfloat16)


def equalize(turned, gains, frames):
    owners = turned.shape[0]
    width = gains.shape[2]
    times = owners * frames
    h = width // 2
    split = jnp.transpose(gains.reshape(SIG, 2, h, 2), (3, 1, 0, 2))
    direct = jnp.concatenate([split[:, 0], split[:, 0]], axis=-1)
    cross = jnp.concatenate([-split[:, 1], split[:, 1]], axis=-1)
    return pl.pallas_call(
        functools.partial(equalize_kernel, owners, frames, width),
        out_shape=jax.ShapeDtypeStruct((2, h * SIG, 2 * times), jnp.bfloat16),
        in_specs=[pl.BlockSpec(memory_space=pltpu.VMEM)] * 3,
        out_specs=pl.BlockSpec(memory_space=pltpu.VMEM),
        scratch_shapes=[
            pltpu.VMEM((times * SIG, LANES), jnp.float32),
            pltpu.VMEM((2 * times // LANES, h * SIG, LANES), jnp.float32),
        ],
        compiler_params=pltpu.CompilerParams(vmem_limit_bytes=VMEM_BYTES),
        name="equalize",
    )(turned, direct, cross)


BATCH = 4


def correlate_kernel(n_row, n_col, h, times, map_ref, place_ref, *refs):
    blocks = refs[: n_col + n_row - 1]
    out_ref, row_panel, col_panel, product, sems = refs[n_col + n_row - 1 :]
    copies = []
    for i in range(n_col):
        copies.append(pltpu.make_async_copy(blocks[i], row_panel.at[place_ref[i]], sems.at[i]))
    for i in range(n_row):
        block = blocks[0] if i == 0 else blocks[n_col + i - 1]
        copies.append(pltpu.make_async_copy(block, col_panel.at[place_ref[n_col + i]], sems.at[n_col + i]))
    for copy in copies:
        copy.start()
    for copy in copies:
        copy.wait()
    rows = BATCH * SIG
    tiles = n_col * rows // LANES

    def batch(step, _):
        parity = step // (h // BATCH)
        inner = step % (h // BATCH)
        here = pl.ds(pl.multiple_of(inner * rows, rows), rows)
        a = jnp.concatenate([row_panel[c, parity, here, :] for c in range(n_col)], axis=0)
        b = jnp.concatenate([col_panel[c, parity, here, :] for c in range(n_row)], axis=0)
        turned = jnp.concatenate([-b[:, times:], b[:, :times]], axis=1)
        both = jnp.concatenate([b, turned], axis=0)
        result = lax.dot_general(both, a, (((1,), (1,)), ((), ())), preferred_element_type=jnp.float32)
        for k in range(2 * n_row):
            for i in range(BATCH):
                channel = 2 * (inner * BATCH + i) + parity
                for tile in range(tiles):
                    product[k * tiles + tile, pl.ds(pl.multiple_of(channel * SIG, SIG), SIG), :] = result[
                        k * rows + i * SIG : k * rows + (i + 1) * SIG, tile * LANES : (tile + 1) * LANES
                    ]
        return 0

    lax.fori_loop(0, 2 * h // BATCH, batch, 0, unroll=4)
    me_row = place_ref[n_col]
    me_col = place_ref[0]
    channels = 2 * h
    lane = lax.broadcasted_iota(jnp.int32, (SIG, channels), 1)
    inner_of = (lane // 2) % BATCH
    for q in range(2):
        for r2 in range(n_row):
            keeps = [
                jnp.where(map_ref[me_row * n_col + c2, r2 * n_col + me_col] == 1, 1.0 / times, 0.0)
                for c2 in range(n_col)
            ]
            for s2 in range(SIG):
                for c2 in range(n_col):
                    if c2 * rows % LANES == 0:
                        tile = (q * n_row + r2) * tiles + c2 * rows // LANES
                        x = product[tile, pl.ds(s2, channels, stride=SIG), :].T
                    start = c2 * rows % LANES
                    kept = x[start : start + SIG]
                    for i in range(1, BATCH):
                        kept = jnp.where(inner_of == i, x[start + i * SIG : start + (i + 1) * SIG], kept)
                    out_ref[q, r2 * SIG + s2, c2 * SIG : (c2 + 1) * SIG, :] = jnp.where(
                        keeps[c2] != 0.0, kept * keeps[c2], 0.0
                    )


def correlate(tile_map, place, blocks, n_row, n_col):
    h = blocks[0].shape[1] // SIG
    times = blocks[0].shape[2] // 2
    return pl.pallas_call(
        functools.partial(correlate_kernel, n_row, n_col, h, times),
        out_shape=jax.ShapeDtypeStruct((2, n_row * SIG, n_col * SIG, 2 * h), jnp.float32),
        in_specs=[pl.BlockSpec(memory_space=pltpu.SMEM)] * 2 + [pl.BlockSpec(memory_space=pl.ANY)] * len(blocks),
        out_specs=pl.BlockSpec(memory_space=pltpu.VMEM),
        scratch_shapes=[
            pltpu.VMEM((n_col,) + blocks[0].shape, jnp.bfloat16),
            pltpu.VMEM((n_row,) + blocks[0].shape, jnp.bfloat16),
            pltpu.VMEM((2 * n_row * n_col * BATCH * SIG // LANES, 2 * h * SIG, LANES), jnp.float32),
            pltpu.SemaphoreType.DMA((n_row + n_col,)),
        ],
        compiler_params=pltpu.CompilerParams(vmem_limit_bytes=VMEM_BYTES),
        name="correlate",
    )(tile_map, place, *blocks)


def shards(voltages, antenna_gains, tile_map):
    owners = lax.axis_size("chan")
    n_row = lax.axis_size("brow")
    n_col = lax.axis_size("bcol")
    frames = voltages.shape[2] // NCHAN
    row = lax.axis_index("brow")
    col = lax.axis_index("bcol")
    spectra = channelize(voltages, owners)
    turned = lax.all_to_all(spectra, "chan", split_axis=0, concat_axis=0, tiled=True)
    own = equalize(turned, antenna_gains, frames)

    chips = n_col // 2
    other_core = [(i, i ^ 1) for i in range(n_col)]
    blocks, places = [own], [col]
    far = []
    for d in range(1, chips):
        route = [(i, (i // 2 + d) % chips * 2 + i % 2) for i in range(n_col)]
        far.append(lax.ppermute(own, "bcol", route))
        places.append((col // 2 + chips - d) % chips * 2 + col % 2)
    blocks += far
    column = []
    for d in range(1, n_row):
        column.append(lax.ppermute(own, "brow", [(i, (i + d) % n_row) for i in range(n_row)]))
    near = [lax.ppermute(own, "bcol", other_core)]
    near += [lax.ppermute(block, "bcol", other_core) for block in far]
    blocks += near
    places += [p + 1 - 2 * (p % 2) for p in places]
    blocks += column
    places += [row] + [(row + n_row - d) % n_row for d in range(1, n_row)]
    place = jnp.stack(places).astype(jnp.int32)
    result = correlate(tile_map, place, blocks, n_row, n_col)
    return jnp.transpose(result, (3, 0, 1, 2))[None, None]


def solution(mesh):
    in_specs = (P(None, ("brow", "bcol"), "chan"), P(("brow", "bcol"), None, "chan"), P())
    out_specs = P("brow", "bcol", "chan", None, None, None)
    return jax.shard_map(shards, mesh=mesh, in_specs=in_specs, out_specs=out_specs, check_vma=False)
```

```python
import functools
import math

import jax
import jax.numpy as jnp
import ml_dtypes
import numpy as np
from jax import lax
from jax.experimental import pallas as pl
from jax.experimental.pallas import tpu as pltpu
from jax.sharding import PartitionSpec as P

NCHAN = 1024
HALF = NCHAN // 2
CHANNELS = 512
TAPS = 4
FIRST = 256
SIG = 8
LANES = 128
GROUP = 4
BATCH = 4
PARTS = 2
VMEM_BYTES = 48 * 1024 * 1024


def fir_coefficients():
    position = np.arange(TAPS * NCHAN, dtype=np.float64) + 0.5
    offsets = position / NCHAN - TAPS / 2.0
    window = 0.5 - 0.5 * np.cos(2.0 * math.pi * position / (TAPS * NCHAN))
    return (np.sinc(offsets) * window).reshape(TAPS, NCHAN)


def dft_tables(owners):
    n = np.arange(HALF, dtype=np.int64)[:, None, None, None, None]
    k = FIRST + np.arange(CHANNELS, dtype=np.int64).reshape(owners, PARTS, -1, 2)
    angles = (n * k % NCHAN) * (2.0 * math.pi / NCHAN)
    cosine, sine = np.cos(angles), np.sin(angles)
    first = np.stack([cosine, -sine], axis=2)
    second = np.stack([sine, cosine], axis=2)
    tables = np.stack([first, second])
    tables = np.transpose(tables, (4, 6, 0, 1, 2, 3, 5))
    return tables.reshape(PARTS, 2, NCHAN, -1).astype(np.float32).astype(ml_dtypes.bfloat16)


def transform(filt, table, scale, stage, out_refs):
    owners = len(out_refs)
    me = lax.axis_index("chan")
    spectra = [jnp.dot(filt[r], table[r], preferred_element_type=jnp.float32) * scale for r in range(2)]
    width = spectra[0].shape[1] // owners
    for owner in range(owners):
        here = slice(owner * width, (owner + 1) * width)
        piece = jnp.concatenate([spectra[0][:, here], spectra[1][:, here]], axis=1)
        stage[jnp.bitwise_xor(me, owner)] = piece.astype(jnp.bfloat16)
    for d in range(owners):
        out_refs[d][...] = stage[d]


def filter_kernel(frames, pieces, scale, volt_hbm, table_hbm, coef_ref, *refs):
    out_refs, filt, volt, table, stage, sems = refs[:-5], refs[-5], refs[-4], refs[-3], refs[-2], refs[-1]
    per = frames // pieces
    lead = TAPS - 1
    copies = []
    for piece in range(pieces):
        copies.append(
            pltpu.make_async_copy(
                volt_hbm.at[:, :, pl.ds(piece * per * NCHAN, per * NCHAN)],
                volt.at[:, :, pl.ds((lead + piece * per) * NCHAN, per * NCHAN)],
                sems.at[piece],
            )
        )
    table_copy = pltpu.make_async_copy(table_hbm, table, sems.at[pieces])
    for copy in copies:
        copy.start()
    table_copy.start()
    tail = volt.shape[2] - (lead + frames) * NCHAN
    volt[:, :, : lead * NCHAN] = jnp.zeros((2, SIG, lead * NCHAN), jnp.int32)
    volt[:, :, (lead + frames) * NCHAN :] = jnp.zeros((2, SIG, tail), jnp.int32)

    def filter_group(group, _):
        base = pl.multiple_of(group * (GROUP * NCHAN), GROUP * NCHAN)
        rows = pl.ds(pl.multiple_of(group * (GROUP * SIG), GROUP * SIG), GROUP * SIG)
        for column in range(HALF // LANES):
            for part in range(2):
                halves = []
                for half in range(2):
                    lane = half * HALF + column * LANES
                    taps = [coef_ref[k : k + 1, lane : lane + LANES] for k in range(TAPS)]
                    near = [
                        volt[part, :, pl.ds(base + f * NCHAN + lane, LANES)].astype(jnp.float32)
                        for f in range(GROUP + TAPS - 1)
                    ]
                    sums = []
                    for m in range(GROUP):
                        total = taps[0] * near[m]
                        for k in range(1, TAPS):
                            total = total + taps[k] * near[m + k]
                        sums.append(total)
                    halves.append(jnp.concatenate(sums, axis=0))
                where = pl.ds(part * HALF + column * LANES, LANES)
                filt[0, rows, where] = (halves[0] + halves[1]).astype(jnp.bfloat16)
                filt[1, rows, where] = (halves[0] - halves[1]).astype(jnp.bfloat16)
        return 0

    groups = per // GROUP
    for piece in range(pieces):
        copies[piece].wait()
        lax.fori_loop(piece * groups, (piece + 1) * groups, filter_group, 0)
    lax.fori_loop(frames // GROUP, frames // GROUP + 1, filter_group, 0)
    table_copy.wait()
    transform(filt, table, scale, stage, out_refs)


def transform_kernel(scale, filt, table_hbm, *refs):
    out_refs, table, stage, sem = refs[:-3], refs[-3], refs[-2], refs[-1]
    copy = pltpu.make_async_copy(table_hbm, table, sem)
    copy.start()
    copy.wait()
    transform(filt, table, scale, stage, out_refs)


IN_VMEM = pl.BlockSpec(memory_space=pltpu.VMEM)
IN_HBM = pl.BlockSpec(memory_space=pltpu.HBM)
IN_SMEM = pl.BlockSpec(memory_space=pltpu.SMEM)


def channelize(voltages, owners):
    frames = voltages.shape[2] // NCHAN
    coefficients = fir_coefficients()
    scale = float(1.0 / (128.0 * np.sqrt(np.sum(coefficients * coefficients))))
    rows = (frames + GROUP) * SIG
    pieces = 4
    tables = dft_tables(owners)
    lanes = 2 * CHANNELS // owners // PARTS
    params = pltpu.CompilerParams(vmem_limit_bytes=VMEM_BYTES)
    piece_shapes = [jax.ShapeDtypeStruct((rows, lanes), jnp.bfloat16)] * owners
    filt_shape = jax.ShapeDtypeStruct((2, rows, NCHAN), jnp.bfloat16)
    common = [pltpu.VMEM(tables.shape[1:], jnp.bfloat16), pltpu.VMEM((owners, rows, lanes), jnp.bfloat16)]
    flops = 2 * 2 * rows * NCHAN * CHANNELS // PARTS * 2
    *first, filt = pl.pallas_call(
        functools.partial(filter_kernel, frames, pieces, scale),
        out_shape=piece_shapes + [filt_shape],
        in_specs=[IN_HBM, IN_HBM, IN_VMEM],
        out_specs=[IN_VMEM] * (owners + 1),
        scratch_shapes=[pltpu.VMEM((2, SIG, (frames + GROUP + TAPS - 1) * NCHAN), jnp.int32)]
        + common
        + [pltpu.SemaphoreType.DMA((pieces + 1,))],
        compiler_params=params,
        cost_estimate=pl.CostEstimate(flops=flops, bytes_accessed=4 << 20, transcendentals=0),
        name="filter_and_transform",
    )(voltages, jnp.asarray(tables[0]), jnp.asarray(coefficients, jnp.float32))
    spectra = [first]
    for part in range(1, PARTS):
        spectra.append(
            pl.pallas_call(
                functools.partial(transform_kernel, scale),
                out_shape=piece_shapes,
                in_specs=[IN_VMEM, IN_HBM],
                out_specs=[IN_VMEM] * owners,
                scratch_shapes=common + [pltpu.SemaphoreType.DMA(())],
                compiler_params=params,
                cost_estimate=pl.CostEstimate(flops=flops, bytes_accessed=2 << 20, transcendentals=0),
                name="transform",
            )(filt, jnp.asarray(tables[part]))
        )
    return spectra


def swap_parts(x, h):
    return jnp.concatenate([x[:, i * h : (i + 1) * h] for i in (1, 0, 3, 2)], axis=1)


def equalize_kernel(owners, frames, h, *refs):
    pieces = refs[:owners]
    direct_ref, cross_ref, out_ref, by_time, by_channel = refs[owners:]
    width = 4 * h
    own_rows = frames * SIG
    over = GROUP * SIG
    times = owners * frames
    tiles = times // LANES
    me = lax.axis_index("chan")
    for d in range(owners):
        source = jnp.bitwise_xor(me, d)
        start = pl.multiple_of(source * own_rows, own_rows)
        by_time[pl.ds(start, own_rows), :width] = pieces[d][:own_rows, :].astype(jnp.float32)
    for d in range(owners):
        source = jnp.bitwise_xor(me, d)

        @pl.when(source < owners - 1)
        def _():
            start = pl.multiple_of((source + 1) * own_rows, own_rows)
            by_time[pl.ds(start, over), :width] += pieces[d][own_rows:, :].astype(jnp.float32)

    for s in range(SIG):
        x = by_time[pl.ds(s, times, stride=SIG), :][:, :width]
        y = x * direct_ref[s : s + 1, :] + swap_parts(x, h) * cross_ref[s : s + 1, :]
        y = y.T
        for r in range(2):
            for q in range(2):
                for tile in range(tiles):
                    by_channel[r * 2 * tiles + q * tiles + tile, pl.ds(s, h, stride=SIG), :] = y[
                        (2 * r + q) * h : (2 * r + q + 1) * h, tile * LANES : (tile + 1) * LANES
                    ]
    for r in range(2):
        for tile in range(2 * tiles):
            out_ref[r, :, tile * LANES : (tile + 1) * LANES] = by_channel[r * 2 * tiles + tile].astype(jnp.bfloat16)


def equalize(pieces, direct, cross, frames):
    owners = len(pieces)
    h = direct.shape[1] // 4
    times = owners * frames
    return pl.pallas_call(
        functools.partial(equalize_kernel, owners, frames, h),
        out_shape=jax.ShapeDtypeStruct((2, h * SIG, 2 * times), jnp.bfloat16),
        in_specs=[IN_VMEM] * (owners + 2),
        out_specs=IN_VMEM,
        scratch_shapes=[
            pltpu.VMEM((times * SIG, LANES), jnp.float32),
            pltpu.VMEM((4 * times // LANES, h * SIG, LANES), jnp.float32),
        ],
        compiler_params=pltpu.CompilerParams(vmem_limit_bytes=VMEM_BYTES),
        cost_estimate=pl.CostEstimate(flops=1 << 20, bytes_accessed=1 << 20, transcendentals=0),
        name="equalize",
    )(*pieces, direct, cross)


def row_places(col, n_col):
    chips = n_col // 2
    chip, core = lax.div(col, 2), lax.rem(col, 2)
    places = [col] + [lax.rem(chip + chips - d, chips) * 2 + core for d in range(1, chips)]
    return places + [jnp.bitwise_xor(p, 1) for p in places]


def column_places(row, n_row):
    return [row] + [lax.rem(row + n_row - d, n_row) for d in range(1, n_row)]


def correlate_kernel(n_row, n_col, h, times, before, map_ref, *refs):
    row_blocks = refs[:n_col]
    col_blocks = (refs[0],) + refs[n_col : n_col + n_row - 1]
    out_ref, product = refs[-2:]
    me_row, me_col = lax.axis_index("brow"), lax.axis_index("bcol")
    row_at, col_at = row_places(me_col, n_col), column_places(me_row, n_row)
    rows = BATCH * SIG
    tiles = n_col * rows // LANES

    def batch(step, _):
        parity = step // (h // BATCH)
        inner = step % (h // BATCH)
        here = pl.ds(pl.multiple_of(inner * rows, rows), rows)
        a = jnp.concatenate([block[parity, here, :] for block in row_blocks], axis=0)
        b = jnp.concatenate([block[parity, here, :] for block in col_blocks], axis=0)
        turned = jnp.concatenate([-b[:, times:], b[:, :times]], axis=1)
        both = jnp.concatenate([b, turned], axis=0)
        result = lax.dot_general(both, a, (((1,), (1,)), ((), ())), preferred_element_type=jnp.float32)
        for k in range(2 * n_row):
            for i in range(BATCH):
                channel = 2 * (inner * BATCH + i) + parity
                for tile in range(tiles):
                    product[k * tiles + tile, pl.ds(pl.multiple_of(channel * SIG, SIG), SIG), :] = result[
                        k * rows + i * SIG : k * rows + (i + 1) * SIG, tile * LANES : (tile + 1) * LANES
                    ]
        return 0

    lax.fori_loop(0, 2 * h // BATCH, batch, 0, unroll=4)
    channels = 2 * h
    lane = lax.broadcasted_iota(jnp.int32, (SIG, channels), 1)
    inner_of = (lane // 2) % BATCH
    for q in range(2):
        for e in range(n_row):
            owned = [map_ref[me_row * n_col + row_at[d], col_at[e] * n_col + me_col] == 1 for d in range(n_col)]
            for s2 in range(SIG):
                b_at = col_at[e] * SIG + s2
                for d in range(n_col):
                    if d * rows % LANES == 0:
                        tile = (q * n_row + e) * tiles + d * rows // LANES
                        x = product[tile, pl.ds(s2, channels, stride=SIG), :].T
                    start = d * rows % LANES
                    kept = x[start : start + SIG]
                    for i in range(1, BATCH):
                        kept = jnp.where(inner_of == i, x[start + i * SIG : start + (i + 1) * SIG], kept)
                    kept = jnp.where(owned[d], kept * (1.0 / times), 0.0)
                    a_at = pl.ds(pl.multiple_of(row_at[d] * SIG, SIG), SIG)
                    if before:
                        kept = jnp.concatenate([refs[-3][q, b_at, a_at, :], kept], axis=1)
                    out_ref[q, b_at, a_at, :] = kept


def correlate(tile_map, blocks, earlier, n_row, n_col):
    h = blocks[0].shape[1] // SIG
    times = blocks[0].shape[2] // 2
    before = earlier.shape[3] if earlier is not None else 0
    operands = list(blocks) + ([earlier] if before else [])
    return pl.pallas_call(
        functools.partial(correlate_kernel, n_row, n_col, h, times, before),
        out_shape=jax.ShapeDtypeStruct((2, n_row * SIG, n_col * SIG, before + 2 * h), jnp.float32),
        in_specs=[IN_SMEM] + [IN_VMEM] * len(operands),
        out_specs=IN_VMEM,
        scratch_shapes=[pltpu.VMEM((2 * n_row * n_col * BATCH * SIG // LANES, 2 * h * SIG, LANES), jnp.float32)],
        compiler_params=pltpu.CompilerParams(vmem_limit_bytes=VMEM_BYTES),
        cost_estimate=pl.CostEstimate(flops=1 << 29, bytes_accessed=4 << 20, transcendentals=0),
        name="correlate",
    )(tile_map, *operands)


def to_owners(pieces):
    owners = len(pieces)
    arrived = [pieces[0]] + [None] * (owners - 1)
    for d in range(owners - 1, 0, -1):
        arrived[d] = lax.ppermute(pieces[d], "chan", [(i, i ^ d) for i in range(owners)])
    return arrived


def gather(own, n_row, n_col):
    chips = n_col // 2
    other_core = [(i, i ^ 1) for i in range(n_col)]
    far = []
    for d in range(1, chips):
        far.append(lax.ppermute(own, "bcol", [(i, (i // 2 + d) % chips * 2 + i % 2) for i in range(n_col)]))
    column = []
    for d in range(1, n_row):
        column.append(lax.ppermute(own, "brow", [(i, (i + d) % n_row) for i in range(n_row)]))
    near = [lax.ppermute(block, "bcol", other_core) for block in [own] + far]
    return [own] + far + near + column


def shards(voltages, antenna_gains, tile_map):
    owners = lax.axis_size("chan")
    n_row = lax.axis_size("brow")
    n_col = lax.axis_size("bcol")
    frames = voltages.shape[2] // NCHAN
    h = antenna_gains.shape[2] // PARTS // 2
    gains = jnp.transpose(antenna_gains.reshape(SIG, 2, PARTS, h, 2), (2, 1, 0, 4, 3))
    direct = jnp.stack([gains[:, 0], gains[:, 0]], axis=3).reshape(PARTS, SIG, 4 * h)
    cross = jnp.stack([-gains[:, 1], gains[:, 1]], axis=3).reshape(PARTS, SIG, 4 * h)
    spectra = channelize(voltages, owners)
    arrived = [to_owners(pieces) for pieces in spectra]
    result = None
    panels = []
    for part in range(PARTS):
        panels.append(gather(equalize(arrived[part], direct[part], cross[part], frames), n_row, n_col))
    for part in range(PARTS):
        result = correlate(tile_map, panels[part], result, n_row, n_col)
    return jnp.transpose(result, (3, 0, 1, 2))[None, None]


def solution(mesh):
    in_specs = (P(None, ("brow", "bcol"), "chan"), P(("brow", "bcol"), None, "chan"), P())
    out_specs = P("brow", "bcol", "chan", None, None, None)
    return jax.shard_map(shards, mesh=mesh, in_specs=in_specs, out_specs=out_specs, check_vma=False)
```

```python
import functools
import math

import jax
import jax.numpy as jnp
import ml_dtypes
import numpy as np
from jax import lax
from jax.experimental import pallas as pl
from jax.experimental.pallas import tpu as pltpu
from jax.sharding import PartitionSpec as P

NCHAN = 1024
HALF = NCHAN // 2
CHANNELS = 512
TAPS = 4
FIRST = 256
SIG = 8
LANES = 128
GROUP = 4
BATCH = 4
PARTS = 2
VMEM_BYTES = 48 * 1024 * 1024
FILTER_VMEM_BYTES = 52 * 1024 * 1024
COEF_ROWS = 64


def fir_coefficients():
    position = np.arange(TAPS * NCHAN, dtype=np.float64) + 0.5
    offsets = position / NCHAN - TAPS / 2.0
    window = 0.5 - 0.5 * np.cos(2.0 * math.pi * position / (TAPS * NCHAN))
    return (np.sinc(offsets) * window).reshape(TAPS, NCHAN)


def spectrum_scale():
    return float(1.0 / (128.0 * np.sqrt(np.sum(fir_coefficients() ** 2))))


def dft_tables(owners):
    n = np.arange(HALF, dtype=np.int64)[:, None, None, None, None]
    k = FIRST + np.arange(CHANNELS, dtype=np.int64).reshape(owners, PARTS, -1, 2)
    angles = (n * k % NCHAN) * (2.0 * math.pi / NCHAN)
    cosine, sine = np.cos(angles), np.sin(angles)
    first = np.stack([cosine, -sine], axis=2)
    second = np.stack([sine, cosine], axis=2)
    tables = np.stack([first, second])
    tables = np.transpose(tables, (4, 6, 0, 1, 2, 3, 5))
    return tables.reshape(PARTS, 2 * NCHAN, -1).astype(np.float32).astype(ml_dtypes.bfloat16)


def constants(owners):
    tables = dft_tables(owners)
    lanes = tables.shape[2]
    left = fir_coefficients().astype(np.float32)
    terms = []
    for _ in range(3):
        terms.append(left.astype(ml_dtypes.bfloat16))
        left = left - terms[-1].astype(np.float32)
    terms = np.stack(terms).reshape(-1, lanes)
    pad = np.zeros((-terms.shape[0] % COEF_ROWS, lanes), ml_dtypes.bfloat16)
    return np.concatenate([tables.reshape(-1, lanes), terms, pad])


def transform(filt, table, scale, stage, out_refs):
    owners = len(out_refs)
    me = lax.axis_index("chan")
    spectra = [
        jnp.dot(filt[r], table[r * NCHAN : (r + 1) * NCHAN], preferred_element_type=jnp.float32) * scale
        for r in range(2)
    ]
    width = spectra[0].shape[1] // owners
    for owner in range(owners):
        here = slice(owner * width, (owner + 1) * width)
        piece = jnp.concatenate([spectra[0][:, here], spectra[1][:, here]], axis=1)
        stage[jnp.bitwise_xor(me, owner)] = piece.astype(jnp.bfloat16)
    for d in range(owners):
        out_refs[d][...] = stage[d]


def filter_kernel(frames, pieces, scale, volt_hbm, table_hbm, *refs):
    out_refs, (filt, volt, table, terms, coef, stage, sems) = refs[:-7], refs[-7:]
    per = frames // pieces
    lead = TAPS - 1
    copies = []
    for piece in range(pieces):
        copies.append(
            pltpu.make_async_copy(
                volt_hbm.at[:, :, pl.ds(piece * per * NCHAN, per * NCHAN)],
                volt.at[:, :, pl.ds((lead + piece * per) * NCHAN, per * NCHAN)],
                sems.at[piece],
            )
        )
    table_copy = pltpu.make_async_copy(table_hbm.at[pl.ds(0, 2 * NCHAN)], table, sems.at[pieces])
    coef_copy = pltpu.make_async_copy(
        table_hbm.at[pl.ds(PARTS * 2 * NCHAN, terms.shape[0])], terms, sems.at[pieces + 1]
    )
    coef_copy.start()
    for copy in copies:
        copy.start()
    table_copy.start()
    tail = volt.shape[2] - (lead + frames) * NCHAN
    volt[:, :, : lead * NCHAN] = jnp.zeros((2, SIG, lead * NCHAN), jnp.int32)
    volt[:, :, (lead + frames) * NCHAN :] = jnp.zeros((2, SIG, tail), jnp.int32)
    coef_copy.wait()
    across = coef.shape[1]
    per_term = TAPS * NCHAN // across
    coef[...] = sum(terms[t * per_term : (t + 1) * per_term, :].astype(jnp.float32) for t in range(3))

    def filter_group(group, _):
        base = pl.multiple_of(group * (GROUP * NCHAN), GROUP * NCHAN)
        rows = pl.ds(pl.multiple_of(group * (GROUP * SIG), GROUP * SIG), GROUP * SIG)
        for column in range(HALF // LANES):
            for part in range(2):
                halves = []
                for half in range(2):
                    lane = half * HALF + column * LANES
                    at = [k * (NCHAN // across) + lane // across for k in range(TAPS)]
                    taps = [coef[i : i + 1, lane % across : lane % across + LANES] for i in at]
                    near = [
                        volt[part, :, pl.ds(base + f * NCHAN + lane, LANES)].astype(jnp.float32)
                        for f in range(GROUP + TAPS - 1)
                    ]
                    sums = []
                    for m in range(GROUP):
                        total = taps[0] * near[m]
                        for k in range(1, TAPS):
                            total = total + taps[k] * near[m + k]
                        sums.append(total)
                    halves.append(jnp.concatenate(sums, axis=0))
                where = pl.ds(part * HALF + column * LANES, LANES)
                filt[0, rows, where] = (halves[0] + halves[1]).astype(jnp.bfloat16)
                filt[1, rows, where] = (halves[0] - halves[1]).astype(jnp.bfloat16)
        return 0

    groups = per // GROUP
    for piece in range(pieces):
        copies[piece].wait()
        lax.fori_loop(piece * groups, (piece + 1) * groups, filter_group, 0)
    lax.fori_loop(frames // GROUP, frames // GROUP + 1, filter_group, 0)
    table_copy.wait()
    transform(filt, table, scale, stage, out_refs)


def transform_kernel(part, scale, filt, table_hbm, *refs):
    out_refs, table, stage, sem = refs[:-3], refs[-3], refs[-2], refs[-1]
    copy = pltpu.make_async_copy(table_hbm.at[pl.ds(part * 2 * NCHAN, 2 * NCHAN)], table, sem)
    copy.start()
    copy.wait()
    transform(filt, table, scale, stage, out_refs)


IN_VMEM = pl.BlockSpec(memory_space=pltpu.VMEM)
IN_HBM = pl.BlockSpec(memory_space=pl.ANY)
IN_SMEM = pl.BlockSpec(memory_space=pltpu.SMEM)


def filtered_and_first(voltages, owners, table):
    frames = voltages.shape[2] // NCHAN
    rows = (frames + GROUP) * SIG
    pieces = 4
    across = table.shape[1]
    terms = table.shape[0] - PARTS * 2 * NCHAN
    lanes = 2 * CHANNELS // owners // PARTS
    *first, filt = pl.pallas_call(
        functools.partial(filter_kernel, frames, pieces, spectrum_scale()),
        out_shape=[jax.ShapeDtypeStruct((rows, lanes), jnp.bfloat16)] * owners
        + [jax.ShapeDtypeStruct((2, rows, NCHAN), jnp.bfloat16)],
        in_specs=[IN_HBM, IN_HBM],
        out_specs=[IN_VMEM] * (owners + 1),
        scratch_shapes=[
            pltpu.VMEM((2, SIG, (frames + GROUP + TAPS - 1) * NCHAN), jnp.int32),
            pltpu.VMEM((2 * NCHAN, across), jnp.bfloat16),
            pltpu.VMEM((terms, across), jnp.bfloat16),
            pltpu.VMEM((TAPS * NCHAN // across, across), jnp.float32),
            pltpu.VMEM((owners, rows, lanes), jnp.bfloat16),
            pltpu.SemaphoreType.DMA((pieces + 2,)),
        ],
        compiler_params=pltpu.CompilerParams(vmem_limit_bytes=FILTER_VMEM_BYTES),
        cost_estimate=pl.CostEstimate(flops=1 << 29, bytes_accessed=4 << 20, transcendentals=0),
        name="filter_and_transform",
    )(voltages, table)
    return filt, first


def next_part(part, filt, table, owners):
    rows = filt.shape[1]
    lanes = 2 * CHANNELS // owners // PARTS
    return pl.pallas_call(
        functools.partial(transform_kernel, part, spectrum_scale()),
        out_shape=[jax.ShapeDtypeStruct((rows, lanes), jnp.bfloat16)] * owners,
        in_specs=[IN_VMEM, IN_HBM],
        out_specs=[IN_VMEM] * owners,
        scratch_shapes=[
            pltpu.VMEM((2 * NCHAN, table.shape[1]), jnp.bfloat16),
            pltpu.VMEM((owners, rows, lanes), jnp.bfloat16),
            pltpu.SemaphoreType.DMA(()),
        ],
        compiler_params=pltpu.CompilerParams(vmem_limit_bytes=FILTER_VMEM_BYTES),
        cost_estimate=pl.CostEstimate(flops=1 << 29, bytes_accessed=2 << 20, transcendentals=0),
        name="transform",
    )(filt, table)


def equalize_kernel(owners, frames, h, part, before, *refs):
    pieces = refs[:owners]
    gains_ref, by_time, by_channel = refs[owners], refs[-2], refs[-1]
    earlier = refs[owners + 1 : owners + 1 + before]
    out_ref = refs[owners + 1 + before]
    if before:
        together = refs[owners + 2 + before]
        for i in range(before):
            together[i] = earlier[i][...]
    width = 4 * h
    own_rows = frames * SIG
    over = GROUP * SIG
    times = owners * frames
    tiles = times // LANES
    me = lax.axis_index("chan")
    for d in range(owners):
        source = jnp.bitwise_xor(me, d)
        start = pl.multiple_of(source * own_rows, own_rows)
        by_time[pl.ds(start, own_rows), :width] = pieces[d][:own_rows, :].astype(jnp.float32)
    for d in range(owners):
        source = jnp.bitwise_xor(me, d)

        @pl.when(source < owners - 1)
        def _():
            start = pl.multiple_of((source + 1) * own_rows, own_rows)
            by_time[pl.ds(start, over), :width] += pieces[d][own_rows:, :].astype(jnp.float32)

    gains = [gains_ref[pl.ds(part * 2 * h + r, h, stride=2), :] for r in range(2)]
    for s in range(SIG):
        x = by_time[pl.ds(s, times, stride=SIG), :][:, :width].T
        for r in range(2):
            real, imag = x[2 * r * h : (2 * r + 1) * h], x[(2 * r + 1) * h : (2 * r + 2) * h]
            gain_real, gain_imag = gains[r][:, 2 * s : 2 * s + 1], gains[r][:, 2 * s + 1 : 2 * s + 2]
            both = [real * gain_real - imag * gain_imag, real * gain_imag + imag * gain_real]
            for q in range(2):
                for tile in range(tiles):
                    by_channel[(2 * r + q) * tiles + tile, pl.ds(s, h, stride=SIG), :] = both[q][
                        :, tile * LANES : (tile + 1) * LANES
                    ]
    for r in range(2):
        for tile in range(2 * tiles):
            ready = by_channel[r * 2 * tiles + tile].astype(jnp.bfloat16)
            out_ref[r, :, tile * LANES : (tile + 1) * LANES] = ready
            if before:
                together[before, r, :, tile * LANES : (tile + 1) * LANES] = ready


def equalize(pieces, gains, earlier, part, frames):
    owners = len(pieces)
    h = gains.shape[0] // PARTS // 2
    times = owners * frames
    before = len(earlier)
    shape = (2, h * SIG, 2 * times)
    shapes = [jax.ShapeDtypeStruct(shape, jnp.bfloat16)]
    if before:
        shapes.append(jax.ShapeDtypeStruct((before + 1,) + shape, jnp.bfloat16))
    return pl.pallas_call(
        functools.partial(equalize_kernel, owners, frames, h, part, before),
        out_shape=shapes,
        in_specs=[IN_VMEM] * (owners + 1 + before),
        out_specs=[IN_VMEM] * len(shapes),
        scratch_shapes=[
            pltpu.VMEM((times * SIG, LANES), jnp.float32),
            pltpu.VMEM((4 * times // LANES, h * SIG, LANES), jnp.float32),
        ],
        compiler_params=pltpu.CompilerParams(vmem_limit_bytes=VMEM_BYTES),
        cost_estimate=pl.CostEstimate(flops=1 << 20, bytes_accessed=1 << 20, transcendentals=0),
        name="equalize",
    )(*pieces, gains, *earlier)


def row_places(col, n_col):
    chips = n_col // 2
    chip, core = lax.div(col, 2), lax.rem(col, 2)
    places = [col] + [lax.rem(chip + chips - d, chips) * 2 + core for d in range(1, chips)]
    return places + [jnp.bitwise_xor(p, 1) for p in places]


def column_places(row, n_row):
    return [row] + [lax.rem(row + n_row - d, n_row) for d in range(1, n_row)]


def correlate_kernel(n_row, n_col, h, times, part, before, map_ref, *refs):
    row_blocks = [ref.at[part] if i == n_col // 2 else ref for i, ref in enumerate(refs[:n_col])]
    col_blocks = (refs[0],) + refs[n_col : n_col + n_row - 1]
    last = part == PARTS - 1
    if last:
        out_hbm, product, out_ref, sems = refs[-4:]
        earlier = refs[-5]
    else:
        out_ref, product = refs[-2:]
        earlier = refs[-3]
    copies = []
    me_row, me_col = lax.axis_index("brow"), lax.axis_index("bcol")
    row_at, col_at = row_places(me_col, n_col), column_places(me_row, n_row)
    rows = BATCH * SIG
    tiles = n_col * rows // LANES

    def batch(step, _):
        parity = step // (h // BATCH)
        inner = step % (h // BATCH)
        here = pl.ds(pl.multiple_of(inner * rows, rows), rows)
        a = jnp.concatenate([block[parity, here, :] for block in row_blocks], axis=0)
        b = jnp.concatenate([block[parity, here, :] for block in col_blocks], axis=0)
        turned = jnp.concatenate([-b[:, times:], b[:, :times]], axis=1)
        both = jnp.concatenate([b, turned], axis=0)
        result = lax.dot_general(both, a, (((1,), (1,)), ((), ())), preferred_element_type=jnp.float32)
        for k in range(2 * n_row):
            for i in range(BATCH):
                channel = 2 * (inner * BATCH + i) + parity
                for tile in range(tiles):
                    product[k * tiles + tile, pl.ds(pl.multiple_of(channel * SIG, SIG), SIG), :] = result[
                        k * rows + i * SIG : k * rows + (i + 1) * SIG, tile * LANES : (tile + 1) * LANES
                    ]
        return 0

    lax.fori_loop(0, 2 * h // BATCH, batch, 0, unroll=4)
    channels = 2 * h
    lane = lax.broadcasted_iota(jnp.int32, (SIG, channels), 1)
    inner_of = (lane // 2) % BATCH
    for q in range(2):
        for e in range(n_row):
            owned = [map_ref[me_row * n_col + row_at[d], col_at[e] * n_col + me_col] == 1 for d in range(n_col)]
            for s2 in range(SIG):
                b_at = col_at[e] * SIG + s2
                for d in range(n_col):
                    if d * rows % LANES == 0:
                        tile = (q * n_row + e) * tiles + d * rows // LANES
                        x = product[tile, pl.ds(s2, channels, stride=SIG), :].T
                    start = d * rows % LANES
                    kept = x[start : start + SIG]
                    for i in range(1, BATCH):
                        kept = jnp.where(inner_of == i, x[start + i * SIG : start + (i + 1) * SIG], kept)
                    kept = jnp.where(owned[d], kept * (1.0 / times), 0.0)
                    a_at = pl.ds(pl.multiple_of(row_at[d] * SIG, SIG), SIG)
                    if before:
                        kept = jnp.concatenate([earlier[q, b_at, a_at, :], kept], axis=1)
                    out_ref[q, b_at, a_at, :] = kept
            if last:
                where = pl.ds(pl.multiple_of(col_at[e] * SIG, SIG), SIG)
                copy = pltpu.make_async_copy(out_ref.at[q, where], out_hbm.at[q, where], sems.at[q * n_row + e])
                copy.start()
                copies.append(copy)
    for copy in copies:
        copy.wait()


def correlate(tile_map, blocks, earlier, part, n_row, n_col):
    h = blocks[0].shape[1] // SIG
    times = blocks[0].shape[2] // 2
    before = earlier.shape[3] if earlier is not None else 0
    operands = list(blocks) + ([earlier] if before else [])
    last = part == PARTS - 1
    out_shape = (2, n_row * SIG, n_col * SIG, before + 2 * h)
    in_last = [pltpu.VMEM(out_shape, jnp.float32), pltpu.SemaphoreType.DMA((2 * n_row,))]
    return pl.pallas_call(
        functools.partial(correlate_kernel, n_row, n_col, h, times, part, before),
        out_shape=jax.ShapeDtypeStruct(out_shape, jnp.float32),
        in_specs=[IN_SMEM] + [IN_VMEM] * len(operands),
        out_specs=IN_HBM if last else IN_VMEM,
        scratch_shapes=[pltpu.VMEM((2 * n_row * n_col * BATCH * SIG // LANES, 2 * h * SIG, LANES), jnp.float32)]
        + (in_last if last else []),
        compiler_params=pltpu.CompilerParams(vmem_limit_bytes=VMEM_BYTES),
        cost_estimate=pl.CostEstimate(flops=1 << 29, bytes_accessed=4 << 20, transcendentals=0),
        name="correlate",
    )(tile_map, *operands)


def to_owners(pieces):
    owners = len(pieces)
    arrived = [pieces[0]] + [None] * (owners - 1)
    for d in range(owners - 1, 0, -1):
        arrived[d] = lax.ppermute(pieces[d], "chan", [(i, i ^ d) for i in range(owners)])
    return arrived


def held_back(blocks, after):
    return pl.pallas_call(
        lambda *refs: None,
        out_shape=[jax.ShapeDtypeStruct(block.shape, block.dtype) for block in blocks],
        in_specs=[IN_HBM] * (len(blocks) + len(after)),
        out_specs=[IN_HBM] * len(blocks),
        input_output_aliases={i: i for i in range(len(blocks))},
        name="held_back",
    )(*blocks, *after)


def shards(voltages, antenna_gains, tile_map):
    owners = lax.axis_size("chan")
    n_row = lax.axis_size("brow")
    n_col = lax.axis_size("bcol")
    chips = n_col // 2
    frames = voltages.shape[2] // NCHAN
    table = jnp.asarray(constants(owners))
    gains = jnp.transpose(antenna_gains, (2, 0, 1)).reshape(-1, 2 * SIG)
    pad = -gains.shape[1] % LANES
    gains = jnp.pad(gains, ((0, 0), (0, pad)))
    across = [[(i, (i // 2 + d) % chips * 2 + i % 2) for i in range(n_col)] for d in range(chips)]
    along = [[(i, (i + d) % n_row) for i in range(n_row)] for d in range(n_row)]
    other_core = [(i, i ^ 1) for i in range(n_col)]

    filt, pieces = filtered_and_first(voltages, owners, table)
    own, far, column = [], [], []
    arrived = to_owners(pieces)
    for part in range(PARTS):
        later = None
        if part < PARTS - 1:
            pieces = next_part(part + 1, filt, table, owners)
            later = to_owners([pieces[0], *held_back(pieces[1:], arrived[-1:])])
        block, *together = equalize(arrived, gains, own if part == PARTS - 1 else [], part, frames)
        own.append(block)
        far.append([lax.ppermute(block, "bcol", across[d]) for d in range(1, chips)])
        column.append([lax.ppermute(block, "brow", along[d]) for d in range(1, n_row)])
        arrived = later
    beside = lax.ppermute(together[0], "bcol", other_core)
    result = None
    for part in range(PARTS):
        if far[part]:
            far[part] = list(held_back(far[part], own[-1:] + column[part]))
        near = [lax.ppermute(block, "bcol", other_core) for block in far[part]]
        blocks = [own[part]] + far[part] + [beside] + near + column[part]
        result = correlate(tile_map, blocks, result, part, n_row, n_col)
    return jnp.transpose(result, (3, 0, 1, 2))[None, None]


def solution(mesh):
    in_specs = (P(None, ("brow", "bcol"), "chan"), P(("brow", "bcol"), None, "chan"), P())
    out_specs = P("brow", "bcol", "chan", None, None, None)
    return jax.shard_map(shards, mesh=mesh, in_specs=in_specs, out_specs=out_specs, check_vma=False)
```

```python
import functools
import math

import jax
import jax.numpy as jnp
import ml_dtypes
import numpy as np
from jax import lax
from jax.experimental import pallas as pl
from jax.experimental.pallas import tpu as pltpu
from jax.sharding import PartitionSpec as P

NCHAN = 1024
HALF = NCHAN // 2
CHANNELS = 512
TAPS = 4
FIRST = 256
SIG = 8
LANES = 128
GROUP = 4
BATCH = 4
PARTS = 2
VMEM_BYTES = 48 * 1024 * 1024
FILTER_VMEM_BYTES = 52 * 1024 * 1024
COEF_ROWS = 64


def fir_coefficients():
    position = np.arange(TAPS * NCHAN, dtype=np.float64) + 0.5
    offsets = position / NCHAN - TAPS / 2.0
    window = 0.5 - 0.5 * np.cos(2.0 * math.pi * position / (TAPS * NCHAN))
    return (np.sinc(offsets) * window).reshape(TAPS, NCHAN)


def spectrum_scale():
    return float(1.0 / (128.0 * np.sqrt(np.sum(fir_coefficients() ** 2))))


def dft_tables(owners):
    n = np.arange(HALF, dtype=np.int64)[:, None, None, None, None]
    k = FIRST + np.arange(CHANNELS, dtype=np.int64).reshape(owners, PARTS, -1, 2)
    angles = (n * k % NCHAN) * (2.0 * math.pi / NCHAN)
    cosine, sine = np.cos(angles), np.sin(angles)
    first = np.stack([cosine, -sine], axis=2)
    second = np.stack([sine, cosine], axis=2)
    tables = np.stack([first, second])
    tables = np.transpose(tables, (4, 6, 0, 1, 2, 3, 5))
    return tables.reshape(PARTS, 2 * NCHAN, -1).astype(np.float32).astype(ml_dtypes.bfloat16)


def constants(owners):
    tables = dft_tables(owners)
    lanes = tables.shape[2]
    left = fir_coefficients().astype(np.float32)
    terms = []
    for _ in range(3):
        terms.append(left.astype(ml_dtypes.bfloat16))
        left = left - terms[-1].astype(np.float32)
    terms = np.stack(terms).reshape(-1, lanes)
    pad = np.zeros((-terms.shape[0] % COEF_ROWS, lanes), ml_dtypes.bfloat16)
    return np.concatenate([tables.reshape(-1, lanes), terms, pad])


def transform(filt, table, scale, stage, out_refs):
    owners = len(out_refs)
    me = lax.axis_index("chan")
    spectra = [
        jnp.dot(filt[r], table[r * NCHAN : (r + 1) * NCHAN], preferred_element_type=jnp.float32) * scale
        for r in range(2)
    ]
    width = spectra[0].shape[1] // owners
    for owner in range(owners):
        here = slice(owner * width, (owner + 1) * width)
        piece = jnp.concatenate([spectra[0][:, here], spectra[1][:, here]], axis=1)
        stage[jnp.bitwise_xor(me, owner)] = piece.astype(jnp.bfloat16)
    for d in range(owners):
        out_refs[d][...] = stage[d]


def filter_kernel(frames, pieces, scale, volt_hbm, table_hbm, *refs):
    out_refs, (filt, volt, table, terms, coef, stage, sems) = refs[:-7], refs[-7:]
    per = frames // pieces
    lead = TAPS - 1
    copies = []
    for piece in range(pieces):
        copies.append(
            pltpu.make_async_copy(
                volt_hbm.at[:, :, pl.ds(piece * per * NCHAN, per * NCHAN)],
                volt.at[:, :, pl.ds((lead + piece * per) * NCHAN, per * NCHAN)],
                sems.at[piece],
            )
        )
    table_copy = pltpu.make_async_copy(table_hbm.at[pl.ds(0, 2 * NCHAN)], table, sems.at[pieces])
    coef_copy = pltpu.make_async_copy(
        table_hbm.at[pl.ds(PARTS * 2 * NCHAN, terms.shape[0])], terms, sems.at[pieces + 1]
    )
    coef_copy.start()
    for copy in copies:
        copy.start()
    table_copy.start()
    tail = volt.shape[2] - (lead + frames) * NCHAN
    volt[:, :, : lead * NCHAN] = jnp.zeros((2, SIG, lead * NCHAN), jnp.int32)
    volt[:, :, (lead + frames) * NCHAN :] = jnp.zeros((2, SIG, tail), jnp.int32)
    coef_copy.wait()
    across = coef.shape[1]
    per_term = TAPS * NCHAN // across
    coef[...] = sum(terms[t * per_term : (t + 1) * per_term, :].astype(jnp.float32) for t in range(3))

    def filter_group(group, _):
        base = pl.multiple_of(group * (GROUP * NCHAN), GROUP * NCHAN)
        rows = pl.ds(pl.multiple_of(group * (GROUP * SIG), GROUP * SIG), GROUP * SIG)
        for column in range(HALF // LANES):
            for part in range(2):
                halves = []
                for half in range(2):
                    lane = half * HALF + column * LANES
                    at = [k * (NCHAN // across) + lane // across for k in range(TAPS)]
                    taps = [coef[i : i + 1, lane % across : lane % across + LANES] for i in at]
                    near = [
                        volt[part, :, pl.ds(base + f * NCHAN + lane, LANES)].astype(jnp.float32)
                        for f in range(GROUP + TAPS - 1)
                    ]
                    sums = []
                    for m in range(GROUP):
                        total = taps[0] * near[m]
                        for k in range(1, TAPS):
                            total = total + taps[k] * near[m + k]
                        sums.append(total)
                    halves.append(jnp.concatenate(sums, axis=0))
                where = pl.ds(part * HALF + column * LANES, LANES)
                filt[0, rows, where] = (halves[0] + halves[1]).astype(jnp.bfloat16)
                filt[1, rows, where] = (halves[0] - halves[1]).astype(jnp.bfloat16)
        return 0

    groups = per // GROUP
    for piece in range(pieces):
        copies[piece].wait()
        lax.fori_loop(piece * groups, (piece + 1) * groups, filter_group, 0)
    lax.fori_loop(frames // GROUP, frames // GROUP + 1, filter_group, 0)
    table_copy.wait()
    transform(filt, table, scale, stage, out_refs)


def transform_kernel(part, scale, filt, table_hbm, *refs):
    out_refs, table, stage, sem = refs[:-3], refs[-3], refs[-2], refs[-1]
    copy = pltpu.make_async_copy(table_hbm.at[pl.ds(part * 2 * NCHAN, 2 * NCHAN)], table, sem)
    copy.start()
    copy.wait()
    transform(filt, table, scale, stage, out_refs)


IN_VMEM = pl.BlockSpec(memory_space=pltpu.VMEM)
IN_HBM = pl.BlockSpec(memory_space=pl.ANY)
IN_SMEM = pl.BlockSpec(memory_space=pltpu.SMEM)


def filtered_and_first(voltages, owners, table):
    frames = voltages.shape[2] // NCHAN
    rows = (frames + GROUP) * SIG
    pieces = 4
    across = table.shape[1]
    terms = table.shape[0] - PARTS * 2 * NCHAN
    lanes = 2 * CHANNELS // owners // PARTS
    *first, filt = pl.pallas_call(
        functools.partial(filter_kernel, frames, pieces, spectrum_scale()),
        out_shape=[jax.ShapeDtypeStruct((rows, lanes), jnp.bfloat16)] * owners
        + [jax.ShapeDtypeStruct((2, rows, NCHAN), jnp.bfloat16)],
        in_specs=[IN_HBM, IN_HBM],
        out_specs=[IN_VMEM] * (owners + 1),
        scratch_shapes=[
            pltpu.VMEM((2, SIG, (frames + GROUP + TAPS - 1) * NCHAN), jnp.int32),
            pltpu.VMEM((2 * NCHAN, across), jnp.bfloat16),
            pltpu.VMEM((terms, across), jnp.bfloat16),
            pltpu.VMEM((TAPS * NCHAN // across, across), jnp.float32),
            pltpu.VMEM((owners, rows, lanes), jnp.bfloat16),
            pltpu.SemaphoreType.DMA((pieces + 2,)),
        ],
        compiler_params=pltpu.CompilerParams(vmem_limit_bytes=FILTER_VMEM_BYTES),
        cost_estimate=pl.CostEstimate(flops=1 << 29, bytes_accessed=4 << 20, transcendentals=0),
        name="filter_and_transform",
    )(voltages, table)
    return filt, first


def next_part(part, filt, table, owners):
    rows = filt.shape[1]
    lanes = 2 * CHANNELS // owners // PARTS
    return pl.pallas_call(
        functools.partial(transform_kernel, part, spectrum_scale()),
        out_shape=[jax.ShapeDtypeStruct((rows, lanes), jnp.bfloat16)] * owners,
        in_specs=[IN_VMEM, IN_HBM],
        out_specs=[IN_VMEM] * owners,
        scratch_shapes=[
            pltpu.VMEM((2 * NCHAN, table.shape[1]), jnp.bfloat16),
            pltpu.VMEM((owners, rows, lanes), jnp.bfloat16),
            pltpu.SemaphoreType.DMA(()),
        ],
        compiler_params=pltpu.CompilerParams(vmem_limit_bytes=FILTER_VMEM_BYTES),
        cost_estimate=pl.CostEstimate(flops=1 << 29, bytes_accessed=2 << 20, transcendentals=0),
        name="transform",
    )(filt, table)


def equalize_kernel(owners, frames, h, part, *refs):
    pieces = refs[:owners]
    gains_ref, by_time, by_channel = refs[owners], refs[-2], refs[-1]
    out_ref = refs[owners + 1]
    width = 4 * h
    own_rows = frames * SIG
    over = GROUP * SIG
    times = owners * frames
    tiles = times // LANES
    me = lax.axis_index("chan")
    for d in range(owners):
        source = jnp.bitwise_xor(me, d)
        start = pl.multiple_of(source * own_rows, own_rows)
        by_time[pl.ds(start, own_rows), :width] = pieces[d][:own_rows, :].astype(jnp.float32)
    for d in range(owners):
        source = jnp.bitwise_xor(me, d)

        @pl.when(source < owners - 1)
        def _():
            start = pl.multiple_of((source + 1) * own_rows, own_rows)
            by_time[pl.ds(start, over), :width] += pieces[d][own_rows:, :].astype(jnp.float32)

    gains = [gains_ref[pl.ds(part * 2 * h + r, h, stride=2), :] for r in range(2)]
    for s in range(SIG):
        x = by_time[pl.ds(s, times, stride=SIG), :][:, :width].T
        for r in range(2):
            real, imag = x[2 * r * h : (2 * r + 1) * h], x[(2 * r + 1) * h : (2 * r + 2) * h]
            gain_real, gain_imag = gains[r][:, 2 * s : 2 * s + 1], gains[r][:, 2 * s + 1 : 2 * s + 2]
            both = [real * gain_real - imag * gain_imag, real * gain_imag + imag * gain_real]
            for q in range(2):
                for tile in range(tiles):
                    by_channel[(2 * r + q) * tiles + tile, pl.ds(s, h, stride=SIG), :] = both[q][
                        :, tile * LANES : (tile + 1) * LANES
                    ]
    for r in range(2):
        for tile in range(2 * tiles):
            out_ref[r, :, tile * LANES : (tile + 1) * LANES] = by_channel[r * 2 * tiles + tile].astype(jnp.bfloat16)


def equalize(pieces, gains, part, frames):
    owners = len(pieces)
    h = gains.shape[0] // PARTS // 2
    times = owners * frames
    return pl.pallas_call(
        functools.partial(equalize_kernel, owners, frames, h, part),
        out_shape=jax.ShapeDtypeStruct((2, h * SIG, 2 * times), jnp.bfloat16),
        in_specs=[IN_VMEM] * (owners + 1),
        out_specs=IN_VMEM,
        scratch_shapes=[
            pltpu.VMEM((times * SIG, LANES), jnp.float32),
            pltpu.VMEM((4 * times // LANES, h * SIG, LANES), jnp.float32),
        ],
        compiler_params=pltpu.CompilerParams(vmem_limit_bytes=VMEM_BYTES),
        cost_estimate=pl.CostEstimate(flops=0, bytes_accessed=1 << 10, transcendentals=0),
        name="equalize",
    )(*pieces, gains)


def row_places(col, n_col):
    chips = n_col // 2
    chip, core = lax.div(col, 2), lax.rem(col, 2)
    places = [col] + [lax.rem(chip + chips - d, chips) * 2 + core for d in range(1, chips)]
    return places + [jnp.bitwise_xor(p, 1) for p in places]


def column_places(row, n_row):
    return [row] + [lax.rem(row + n_row - d, n_row) for d in range(1, n_row)]


def correlate_kernel(n_row, n_col, h, times, part, before, map_ref, *refs):
    row_blocks = [ref.at[part] if i == n_col // 2 else ref for i, ref in enumerate(refs[:n_col])]
    col_blocks = (refs[0],) + refs[n_col : n_col + n_row - 1]
    last = part == PARTS - 1
    if last:
        out_hbm, product, out_ref, sems = refs[-4:]
        earlier = refs[-5]
    else:
        out_ref, product = refs[-2:]
        earlier = refs[-3]
    copies = []
    me_row, me_col = lax.axis_index("brow"), lax.axis_index("bcol")
    row_at, col_at = row_places(me_col, n_col), column_places(me_row, n_row)
    rows = BATCH * SIG
    tiles = n_col * rows // LANES

    def batch(step, _):
        parity = step // (h // BATCH)
        inner = step % (h // BATCH)
        here = pl.ds(pl.multiple_of(inner * rows, rows), rows)
        a = jnp.concatenate([block[parity, here, :] for block in row_blocks], axis=0)
        b = jnp.concatenate([block[parity, here, :] for block in col_blocks], axis=0)
        turned = jnp.concatenate([-b[:, times:], b[:, :times]], axis=1)
        both = jnp.concatenate([b, turned], axis=0)
        result = lax.dot_general(both, a, (((1,), (1,)), ((), ())), preferred_element_type=jnp.float32)
        for k in range(2 * n_row):
            for i in range(BATCH):
                channel = 2 * (inner * BATCH + i) + parity
                for tile in range(tiles):
                    product[k * tiles + tile, pl.ds(pl.multiple_of(channel * SIG, SIG), SIG), :] = result[
                        k * rows + i * SIG : k * rows + (i + 1) * SIG, tile * LANES : (tile + 1) * LANES
                    ]
        return 0

    lax.fori_loop(0, 2 * h // BATCH, batch, 0, unroll=4)
    channels = 2 * h
    lane = lax.broadcasted_iota(jnp.int32, (SIG, channels), 1)
    inner_of = (lane // 2) % BATCH
    for q in range(2):
        for e in range(n_row):
            owned = [map_ref[me_row * n_col + row_at[d], col_at[e] * n_col + me_col] == 1 for d in range(n_col)]
            for s2 in range(SIG):
                b_at = col_at[e] * SIG + s2
                for d in range(n_col):
                    if d * rows % LANES == 0:
                        tile = (q * n_row + e) * tiles + d * rows // LANES
                        x = product[tile, pl.ds(s2, channels, stride=SIG), :].T
                    start = d * rows % LANES
                    kept = x[start : start + SIG]
                    for i in range(1, BATCH):
                        kept = jnp.where(inner_of == i, x[start + i * SIG : start + (i + 1) * SIG], kept)
                    kept = jnp.where(owned[d], kept * (1.0 / times), 0.0)
                    a_at = pl.ds(pl.multiple_of(row_at[d] * SIG, SIG), SIG)
                    if before:
                        kept = jnp.concatenate([earlier[q, b_at, a_at, :], kept], axis=1)
                    out_ref[q, b_at, a_at, :] = kept
            if last:
                where = pl.ds(pl.multiple_of(col_at[e] * SIG, SIG), SIG)
                copy = pltpu.make_async_copy(out_ref.at[q, where], out_hbm.at[q, where], sems.at[q * n_row + e])
                copy.start()
                copies.append(copy)
    for copy in copies:
        copy.wait()


def correlate(tile_map, blocks, earlier, part, n_row, n_col):
    h = blocks[0].shape[1] // SIG
    times = blocks[0].shape[2] // 2
    before = earlier.shape[3] if earlier is not None else 0
    operands = list(blocks) + ([earlier] if before else [])
    last = part == PARTS - 1
    out_shape = (2, n_row * SIG, n_col * SIG, before + 2 * h)
    in_last = [pltpu.VMEM(out_shape, jnp.float32), pltpu.SemaphoreType.DMA((2 * n_row,))]
    return pl.pallas_call(
        functools.partial(correlate_kernel, n_row, n_col, h, times, part, before),
        out_shape=jax.ShapeDtypeStruct(out_shape, jnp.float32),
        in_specs=[IN_SMEM] + [IN_VMEM] * len(operands),
        out_specs=IN_HBM if last else IN_VMEM,
        scratch_shapes=[pltpu.VMEM((2 * n_row * n_col * BATCH * SIG // LANES, 2 * h * SIG, LANES), jnp.float32)]
        + (in_last if last else []),
        compiler_params=pltpu.CompilerParams(vmem_limit_bytes=VMEM_BYTES),
        cost_estimate=pl.CostEstimate(flops=0, bytes_accessed=1 << 10, transcendentals=0),
        name="correlate",
    )(tile_map, *operands)


def to_owners(pieces):
    owners = len(pieces)
    arrived = [pieces[0]] + [None] * (owners - 1)
    for d in range(owners - 1, 0, -1):
        arrived[d] = lax.ppermute(pieces[d], "chan", [(i, i ^ d) for i in range(owners)])
    return arrived


def held_back(blocks, after):
    def kernel(*refs):
        for i in range(len(blocks)):
            refs[len(blocks) + len(after) + i][...] = refs[i][...]

    return pl.pallas_call(
        kernel,
        out_shape=[jax.ShapeDtypeStruct(block.shape, block.dtype) for block in blocks],
        in_specs=[IN_VMEM] * (len(blocks) + len(after)),
        out_specs=[IN_VMEM] * len(blocks),
        cost_estimate=pl.CostEstimate(flops=0, bytes_accessed=1 << 10, transcendentals=0),
        name="held_back",
    )(*blocks, *after)


def together(blocks):
    def kernel(*refs):
        for i in range(len(blocks)):
            refs[-1][i] = refs[i][...]

    return pl.pallas_call(
        kernel,
        out_shape=jax.ShapeDtypeStruct((len(blocks),) + blocks[0].shape, blocks[0].dtype),
        in_specs=[IN_VMEM] * len(blocks),
        out_specs=IN_VMEM,
        cost_estimate=pl.CostEstimate(flops=0, bytes_accessed=1 << 10, transcendentals=0),
        name="together",
    )(*blocks)


def shards(voltages, antenna_gains, tile_map):
    owners = lax.axis_size("chan")
    n_row = lax.axis_size("brow")
    n_col = lax.axis_size("bcol")
    chips = n_col // 2
    frames = voltages.shape[2] // NCHAN
    table = jnp.asarray(constants(owners))
    gains = jnp.transpose(antenna_gains, (2, 0, 1)).reshape(-1, 2 * SIG)
    pad = -gains.shape[1] % LANES
    gains = jnp.pad(gains, ((0, 0), (0, pad)))
    across = [[(i, (i // 2 + d) % chips * 2 + i % 2) for i in range(n_col)] for d in range(chips)]
    along = [[(i, (i + d) % n_row) for i in range(n_row)] for d in range(n_row)]
    other_core = [(i, i ^ 1) for i in range(n_col)]

    filt, pieces = filtered_and_first(voltages, owners, table)
    own, far, column = [], [], []
    arrived = to_owners(pieces)
    for part in range(PARTS):
        later = None
        if part < PARTS - 1:
            pieces = next_part(part + 1, filt, table, owners)
            later = to_owners([pieces[0], *held_back(pieces[1:], arrived[1:2])])
        own.append(equalize(arrived, gains, part, frames))
        far.append([lax.ppermute(own[part], "bcol", across[d]) for d in range(1, chips)])
        column.append([lax.ppermute(own[part], "brow", along[d]) for d in range(1, n_row)])
        arrived = later
    beside = lax.ppermute(together(own), "bcol", other_core)
    result = None
    for part in range(PARTS):
        after = own[-1:] + column[part] + ([] if result is None else [result])
        far[part] = list(held_back(far[part], after))
        near = [lax.ppermute(block, "bcol", other_core) for block in far[part]]
        blocks = [own[part]] + far[part] + [beside] + near + column[part]
        result = correlate(tile_map, blocks, result, part, n_row, n_col)
    return jnp.transpose(result, (3, 0, 1, 2))[None, None]


def solution(mesh):
    in_specs = (P(None, ("brow", "bcol"), "chan"), P(("brow", "bcol"), None, "chan"), P())
    out_specs = P("brow", "bcol", "chan", None, None, None)
    return jax.shard_map(shards, mesh=mesh, in_specs=in_specs, out_specs=out_specs, check_vma=False)
```

```python
import functools
import math

import jax
import jax.numpy as jnp
import ml_dtypes
import numpy as np
from jax import lax
from jax.experimental import pallas as pl
from jax.experimental.pallas import tpu as pltpu
from jax.sharding import PartitionSpec as P

NCHAN = 1024
HALF = NCHAN // 2
CHANNELS = 512
TAPS = 4
FIRST = 256
SIG = 8
LANES = 128
GROUP = 4
BATCH = 4
PARTS = 2
VMEM_BYTES = 16 * 1024 * 1024
FILTER_VMEM_BYTES = 52 * 1024 * 1024
COEF_ROWS = 64


def fir_coefficients():
    position = np.arange(TAPS * NCHAN, dtype=np.float64) + 0.5
    offsets = position / NCHAN - TAPS / 2.0
    window = 0.5 - 0.5 * np.cos(2.0 * math.pi * position / (TAPS * NCHAN))
    return (np.sinc(offsets) * window).reshape(TAPS, NCHAN)


def spectrum_scale():
    return float(1.0 / (128.0 * np.sqrt(np.sum(fir_coefficients() ** 2))))


def dft_tables(owners):
    n = np.arange(HALF, dtype=np.int64)[:, None, None, None, None]
    k = FIRST + np.arange(CHANNELS, dtype=np.int64).reshape(owners, PARTS, -1, 2)
    angles = (n * k % NCHAN) * (2.0 * math.pi / NCHAN)
    cosine, sine = np.cos(angles), np.sin(angles)
    first = np.stack([cosine, -sine], axis=2)
    second = np.stack([sine, cosine], axis=2)
    tables = np.stack([first, second])
    tables = np.transpose(tables, (4, 6, 0, 1, 2, 3, 5))
    return tables.reshape(PARTS, 2 * NCHAN, -1).astype(np.float32).astype(ml_dtypes.bfloat16)


def constants(owners):
    tables = dft_tables(owners)
    lanes = tables.shape[2]
    left = fir_coefficients().astype(np.float32)
    terms = []
    for _ in range(3):
        terms.append(left.astype(ml_dtypes.bfloat16))
        left = left - terms[-1].astype(np.float32)
    terms = np.stack(terms).reshape(-1, lanes)
    pad = np.zeros((-terms.shape[0] % COEF_ROWS, lanes), ml_dtypes.bfloat16)
    return np.concatenate([tables.reshape(-1, lanes), terms, pad])


def transform(filt, table, scale, stage, out_refs):
    owners = len(out_refs)
    me = lax.axis_index("chan")
    spectra = [
        jnp.dot(filt[r], table[r * NCHAN : (r + 1) * NCHAN], preferred_element_type=jnp.float32) * scale
        for r in range(2)
    ]
    width = spectra[0].shape[1] // owners
    for owner in range(owners):
        here = slice(owner * width, (owner + 1) * width)
        piece = jnp.concatenate([spectra[0][:, here], spectra[1][:, here]], axis=1)
        stage[jnp.bitwise_xor(me, owner)] = piece.astype(jnp.bfloat16)
    for d in range(owners):
        out_refs[d][...] = stage[d]


def filter_kernel(frames, pieces, scale, volt_hbm, table_hbm, *refs):
    out_refs, (filt, volt, table, terms, coef, stage, sems) = refs[:-7], refs[-7:]
    per = frames // pieces
    lead = TAPS - 1
    copies = []
    for piece in range(pieces):
        copies.append(
            pltpu.make_async_copy(
                volt_hbm.at[:, :, pl.ds(piece * per * NCHAN, per * NCHAN)],
                volt.at[:, :, pl.ds((lead + piece * per) * NCHAN, per * NCHAN)],
                sems.at[piece],
            )
        )
    table_copy = pltpu.make_async_copy(table_hbm.at[pl.ds(0, 2 * NCHAN)], table, sems.at[pieces])
    coef_copy = pltpu.make_async_copy(
        table_hbm.at[pl.ds(PARTS * 2 * NCHAN, terms.shape[0])], terms, sems.at[pieces + 1]
    )
    coef_copy.start()
    for copy in copies:
        copy.start()
    table_copy.start()
    tail = volt.shape[2] - (lead + frames) * NCHAN
    volt[:, :, : lead * NCHAN] = jnp.zeros((2, SIG, lead * NCHAN), jnp.int32)
    volt[:, :, (lead + frames) * NCHAN :] = jnp.zeros((2, SIG, tail), jnp.int32)
    coef_copy.wait()
    across = coef.shape[1]
    per_term = TAPS * NCHAN // across
    coef[...] = sum(terms[t * per_term : (t + 1) * per_term, :].astype(jnp.float32) for t in range(3))

    def filter_group(group, _):
        base = pl.multiple_of(group * (GROUP * NCHAN), GROUP * NCHAN)
        rows = pl.ds(pl.multiple_of(group * (GROUP * SIG), GROUP * SIG), GROUP * SIG)
        for column in range(HALF // LANES):
            for part in range(2):
                halves = []
                for half in range(2):
                    lane = half * HALF + column * LANES
                    at = [k * (NCHAN // across) + lane // across for k in range(TAPS)]
                    taps = [coef[i : i + 1, lane % across : lane % across + LANES] for i in at]
                    near = [
                        volt[part, :, pl.ds(base + f * NCHAN + lane, LANES)].astype(jnp.float32)
                        for f in range(GROUP + TAPS - 1)
                    ]
                    sums = []
                    for m in range(GROUP):
                        total = taps[0] * near[m]
                        for k in range(1, TAPS):
                            total = total + taps[k] * near[m + k]
                        sums.append(total)
                    halves.append(jnp.concatenate(sums, axis=0))
                where = pl.ds(part * HALF + column * LANES, LANES)
                filt[0, rows, where] = (halves[0] + halves[1]).astype(jnp.bfloat16)
                filt[1, rows, where] = (halves[0] - halves[1]).astype(jnp.bfloat16)
        return 0

    groups = per // GROUP
    for piece in range(pieces):
        copies[piece].wait()
        lax.fori_loop(piece * groups, (piece + 1) * groups, filter_group, 0)
    lax.fori_loop(frames // GROUP, frames // GROUP + 1, filter_group, 0)
    table_copy.wait()
    transform(filt, table, scale, stage, out_refs)


def transform_kernel(part, scale, filt, table_hbm, *refs):
    out_refs, table, stage, sem = refs[:-3], refs[-3], refs[-2], refs[-1]
    copy = pltpu.make_async_copy(table_hbm.at[pl.ds(part * 2 * NCHAN, 2 * NCHAN)], table, sem)
    copy.start()
    copy.wait()
    transform(filt, table, scale, stage, out_refs)


IN_VMEM = pl.BlockSpec(memory_space=pltpu.VMEM)
IN_HBM = pl.BlockSpec(memory_space=pl.ANY)
IN_SMEM = pl.BlockSpec(memory_space=pltpu.SMEM)


def filtered_and_first(voltages, owners, table):
    frames = voltages.shape[2] // NCHAN
    rows = (frames + GROUP) * SIG
    pieces = 4
    across = table.shape[1]
    terms = table.shape[0] - PARTS * 2 * NCHAN
    lanes = 2 * CHANNELS // owners // PARTS
    *first, filt = pl.pallas_call(
        functools.partial(filter_kernel, frames, pieces, spectrum_scale()),
        out_shape=[jax.ShapeDtypeStruct((rows, lanes), jnp.bfloat16)] * owners
        + [jax.ShapeDtypeStruct((2, rows, NCHAN), jnp.bfloat16)],
        in_specs=[IN_HBM, IN_HBM],
        out_specs=[IN_VMEM] * (owners + 1),
        scratch_shapes=[
            pltpu.VMEM((2, SIG, (frames + GROUP + TAPS - 1) * NCHAN), jnp.int32),
            pltpu.VMEM((2 * NCHAN, across), jnp.bfloat16),
            pltpu.VMEM((terms, across), jnp.bfloat16),
            pltpu.VMEM((TAPS * NCHAN // across, across), jnp.float32),
            pltpu.VMEM((owners, rows, lanes), jnp.bfloat16),
            pltpu.SemaphoreType.DMA((pieces + 2,)),
        ],
        compiler_params=pltpu.CompilerParams(vmem_limit_bytes=FILTER_VMEM_BYTES),
        cost_estimate=pl.CostEstimate(flops=1 << 29, bytes_accessed=4 << 20, transcendentals=0),
        name="filter_and_transform",
    )(voltages, table)
    return filt, first


def next_part(part, filt, table, owners):
    rows = filt.shape[1]
    lanes = 2 * CHANNELS // owners // PARTS
    return pl.pallas_call(
        functools.partial(transform_kernel, part, spectrum_scale()),
        out_shape=[jax.ShapeDtypeStruct((rows, lanes), jnp.bfloat16)] * owners,
        in_specs=[IN_VMEM, IN_HBM],
        out_specs=[IN_VMEM] * owners,
        scratch_shapes=[
            pltpu.VMEM((2 * NCHAN, table.shape[1]), jnp.bfloat16),
            pltpu.VMEM((owners, rows, lanes), jnp.bfloat16),
            pltpu.SemaphoreType.DMA(()),
        ],
        compiler_params=pltpu.CompilerParams(vmem_limit_bytes=FILTER_VMEM_BYTES),
        cost_estimate=pl.CostEstimate(flops=1 << 29, bytes_accessed=2 << 20, transcendentals=0),
        name="transform",
    )(filt, table)


def equalize_kernel(owners, frames, h, part, *refs):
    pieces = refs[:owners]
    gains_ref, by_time, by_channel = refs[owners], refs[-2], refs[-1]
    out_ref = refs[owners + 1]
    width = 4 * h
    own_rows = frames * SIG
    over = GROUP * SIG
    times = owners * frames
    tiles = times // LANES
    me = lax.axis_index("chan")
    for d in range(owners):
        source = jnp.bitwise_xor(me, d)
        start = pl.multiple_of(source * own_rows, own_rows)
        by_time[pl.ds(start, own_rows), :width] = pieces[d][:own_rows, :].astype(jnp.float32)
    for d in range(owners):
        source = jnp.bitwise_xor(me, d)

        @pl.when(source < owners - 1)
        def _():
            start = pl.multiple_of((source + 1) * own_rows, own_rows)
            by_time[pl.ds(start, over), :width] += pieces[d][own_rows:, :].astype(jnp.float32)

    gains = [gains_ref[pl.ds(part * 2 * h + r, h, stride=2), :] for r in range(2)]
    for s in range(SIG):
        x = by_time[pl.ds(s, times, stride=SIG), :][:, :width].T
        for r in range(2):
            real, imag = x[2 * r * h : (2 * r + 1) * h], x[(2 * r + 1) * h : (2 * r + 2) * h]
            gain_real, gain_imag = gains[r][:, 2 * s : 2 * s + 1], gains[r][:, 2 * s + 1 : 2 * s + 2]
            both = [real * gain_real - imag * gain_imag, real * gain_imag + imag * gain_real]
            for q in range(2):
                for tile in range(tiles):
                    by_channel[(2 * r + q) * tiles + tile, pl.ds(s, h, stride=SIG), :] = both[q][
                        :, tile * LANES : (tile + 1) * LANES
                    ]
    for r in range(2):
        for tile in range(2 * tiles):
            out_ref[r, :, tile * LANES : (tile + 1) * LANES] = by_channel[r * 2 * tiles + tile].astype(jnp.bfloat16)


def equalize(pieces, gains, part, frames):
    owners = len(pieces)
    h = gains.shape[0] // PARTS // 2
    times = owners * frames
    return pl.pallas_call(
        functools.partial(equalize_kernel, owners, frames, h, part),
        out_shape=jax.ShapeDtypeStruct((2, h * SIG, 2 * times), jnp.bfloat16),
        in_specs=[IN_VMEM] * (owners + 1),
        out_specs=IN_VMEM,
        scratch_shapes=[
            pltpu.VMEM((times * SIG, LANES), jnp.float32),
            pltpu.VMEM((4 * times // LANES, h * SIG, LANES), jnp.float32),
        ],
        compiler_params=pltpu.CompilerParams(vmem_limit_bytes=VMEM_BYTES),
        cost_estimate=pl.CostEstimate(flops=0, bytes_accessed=1 << 10, transcendentals=0),
        name="equalize",
    )(*pieces, gains)


def row_places(col, n_col):
    chips = n_col // 2
    chip, core = lax.div(col, 2), lax.rem(col, 2)
    places = [col] + [lax.rem(chip + chips - d, chips) * 2 + core for d in range(1, chips)]
    return places + [jnp.bitwise_xor(p, 1) for p in places]


def column_places(row, n_row):
    return [row] + [lax.rem(row + n_row - d, n_row) for d in range(1, n_row)]


def correlate_kernel(n_row, n_col, h, times, part, before, map_ref, *refs):
    row_blocks = [ref.at[part] if i == n_col // 2 else ref for i, ref in enumerate(refs[:n_col])]
    col_blocks = (refs[0],) + refs[n_col : n_col + n_row - 1]
    last = part == PARTS - 1
    if last:
        out_hbm, product, out_ref, sems = refs[-4:]
        earlier = refs[-5]
    else:
        out_ref, product = refs[-2:]
        earlier = refs[-3]
    copies = []
    me_row, me_col = lax.axis_index("brow"), lax.axis_index("bcol")
    row_at, col_at = row_places(me_col, n_col), column_places(me_row, n_row)
    rows = BATCH * SIG
    tiles = n_col * rows // LANES

    def batch(step, _):
        parity = step // (h // BATCH)
        inner = step % (h // BATCH)
        here = pl.ds(pl.multiple_of(inner * rows, rows), rows)
        a = jnp.concatenate([block[parity, here, :] for block in row_blocks], axis=0)
        b = jnp.concatenate([block[parity, here, :] for block in col_blocks], axis=0)
        turned = jnp.concatenate([-b[:, times:], b[:, :times]], axis=1)
        both = jnp.concatenate([b, turned], axis=0)
        result = lax.dot_general(both, a, (((1,), (1,)), ((), ())), preferred_element_type=jnp.float32)
        for k in range(2 * n_row):
            for i in range(BATCH):
                channel = 2 * (inner * BATCH + i) + parity
                for tile in range(tiles):
                    product[k * tiles + tile, pl.ds(pl.multiple_of(channel * SIG, SIG), SIG), :] = result[
                        k * rows + i * SIG : k * rows + (i + 1) * SIG, tile * LANES : (tile + 1) * LANES
                    ]
        return 0

    lax.fori_loop(0, 2 * h // BATCH, batch, 0, unroll=4)
    channels = 2 * h
    lane = lax.broadcasted_iota(jnp.int32, (SIG, channels), 1)
    inner_of = (lane // 2) % BATCH
    for q in range(2):
        for e in range(n_row):
            owned = [map_ref[me_row * n_col + row_at[d], col_at[e] * n_col + me_col] == 1 for d in range(n_col)]
            for s2 in range(SIG):
                b_at = col_at[e] * SIG + s2
                for d in range(n_col):
                    if d * rows % LANES == 0:
                        tile = (q * n_row + e) * tiles + d * rows // LANES
                        x = product[tile, pl.ds(s2, channels, stride=SIG), :].T
                    start = d * rows % LANES
                    kept = x[start : start + SIG]
                    for i in range(1, BATCH):
                        kept = jnp.where(inner_of == i, x[start + i * SIG : start + (i + 1) * SIG], kept)
                    kept = jnp.where(owned[d], kept * (1.0 / times), 0.0)
                    a_at = pl.ds(pl.multiple_of(row_at[d] * SIG, SIG), SIG)
                    if before:
                        kept = jnp.concatenate([earlier[q, b_at, a_at, :], kept], axis=1)
                    out_ref[q, b_at, a_at, :] = kept
            if last:
                where = pl.ds(pl.multiple_of(col_at[e] * SIG, SIG), SIG)
                copy = pltpu.make_async_copy(out_ref.at[q, where], out_hbm.at[q, where], sems.at[q * n_row + e])
                copy.start()
                copies.append(copy)
    for copy in copies:
        copy.wait()


def correlate(tile_map, blocks, earlier, part, n_row, n_col):
    h = blocks[0].shape[1] // SIG
    times = blocks[0].shape[2] // 2
    before = earlier.shape[3] if earlier is not None else 0
    operands = list(blocks) + ([earlier] if before else [])
    last = part == PARTS - 1
    out_shape = (2, n_row * SIG, n_col * SIG, before + 2 * h)
    in_last = [pltpu.VMEM(out_shape, jnp.float32), pltpu.SemaphoreType.DMA((2 * n_row,))]
    return pl.pallas_call(
        functools.partial(correlate_kernel, n_row, n_col, h, times, part, before),
        out_shape=jax.ShapeDtypeStruct(out_shape, jnp.float32),
        in_specs=[IN_SMEM] + [IN_VMEM] * len(operands),
        out_specs=IN_HBM if last else IN_VMEM,
        scratch_shapes=[pltpu.VMEM((2 * n_row * n_col * BATCH * SIG // LANES, 2 * h * SIG, LANES), jnp.float32)]
        + (in_last if last else []),
        compiler_params=pltpu.CompilerParams(vmem_limit_bytes=VMEM_BYTES),
        cost_estimate=pl.CostEstimate(flops=0, bytes_accessed=1 << 10, transcendentals=0),
        name="correlate",
    )(tile_map, *operands)


def to_owners(pieces):
    owners = len(pieces)
    arrived = [pieces[0]] + [None] * (owners - 1)
    for d in range(owners - 1, 0, -1):
        arrived[d] = lax.ppermute(pieces[d], "chan", [(i, i ^ d) for i in range(owners)])
    return arrived


def held_back(blocks, after):
    def kernel(*refs):
        for i in range(len(blocks)):
            refs[len(blocks) + len(after) + i][...] = refs[i][...]

    return pl.pallas_call(
        kernel,
        out_shape=[jax.ShapeDtypeStruct(block.shape, block.dtype) for block in blocks],
        in_specs=[IN_VMEM] * (len(blocks) + len(after)),
        out_specs=[IN_VMEM] * len(blocks),
        compiler_params=pltpu.CompilerParams(vmem_limit_bytes=VMEM_BYTES),
        cost_estimate=pl.CostEstimate(flops=0, bytes_accessed=1 << 10, transcendentals=0),
        name="held_back",
    )(*blocks, *after)


def together(blocks):
    def kernel(*refs):
        for i in range(len(blocks)):
            refs[-1][i] = refs[i][...]

    return pl.pallas_call(
        kernel,
        out_shape=jax.ShapeDtypeStruct((len(blocks),) + blocks[0].shape, blocks[0].dtype),
        in_specs=[IN_VMEM] * len(blocks),
        out_specs=IN_VMEM,
        compiler_params=pltpu.CompilerParams(vmem_limit_bytes=VMEM_BYTES),
        cost_estimate=pl.CostEstimate(flops=0, bytes_accessed=1 << 10, transcendentals=0),
        name="together",
    )(*blocks)


def shards(voltages, antenna_gains, tile_map):
    owners = lax.axis_size("chan")
    n_row = lax.axis_size("brow")
    n_col = lax.axis_size("bcol")
    chips = n_col // 2
    frames = voltages.shape[2] // NCHAN
    table = jnp.asarray(constants(owners))
    gains = jnp.transpose(antenna_gains, (2, 0, 1)).reshape(-1, 2 * SIG)
    pad = -gains.shape[1] % LANES
    gains = jnp.pad(gains, ((0, 0), (0, pad)))
    across = [[(i, (i // 2 + d) % chips * 2 + i % 2) for i in range(n_col)] for d in range(chips)]
    along = [[(i, (i + d) % n_row) for i in range(n_row)] for d in range(n_row)]
    other_core = [(i, i ^ 1) for i in range(n_col)]

    filt, pieces = filtered_and_first(voltages, owners, table)
    own, far, column = [], [], []
    arrived = to_owners(pieces)
    for part in range(PARTS):
        later = None
        if part < PARTS - 1:
            pieces = next_part(part + 1, filt, table, owners)
            later = to_owners([pieces[0], *held_back(pieces[1:], arrived[1:2])])
        own.append(equalize(arrived, gains, part, frames))
        far.append([lax.ppermute(own[part], "bcol", across[d]) for d in range(1, chips)])
        column.append([lax.ppermute(own[part], "brow", along[d]) for d in range(1, n_row)])
        arrived = later
    beside = lax.ppermute(together(own), "bcol", other_core)
    result = None
    for part in range(PARTS):
        after = own[-1:] + column[part] + ([] if result is None else [result])
        far[part] = list(held_back(far[part], after))
        near = [lax.ppermute(block, "bcol", other_core) for block in far[part]]
        blocks = [own[part]] + far[part] + [beside] + near + column[part]
        result = correlate(tile_map, blocks, result, part, n_row, n_col)
    return jnp.transpose(result, (3, 0, 1, 2))[None, None]


def solution(mesh):
    in_specs = (P(None, ("brow", "bcol"), "chan"), P(("brow", "bcol"), None, "chan"), P())
    out_specs = P("brow", "bcol", "chan", None, None, None)
    return jax.shard_map(shards, mesh=mesh, in_specs=in_specs, out_specs=out_specs, check_vma=False)
```

```python
import functools
import math

import jax
import jax.numpy as jnp
import ml_dtypes
import numpy as np
from jax import lax
from jax.experimental import pallas as pl
from jax.experimental.pallas import tpu as pltpu
from jax.sharding import PartitionSpec as P

NCHAN = 1024
HALF = NCHAN // 2
CHANNELS = 512
TAPS = 4
FIRST = 256
SIG = 8
LANES = 128
GROUP = 4
BATCH = 4
PARTS = 2
VMEM_BYTES = 16 * 1024 * 1024
FILTER_VMEM_BYTES = 101 * 512 * 1024
COEF_ROWS = 64


def fir_coefficients():
    position = np.arange(TAPS * NCHAN, dtype=np.float64) + 0.5
    offsets = position / NCHAN - TAPS / 2.0
    window = 0.5 - 0.5 * np.cos(2.0 * math.pi * position / (TAPS * NCHAN))
    return (np.sinc(offsets) * window).reshape(TAPS, NCHAN)


def spectrum_scale():
    return float(1.0 / (128.0 * np.sqrt(np.sum(fir_coefficients() ** 2))))


def dft_tables(owners):
    n = np.arange(HALF, dtype=np.int64)[:, None, None, None, None]
    k = FIRST + np.arange(CHANNELS, dtype=np.int64).reshape(owners, PARTS, -1, 2)
    angles = (n * k % NCHAN) * (2.0 * math.pi / NCHAN)
    cosine, sine = np.cos(angles), np.sin(angles)
    first = np.stack([cosine, -sine], axis=2)
    second = np.stack([sine, cosine], axis=2)
    tables = np.stack([first, second])
    tables = np.transpose(tables, (4, 6, 0, 1, 2, 3, 5))
    return tables.reshape(PARTS, 2 * NCHAN, -1).astype(np.float32).astype(ml_dtypes.bfloat16)


def constants(owners):
    tables = dft_tables(owners)
    lanes = tables.shape[2]
    left = fir_coefficients().astype(np.float32)
    terms = []
    for _ in range(3):
        terms.append(left.astype(ml_dtypes.bfloat16))
        left = left - terms[-1].astype(np.float32)
    terms = np.stack(terms).reshape(-1, lanes)
    pad = np.zeros((-terms.shape[0] % COEF_ROWS, lanes), ml_dtypes.bfloat16)
    return np.concatenate([tables.reshape(-1, lanes), terms, pad])


def transform(filt, table, scale, stage, out_refs):
    owners = len(out_refs)
    me = lax.axis_index("chan")
    spectra = [
        jnp.dot(filt[r], table[r * NCHAN : (r + 1) * NCHAN], preferred_element_type=jnp.float32) * scale
        for r in range(2)
    ]
    width = spectra[0].shape[1] // owners
    for owner in range(owners):
        here = slice(owner * width, (owner + 1) * width)
        piece = jnp.concatenate([spectra[0][:, here], spectra[1][:, here]], axis=1)
        stage[jnp.bitwise_xor(me, owner)] = piece[: stage.shape[1]].astype(jnp.bfloat16)
    for d in range(owners):
        out_refs[d][...] = stage[d]


def filter_kernel(frames, pieces, scale, volt_hbm, table_hbm, *refs):
    out_refs, (filt, later, volt, table, terms, coef, stage, sems) = refs[:-8], refs[-8:]
    per = frames // pieces
    lead = TAPS - 1
    copies = []
    for piece in range(pieces):
        copies.append(
            pltpu.make_async_copy(
                volt_hbm.at[:, :, pl.ds(piece * per * NCHAN, per * NCHAN)],
                volt.at[:, :, pl.ds((lead + piece * per) * NCHAN, per * NCHAN)],
                sems.at[piece],
            )
        )
    table_copy = pltpu.make_async_copy(table_hbm.at[pl.ds(0, 2 * NCHAN)], table, sems.at[pieces])
    coef_copy = pltpu.make_async_copy(
        table_hbm.at[pl.ds(PARTS * 2 * NCHAN, terms.shape[0])], terms, sems.at[pieces + 1]
    )
    coef_copy.start()
    for copy in copies:
        copy.start()
    table_copy.start()
    later_copy = pltpu.make_async_copy(
        table_hbm.at[pl.ds(2 * NCHAN, (PARTS - 1) * 2 * NCHAN)], later, sems.at[pieces + 2]
    )
    later_copy.start()
    tail = volt.shape[2] - (lead + frames) * NCHAN
    volt[:, :, : lead * NCHAN] = jnp.zeros((2, SIG, lead * NCHAN), jnp.int32)
    volt[:, :, (lead + frames) * NCHAN :] = jnp.zeros((2, SIG, tail), jnp.int32)
    coef_copy.wait()
    across = coef.shape[1]
    per_term = TAPS * NCHAN // across
    coef[...] = sum(terms[t * per_term : (t + 1) * per_term, :].astype(jnp.float32) for t in range(3))

    def filter_group(group, _):
        base = pl.multiple_of(group * (GROUP * NCHAN), GROUP * NCHAN)
        rows = pl.ds(pl.multiple_of(group * (GROUP * SIG), GROUP * SIG), GROUP * SIG)
        for column in range(HALF // LANES):
            for part in range(2):
                halves = []
                for half in range(2):
                    lane = half * HALF + column * LANES
                    at = [k * (NCHAN // across) + lane // across for k in range(TAPS)]
                    taps = [coef[i : i + 1, lane % across : lane % across + LANES] for i in at]
                    near = [
                        volt[part, :, pl.ds(base + f * NCHAN + lane, LANES)].astype(jnp.float32)
                        for f in range(GROUP + TAPS - 1)
                    ]
                    sums = []
                    for m in range(GROUP):
                        total = taps[0] * near[m]
                        for k in range(1, TAPS):
                            total = total + taps[k] * near[m + k]
                        sums.append(total)
                    halves.append(jnp.concatenate(sums, axis=0))
                where = pl.ds(part * HALF + column * LANES, LANES)
                filt[0, rows, where] = (halves[0] + halves[1]).astype(jnp.bfloat16)
                filt[1, rows, where] = (halves[0] - halves[1]).astype(jnp.bfloat16)
        return 0

    groups = per // GROUP
    for piece in range(pieces):
        copies[piece].wait()
        lax.fori_loop(piece * groups, (piece + 1) * groups, filter_group, 0)
    lax.fori_loop(frames // GROUP, frames // GROUP + 1, filter_group, 0)
    table_copy.wait()
    transform(filt, table, scale, stage, out_refs)
    later_copy.wait()


def transform_kernel(part, scale, filt, later, *refs):
    table = later.at[pl.ds((part - 1) * 2 * NCHAN, 2 * NCHAN)]
    transform(filt, table, scale, refs[-1], refs[:-1])


IN_VMEM = pl.BlockSpec(memory_space=pltpu.VMEM)
IN_HBM = pl.BlockSpec(memory_space=pl.ANY)
IN_SMEM = pl.BlockSpec(memory_space=pltpu.SMEM)


def filtered_and_first(voltages, owners, table):
    frames = voltages.shape[2] // NCHAN
    rows = (frames + GROUP) * SIG
    sent = (frames + TAPS - 1) * SIG
    pieces = 4
    across = table.shape[1]
    terms = table.shape[0] - PARTS * 2 * NCHAN
    lanes = 2 * CHANNELS // owners // PARTS
    *first, filt, later = pl.pallas_call(
        functools.partial(filter_kernel, frames, pieces, spectrum_scale()),
        out_shape=[jax.ShapeDtypeStruct((sent, lanes), jnp.bfloat16)] * owners
        + [
            jax.ShapeDtypeStruct((2, rows, NCHAN), jnp.bfloat16),
            jax.ShapeDtypeStruct(((PARTS - 1) * 2 * NCHAN, across), jnp.bfloat16),
        ],
        in_specs=[IN_HBM, IN_HBM],
        out_specs=[IN_VMEM] * (owners + 2),
        scratch_shapes=[
            pltpu.VMEM((2, SIG, (frames + GROUP + TAPS - 1) * NCHAN), jnp.int32),
            pltpu.VMEM((2 * NCHAN, across), jnp.bfloat16),
            pltpu.VMEM((terms, across), jnp.bfloat16),
            pltpu.VMEM((TAPS * NCHAN // across, across), jnp.float32),
            pltpu.VMEM((owners, sent, lanes), jnp.bfloat16),
            pltpu.SemaphoreType.DMA((pieces + 3,)),
        ],
        compiler_params=pltpu.CompilerParams(vmem_limit_bytes=FILTER_VMEM_BYTES),
        cost_estimate=pl.CostEstimate(flops=1 << 29, bytes_accessed=4 << 20, transcendentals=0),
        name="filter_and_transform",
    )(voltages, table)
    return filt, later, first


def next_part(part, filt, later, owners):
    rows = filt.shape[1] - (GROUP - TAPS + 1) * SIG
    lanes = 2 * CHANNELS // owners // PARTS
    return pl.pallas_call(
        functools.partial(transform_kernel, part, spectrum_scale()),
        out_shape=[jax.ShapeDtypeStruct((rows, lanes), jnp.bfloat16)] * owners,
        in_specs=[IN_VMEM, IN_VMEM],
        out_specs=[IN_VMEM] * owners,
        scratch_shapes=[pltpu.VMEM((owners, rows, lanes), jnp.bfloat16)],
        compiler_params=pltpu.CompilerParams(vmem_limit_bytes=VMEM_BYTES),
        cost_estimate=pl.CostEstimate(flops=1 << 29, bytes_accessed=2 << 20, transcendentals=0),
        name="transform",
    )(filt, later)


def equalize_kernel(owners, frames, h, part, *refs):
    pieces = refs[owners - 1 :: -1]
    gains_ref, by_time, by_channel = refs[owners], refs[-2], refs[-1]
    out_ref = refs[owners + 1]
    width = 4 * h
    own_rows = frames * SIG
    over = (TAPS - 1) * SIG
    times = owners * frames
    tiles = times // LANES
    me = lax.axis_index("chan")
    for d in range(owners):
        source = jnp.bitwise_xor(me, d)
        start = pl.multiple_of(source * own_rows, own_rows)
        by_time[pl.ds(start, own_rows), :width] = pieces[d][:own_rows, :].astype(jnp.float32)
    for d in range(owners):
        source = jnp.bitwise_xor(me, d)

        @pl.when(source < owners - 1)
        def _():
            start = pl.multiple_of((source + 1) * own_rows, own_rows)
            by_time[pl.ds(start, over), :width] += pieces[d][own_rows:, :].astype(jnp.float32)

    gains = [gains_ref[pl.ds(part * 2 * h + r, h, stride=2), :] for r in range(2)]
    for s in range(SIG):
        x = by_time[pl.ds(s, times, stride=SIG), :][:, :width].T
        for r in range(2):
            real, imag = x[2 * r * h : (2 * r + 1) * h], x[(2 * r + 1) * h : (2 * r + 2) * h]
            gain_real, gain_imag = gains[r][:, 2 * s : 2 * s + 1], gains[r][:, 2 * s + 1 : 2 * s + 2]
            both = [real * gain_real - imag * gain_imag, real * gain_imag + imag * gain_real]
            for q in range(2):
                for tile in range(tiles):
                    by_channel[(2 * r + q) * tiles + tile, pl.ds(s, h, stride=SIG), :] = both[q][
                        :, tile * LANES : (tile + 1) * LANES
                    ]
    for r in range(2):
        for tile in range(2 * tiles):
            out_ref[r, :, tile * LANES : (tile + 1) * LANES] = by_channel[r * 2 * tiles + tile].astype(jnp.bfloat16)


def equalize(pieces, gains, part, frames):
    owners = len(pieces)
    h = gains.shape[0] // PARTS // 2
    times = owners * frames
    return pl.pallas_call(
        functools.partial(equalize_kernel, owners, frames, h, part),
        out_shape=jax.ShapeDtypeStruct((2, h * SIG, 2 * times), jnp.bfloat16),
        in_specs=[IN_VMEM] * (owners + 1),
        out_specs=IN_VMEM,
        scratch_shapes=[
            pltpu.VMEM((times * SIG, LANES), jnp.float32),
            pltpu.VMEM((4 * times // LANES, h * SIG, LANES), jnp.float32),
        ],
        compiler_params=pltpu.CompilerParams(vmem_limit_bytes=VMEM_BYTES),
        cost_estimate=pl.CostEstimate(flops=0, bytes_accessed=1 << 10, transcendentals=0),
        name="equalize",
    )(*pieces[::-1], gains)


def row_places(col, n_col):
    chips = n_col // 2
    chip, core = lax.div(col, 2), lax.rem(col, 2)
    places = [col] + [lax.rem(chip + chips - d, chips) * 2 + core for d in range(1, chips)]
    return places + [jnp.bitwise_xor(p, 1) for p in places]


def column_places(row, n_row):
    return [row] + [lax.rem(row + n_row - d, n_row) for d in range(1, n_row)]


def correlate_kernel(n_row, n_col, h, times, part, before, map_ref, *refs):
    row_blocks = [ref for ref in refs[:n_col]]
    col_blocks = (refs[0],) + refs[n_col : n_col + n_row - 1]
    last = part == PARTS - 1
    if last:
        out_hbm, product, out_ref, sems = refs[-4:]
        earlier = refs[-5]
    else:
        out_ref, product = refs[-2:]
        earlier = refs[-3]
    copies = []
    me_row, me_col = lax.axis_index("brow"), lax.axis_index("bcol")
    row_at, col_at = row_places(me_col, n_col), column_places(me_row, n_row)
    rows = BATCH * SIG
    tiles = n_col * rows // LANES

    def batch(step, _):
        parity = step // (h // BATCH)
        inner = step % (h // BATCH)
        here = pl.ds(pl.multiple_of(inner * rows, rows), rows)
        a = jnp.concatenate([block[parity, here, :] for block in row_blocks], axis=0)
        b = jnp.concatenate([block[parity, here, :] for block in col_blocks], axis=0)
        turned = jnp.concatenate([-b[:, times:], b[:, :times]], axis=1)
        both = jnp.concatenate([b, turned], axis=0)
        result = lax.dot_general(both, a, (((1,), (1,)), ((), ())), preferred_element_type=jnp.float32)
        for k in range(2 * n_row):
            for i in range(BATCH):
                channel = 2 * (inner * BATCH + i) + parity
                for tile in range(tiles):
                    product[k * tiles + tile, pl.ds(pl.multiple_of(channel * SIG, SIG), SIG), :] = result[
                        k * rows + i * SIG : k * rows + (i + 1) * SIG, tile * LANES : (tile + 1) * LANES
                    ]
        return 0

    lax.fori_loop(0, 2 * h // BATCH, batch, 0, unroll=4)
    channels = 2 * h
    lane = lax.broadcasted_iota(jnp.int32, (SIG, channels), 1)
    inner_of = (lane // 2) % BATCH
    for q in range(2):
        for e in range(n_row):
            owned = [map_ref[me_row * n_col + row_at[d], col_at[e] * n_col + me_col] == 1 for d in range(n_col)]
            for s2 in range(SIG):
                b_at = col_at[e] * SIG + s2
                for d in range(n_col):
                    if d * rows % LANES == 0:
                        tile = (q * n_row + e) * tiles + d * rows // LANES
                        x = product[tile, pl.ds(s2, channels, stride=SIG), :].T
                    start = d * rows % LANES
                    kept = x[start : start + SIG]
                    for i in range(1, BATCH):
                        kept = jnp.where(inner_of == i, x[start + i * SIG : start + (i + 1) * SIG], kept)
                    kept = jnp.where(owned[d], kept * (1.0 / times), 0.0)
                    a_at = pl.ds(pl.multiple_of(row_at[d] * SIG, SIG), SIG)
                    if before:
                        kept = jnp.concatenate([earlier[q, b_at, a_at, :], kept], axis=1)
                    out_ref[q, b_at, a_at, :] = kept
            if last:
                where = pl.ds(pl.multiple_of(col_at[e] * SIG, SIG), SIG)
                copy = pltpu.make_async_copy(out_ref.at[q, where], out_hbm.at[q, where], sems.at[q * n_row + e])
                copy.start()
                copies.append(copy)
    for copy in copies:
        copy.wait()


def correlate(tile_map, blocks, earlier, part, n_row, n_col):
    h = blocks[0].shape[1] // SIG
    times = blocks[0].shape[2] // 2
    before = earlier.shape[3] if earlier is not None else 0
    operands = list(blocks) + ([earlier] if before else [])
    last = part == PARTS - 1
    out_shape = (2, n_row * SIG, n_col * SIG, before + 2 * h)
    in_last = [pltpu.VMEM(out_shape, jnp.float32), pltpu.SemaphoreType.DMA((2 * n_row,))]
    return pl.pallas_call(
        functools.partial(correlate_kernel, n_row, n_col, h, times, part, before),
        out_shape=jax.ShapeDtypeStruct(out_shape, jnp.float32),
        in_specs=[IN_SMEM] + [IN_VMEM] * len(operands),
        out_specs=IN_HBM if last else IN_VMEM,
        scratch_shapes=[pltpu.VMEM((2 * n_row * n_col * BATCH * SIG // LANES, 2 * h * SIG, LANES), jnp.float32)]
        + (in_last if last else []),
        compiler_params=pltpu.CompilerParams(vmem_limit_bytes=VMEM_BYTES),
        cost_estimate=pl.CostEstimate(flops=0, bytes_accessed=1 << 10, transcendentals=0),
        name="correlate",
    )(tile_map, *operands)


def to_owners(pieces):
    owners = len(pieces)
    arrived = [pieces[0]] + [None] * (owners - 1)
    for d in range(owners - 1, 0, -1):
        arrived[d] = lax.ppermute(pieces[d], "chan", [(i, i ^ d) for i in range(owners)])
    return arrived


def held_back(blocks, after):
    def kernel(*refs):
        for i in range(len(blocks)):
            refs[len(blocks) + len(after) + i][...] = refs[i][...]

    return pl.pallas_call(
        kernel,
        out_shape=[jax.ShapeDtypeStruct(block.shape, block.dtype) for block in blocks],
        in_specs=[IN_VMEM] * (len(blocks) + len(after)),
        out_specs=[IN_VMEM] * len(blocks),
        compiler_params=pltpu.CompilerParams(vmem_limit_bytes=VMEM_BYTES),
        cost_estimate=pl.CostEstimate(flops=0, bytes_accessed=1 << 10, transcendentals=0),
        name="held_back",
    )(*blocks, *after)


def together(blocks):
    def kernel(*refs):
        for i in range(len(blocks)):
            refs[-1][i] = refs[i][...]

    return pl.pallas_call(
        kernel,
        out_shape=jax.ShapeDtypeStruct((len(blocks),) + blocks[0].shape, blocks[0].dtype),
        in_specs=[IN_VMEM] * len(blocks),
        out_specs=IN_VMEM,
        compiler_params=pltpu.CompilerParams(vmem_limit_bytes=VMEM_BYTES),
        cost_estimate=pl.CostEstimate(flops=0, bytes_accessed=1 << 10, transcendentals=0),
        name="together",
    )(*blocks)


def shards(voltages, antenna_gains, tile_map):
    owners = lax.axis_size("chan")
    n_row = lax.axis_size("brow")
    n_col = lax.axis_size("bcol")
    chips = n_col // 2
    frames = voltages.shape[2] // NCHAN
    table = jnp.asarray(constants(owners))
    gains = jnp.transpose(antenna_gains, (2, 0, 1)).reshape(-1, 2 * SIG)
    pad = -gains.shape[1] % LANES
    gains = jnp.pad(gains, ((0, 0), (0, pad)))
    across = [[(i, (i // 2 + d) % chips * 2 + i % 2) for i in range(n_col)] for d in range(chips)]
    along = [[(i, (i + d) % n_row) for i in range(n_row)] for d in range(n_row)]
    other_core = [(i, i ^ 1) for i in range(n_col)]

    filt, tables, pieces = filtered_and_first(voltages, owners, table)
    own, far, column = [], [], []
    arrived = to_owners(pieces)
    for part in range(PARTS):
        later = None
        if part < PARTS - 1:
            pieces = next_part(part + 1, filt, tables, owners)
            later = to_owners([pieces[0], *held_back(pieces[1:], arrived[-1:])])
        own.append(equalize(arrived, gains, part, frames))
        far.append([lax.ppermute(own[part], "bcol", across[d]) for d in range(1, chips)])
        column.append([lax.ppermute(own[part], "brow", along[d]) for d in range(1, n_row)])
        arrived = later
    beside = [lax.ppermute(block, "bcol", other_core) for block in own]
    result = None
    for part in range(PARTS):
        after = own[-1:] + column[part]
        far[part] = list(held_back(far[part], after))
        near = [lax.ppermute(block, "bcol", other_core) for block in far[part]]
        blocks = [own[part]] + far[part] + [beside[part]] + near + column[part]
        result = correlate(tile_map, blocks, result, part, n_row, n_col)
    return jnp.transpose(result, (3, 0, 1, 2))[None, None]


def solution(mesh):
    in_specs = (P(None, ("brow", "bcol"), "chan"), P(("brow", "bcol"), None, "chan"), P())
    out_specs = P("brow", "bcol", "chan", None, None, None)
    return jax.shard_map(shards, mesh=mesh, in_specs=in_specs, out_specs=out_specs, check_vma=False)
```

```python
import functools
import math

import jax
import jax.numpy as jnp
import ml_dtypes
import numpy as np
from jax import lax
from jax.experimental import pallas as pl
from jax.experimental.pallas import tpu as pltpu
from jax.sharding import PartitionSpec as P

NCHAN = 1024
HALF = NCHAN // 2
CHANNELS = 512
TAPS = 4
FIRST = 256
SIG = 8
LANES = 128
GROUP = 4
BATCH = 4
PARTS = 2
VMEM_BYTES = 16 * 1024 * 1024
FILTER_VMEM_BYTES = 101 * 512 * 1024
COEF_ROWS = 64


def fir_coefficients():
    position = np.arange(TAPS * NCHAN, dtype=np.float64) + 0.5
    offsets = position / NCHAN - TAPS / 2.0
    window = 0.5 - 0.5 * np.cos(2.0 * math.pi * position / (TAPS * NCHAN))
    return (np.sinc(offsets) * window).reshape(TAPS, NCHAN)


def spectrum_scale():
    return float(1.0 / (128.0 * np.sqrt(np.sum(fir_coefficients() ** 2))))


def dft_tables(owners):
    n = np.arange(HALF, dtype=np.int64)[:, None, None, None, None]
    k = FIRST + np.arange(CHANNELS, dtype=np.int64).reshape(owners, PARTS, -1, 2)
    angles = (n * k % NCHAN) * (2.0 * math.pi / NCHAN)
    cosine, sine = np.cos(angles), np.sin(angles)
    first = np.stack([cosine, -sine], axis=2)
    second = np.stack([sine, cosine], axis=2)
    tables = np.stack([first, second])
    tables = np.transpose(tables, (4, 6, 0, 1, 2, 3, 5))
    return tables.reshape(PARTS, 2 * NCHAN, -1).astype(np.float32).astype(ml_dtypes.bfloat16)


def constants(owners):
    tables = dft_tables(owners)
    lanes = tables.shape[2]
    left = fir_coefficients().astype(np.float32)
    terms = []
    for _ in range(3):
        terms.append(left.astype(ml_dtypes.bfloat16))
        left = left - terms[-1].astype(np.float32)
    terms = np.stack(terms).reshape(-1, lanes)
    pad = np.zeros((-terms.shape[0] % COEF_ROWS, lanes), ml_dtypes.bfloat16)
    return np.concatenate([tables.reshape(-1, lanes), terms, pad])


def transform(filt, table, scale, stage, out_refs):
    owners = len(out_refs)
    me = lax.axis_index("chan")
    spectra = [
        jnp.dot(filt[r], table[r * NCHAN : (r + 1) * NCHAN], preferred_element_type=jnp.float32) * scale
        for r in range(2)
    ]
    width = spectra[0].shape[1] // owners
    for owner in range(owners):
        here = slice(owner * width, (owner + 1) * width)
        piece = jnp.concatenate([spectra[0][:, here], spectra[1][:, here]], axis=1)
        stage[jnp.bitwise_xor(me, owner)] = piece[: stage.shape[1]].astype(jnp.bfloat16)
    for d in range(owners):
        out_refs[d][...] = stage[d]


def filter_kernel(frames, pieces, scale, volt_hbm, table_hbm, *refs):
    out_refs, (filt, later, volt, table, terms, coef, stage, sems) = refs[:-8], refs[-8:]
    per = frames // pieces
    lead = TAPS - 1
    copies = []
    for piece in range(pieces):
        copies.append(
            pltpu.make_async_copy(
                volt_hbm.at[:, :, pl.ds(piece * per * NCHAN, per * NCHAN)],
                volt.at[:, :, pl.ds((lead + piece * per) * NCHAN, per * NCHAN)],
                sems.at[piece],
            )
        )
    table_copy = pltpu.make_async_copy(table_hbm.at[pl.ds(0, 2 * NCHAN)], table, sems.at[pieces])
    coef_copy = pltpu.make_async_copy(
        table_hbm.at[pl.ds(PARTS * 2 * NCHAN, terms.shape[0])], terms, sems.at[pieces + 1]
    )
    coef_copy.start()
    for copy in copies:
        copy.start()
    table_copy.start()
    later_copy = pltpu.make_async_copy(
        table_hbm.at[pl.ds(2 * NCHAN, (PARTS - 1) * 2 * NCHAN)], later, sems.at[pieces + 2]
    )
    later_copy.start()
    tail = volt.shape[2] - (lead + frames) * NCHAN
    volt[:, :, : lead * NCHAN] = jnp.zeros((2, SIG, lead * NCHAN), jnp.int32)
    volt[:, :, (lead + frames) * NCHAN :] = jnp.zeros((2, SIG, tail), jnp.int32)
    coef_copy.wait()
    across = coef.shape[1]
    per_term = TAPS * NCHAN // across
    coef[...] = sum(terms[t * per_term : (t + 1) * per_term, :].astype(jnp.float32) for t in range(3))

    def filter_group(group, _):
        base = pl.multiple_of(group * (GROUP * NCHAN), GROUP * NCHAN)
        rows = pl.ds(pl.multiple_of(group * (GROUP * SIG), GROUP * SIG), GROUP * SIG)
        for column in range(HALF // LANES):
            for part in range(2):
                halves = []
                for half in range(2):
                    lane = half * HALF + column * LANES
                    at = [k * (NCHAN // across) + lane // across for k in range(TAPS)]
                    taps = [coef[i : i + 1, lane % across : lane % across + LANES] for i in at]
                    near = [
                        volt[part, :, pl.ds(base + f * NCHAN + lane, LANES)].astype(jnp.float32)
                        for f in range(GROUP + TAPS - 1)
                    ]
                    sums = []
                    for m in range(GROUP):
                        total = taps[0] * near[m]
                        for k in range(1, TAPS):
                            total = total + taps[k] * near[m + k]
                        sums.append(total)
                    halves.append(jnp.concatenate(sums, axis=0))
                where = pl.ds(part * HALF + column * LANES, LANES)
                filt[0, rows, where] = (halves[0] + halves[1]).astype(jnp.bfloat16)
                filt[1, rows, where] = (halves[0] - halves[1]).astype(jnp.bfloat16)
        return 0

    groups = per // GROUP
    for piece in range(pieces):
        copies[piece].wait()
        lax.fori_loop(piece * groups, (piece + 1) * groups, filter_group, 0)
    lax.fori_loop(frames // GROUP, frames // GROUP + 1, filter_group, 0)
    table_copy.wait()
    transform(filt, table, scale, stage, out_refs)
    later_copy.wait()


def transform_kernel(part, scale, filt, later, *refs):
    table = later.at[pl.ds((part - 1) * 2 * NCHAN, 2 * NCHAN)]
    transform(filt, table, scale, refs[-1], refs[:-1])


IN_VMEM = pl.BlockSpec(memory_space=pltpu.VMEM)
IN_HBM = pl.BlockSpec(memory_space=pl.ANY)
IN_SMEM = pl.BlockSpec(memory_space=pltpu.SMEM)


def filtered_and_first(voltages, owners, table):
    frames = voltages.shape[2] // NCHAN
    rows = (frames + GROUP) * SIG
    sent = (frames + TAPS - 1) * SIG
    pieces = 4
    across = table.shape[1]
    terms = table.shape[0] - PARTS * 2 * NCHAN
    lanes = 2 * CHANNELS // owners // PARTS
    *first, filt, later = pl.pallas_call(
        functools.partial(filter_kernel, frames, pieces, spectrum_scale()),
        out_shape=[jax.ShapeDtypeStruct((sent, lanes), jnp.bfloat16)] * owners
        + [
            jax.ShapeDtypeStruct((2, rows, NCHAN), jnp.bfloat16),
            jax.ShapeDtypeStruct(((PARTS - 1) * 2 * NCHAN, across), jnp.bfloat16),
        ],
        in_specs=[IN_HBM, IN_HBM],
        out_specs=[IN_VMEM] * (owners + 2),
        scratch_shapes=[
            pltpu.VMEM((2, SIG, (frames + GROUP + TAPS - 1) * NCHAN), jnp.int32),
            pltpu.VMEM((2 * NCHAN, across), jnp.bfloat16),
            pltpu.VMEM((terms, across), jnp.bfloat16),
            pltpu.VMEM((TAPS * NCHAN // across, across), jnp.float32),
            pltpu.VMEM((owners, sent, lanes), jnp.bfloat16),
            pltpu.SemaphoreType.DMA((pieces + 3,)),
        ],
        compiler_params=pltpu.CompilerParams(vmem_limit_bytes=FILTER_VMEM_BYTES),
        cost_estimate=pl.CostEstimate(flops=1 << 29, bytes_accessed=4 << 20, transcendentals=0),
        name="filter_and_transform",
    )(voltages, table)
    return filt, later, first


def next_part(part, filt, later, owners):
    rows = filt.shape[1] - (GROUP - TAPS + 1) * SIG
    lanes = 2 * CHANNELS // owners // PARTS
    return pl.pallas_call(
        functools.partial(transform_kernel, part, spectrum_scale()),
        out_shape=[jax.ShapeDtypeStruct((rows, lanes), jnp.bfloat16)] * owners,
        in_specs=[IN_VMEM, IN_VMEM],
        out_specs=[IN_VMEM] * owners,
        scratch_shapes=[pltpu.VMEM((owners, rows, lanes), jnp.bfloat16)],
        compiler_params=pltpu.CompilerParams(vmem_limit_bytes=VMEM_BYTES),
        cost_estimate=pl.CostEstimate(flops=1 << 29, bytes_accessed=2 << 20, transcendentals=0),
        name="transform",
    )(filt, later)


def equalize_kernel(owners, frames, h, part, *refs):
    pieces = refs[owners - 1 :: -1]
    gains_ref, by_time, by_channel = refs[owners], refs[-2], refs[-1]
    out_ref = refs[owners + 1]
    width = 4 * h
    own_rows = frames * SIG
    over = (TAPS - 1) * SIG
    times = owners * frames
    tiles = times // LANES
    me = lax.axis_index("chan")
    for d in range(owners):
        source = jnp.bitwise_xor(me, d)
        start = pl.multiple_of(source * own_rows, own_rows)
        by_time[pl.ds(start, own_rows), :width] = pieces[d][:own_rows, :].astype(jnp.float32)
    for d in range(owners):
        source = jnp.bitwise_xor(me, d)

        @pl.when(source < owners - 1)
        def _():
            start = pl.multiple_of((source + 1) * own_rows, own_rows)
            by_time[pl.ds(start, over), :width] += pieces[d][own_rows:, :].astype(jnp.float32)

    gains = [gains_ref[pl.ds(part * 2 * h + r, h, stride=2), :] for r in range(2)]
    for s in range(SIG):
        x = by_time[pl.ds(s, times, stride=SIG), :][:, :width].T
        for r in range(2):
            real, imag = x[2 * r * h : (2 * r + 1) * h], x[(2 * r + 1) * h : (2 * r + 2) * h]
            gain_real, gain_imag = gains[r][:, 2 * s : 2 * s + 1], gains[r][:, 2 * s + 1 : 2 * s + 2]
            both = [real * gain_real - imag * gain_imag, real * gain_imag + imag * gain_real]
            for q in range(2):
                for tile in range(tiles):
                    for i in range(BATCH):
                        where = pl.ds(i * SIG + s, h // BATCH, stride=BATCH * SIG)
                        by_channel[(2 * r + q) * tiles + tile, where, :] = both[q][
                            i * h // BATCH : (i + 1) * h // BATCH, tile * LANES : (tile + 1) * LANES
                        ]
    for r in range(2):
        for tile in range(2 * tiles):
            out_ref[r, :, tile * LANES : (tile + 1) * LANES] = by_channel[r * 2 * tiles + tile].astype(jnp.bfloat16)


def equalize(pieces, gains, part, frames):
    owners = len(pieces)
    h = gains.shape[0] // PARTS // 2
    times = owners * frames
    return pl.pallas_call(
        functools.partial(equalize_kernel, owners, frames, h, part),
        out_shape=jax.ShapeDtypeStruct((2, h * SIG, 2 * times), jnp.bfloat16),
        in_specs=[IN_VMEM] * (owners + 1),
        out_specs=IN_VMEM,
        scratch_shapes=[
            pltpu.VMEM((times * SIG, LANES), jnp.float32),
            pltpu.VMEM((4 * times // LANES, h * SIG, LANES), jnp.float32),
        ],
        compiler_params=pltpu.CompilerParams(vmem_limit_bytes=VMEM_BYTES),
        cost_estimate=pl.CostEstimate(flops=0, bytes_accessed=1 << 10, transcendentals=0),
        name="equalize",
    )(*pieces[::-1], gains)


def row_places(col, n_col):
    chips = n_col // 2
    chip, core = lax.div(col, 2), lax.rem(col, 2)
    places = [col] + [lax.rem(chip + chips - d, chips) * 2 + core for d in range(1, chips)]
    return places + [jnp.bitwise_xor(p, 1) for p in places]


def column_places(row, n_row):
    return [row] + [lax.rem(row + n_row - d, n_row) for d in range(1, n_row)]


def regroup(v):
    lane = lax.broadcasted_iota(jnp.int32, v[0].shape, 1)
    v = list(v)
    for bit in (2, 1):
        width = bit * LANES // 8
        low = (lane // width) % 2 == 0
        for i in range(4):
            if i & bit == 0:
                a, b = v[i], v[i + bit]
                v[i] = jnp.where(low, a, pltpu.roll(b, width, axis=1))
                v[i + bit] = jnp.where(low, pltpu.roll(a, LANES - width, axis=1), b)
    return v


def correlate_kernel(n_row, n_col, h, times, part, dense, map_ref, *refs):
    row_blocks = refs[:n_col]
    col_blocks = (refs[0],) + refs[n_col : n_col + n_row - 1]
    last = part == PARTS - 1
    if last:
        out_hbm, chosen, out_ref, sems = refs[-4:]
    else:
        out_ref, chosen = refs[-2:]
    earlier = refs[n_col + n_row - 1]
    me_row, me_col = lax.axis_index("brow"), lax.axis_index("bcol")
    row_at, col_at = row_places(me_col, n_col), column_places(me_row, n_row)
    rows = BATCH * SIG
    tiles = n_col * rows // LANES
    steps = 2 * h // BATCH
    index_in_batch = (lax.broadcasted_iota(jnp.int32, (SIG, LANES), 1) // SIG) % BATCH

    for step in range(steps):
        inner, parity = step // 2, step % 2
        here = slice(inner * rows, (inner + 1) * rows)
        a = jnp.concatenate([block[parity, here, :] for block in row_blocks], axis=0)
        b = jnp.concatenate([block[parity, here, :] for block in col_blocks], axis=0)
        turned = jnp.concatenate([-b[:, times:], b[:, :times]], axis=1)
        both = jnp.concatenate([b, turned], axis=0)
        result = lax.dot_general(both, a, (((1,), (1,)), ((), ())), preferred_element_type=jnp.float32)
        for k in range(2 * n_row):
            for tile in range(tiles):
                lanes = slice(tile * LANES, (tile + 1) * LANES)
                own = [result[k * rows + i * SIG : k * rows + (i + 1) * SIG, lanes] for i in range(BATCH)]
                kept = own[0]
                for i in range(1, BATCH):
                    kept = jnp.where(index_in_batch == i, own[i], kept)
                chosen[k * tiles + tile, pl.ds(step, SIG, stride=steps), :] = kept

    copies = []
    low = lax.broadcasted_iota(jnp.int32, (SIG, LANES), 1) < LANES // 2
    for q in range(2):
        for e in range(n_row):
            for d in range(n_col):
                if d % (LANES // rows) == 0:
                    x = chosen[(q * n_row + e) * tiles + d * rows // LANES].T
                start = d * rows % LANES
                v = [x[start + i * SIG : start + (i + 1) * SIG] for i in range(BATCH)]
                if last:
                    owned = map_ref[me_row * n_col + row_at[d], col_at[e] * n_col + me_col] == 1
                    keep = jnp.where(owned, 1.0 / times, 0.0)
                a_at = pl.ds(pl.multiple_of(row_at[d] * SIG, SIG), SIG)
                mine = slice(d * SIG, (d + 1) * SIG)
                if dense:
                    for g, w in enumerate(regroup(v)):
                        if last:
                            before = earlier[q, e, g, mine, :]
                            pair = [
                                jnp.where(low, before, pltpu.roll(w, LANES // 2, axis=1)),
                                jnp.where(low, pltpu.roll(before, LANES // 2, axis=1), w),
                            ]
                            for half in range(2):
                                out_ref[q, col_at[e] * SIG + half * BATCH + g, a_at, :] = pair[half] * keep
                        else:
                            out_ref[q, e, g, mine, :] = w
                else:
                    for s2 in range(SIG):
                        w = jnp.concatenate([each[:, s2 * steps : (s2 + 1) * steps] for each in v], axis=1)
                        if part > 0:
                            w = jnp.concatenate([earlier[q, e, s2, mine, :], w], axis=1)
                        if last:
                            out_ref[q, col_at[e] * SIG + s2, a_at, :] = w * keep
                        else:
                            out_ref[q, e, s2, mine, :] = w
            if last:
                where = pl.ds(pl.multiple_of(col_at[e] * SIG, SIG), SIG)
                copy = pltpu.make_async_copy(out_ref.at[q, where], out_hbm.at[q, where], sems.at[q * n_row + e])
                copy.start()
                copies.append(copy)
    for copy in copies:
        copy.wait()


def correlate(tile_map, blocks, earlier, part, n_row, n_col):
    h = blocks[0].shape[1] // SIG
    times = blocks[0].shape[2] // 2
    channels = 2 * h
    dense = channels * 2 == LANES and PARTS == 2
    operands = list(blocks) + ([earlier] if part else [])
    last = part == PARTS - 1
    if last:
        out_shape = (2, n_row * SIG, n_col * SIG, (part + 1) * channels)
    elif dense:
        out_shape = (2, n_row, SIG // 2, n_col * SIG, LANES)
    else:
        out_shape = (2, n_row, SIG, n_col * SIG, (part + 1) * channels)
    in_last = [pltpu.VMEM(out_shape, jnp.float32), pltpu.SemaphoreType.DMA((2 * n_row,))]
    kept = pltpu.VMEM((2 * n_row * n_col * BATCH * SIG // LANES, SIG * channels // BATCH, LANES), jnp.float32)
    return pl.pallas_call(
        functools.partial(correlate_kernel, n_row, n_col, h, times, part, dense),
        out_shape=jax.ShapeDtypeStruct(out_shape, jnp.float32),
        in_specs=[IN_SMEM] + [IN_VMEM] * len(operands),
        out_specs=IN_HBM if last else IN_VMEM,
        scratch_shapes=[kept] + (in_last if last else []),
        compiler_params=pltpu.CompilerParams(vmem_limit_bytes=VMEM_BYTES),
        cost_estimate=pl.CostEstimate(flops=0, bytes_accessed=1 << 10, transcendentals=0),
        name="correlate",
    )(tile_map, *operands)


def to_owners(pieces):
    owners = len(pieces)
    arrived = [pieces[0]] + [None] * (owners - 1)
    for d in range(owners - 1, 0, -1):
        arrived[d] = lax.ppermute(pieces[d], "chan", [(i, i ^ d) for i in range(owners)])
    return arrived


def held_back(blocks, after):
    def kernel(*refs):
        for i in range(len(blocks)):
            refs[len(blocks) + len(after) + i][...] = refs[i][...]

    return pl.pallas_call(
        kernel,
        out_shape=[jax.ShapeDtypeStruct(block.shape, block.dtype) for block in blocks],
        in_specs=[IN_VMEM] * (len(blocks) + len(after)),
        out_specs=[IN_VMEM] * len(blocks),
        compiler_params=pltpu.CompilerParams(vmem_limit_bytes=VMEM_BYTES),
        cost_estimate=pl.CostEstimate(flops=0, bytes_accessed=1 << 10, transcendentals=0),
        name="held_back",
    )(*blocks, *after)


def together(blocks):
    def kernel(*refs):
        for i in range(len(blocks)):
            refs[-1][i] = refs[i][...]

    return pl.pallas_call(
        kernel,
        out_shape=jax.ShapeDtypeStruct((len(blocks),) + blocks[0].shape, blocks[0].dtype),
        in_specs=[IN_VMEM] * len(blocks),
        out_specs=IN_VMEM,
        compiler_params=pltpu.CompilerParams(vmem_limit_bytes=VMEM_BYTES),
        cost_estimate=pl.CostEstimate(flops=0, bytes_accessed=1 << 10, transcendentals=0),
        name="together",
    )(*blocks)


def shards(voltages, antenna_gains, tile_map):
    owners = lax.axis_size("chan")
    n_row = lax.axis_size("brow")
    n_col = lax.axis_size("bcol")
    chips = n_col // 2
    frames = voltages.shape[2] // NCHAN
    table = jnp.asarray(constants(owners))
    gains = jnp.transpose(antenna_gains, (2, 0, 1)).reshape(-1, 2 * SIG)
    pad = -gains.shape[1] % LANES
    gains = jnp.pad(gains, ((0, 0), (0, pad)))
    across = [[(i, (i // 2 + d) % chips * 2 + i % 2) for i in range(n_col)] for d in range(chips)]
    along = [[(i, (i + d) % n_row) for i in range(n_row)] for d in range(n_row)]
    other_core = [(i, i ^ 1) for i in range(n_col)]

    filt, tables, pieces = filtered_and_first(voltages, owners, table)
    own, far, column = [], [], []
    arrived = to_owners(pieces)
    for part in range(PARTS):
        later = None
        if part < PARTS - 1:
            pieces = next_part(part + 1, filt, tables, owners)
            later = to_owners([pieces[0], *held_back(pieces[1:], arrived[-1:])])
        own.append(equalize(arrived, gains, part, frames))
        far.append([lax.ppermute(own[part], "bcol", across[d]) for d in range(1, chips)])
        column.append([lax.ppermute(own[part], "brow", along[d]) for d in range(1, n_row)])
        arrived = later
    beside = [lax.ppermute(block, "bcol", other_core) for block in own]
    result = None
    for part in range(PARTS):
        after = own[-1:] + column[part]
        far[part] = list(held_back(far[part], after))
        near = [lax.ppermute(block, "bcol", other_core) for block in far[part]]
        blocks = [own[part]] + far[part] + [beside[part]] + near + column[part]
        result = correlate(tile_map, blocks, result, part, n_row, n_col)
    return jnp.transpose(result, (3, 0, 1, 2))[None, None]


def solution(mesh):
    in_specs = (P(None, ("brow", "bcol"), "chan"), P(("brow", "bcol"), None, "chan"), P())
    out_specs = P("brow", "bcol", "chan", None, None, None)
    return jax.shard_map(shards, mesh=mesh, in_specs=in_specs, out_specs=out_specs, check_vma=False)
```

```python
import functools
import math

import jax
import jax.numpy as jnp
import ml_dtypes
import numpy as np
from jax import lax
from jax.experimental import pallas as pl
from jax.experimental.pallas import tpu as pltpu
from jax.sharding import PartitionSpec as P

NCHAN = 1024
HALF = NCHAN // 2
CHANNELS = 512
TAPS = 4
FIRST = 256
SIG = 8
LANES = 128
GROUP = 4
BATCH = 4
PARTS = 2
VMEM_BYTES = 16 * 1024 * 1024
FILTER_VMEM_BYTES = 101 * 512 * 1024
COEF_ROWS = 64


def fir_coefficients():
    position = np.arange(TAPS * NCHAN, dtype=np.float64) + 0.5
    offsets = position / NCHAN - TAPS / 2.0
    window = 0.5 - 0.5 * np.cos(2.0 * math.pi * position / (TAPS * NCHAN))
    return (np.sinc(offsets) * window).reshape(TAPS, NCHAN)


def spectrum_scale():
    return float(1.0 / (128.0 * np.sqrt(np.sum(fir_coefficients() ** 2))))


def dft_tables(owners):
    n = np.arange(HALF, dtype=np.int64).reshape(HALF, 1, 1, 1, 1, 1)
    k = FIRST + np.arange(CHANNELS, dtype=np.int64).reshape(owners, PARTS, BATCH, -1, 2)
    angles = (n * k % NCHAN) * (2.0 * math.pi / NCHAN)
    cosine, sine = np.cos(angles), np.sin(angles)
    first = np.stack([cosine, -sine], axis=2)
    second = np.stack([sine, cosine], axis=2)
    tables = np.stack([first, second])
    tables = np.transpose(tables, (4, 7, 0, 1, 2, 3, 6, 5))
    return tables.reshape(PARTS, 2 * NCHAN, -1).astype(np.float32).astype(ml_dtypes.bfloat16)


def constants(owners):
    tables = dft_tables(owners)
    lanes = tables.shape[2]
    left = fir_coefficients().astype(np.float32)
    terms = []
    for _ in range(3):
        terms.append(left.astype(ml_dtypes.bfloat16))
        left = left - terms[-1].astype(np.float32)
    terms = np.stack(terms).reshape(-1, lanes)
    pad = np.zeros((-terms.shape[0] % COEF_ROWS, lanes), ml_dtypes.bfloat16)
    return np.concatenate([tables.reshape(-1, lanes), terms, pad])


def transform(filt, table, scale, stage, out_refs):
    owners = len(out_refs)
    me = lax.axis_index("chan")
    spectra = [
        jnp.dot(filt[r], table[r * NCHAN : (r + 1) * NCHAN], preferred_element_type=jnp.float32) * scale
        for r in range(2)
    ]
    width = spectra[0].shape[1] // owners
    for owner in range(owners):
        here = slice(owner * width, (owner + 1) * width)
        piece = jnp.concatenate([spectra[0][:, here], spectra[1][:, here]], axis=1)
        stage[jnp.bitwise_xor(me, owner)] = piece[: stage.shape[1]].astype(jnp.bfloat16)
    for d in range(owners):
        out_refs[d][...] = stage[d]


def filter_kernel(frames, pieces, scale, volt_hbm, table_hbm, *refs):
    out_refs, (filt, later, volt, table, terms, coef, stage, sems) = refs[:-8], refs[-8:]
    per = frames // pieces
    lead = TAPS - 1
    copies = []
    for piece in range(pieces):
        copies.append(
            pltpu.make_async_copy(
                volt_hbm.at[:, :, pl.ds(piece * per * NCHAN, per * NCHAN)],
                volt.at[:, :, pl.ds((lead + piece * per) * NCHAN, per * NCHAN)],
                sems.at[piece],
            )
        )
    table_copy = pltpu.make_async_copy(table_hbm.at[pl.ds(0, 2 * NCHAN)], table, sems.at[pieces])
    coef_copy = pltpu.make_async_copy(
        table_hbm.at[pl.ds(PARTS * 2 * NCHAN, terms.shape[0])], terms, sems.at[pieces + 1]
    )
    coef_copy.start()
    for copy in copies:
        copy.start()
    later_copy = pltpu.make_async_copy(
        table_hbm.at[pl.ds(2 * NCHAN, (PARTS - 1) * 2 * NCHAN)], later, sems.at[pieces + 2]
    )
    tail = volt.shape[2] - (lead + frames) * NCHAN
    volt[:, :, : lead * NCHAN] = jnp.zeros((2, SIG, lead * NCHAN), jnp.int32)
    volt[:, :, (lead + frames) * NCHAN :] = jnp.zeros((2, SIG, tail), jnp.int32)
    coef_copy.wait()
    across = coef.shape[1]
    per_term = TAPS * NCHAN // across
    coef[...] = sum(terms[t * per_term : (t + 1) * per_term, :].astype(jnp.float32) for t in range(3))

    def filter_group(group, _):
        base = pl.multiple_of(group * (GROUP * NCHAN), GROUP * NCHAN)
        rows = pl.ds(pl.multiple_of(group * (GROUP * SIG), GROUP * SIG), GROUP * SIG)
        for column in range(HALF // LANES):
            for part in range(2):
                halves = []
                for half in range(2):
                    lane = half * HALF + column * LANES
                    at = [k * (NCHAN // across) + lane // across for k in range(TAPS)]
                    taps = [coef[i : i + 1, lane % across : lane % across + LANES] for i in at]
                    near = [
                        volt[part, :, pl.ds(base + f * NCHAN + lane, LANES)].astype(jnp.float32)
                        for f in range(GROUP + TAPS - 1)
                    ]
                    sums = []
                    for m in range(GROUP):
                        total = taps[0] * near[m]
                        for k in range(1, TAPS):
                            total = total + taps[k] * near[m + k]
                        sums.append(total)
                    halves.append(jnp.concatenate(sums, axis=0))
                where = pl.ds(part * HALF + column * LANES, LANES)
                filt[0, rows, where] = (halves[0] + halves[1]).astype(jnp.bfloat16)
                filt[1, rows, where] = (halves[0] - halves[1]).astype(jnp.bfloat16)
        return 0

    groups = per // GROUP
    for piece in range(pieces):
        copies[piece].wait()
        if piece == pieces // 4:
            table_copy.start()
        if piece == pieces // 2:
            later_copy.start()
        lax.fori_loop(piece * groups, (piece + 1) * groups, filter_group, 0)
    lax.fori_loop(frames // GROUP, frames // GROUP + 1, filter_group, 0)
    table_copy.wait()
    transform(filt, table, scale, stage, out_refs)
    later_copy.wait()


def transform_kernel(part, scale, filt, later, *refs):
    table = later.at[pl.ds((part - 1) * 2 * NCHAN, 2 * NCHAN)]
    transform(filt, table, scale, refs[-1], refs[:-1])


IN_VMEM = pl.BlockSpec(memory_space=pltpu.VMEM)
IN_HBM = pl.BlockSpec(memory_space=pl.ANY)
IN_SMEM = pl.BlockSpec(memory_space=pltpu.SMEM)


def filtered_and_first(voltages, owners, table):
    frames = voltages.shape[2] // NCHAN
    rows = (frames + GROUP) * SIG
    sent = (frames + TAPS - 1) * SIG
    pieces = 8
    across = table.shape[1]
    terms = table.shape[0] - PARTS * 2 * NCHAN
    lanes = 2 * CHANNELS // owners // PARTS
    *first, filt, later = pl.pallas_call(
        functools.partial(filter_kernel, frames, pieces, spectrum_scale()),
        out_shape=[jax.ShapeDtypeStruct((sent, lanes), jnp.bfloat16)] * owners
        + [
            jax.ShapeDtypeStruct((2, rows, NCHAN), jnp.bfloat16),
            jax.ShapeDtypeStruct(((PARTS - 1) * 2 * NCHAN, across), jnp.bfloat16),
        ],
        in_specs=[IN_HBM, IN_HBM],
        out_specs=[IN_VMEM] * (owners + 2),
        scratch_shapes=[
            pltpu.VMEM((2, SIG, (frames + GROUP + TAPS - 1) * NCHAN), jnp.int32),
            pltpu.VMEM((2 * NCHAN, across), jnp.bfloat16),
            pltpu.VMEM((terms, across), jnp.bfloat16),
            pltpu.VMEM((TAPS * NCHAN // across, across), jnp.float32),
            pltpu.VMEM((owners, sent, lanes), jnp.bfloat16),
            pltpu.SemaphoreType.DMA((pieces + 3,)),
        ],
        compiler_params=pltpu.CompilerParams(vmem_limit_bytes=FILTER_VMEM_BYTES),
        cost_estimate=pl.CostEstimate(flops=1 << 29, bytes_accessed=4 << 20, transcendentals=0),
        name="filter_and_transform",
    )(voltages, table)
    return filt, later, first


def next_part(part, filt, later, owners):
    rows = filt.shape[1] - (GROUP - TAPS + 1) * SIG
    lanes = 2 * CHANNELS // owners // PARTS
    return pl.pallas_call(
        functools.partial(transform_kernel, part, spectrum_scale()),
        out_shape=[jax.ShapeDtypeStruct((rows, lanes), jnp.bfloat16)] * owners,
        in_specs=[IN_VMEM, IN_VMEM],
        out_specs=[IN_VMEM] * owners,
        scratch_shapes=[pltpu.VMEM((owners, rows, lanes), jnp.bfloat16)],
        compiler_params=pltpu.CompilerParams(vmem_limit_bytes=VMEM_BYTES),
        cost_estimate=pl.CostEstimate(flops=1 << 29, bytes_accessed=2 << 20, transcendentals=0),
        name="transform",
    )(filt, later)


def equalize_kernel(owners, frames, h, part, *refs):
    pieces = refs[owners - 1 :: -1]
    gains_ref, by_time, by_channel = refs[owners], refs[-2], refs[-1]
    out_ref = refs[owners + 1]
    width = 4 * h
    own_rows = frames * SIG
    over = (TAPS - 1) * SIG
    times = owners * frames
    tiles = times // LANES
    me = lax.axis_index("chan")
    for d in range(owners):
        source = jnp.bitwise_xor(me, d)
        start = pl.multiple_of(source * own_rows, own_rows)
        by_time[pl.ds(start, own_rows), :width] = pieces[d][:own_rows, :].astype(jnp.float32)
    for d in range(owners):
        source = jnp.bitwise_xor(me, d)

        @pl.when(source < owners - 1)
        def _():
            start = pl.multiple_of((source + 1) * own_rows, own_rows)
            by_time[pl.ds(start, over), :width] += pieces[d][own_rows:, :].astype(jnp.float32)

    gains = [gains_ref[(2 * part + r) * h : (2 * part + r + 1) * h, :] for r in range(2)]
    for s in range(SIG):
        x = by_time[pl.ds(s, times, stride=SIG), :][:, :width].T
        for r in range(2):
            real, imag = x[2 * r * h : (2 * r + 1) * h], x[(2 * r + 1) * h : (2 * r + 2) * h]
            gain_real, gain_imag = gains[r][:, 2 * s : 2 * s + 1], gains[r][:, 2 * s + 1 : 2 * s + 2]
            both = [real * gain_real - imag * gain_imag, real * gain_imag + imag * gain_real]
            for q in range(2):
                for tile in range(tiles):
                    by_channel[(2 * r + q) * tiles + tile, pl.ds(s, h, stride=SIG), :] = both[q][
                        :, tile * LANES : (tile + 1) * LANES
                    ]
    for r in range(2):
        for tile in range(2 * tiles):
            out_ref[r, :, tile * LANES : (tile + 1) * LANES] = by_channel[r * 2 * tiles + tile].astype(jnp.bfloat16)


def equalize(pieces, gains, part, frames):
    owners = len(pieces)
    h = gains.shape[0] // PARTS // 2
    times = owners * frames
    return pl.pallas_call(
        functools.partial(equalize_kernel, owners, frames, h, part),
        out_shape=jax.ShapeDtypeStruct((2, h * SIG, 2 * times), jnp.bfloat16),
        in_specs=[IN_VMEM] * (owners + 1),
        out_specs=IN_VMEM,
        scratch_shapes=[
            pltpu.VMEM((times * SIG, LANES), jnp.float32),
            pltpu.VMEM((4 * times // LANES, h * SIG, LANES), jnp.float32),
        ],
        compiler_params=pltpu.CompilerParams(vmem_limit_bytes=VMEM_BYTES),
        cost_estimate=pl.CostEstimate(flops=0, bytes_accessed=1 << 10, transcendentals=0),
        name="equalize",
    )(*pieces[::-1], gains)


def row_places(col, n_col):
    chips = n_col // 2
    chip, core = lax.div(col, 2), lax.rem(col, 2)
    places = [col] + [lax.rem(chip + chips - d, chips) * 2 + core for d in range(1, chips)]
    return places + [jnp.bitwise_xor(p, 1) for p in places]


def column_places(row, n_row):
    return [row] + [lax.rem(row + n_row - d, n_row) for d in range(1, n_row)]


def regroup(v):
    lane = lax.broadcasted_iota(jnp.int32, v[0].shape, 1)
    v = list(v)
    for bit in (2, 1):
        width = bit * LANES // 8
        low = (lane // width) % 2 == 0
        for i in range(4):
            if i & bit == 0:
                a, b = v[i], v[i + bit]
                v[i] = jnp.where(low, a, pltpu.roll(b, width, axis=1))
                v[i + bit] = jnp.where(low, pltpu.roll(a, LANES - width, axis=1), b)
    return v


def correlate_kernel(n_row, n_col, h, times, part, dense, map_ref, *refs):
    row_blocks = refs[:n_col]
    col_blocks = (refs[0],) + refs[n_col : n_col + n_row - 1]
    last = part == PARTS - 1
    if last:
        out_hbm, chosen, out_ref, sems = refs[-4:]
    else:
        out_ref, chosen = refs[-2:]
    earlier = refs[n_col + n_row - 1]
    me_row, me_col = lax.axis_index("brow"), lax.axis_index("bcol")
    row_at, col_at = row_places(me_col, n_col), column_places(me_row, n_row)
    rows = BATCH * SIG
    tiles = n_col * rows // LANES
    steps = 2 * h // BATCH
    index_in_batch = (lax.broadcasted_iota(jnp.int32, (SIG, LANES), 1) // SIG) % BATCH

    for step in range(steps):
        inner, parity = step // 2, step % 2
        here = slice(inner * rows, (inner + 1) * rows)
        a = jnp.concatenate([block[parity, here, :] for block in row_blocks], axis=0)
        b = jnp.concatenate([block[parity, here, :] for block in col_blocks], axis=0)
        turned = jnp.concatenate([-b[:, times:], b[:, :times]], axis=1)
        both = jnp.concatenate([b, turned], axis=0)
        result = lax.dot_general(both, a, (((1,), (1,)), ((), ())), preferred_element_type=jnp.float32)
        for k in range(2 * n_row):
            for tile in range(tiles):
                lanes = slice(tile * LANES, (tile + 1) * LANES)
                own = [result[k * rows + i * SIG : k * rows + (i + 1) * SIG, lanes] for i in range(BATCH)]
                kept = own[0]
                for i in range(1, BATCH):
                    kept = jnp.where(index_in_batch == i, own[i], kept)
                chosen[k * tiles + tile, pl.ds(step, SIG, stride=steps), :] = kept

    copies = []
    low = lax.broadcasted_iota(jnp.int32, (SIG, LANES), 1) < LANES // 2
    for q in range(2):
        for e in range(n_row):
            for d in range(n_col):
                if d % (LANES // rows) == 0:
                    x = chosen[(q * n_row + e) * tiles + d * rows // LANES].T
                start = d * rows % LANES
                v = [x[start + i * SIG : start + (i + 1) * SIG] for i in range(BATCH)]
                if last:
                    owned = map_ref[me_row * n_col + row_at[d], col_at[e] * n_col + me_col] == 1
                    keep = jnp.where(owned, 1.0 / times, 0.0)
                a_at = pl.ds(pl.multiple_of(row_at[d] * SIG, SIG), SIG)
                mine = slice(d * SIG, (d + 1) * SIG)
                if dense:
                    for g, w in enumerate(regroup(v)):
                        if last:
                            before = earlier[q, e, g, mine, :]
                            pair = [
                                jnp.where(low, before, pltpu.roll(w, LANES // 2, axis=1)),
                                jnp.where(low, pltpu.roll(before, LANES // 2, axis=1), w),
                            ]
                            for half in range(2):
                                out_ref[q, col_at[e] * SIG + half * BATCH + g, a_at, :] = pair[half] * keep
                        else:
                            out_ref[q, e, g, mine, :] = w
                else:
                    for s2 in range(SIG):
                        w = jnp.concatenate([each[:, s2 * steps : (s2 + 1) * steps] for each in v], axis=1)
                        if part > 0:
                            w = jnp.concatenate([earlier[q, e, s2, mine, :], w], axis=1)
                        if last:
                            out_ref[q, col_at[e] * SIG + s2, a_at, :] = w * keep
                        else:
                            out_ref[q, e, s2, mine, :] = w
            if last:
                where = pl.ds(col_at[e] * SIG, SIG)
                copy = pltpu.make_async_copy(out_ref.at[q, where], out_hbm.at[q, where], sems.at[q * n_row + e])
                copy.start()
                copies.append(copy)
    for copy in copies:
        copy.wait()


def correlate(tile_map, blocks, earlier, part, n_row, n_col):
    h = blocks[0].shape[1] // SIG
    times = blocks[0].shape[2] // 2
    channels = 2 * h
    dense = channels * 2 == LANES and PARTS == 2
    operands = list(blocks) + ([earlier] if part else [])
    last = part == PARTS - 1
    if last:
        out_shape = (2, n_row * SIG, n_col * SIG, (part + 1) * channels)
    elif dense:
        out_shape = (2, n_row, SIG // 2, n_col * SIG, LANES)
    else:
        out_shape = (2, n_row, SIG, n_col * SIG, (part + 1) * channels)
    in_last = [pltpu.VMEM(out_shape, jnp.float32), pltpu.SemaphoreType.DMA((2 * n_row,))]
    kept = pltpu.VMEM((2 * n_row * n_col * BATCH * SIG // LANES, SIG * channels // BATCH, LANES), jnp.float32)
    return pl.pallas_call(
        functools.partial(correlate_kernel, n_row, n_col, h, times, part, dense),
        out_shape=jax.ShapeDtypeStruct(out_shape, jnp.float32),
        in_specs=[IN_SMEM] + [IN_VMEM] * len(operands),
        out_specs=IN_HBM if last else IN_VMEM,
        scratch_shapes=[kept] + (in_last if last else []),
        compiler_params=pltpu.CompilerParams(vmem_limit_bytes=VMEM_BYTES),
        cost_estimate=pl.CostEstimate(flops=0, bytes_accessed=1 << 10, transcendentals=0),
        name="correlate",
    )(tile_map, *operands)


def to_owners(pieces):
    owners = len(pieces)
    arrived = [pieces[0]] + [None] * (owners - 1)
    for d in range(owners - 1, 0, -1):
        arrived[d] = lax.ppermute(pieces[d], "chan", [(i, i ^ d) for i in range(owners)])
    return arrived


def held_back(blocks, after):
    def kernel(*refs):
        for i in range(len(blocks)):
            refs[len(blocks) + len(after) + i][...] = refs[i][...]

    return pl.pallas_call(
        kernel,
        out_shape=[jax.ShapeDtypeStruct(block.shape, block.dtype) for block in blocks],
        in_specs=[IN_VMEM] * (len(blocks) + len(after)),
        out_specs=[IN_VMEM] * len(blocks),
        compiler_params=pltpu.CompilerParams(vmem_limit_bytes=VMEM_BYTES),
        cost_estimate=pl.CostEstimate(flops=0, bytes_accessed=1 << 10, transcendentals=0),
        name="held_back",
    )(*blocks, *after)


def together(blocks):
    def kernel(*refs):
        for i in range(len(blocks)):
            refs[-1][i] = refs[i][...]

    return pl.pallas_call(
        kernel,
        out_shape=jax.ShapeDtypeStruct((len(blocks),) + blocks[0].shape, blocks[0].dtype),
        in_specs=[IN_VMEM] * len(blocks),
        out_specs=IN_VMEM,
        compiler_params=pltpu.CompilerParams(vmem_limit_bytes=VMEM_BYTES),
        cost_estimate=pl.CostEstimate(flops=0, bytes_accessed=1 << 10, transcendentals=0),
        name="together",
    )(*blocks)


def shards(voltages, antenna_gains, tile_map):
    owners = lax.axis_size("chan")
    n_row = lax.axis_size("brow")
    n_col = lax.axis_size("bcol")
    chips = n_col // 2
    frames = voltages.shape[2] // NCHAN
    table = jnp.asarray(constants(owners))
    gains = antenna_gains.reshape(2 * SIG, PARTS, BATCH, -1, 2)
    gains = jnp.transpose(gains, (1, 4, 3, 2, 0)).reshape(-1, 2 * SIG)
    pad = -gains.shape[1] % LANES
    gains = jnp.pad(gains, ((0, 0), (0, pad)))
    across = [[(i, (i // 2 + d) % chips * 2 + i % 2) for i in range(n_col)] for d in range(chips)]
    along = [[(i, (i + d) % n_row) for i in range(n_row)] for d in range(n_row)]
    other_core = [(i, i ^ 1) for i in range(n_col)]

    filt, tables, pieces = filtered_and_first(voltages, owners, table)
    own, far, column = [], [], []
    arrived = to_owners(pieces)
    for part in range(PARTS):
        later = None
        if part < PARTS - 1:
            pieces = next_part(part + 1, filt, tables, owners)
            later = to_owners([pieces[0], *held_back(pieces[1:], arrived[-1:])])
        own.append(equalize(arrived, gains, part, frames))
        far.append([lax.ppermute(own[part], "bcol", across[d]) for d in range(1, chips)])
        column.append([lax.ppermute(own[part], "brow", along[d]) for d in range(1, n_row)])
        arrived = later
    beside = [lax.ppermute(block, "bcol", other_core) for block in own]
    result = None
    for part in range(PARTS):
        after = own[-1:] + column[part]
        far[part] = list(held_back(far[part], after))
        near = [lax.ppermute(block, "bcol", other_core) for block in far[part]]
        blocks = [own[part]] + far[part] + [beside[part]] + near + column[part]
        result = correlate(tile_map, blocks, result, part, n_row, n_col)
    return jnp.transpose(result, (3, 0, 1, 2))[None, None]


def solution(mesh):
    in_specs = (P(None, ("brow", "bcol"), "chan"), P(("brow", "bcol"), None, "chan"), P())
    out_specs = P("brow", "bcol", "chan", None, None, None)
    return jax.shard_map(shards, mesh=mesh, in_specs=in_specs, out_specs=out_specs, check_vma=False)
```

```python
import functools
import math

import jax
import jax.numpy as jnp
import ml_dtypes
import numpy as np
from jax import lax
from jax.experimental import pallas as pl
from jax.experimental.pallas import tpu as pltpu
from jax.sharding import PartitionSpec as P

NCHAN = 1024
HALF = NCHAN // 2
CHANNELS = 512
TAPS = 4
FIRST = 256
SIG = 8
LANES = 128
GROUP = 4
BATCH = 4
PARTS = 2
VMEM_BYTES = 16 * 1024 * 1024
FILTER_VMEM_BYTES = 101 * 512 * 1024
COEF_ROWS = 64


def fir_coefficients():
    position = np.arange(TAPS * NCHAN, dtype=np.float64) + 0.5
    offsets = position / NCHAN - TAPS / 2.0
    window = 0.5 - 0.5 * np.cos(2.0 * math.pi * position / (TAPS * NCHAN))
    return (np.sinc(offsets) * window).reshape(TAPS, NCHAN)


def spectrum_scale():
    return float(1.0 / (128.0 * np.sqrt(np.sum(fir_coefficients() ** 2))))


def dft_tables(owners):
    n = np.arange(HALF, dtype=np.int64).reshape(HALF, 1, 1, 1, 1, 1)
    k = FIRST + np.arange(CHANNELS, dtype=np.int64).reshape(owners, PARTS, BATCH, -1, 2)
    angles = (n * k % NCHAN) * (2.0 * math.pi / NCHAN)
    cosine, sine = np.cos(angles), np.sin(angles)
    first = np.stack([cosine, -sine], axis=2)
    second = np.stack([sine, cosine], axis=2)
    tables = np.stack([first, second])
    tables = np.transpose(tables, (4, 7, 0, 1, 2, 3, 6, 5))
    return tables.reshape(PARTS, 2 * NCHAN, -1).astype(np.float32).astype(ml_dtypes.bfloat16)


def constants(owners):
    tables = dft_tables(owners)
    lanes = tables.shape[2]
    left = fir_coefficients().astype(np.float32)
    terms = []
    for _ in range(3):
        terms.append(left.astype(ml_dtypes.bfloat16))
        left = left - terms[-1].astype(np.float32)
    terms = np.stack(terms).reshape(-1, lanes)
    pad = np.zeros((-terms.shape[0] % COEF_ROWS, lanes), ml_dtypes.bfloat16)
    return np.concatenate([tables.reshape(-1, lanes), terms, pad])


def transform(filt, table, scale, stage, out_refs):
    owners = len(out_refs)
    me = lax.axis_index("chan")
    spectra = [
        jnp.dot(filt[r], table[r * NCHAN : (r + 1) * NCHAN], preferred_element_type=jnp.float32) * scale
        for r in range(2)
    ]
    width = spectra[0].shape[1] // owners
    for owner in range(owners):
        here = slice(owner * width, (owner + 1) * width)
        piece = jnp.concatenate([spectra[0][:, here], spectra[1][:, here]], axis=1)
        stage[jnp.bitwise_xor(me, owner)] = piece[: stage.shape[1]].astype(jnp.bfloat16)
    for d in range(owners):
        out_refs[d][...] = stage[d]


def filter_kernel(frames, pieces, scale, volt_hbm, table_hbm, *refs):
    out_refs, (filt, later, volt, table, terms, coef, stage, sems) = refs[:-8], refs[-8:]
    per = frames // pieces
    lead = TAPS - 1
    copies = []
    for piece in range(pieces):
        copies.append(
            pltpu.make_async_copy(
                volt_hbm.at[:, :, pl.ds(piece * per * NCHAN, per * NCHAN)],
                volt.at[:, :, pl.ds((lead + piece * per) * NCHAN, per * NCHAN)],
                sems.at[piece],
            )
        )
    table_copy = pltpu.make_async_copy(table_hbm.at[pl.ds(0, 2 * NCHAN)], table, sems.at[pieces])
    coef_copy = pltpu.make_async_copy(
        table_hbm.at[pl.ds(PARTS * 2 * NCHAN, terms.shape[0])], terms, sems.at[pieces + 1]
    )
    coef_copy.start()
    for copy in copies:
        copy.start()
    later_copy = pltpu.make_async_copy(
        table_hbm.at[pl.ds(2 * NCHAN, (PARTS - 1) * 2 * NCHAN)], later, sems.at[pieces + 2]
    )
    table_copy.start()
    later_copy.start()
    tail = volt.shape[2] - (lead + frames) * NCHAN
    volt[:, :, : lead * NCHAN] = jnp.zeros((2, SIG, lead * NCHAN), jnp.int32)
    volt[:, :, (lead + frames) * NCHAN :] = jnp.zeros((2, SIG, tail), jnp.int32)
    coef_copy.wait()
    across = coef.shape[1]
    per_term = TAPS * NCHAN // across
    coef[...] = sum(terms[t * per_term : (t + 1) * per_term, :].astype(jnp.float32) for t in range(3))

    def filter_group(group, _):
        base = pl.multiple_of(group * (GROUP * NCHAN), GROUP * NCHAN)
        rows = pl.ds(pl.multiple_of(group * (GROUP * SIG), GROUP * SIG), GROUP * SIG)
        for column in range(HALF // LANES):
            for part in range(2):
                halves = []
                for half in range(2):
                    lane = half * HALF + column * LANES
                    at = [k * (NCHAN // across) + lane // across for k in range(TAPS)]
                    taps = [coef[i : i + 1, lane % across : lane % across + LANES] for i in at]
                    near = [
                        volt[part, :, pl.ds(base + f * NCHAN + lane, LANES)].astype(jnp.float32)
                        for f in range(GROUP + TAPS - 1)
                    ]
                    sums = []
                    for m in range(GROUP):
                        total = taps[0] * near[m]
                        for k in range(1, TAPS):
                            total = total + taps[k] * near[m + k]
                        sums.append(total)
                    halves.append(jnp.concatenate(sums, axis=0))
                where = pl.ds(part * HALF + column * LANES, LANES)
                filt[0, rows, where] = (halves[0] + halves[1]).astype(jnp.bfloat16)
                filt[1, rows, where] = (halves[0] - halves[1]).astype(jnp.bfloat16)
        return 0

    groups = per // GROUP
    for piece in range(pieces):
        copies[piece].wait()
        lax.fori_loop(piece * groups, (piece + 1) * groups, filter_group, 0)
    lax.fori_loop(frames // GROUP, frames // GROUP + 1, filter_group, 0)
    table_copy.wait()
    transform(filt, table, scale, stage, out_refs)
    later_copy.wait()


def transform_kernel(part, scale, filt, later, gains_ref, pick_ref, *refs):
    table = later.at[pl.ds((part - 1) * 2 * NCHAN, 2 * NCHAN)]
    if part == 1:
        columns, stage = refs[-2:]
        gains = jnp.concatenate([gains_ref[:, 0, :], gains_ref[:, 1, :]], axis=0)
        columns[...] = lax.dot_general(
            pick_ref[...],
            gains,
            (((1,), (1,)), ((), ())),
            precision=lax.Precision.HIGHEST,
            preferred_element_type=jnp.float32,
        )
        transform(filt, table, scale, stage, refs[:-2])
    else:
        transform(filt, table, scale, refs[-1], refs[:-1])


IN_VMEM = pl.BlockSpec(memory_space=pltpu.VMEM)
IN_HBM = pl.BlockSpec(memory_space=pl.ANY)
IN_SMEM = pl.BlockSpec(memory_space=pltpu.SMEM)


def filtered_and_first(voltages, owners, table):
    frames = voltages.shape[2] // NCHAN
    rows = (frames + GROUP) * SIG
    sent = (frames + TAPS - 1) * SIG
    pieces = 4
    across = table.shape[1]
    terms = table.shape[0] - PARTS * 2 * NCHAN
    lanes = 2 * CHANNELS // owners // PARTS
    *first, filt, later = pl.pallas_call(
        functools.partial(filter_kernel, frames, pieces, spectrum_scale()),
        out_shape=[jax.ShapeDtypeStruct((sent, lanes), jnp.bfloat16)] * owners
        + [
            jax.ShapeDtypeStruct((2, rows, NCHAN), jnp.bfloat16),
            jax.ShapeDtypeStruct(((PARTS - 1) * 2 * NCHAN, across), jnp.bfloat16),
        ],
        in_specs=[IN_HBM, IN_HBM],
        out_specs=[IN_VMEM] * (owners + 2),
        scratch_shapes=[
            pltpu.VMEM((2, SIG, (frames + GROUP + TAPS - 1) * NCHAN), jnp.int32),
            pltpu.VMEM((2 * NCHAN, across), jnp.bfloat16),
            pltpu.VMEM((terms, across), jnp.bfloat16),
            pltpu.VMEM((TAPS * NCHAN // across, across), jnp.float32),
            pltpu.VMEM((owners, sent, lanes), jnp.bfloat16),
            pltpu.SemaphoreType.DMA((pieces + 3,)),
        ],
        compiler_params=pltpu.CompilerParams(vmem_limit_bytes=FILTER_VMEM_BYTES),
        cost_estimate=pl.CostEstimate(flops=1 << 29, bytes_accessed=4 << 20, transcendentals=0),
        name="filter_and_transform",
    )(voltages, table)
    return filt, later, first


def pick_rows(channels):
    order = np.arange(channels).reshape(PARTS, BATCH, -1, 2)
    return np.eye(channels, dtype=np.float32)[np.transpose(order, (0, 3, 2, 1)).reshape(-1)]


def next_part(part, filt, later, gains, owners):
    rows = filt.shape[1] - (GROUP - TAPS + 1) * SIG
    lanes = 2 * CHANNELS // owners // PARTS
    channels = gains.shape[2]
    shapes = [jax.ShapeDtypeStruct((rows, lanes), jnp.bfloat16)] * owners
    if part == 1:
        shapes.append(jax.ShapeDtypeStruct((channels, 2 * SIG), jnp.float32))
    return pl.pallas_call(
        functools.partial(transform_kernel, part, spectrum_scale()),
        out_shape=shapes,
        in_specs=[IN_VMEM] * 4,
        out_specs=[IN_VMEM] * len(shapes),
        scratch_shapes=[pltpu.VMEM((owners, rows, lanes), jnp.bfloat16)],
        compiler_params=pltpu.CompilerParams(vmem_limit_bytes=VMEM_BYTES),
        cost_estimate=pl.CostEstimate(flops=1 << 29, bytes_accessed=2 << 20, transcendentals=0),
        name="transform",
    )(filt, later, gains, jnp.asarray(pick_rows(channels)))


def equalize_kernel(owners, frames, h, part, *refs):
    pieces = refs[owners - 1 :: -1]
    gains_ref, by_time, by_channel = refs[owners], refs[-2], refs[-1]
    out_ref = refs[owners + 1]
    width = 4 * h
    own_rows = frames * SIG
    over = (TAPS - 1) * SIG
    times = owners * frames
    tiles = times // LANES
    me = lax.axis_index("chan")
    for d in range(owners):
        source = jnp.bitwise_xor(me, d)
        start = pl.multiple_of(source * own_rows, own_rows)
        by_time[pl.ds(start, own_rows), :width] = pieces[d][:own_rows, :].astype(jnp.float32)
    for d in range(owners):
        source = jnp.bitwise_xor(me, d)

        @pl.when(source < owners - 1)
        def _():
            start = pl.multiple_of((source + 1) * own_rows, own_rows)
            by_time[pl.ds(start, over), :width] += pieces[d][own_rows:, :].astype(jnp.float32)

    gains = [gains_ref[(2 * part + r) * h : (2 * part + r + 1) * h, :] for r in range(2)]
    for s in range(SIG):
        x = by_time[pl.ds(s, times, stride=SIG), :][:, :width].T
        for r in range(2):
            real, imag = x[2 * r * h : (2 * r + 1) * h], x[(2 * r + 1) * h : (2 * r + 2) * h]
            gain_real, gain_imag = gains[r][:, s : s + 1], gains[r][:, SIG + s : SIG + s + 1]
            both = [real * gain_real - imag * gain_imag, real * gain_imag + imag * gain_real]
            for q in range(2):
                for tile in range(tiles):
                    by_channel[(2 * r + q) * tiles + tile, pl.ds(s, h, stride=SIG), :] = both[q][
                        :, tile * LANES : (tile + 1) * LANES
                    ]
    for r in range(2):
        for tile in range(2 * tiles):
            out_ref[r, :, tile * LANES : (tile + 1) * LANES] = by_channel[r * 2 * tiles + tile].astype(jnp.bfloat16)


def equalize(pieces, gains, part, frames):
    owners = len(pieces)
    h = gains.shape[0] // PARTS // 2
    times = owners * frames
    return pl.pallas_call(
        functools.partial(equalize_kernel, owners, frames, h, part),
        out_shape=jax.ShapeDtypeStruct((2, h * SIG, 2 * times), jnp.bfloat16),
        in_specs=[IN_VMEM] * (owners + 1),
        out_specs=IN_VMEM,
        scratch_shapes=[
            pltpu.VMEM((times * SIG, LANES), jnp.float32),
            pltpu.VMEM((4 * times // LANES, h * SIG, LANES), jnp.float32),
        ],
        compiler_params=pltpu.CompilerParams(vmem_limit_bytes=VMEM_BYTES),
        cost_estimate=pl.CostEstimate(flops=0, bytes_accessed=1 << 10, transcendentals=0),
        name="equalize",
    )(*pieces[::-1], gains)


def row_places(col, n_col):
    chips = n_col // 2
    chip, core = lax.div(col, 2), lax.rem(col, 2)
    places = [col] + [lax.rem(chip + chips - d, chips) * 2 + core for d in range(1, chips)]
    return places + [jnp.bitwise_xor(p, 1) for p in places]


def column_places(row, n_row):
    return [row] + [lax.rem(row + n_row - d, n_row) for d in range(1, n_row)]


def regroup(v):
    lane = lax.broadcasted_iota(jnp.int32, v[0].shape, 1)
    v = list(v)
    for bit in (2, 1):
        width = bit * LANES // 8
        low = (lane // width) % 2 == 0
        for i in range(4):
            if i & bit == 0:
                a, b = v[i], v[i + bit]
                v[i] = jnp.where(low, a, pltpu.roll(b, width, axis=1))
                v[i + bit] = jnp.where(low, pltpu.roll(a, LANES - width, axis=1), b)
    return v


def correlate_kernel(n_row, n_col, h, times, part, dense, map_ref, *refs):
    row_blocks = refs[:n_col]
    col_blocks = (refs[0],) + refs[n_col : n_col + n_row - 1]
    last = part == PARTS - 1
    if last:
        out_hbm, chosen, out_ref, sems = refs[-4:]
    else:
        out_ref, chosen = refs[-2:]
    earlier = refs[n_col + n_row - 1]
    me_row, me_col = lax.axis_index("brow"), lax.axis_index("bcol")
    row_at, col_at = row_places(me_col, n_col), column_places(me_row, n_row)
    rows = BATCH * SIG
    tiles = n_col * rows // LANES
    steps = 2 * h // BATCH
    index_in_batch = (lax.broadcasted_iota(jnp.int32, (SIG, LANES), 1) // SIG) % BATCH

    for step in range(steps):
        inner, parity = step // 2, step % 2
        here = slice(inner * rows, (inner + 1) * rows)
        a = jnp.concatenate([block[parity, here, :] for block in row_blocks], axis=0)
        b = jnp.concatenate([block[parity, here, :] for block in col_blocks], axis=0)
        turned = jnp.concatenate([-b[:, times:], b[:, :times]], axis=1)
        both = jnp.concatenate([b, turned], axis=0)
        result = lax.dot_general(both, a, (((1,), (1,)), ((), ())), preferred_element_type=jnp.float32)
        for k in range(2 * n_row):
            for tile in range(tiles):
                lanes = slice(tile * LANES, (tile + 1) * LANES)
                own = [result[k * rows + i * SIG : k * rows + (i + 1) * SIG, lanes] for i in range(BATCH)]
                kept = own[0]
                for i in range(1, BATCH):
                    kept = jnp.where(index_in_batch == i, own[i], kept)
                chosen[k * tiles + tile, pl.ds(step, SIG, stride=steps), :] = kept

    copies = []
    low = lax.broadcasted_iota(jnp.int32, (SIG, LANES), 1) < LANES // 2
    for q in range(2):
        for e in range(n_row):
            for d in range(n_col):
                if d % (LANES // rows) == 0:
                    x = chosen[(q * n_row + e) * tiles + d * rows // LANES].T
                start = d * rows % LANES
                v = [x[start + i * SIG : start + (i + 1) * SIG] for i in range(BATCH)]
                if last:
                    owned = map_ref[me_row * n_col + row_at[d], col_at[e] * n_col + me_col] == 1
                    keep = jnp.where(owned, 1.0 / times, 0.0)
                a_at = pl.ds(pl.multiple_of(row_at[d] * SIG, SIG), SIG)
                mine = slice(d * SIG, (d + 1) * SIG)
                if dense:
                    for g, w in enumerate(regroup(v)):
                        if last:
                            before = earlier[q, e, g, mine, :]
                            pair = [
                                jnp.where(low, before, pltpu.roll(w, LANES // 2, axis=1)),
                                jnp.where(low, pltpu.roll(before, LANES // 2, axis=1), w),
                            ]
                            for half in range(2):
                                out_ref[q, col_at[e] * SIG + half * BATCH + g, a_at, :] = pair[half] * keep
                        else:
                            out_ref[q, e, g, mine, :] = w
                else:
                    for s2 in range(SIG):
                        w = jnp.concatenate([each[:, s2 * steps : (s2 + 1) * steps] for each in v], axis=1)
                        if part > 0:
                            w = jnp.concatenate([earlier[q, e, s2, mine, :], w], axis=1)
                        if last:
                            out_ref[q, col_at[e] * SIG + s2, a_at, :] = w * keep
                        else:
                            out_ref[q, e, s2, mine, :] = w
            if last:
                where = pl.ds(col_at[e] * SIG, SIG)
                copy = pltpu.make_async_copy(out_ref.at[q, where], out_hbm.at[q, where], sems.at[q * n_row + e])
                copy.start()
                copies.append(copy)
    for copy in copies:
        copy.wait()


def correlate(tile_map, blocks, earlier, part, n_row, n_col):
    h = blocks[0].shape[1] // SIG
    times = blocks[0].shape[2] // 2
    channels = 2 * h
    dense = channels * 2 == LANES and PARTS == 2
    operands = list(blocks) + ([earlier] if part else [])
    last = part == PARTS - 1
    if last:
        out_shape = (2, n_row * SIG, n_col * SIG, (part + 1) * channels)
    elif dense:
        out_shape = (2, n_row, SIG // 2, n_col * SIG, LANES)
    else:
        out_shape = (2, n_row, SIG, n_col * SIG, (part + 1) * channels)
    in_last = [pltpu.VMEM(out_shape, jnp.float32), pltpu.SemaphoreType.DMA((2 * n_row,))]
    kept = pltpu.VMEM((2 * n_row * n_col * BATCH * SIG // LANES, SIG * channels // BATCH, LANES), jnp.float32)
    return pl.pallas_call(
        functools.partial(correlate_kernel, n_row, n_col, h, times, part, dense),
        out_shape=jax.ShapeDtypeStruct(out_shape, jnp.float32),
        in_specs=[IN_SMEM] + [IN_VMEM] * len(operands),
        out_specs=IN_HBM if last else IN_VMEM,
        scratch_shapes=[kept] + (in_last if last else []),
        compiler_params=pltpu.CompilerParams(vmem_limit_bytes=VMEM_BYTES),
        cost_estimate=pl.CostEstimate(flops=0, bytes_accessed=1 << 10, transcendentals=0),
        name="correlate",
    )(tile_map, *operands)


def to_owners(pieces):
    owners = len(pieces)
    arrived = [pieces[0]] + [None] * (owners - 1)
    for d in range(owners - 1, 0, -1):
        arrived[d] = lax.ppermute(pieces[d], "chan", [(i, i ^ d) for i in range(owners)])
    return arrived


def held_back(blocks, after):
    def kernel(*refs):
        for i in range(len(blocks)):
            refs[len(blocks) + len(after) + i][...] = refs[i][...]

    return pl.pallas_call(
        kernel,
        out_shape=[jax.ShapeDtypeStruct(block.shape, block.dtype) for block in blocks],
        in_specs=[IN_VMEM] * (len(blocks) + len(after)),
        out_specs=[IN_VMEM] * len(blocks),
        compiler_params=pltpu.CompilerParams(vmem_limit_bytes=VMEM_BYTES),
        cost_estimate=pl.CostEstimate(flops=0, bytes_accessed=1 << 10, transcendentals=0),
        name="held_back",
    )(*blocks, *after)


def together(blocks):
    def kernel(*refs):
        for i in range(len(blocks)):
            refs[-1][i] = refs[i][...]

    return pl.pallas_call(
        kernel,
        out_shape=jax.ShapeDtypeStruct((len(blocks),) + blocks[0].shape, blocks[0].dtype),
        in_specs=[IN_VMEM] * len(blocks),
        out_specs=IN_VMEM,
        compiler_params=pltpu.CompilerParams(vmem_limit_bytes=VMEM_BYTES),
        cost_estimate=pl.CostEstimate(flops=0, bytes_accessed=1 << 10, transcendentals=0),
        name="together",
    )(*blocks)


def shards(voltages, antenna_gains, tile_map):
    owners = lax.axis_size("chan")
    n_row = lax.axis_size("brow")
    n_col = lax.axis_size("bcol")
    chips = n_col // 2
    frames = voltages.shape[2] // NCHAN
    table = jnp.asarray(constants(owners))
    across = [[(i, (i // 2 + d) % chips * 2 + i % 2) for i in range(n_col)] for d in range(chips)]
    along = [[(i, (i + d) % n_row) for i in range(n_row)] for d in range(n_row)]
    other_core = [(i, i ^ 1) for i in range(n_col)]

    filt, tables, pieces = filtered_and_first(voltages, owners, table)
    own, far, column = [], [], []
    arrived = to_owners(pieces)
    for part in range(PARTS):
        later = None
        if part < PARTS - 1:
            pieces = next_part(part + 1, filt, tables, antenna_gains, owners)
            if part == 0:
                *pieces, gains = pieces
            later = to_owners([pieces[0], *held_back(pieces[1:], arrived[-1:])])
        own.append(equalize(arrived, gains, part, frames))
        far.append([lax.ppermute(own[part], "bcol", across[d]) for d in range(1, chips)])
        column.append([lax.ppermute(own[part], "brow", along[d]) for d in range(1, n_row)])
        arrived = later
    beside = [lax.ppermute(block, "bcol", other_core) for block in own]
    result = None
    for part in range(PARTS):
        after = own[-1:] + column[part]
        far[part] = list(held_back(far[part], after))
        near = [lax.ppermute(block, "bcol", other_core) for block in far[part]]
        blocks = [own[part]] + far[part] + [beside[part]] + near + column[part]
        result = correlate(tile_map, blocks, result, part, n_row, n_col)
    return jnp.transpose(result, (3, 0, 1, 2))[None, None]


def solution(mesh):
    in_specs = (P(None, ("brow", "bcol"), "chan"), P(("brow", "bcol"), None, "chan"), P())
    out_specs = P("brow", "bcol", "chan", None, None, None)
    return jax.shard_map(shards, mesh=mesh, in_specs=in_specs, out_specs=out_specs, check_vma=False)
```

```python
import functools
import math

import jax
import jax.numpy as jnp
import ml_dtypes
import numpy as np
from jax import lax
from jax.experimental import pallas as pl
from jax.experimental.pallas import tpu as pltpu
from jax.sharding import PartitionSpec as P

NCHAN = 1024
HALF = NCHAN // 2
CHANNELS = 512
TAPS = 4
FIRST = 256
SIG = 8
LANES = 128
GROUP = 4
BATCH = 4
PARTS = 2
VMEM_BYTES = 16 * 1024 * 1024
FILTER_VMEM_BYTES = 101 * 512 * 1024
COEF_ROWS = 64


def fir_coefficients():
    position = np.arange(TAPS * NCHAN, dtype=np.float64) + 0.5
    offsets = position / NCHAN - TAPS / 2.0
    window = 0.5 - 0.5 * np.cos(2.0 * math.pi * position / (TAPS * NCHAN))
    return (np.sinc(offsets) * window).reshape(TAPS, NCHAN)


def spectrum_scale():
    return float(1.0 / (128.0 * np.sqrt(np.sum(fir_coefficients() ** 2))))


def dft_tables(owners):
    n = np.arange(HALF, dtype=np.int64).reshape(HALF, 1, 1, 1, 1, 1)
    k = FIRST + np.arange(CHANNELS, dtype=np.int64).reshape(owners, PARTS, BATCH, -1, 2)
    angles = (n * k % NCHAN) * (2.0 * math.pi / NCHAN)
    cosine, sine = np.cos(angles), np.sin(angles)
    first = np.stack([cosine, -sine], axis=2)
    second = np.stack([sine, cosine], axis=2)
    tables = np.stack([first, second])
    tables = np.transpose(tables, (4, 7, 0, 1, 2, 3, 6, 5))
    return tables.reshape(PARTS, 2 * NCHAN, -1).astype(np.float32).astype(ml_dtypes.bfloat16)


def constants(owners):
    tables = dft_tables(owners)
    lanes = tables.shape[2]
    left = fir_coefficients().astype(np.float32)
    terms = []
    for _ in range(3):
        terms.append(left.astype(ml_dtypes.bfloat16))
        left = left - terms[-1].astype(np.float32)
    terms = np.stack(terms).reshape(-1, lanes)
    pad = np.zeros((-terms.shape[0] % COEF_ROWS, lanes), ml_dtypes.bfloat16)
    return np.concatenate([tables.reshape(-1, lanes), terms, pad])


def transform(filt, table, scale, stage, out_refs):
    owners = len(out_refs)
    me = lax.axis_index("chan")
    spectra = [
        jnp.dot(filt[r], table[r * NCHAN : (r + 1) * NCHAN], preferred_element_type=jnp.float32) * scale
        for r in range(2)
    ]
    width = spectra[0].shape[1] // owners
    for owner in range(owners):
        here = slice(owner * width, (owner + 1) * width)
        piece = jnp.concatenate([spectra[0][:, here], spectra[1][:, here]], axis=1)
        stage[jnp.bitwise_xor(me, owner)] = piece[: stage.shape[1]].astype(jnp.bfloat16)
    for d in range(owners):
        out_refs[d][...] = stage[d]


def filter_kernel(frames, pieces, scale, volt_hbm, table_hbm, *refs):
    out_refs, (filt, later, volt, table, terms, coef, stage, sems) = refs[:-8], refs[-8:]
    per = frames // pieces
    lead = TAPS - 1
    copies = []
    for piece in range(pieces):
        copies.append(
            pltpu.make_async_copy(
                volt_hbm.at[:, :, pl.ds(piece * per * NCHAN, per * NCHAN)],
                volt.at[:, :, pl.ds((lead + piece * per) * NCHAN, per * NCHAN)],
                sems.at[piece],
            )
        )
    table_copy = pltpu.make_async_copy(table_hbm.at[pl.ds(0, 2 * NCHAN)], table, sems.at[pieces])
    coef_copy = pltpu.make_async_copy(
        table_hbm.at[pl.ds(PARTS * 2 * NCHAN, terms.shape[0])], terms, sems.at[pieces + 1]
    )
    coef_copy.start()
    for copy in copies:
        copy.start()
    later_copy = pltpu.make_async_copy(
        table_hbm.at[pl.ds(2 * NCHAN, (PARTS - 1) * 2 * NCHAN)], later, sems.at[pieces + 2]
    )
    table_copy.start()
    later_copy.start()
    tail = volt.shape[2] - (lead + frames) * NCHAN
    volt[:, :, : lead * NCHAN] = jnp.zeros((2, SIG, lead * NCHAN), jnp.int32)
    volt[:, :, (lead + frames) * NCHAN :] = jnp.zeros((2, SIG, tail), jnp.int32)
    coef_copy.wait()
    across = coef.shape[1]
    per_term = TAPS * NCHAN // across
    coef[...] = sum(terms[t * per_term : (t + 1) * per_term, :].astype(jnp.float32) for t in range(3))

    def filter_group(group, _):
        base = pl.multiple_of(group * (GROUP * NCHAN), GROUP * NCHAN)
        rows = pl.ds(pl.multiple_of(group * (GROUP * SIG), GROUP * SIG), GROUP * SIG)
        for column in range(HALF // LANES):
            for part in range(2):
                halves = []
                for half in range(2):
                    lane = half * HALF + column * LANES
                    at = [k * (NCHAN // across) + lane // across for k in range(TAPS)]
                    taps = [coef[i : i + 1, lane % across : lane % across + LANES] for i in at]
                    near = [
                        volt[part, :, pl.ds(base + f * NCHAN + lane, LANES)].astype(jnp.float32)
                        for f in range(GROUP + TAPS - 1)
                    ]
                    sums = []
                    for m in range(GROUP):
                        total = taps[0] * near[m]
                        for k in range(1, TAPS):
                            total = total + taps[k] * near[m + k]
                        sums.append(total)
                    halves.append(jnp.concatenate(sums, axis=0))
                where = pl.ds(part * HALF + column * LANES, LANES)
                filt[0, rows, where] = (halves[0] + halves[1]).astype(jnp.bfloat16)
                filt[1, rows, where] = (halves[0] - halves[1]).astype(jnp.bfloat16)
        return 0

    groups = per // GROUP
    for piece in range(pieces):
        copies[piece].wait()
        lax.fori_loop(piece * groups, (piece + 1) * groups, filter_group, 0)
    lax.fori_loop(frames // GROUP, frames // GROUP + 1, filter_group, 0)
    table_copy.wait()
    transform(filt, table, scale, stage, out_refs)
    later_copy.wait()


def transform_kernel(part, scale, filt, later, gains_ref, pick_ref, *refs):
    table = later.at[pl.ds((part - 1) * 2 * NCHAN, 2 * NCHAN)]
    if part == 1:
        columns, stage = refs[-2:]
        gains = jnp.concatenate([gains_ref[:, 0, :], gains_ref[:, 1, :]], axis=0)
        columns[...] = lax.dot_general(
            pick_ref[...],
            gains,
            (((1,), (1,)), ((), ())),
            precision=lax.Precision.HIGHEST,
            preferred_element_type=jnp.float32,
        )
        transform(filt, table, scale, stage, refs[:-2])
    else:
        transform(filt, table, scale, refs[-1], refs[:-1])


IN_VMEM = pl.BlockSpec(memory_space=pltpu.VMEM)
IN_HBM = pl.BlockSpec(memory_space=pl.ANY)


def filtered_and_first(voltages, owners, table):
    frames = voltages.shape[2] // NCHAN
    rows = (frames + GROUP) * SIG
    sent = (frames + TAPS - 1) * SIG
    pieces = 4
    across = table.shape[1]
    terms = table.shape[0] - PARTS * 2 * NCHAN
    lanes = 2 * CHANNELS // owners // PARTS
    *first, filt, later = pl.pallas_call(
        functools.partial(filter_kernel, frames, pieces, spectrum_scale()),
        out_shape=[jax.ShapeDtypeStruct((sent, lanes), jnp.bfloat16)] * owners
        + [
            jax.ShapeDtypeStruct((2, rows, NCHAN), jnp.bfloat16),
            jax.ShapeDtypeStruct(((PARTS - 1) * 2 * NCHAN, across), jnp.bfloat16),
        ],
        in_specs=[IN_HBM, IN_HBM],
        out_specs=[IN_VMEM] * (owners + 2),
        scratch_shapes=[
            pltpu.VMEM((2, SIG, (frames + GROUP + TAPS - 1) * NCHAN), jnp.int32),
            pltpu.VMEM((2 * NCHAN, across), jnp.bfloat16),
            pltpu.VMEM((terms, across), jnp.bfloat16),
            pltpu.VMEM((TAPS * NCHAN // across, across), jnp.float32),
            pltpu.VMEM((owners, sent, lanes), jnp.bfloat16),
            pltpu.SemaphoreType.DMA((pieces + 3,)),
        ],
        compiler_params=pltpu.CompilerParams(vmem_limit_bytes=FILTER_VMEM_BYTES),
        cost_estimate=pl.CostEstimate(flops=1 << 29, bytes_accessed=4 << 20, transcendentals=0),
        name="filter_and_transform",
    )(voltages, table)
    return filt, later, first


def pick_rows(channels):
    order = np.arange(channels).reshape(PARTS, BATCH, -1, 2)
    return np.eye(channels, dtype=np.float32)[np.transpose(order, (0, 3, 2, 1)).reshape(-1)]


def next_part(part, filt, later, gains, owners):
    rows = filt.shape[1] - (GROUP - TAPS + 1) * SIG
    lanes = 2 * CHANNELS // owners // PARTS
    channels = gains.shape[2]
    shapes = [jax.ShapeDtypeStruct((rows, lanes), jnp.bfloat16)] * owners
    if part == 1:
        shapes.append(jax.ShapeDtypeStruct((channels, 2 * SIG), jnp.float32))
    return pl.pallas_call(
        functools.partial(transform_kernel, part, spectrum_scale()),
        out_shape=shapes,
        in_specs=[IN_VMEM] * 4,
        out_specs=[IN_VMEM] * len(shapes),
        scratch_shapes=[pltpu.VMEM((owners, rows, lanes), jnp.bfloat16)],
        compiler_params=pltpu.CompilerParams(vmem_limit_bytes=VMEM_BYTES),
        cost_estimate=pl.CostEstimate(flops=1 << 29, bytes_accessed=2 << 20, transcendentals=0),
        name="transform",
    )(filt, later, gains, jnp.asarray(pick_rows(channels)))


def equalize_kernel(owners, frames, h, part, *refs):
    pieces = refs[owners - 1 :: -1]
    gains_ref, by_time, by_channel = refs[owners], refs[-2], refs[-1]
    out_ref = refs[owners + 1]
    width = 4 * h
    own_rows = frames * SIG
    over = (TAPS - 1) * SIG
    times = owners * frames
    tiles = times // LANES
    me = lax.axis_index("chan")
    for d in range(owners):
        source = jnp.bitwise_xor(me, d)
        start = pl.multiple_of(source * own_rows, own_rows)
        by_time[pl.ds(start, own_rows), :width] = pieces[d][:own_rows, :].astype(jnp.float32)
    for d in range(owners):
        source = jnp.bitwise_xor(me, d)

        @pl.when(source < owners - 1)
        def _():
            start = pl.multiple_of((source + 1) * own_rows, own_rows)
            by_time[pl.ds(start, over), :width] += pieces[d][own_rows:, :].astype(jnp.float32)

    gains = [gains_ref[(2 * part + r) * h : (2 * part + r + 1) * h, :] for r in range(2)]
    for s in range(SIG):
        x = by_time[pl.ds(s, times, stride=SIG), :][:, :width].T
        for r in range(2):
            real, imag = x[2 * r * h : (2 * r + 1) * h], x[(2 * r + 1) * h : (2 * r + 2) * h]
            gain_real, gain_imag = gains[r][:, s : s + 1], gains[r][:, SIG + s : SIG + s + 1]
            both = [real * gain_real - imag * gain_imag, real * gain_imag + imag * gain_real]
            for q in range(2):
                for tile in range(tiles):
                    by_channel[(2 * r + q) * tiles + tile, pl.ds(s, h, stride=SIG), :] = both[q][
                        :, tile * LANES : (tile + 1) * LANES
                    ]
    for r in range(2):
        for tile in range(2 * tiles):
            out_ref[r, :, tile * LANES : (tile + 1) * LANES] = by_channel[r * 2 * tiles + tile].astype(jnp.bfloat16)


def equalize(pieces, gains, part, frames):
    owners = len(pieces)
    h = gains.shape[0] // PARTS // 2
    times = owners * frames
    return pl.pallas_call(
        functools.partial(equalize_kernel, owners, frames, h, part),
        out_shape=jax.ShapeDtypeStruct((2, h * SIG, 2 * times), jnp.bfloat16),
        in_specs=[IN_VMEM] * (owners + 1),
        out_specs=IN_VMEM,
        scratch_shapes=[
            pltpu.VMEM((times * SIG, LANES), jnp.float32),
            pltpu.VMEM((4 * times // LANES, h * SIG, LANES), jnp.float32),
        ],
        compiler_params=pltpu.CompilerParams(vmem_limit_bytes=VMEM_BYTES),
        cost_estimate=pl.CostEstimate(flops=0, bytes_accessed=1 << 10, transcendentals=0),
        name="equalize",
    )(*pieces[::-1], gains)


def row_places(col, n_col):
    chips = n_col // 2
    chip, core = lax.div(col, 2), lax.rem(col, 2)
    places = [col] + [lax.rem(chip + chips - d, chips) * 2 + core for d in range(1, chips)]
    return places + [jnp.bitwise_xor(p, 1) for p in places]


def column_places(row, n_row):
    return [row] + [lax.rem(row + n_row - d, n_row) for d in range(1, n_row)]


def regroup(v):
    lane = lax.broadcasted_iota(jnp.int32, v[0].shape, 1)
    v = list(v)
    for bit in (2, 1):
        width = bit * LANES // 8
        low = (lane // width) % 2 == 0
        for i in range(4):
            if i & bit == 0:
                a, b = v[i], v[i + bit]
                v[i] = jnp.where(low, a, pltpu.roll(b, width, axis=1))
                v[i + bit] = jnp.where(low, pltpu.roll(a, LANES - width, axis=1), b)
    return v


def correlate_kernel(n_row, n_col, h, times, part, dense, *refs):
    row_blocks = refs[:n_col]
    col_blocks = (refs[0],) + refs[n_col : n_col + n_row - 1]
    last = part == PARTS - 1
    given = refs[n_col + n_row - 1 :]
    if part > 0:
        earlier, keeps = given[:2]
    if last:
        out_hbm, chosen, out_ref, sems = refs[-4:]
    else:
        out_ref, keeps_out, chosen = refs[-3:]
    me_row, me_col = lax.axis_index("brow"), lax.axis_index("bcol")
    row_at, col_at = row_places(me_col, n_col), column_places(me_row, n_row)
    rows = BATCH * SIG
    tiles = n_col * rows // LANES
    steps = 2 * h // BATCH
    if part == 0:
        owned = given[0][...]
        first, second = (lax.broadcasted_iota(jnp.int32, owned.shape, axis) for axis in range(2))
        for e in range(n_row):
            for d in range(n_col):
                here = (first == me_row * n_col + row_at[d]) & (second == col_at[e] * n_col + me_col)
                found = jnp.max(jnp.where(here, (owned == 1).astype(jnp.float32), 0.0), axis=(0, 1), keepdims=True)
                keeps_out[e, d] = jnp.broadcast_to(found * (1.0 / times), (SIG, LANES))
    elif not last:
        keeps_out[...] = keeps[...]
    index_in_batch = (lax.broadcasted_iota(jnp.int32, (SIG, LANES), 1) // SIG) % BATCH

    for step in range(steps):
        inner, parity = step // 2, step % 2
        here = slice(inner * rows, (inner + 1) * rows)
        a = jnp.concatenate([block[parity, here, :] for block in row_blocks], axis=0)
        b = jnp.concatenate([block[parity, here, :] for block in col_blocks], axis=0)
        turned = jnp.concatenate([-b[:, times:], b[:, :times]], axis=1)
        both = jnp.concatenate([b, turned], axis=0)
        result = lax.dot_general(both, a, (((1,), (1,)), ((), ())), preferred_element_type=jnp.float32)
        for k in range(2 * n_row):
            for tile in range(tiles):
                lanes = slice(tile * LANES, (tile + 1) * LANES)
                own = [result[k * rows + i * SIG : k * rows + (i + 1) * SIG, lanes] for i in range(BATCH)]
                kept = own[0]
                for i in range(1, BATCH):
                    kept = jnp.where(index_in_batch == i, own[i], kept)
                chosen[k * tiles + tile, pl.ds(step, SIG, stride=steps), :] = kept

    copies = []
    low = lax.broadcasted_iota(jnp.int32, (SIG, LANES), 1) < LANES // 2
    for q in range(2):
        for e in range(n_row):
            for d in range(n_col):
                if d % (LANES // rows) == 0:
                    x = chosen[(q * n_row + e) * tiles + d * rows // LANES].T
                start = d * rows % LANES
                v = [x[start + i * SIG : start + (i + 1) * SIG] for i in range(BATCH)]
                if last:
                    keep = keeps[e, d]
                a_at = pl.ds(pl.multiple_of(row_at[d] * SIG, SIG), SIG)
                mine = slice(d * SIG, (d + 1) * SIG)
                if dense:
                    for g, w in enumerate(regroup(v)):
                        if last:
                            before = earlier[q, e, g, mine, :]
                            pair = [
                                jnp.where(low, before, pltpu.roll(w, LANES // 2, axis=1)),
                                jnp.where(low, pltpu.roll(before, LANES // 2, axis=1), w),
                            ]
                            for half in range(2):
                                out_ref[q, col_at[e] * SIG + half * BATCH + g, a_at, :] = pair[half] * keep
                        else:
                            out_ref[q, e, g, mine, :] = w
                else:
                    for s2 in range(SIG):
                        w = jnp.concatenate([each[:, s2 * steps : (s2 + 1) * steps] for each in v], axis=1)
                        if part > 0:
                            w = jnp.concatenate([earlier[q, e, s2, mine, :], w], axis=1)
                        if last:
                            out_ref[q, col_at[e] * SIG + s2, a_at, :] = w * keep[:, : w.shape[1]]
                        else:
                            out_ref[q, e, s2, mine, :] = w
            if last:
                where = pl.ds(col_at[e] * SIG, SIG)
                copy = pltpu.make_async_copy(out_ref.at[q, where], out_hbm.at[q, where], sems.at[q * n_row + e])
                copy.start()
                copies.append(copy)
    for copy in copies:
        copy.wait()


def correlate(blocks, given, part, n_row, n_col):
    h = blocks[0].shape[1] // SIG
    times = blocks[0].shape[2] // 2
    channels = 2 * h
    dense = channels * 2 == LANES and PARTS == 2
    operands = list(blocks) + list(given)
    last = part == PARTS - 1
    if last:
        out_shape = (2, n_row * SIG, n_col * SIG, (part + 1) * channels)
    elif dense:
        out_shape = (2, n_row, SIG // 2, n_col * SIG, LANES)
    else:
        out_shape = (2, n_row, SIG, n_col * SIG, (part + 1) * channels)
    shapes = [out_shape] if last else [out_shape, (n_row, n_col, SIG, LANES)]
    in_last = [pltpu.VMEM(out_shape, jnp.float32), pltpu.SemaphoreType.DMA((2 * n_row,))]
    kept = pltpu.VMEM((2 * n_row * n_col * BATCH * SIG // LANES, SIG * channels // BATCH, LANES), jnp.float32)
    return pl.pallas_call(
        functools.partial(correlate_kernel, n_row, n_col, h, times, part, dense),
        out_shape=[jax.ShapeDtypeStruct(shape, jnp.float32) for shape in shapes],
        in_specs=[IN_VMEM] * len(operands),
        out_specs=[IN_HBM] if last else [IN_VMEM] * len(shapes),
        scratch_shapes=[kept] + (in_last if last else []),
        compiler_params=pltpu.CompilerParams(vmem_limit_bytes=VMEM_BYTES),
        cost_estimate=pl.CostEstimate(flops=0, bytes_accessed=1 << 10, transcendentals=0),
        name="correlate",
    )(*operands)


def to_owners(pieces):
    owners = len(pieces)
    arrived = [pieces[0]] + [None] * (owners - 1)
    for d in range(owners - 1, 0, -1):
        arrived[d] = lax.ppermute(pieces[d], "chan", [(i, i ^ d) for i in range(owners)])
    return arrived


def held_back(blocks, after):
    def kernel(*refs):
        for i in range(len(blocks)):
            refs[len(blocks) + len(after) + i][...] = refs[i][...]

    return pl.pallas_call(
        kernel,
        out_shape=[jax.ShapeDtypeStruct(block.shape, block.dtype) for block in blocks],
        in_specs=[IN_VMEM] * (len(blocks) + len(after)),
        out_specs=[IN_VMEM] * len(blocks),
        compiler_params=pltpu.CompilerParams(vmem_limit_bytes=VMEM_BYTES),
        cost_estimate=pl.CostEstimate(flops=0, bytes_accessed=1 << 10, transcendentals=0),
        name="held_back",
    )(*blocks, *after)


def together(blocks):
    def kernel(*refs):
        for i in range(len(blocks)):
            refs[-1][i] = refs[i][...]

    return pl.pallas_call(
        kernel,
        out_shape=jax.ShapeDtypeStruct((len(blocks),) + blocks[0].shape, blocks[0].dtype),
        in_specs=[IN_VMEM] * len(blocks),
        out_specs=IN_VMEM,
        compiler_params=pltpu.CompilerParams(vmem_limit_bytes=VMEM_BYTES),
        cost_estimate=pl.CostEstimate(flops=0, bytes_accessed=1 << 10, transcendentals=0),
        name="together",
    )(*blocks)


def shards(voltages, antenna_gains, tile_map):
    owners = lax.axis_size("chan")
    n_row = lax.axis_size("brow")
    n_col = lax.axis_size("bcol")
    chips = n_col // 2
    frames = voltages.shape[2] // NCHAN
    table = jnp.asarray(constants(owners))
    across = [[(i, (i // 2 + d) % chips * 2 + i % 2) for i in range(n_col)] for d in range(chips)]
    along = [[(i, (i + d) % n_row) for i in range(n_row)] for d in range(n_row)]
    other_core = [(i, i ^ 1) for i in range(n_col)]

    filt, tables, pieces = filtered_and_first(voltages, owners, table)
    own, far, column = [], [], []
    arrived = to_owners(pieces)
    for part in range(PARTS):
        later = None
        if part < PARTS - 1:
            pieces = next_part(part + 1, filt, tables, antenna_gains, owners)
            if part == 0:
                *pieces, gains = pieces
            later = to_owners([pieces[0], *held_back(pieces[1:], arrived[-1:])])
        own.append(equalize(arrived, gains, part, frames))
        far.append([lax.ppermute(own[part], "bcol", across[d]) for d in range(1, chips)])
        column.append([lax.ppermute(own[part], "brow", along[d]) for d in range(1, n_row)])
        arrived = later
    beside = [lax.ppermute(block, "bcol", other_core) for block in own]
    result = [tile_map]
    for part in range(PARTS):
        after = own[-1:] + column[part]
        far[part] = list(held_back(far[part], after))
        near = [lax.ppermute(block, "bcol", other_core) for block in far[part]]
        blocks = [own[part]] + far[part] + [beside[part]] + near + column[part]
        result = correlate(blocks, result, part, n_row, n_col)
    return jnp.transpose(result[0], (3, 0, 1, 2))[None, None]


def solution(mesh):
    in_specs = (P(None, ("brow", "bcol"), "chan"), P(("brow", "bcol"), None, "chan"), P())
    out_specs = P("brow", "bcol", "chan", None, None, None)
    return jax.shard_map(shards, mesh=mesh, in_specs=in_specs, out_specs=out_specs, check_vma=False)
```

```python
import functools
import math

import jax
import jax.numpy as jnp
import ml_dtypes
import numpy as np
from jax import lax
from jax.experimental import pallas as pl
from jax.experimental.pallas import tpu as pltpu
from jax.sharding import PartitionSpec as P

NCHAN = 1024
HALF = NCHAN // 2
CHANNELS = 512
TAPS = 4
FIRST = 256
SIG = 8
LANES = 128
GROUP = 4
BATCH = 4
PARTS = 2
VMEM_BYTES = 16 * 1024 * 1024
FILTER_VMEM_BYTES = 101 * 512 * 1024
COEF_ROWS = 64


def fir_coefficients():
    position = np.arange(TAPS * NCHAN, dtype=np.float64) + 0.5
    offsets = position / NCHAN - TAPS / 2.0
    window = 0.5 - 0.5 * np.cos(2.0 * math.pi * position / (TAPS * NCHAN))
    return (np.sinc(offsets) * window).reshape(TAPS, NCHAN)


def spectrum_scale():
    return float(1.0 / (128.0 * np.sqrt(np.sum(fir_coefficients() ** 2))))


def dft_tables(owners):
    n = np.arange(HALF, dtype=np.int64).reshape(HALF, 1, 1, 1, 1, 1)
    k = FIRST + np.arange(CHANNELS, dtype=np.int64).reshape(owners, PARTS, BATCH, -1, 2)
    angles = (n * k % NCHAN) * (2.0 * math.pi / NCHAN)
    cosine, sine = np.cos(angles), np.sin(angles)
    first = np.stack([cosine, -sine], axis=2)
    second = np.stack([sine, cosine], axis=2)
    tables = np.stack([first, second])
    tables = np.transpose(tables, (4, 7, 0, 1, 2, 3, 6, 5))
    return tables.reshape(PARTS, 2 * NCHAN, -1).astype(np.float32).astype(ml_dtypes.bfloat16)


def constants(owners):
    tables = dft_tables(owners)
    lanes = tables.shape[2]
    left = fir_coefficients().astype(np.float32)
    terms = []
    for _ in range(3):
        terms.append(left.astype(ml_dtypes.bfloat16))
        left = left - terms[-1].astype(np.float32)
    terms = np.stack(terms).reshape(-1, lanes)
    pad = np.zeros((-terms.shape[0] % COEF_ROWS, lanes), ml_dtypes.bfloat16)
    return np.concatenate([tables.reshape(-1, lanes), terms, pad])


def transform(filt, table, scale, stage, out_refs):
    owners = len(out_refs)
    me = lax.axis_index("chan")
    spectra = [
        jnp.dot(filt[r], table[r * NCHAN : (r + 1) * NCHAN], preferred_element_type=jnp.float32) * scale
        for r in range(2)
    ]
    width = spectra[0].shape[1] // owners
    for owner in range(owners):
        here = slice(owner * width, (owner + 1) * width)
        piece = jnp.concatenate([spectra[0][:, here], spectra[1][:, here]], axis=1)
        stage[jnp.bitwise_xor(me, owner)] = piece[: stage.shape[1]].astype(jnp.bfloat16)
    for d in range(owners):
        out_refs[d][...] = stage[d]


def filter_kernel(frames, pieces, scale, volt_hbm, table_hbm, *refs):
    out_refs, (filt, later, volt, table, terms, coef, stage, sems) = refs[:-8], refs[-8:]
    per = frames // pieces
    lead = TAPS - 1
    copies = []
    for piece in range(pieces):
        copies.append(
            pltpu.make_async_copy(
                volt_hbm.at[:, :, pl.ds(piece * per * NCHAN, per * NCHAN)],
                volt.at[:, :, pl.ds((lead + piece * per) * NCHAN, per * NCHAN)],
                sems.at[piece],
            )
        )
    table_copy = pltpu.make_async_copy(table_hbm.at[pl.ds(0, 2 * NCHAN)], table, sems.at[pieces])
    coef_copy = pltpu.make_async_copy(
        table_hbm.at[pl.ds(PARTS * 2 * NCHAN, terms.shape[0])], terms, sems.at[pieces + 1]
    )
    coef_copy.start()
    for copy in copies:
        copy.start()
    later_copy = pltpu.make_async_copy(
        table_hbm.at[pl.ds(2 * NCHAN, (PARTS - 1) * 2 * NCHAN)], later, sems.at[pieces + 2]
    )
    table_copy.start()
    later_copy.start()
    tail = volt.shape[2] - (lead + frames) * NCHAN
    volt[:, :, : lead * NCHAN] = jnp.zeros((2, SIG, lead * NCHAN), jnp.int32)
    volt[:, :, (lead + frames) * NCHAN :] = jnp.zeros((2, SIG, tail), jnp.int32)
    coef_copy.wait()
    across = coef.shape[1]
    per_term = TAPS * NCHAN // across
    coef[...] = sum(terms[t * per_term : (t + 1) * per_term, :].astype(jnp.float32) for t in range(3))

    def filter_group(group, _):
        base = pl.multiple_of(group * (GROUP * NCHAN), GROUP * NCHAN)
        rows = pl.ds(pl.multiple_of(group * (GROUP * SIG), GROUP * SIG), GROUP * SIG)
        for column in range(HALF // LANES):
            for part in range(2):
                halves = []
                for half in range(2):
                    lane = half * HALF + column * LANES
                    at = [k * (NCHAN // across) + lane // across for k in range(TAPS)]
                    taps = [coef[i : i + 1, lane % across : lane % across + LANES] for i in at]
                    near = [
                        volt[part, :, pl.ds(base + f * NCHAN + lane, LANES)].astype(jnp.float32)
                        for f in range(GROUP + TAPS - 1)
                    ]
                    sums = []
                    for m in range(GROUP):
                        total = taps[0] * near[m]
                        for k in range(1, TAPS):
                            total = total + taps[k] * near[m + k]
                        sums.append(total)
                    halves.append(jnp.concatenate(sums, axis=0))
                where = pl.ds(part * HALF + column * LANES, LANES)
                filt[0, rows, where] = (halves[0] + halves[1]).astype(jnp.bfloat16)
                filt[1, rows, where] = (halves[0] - halves[1]).astype(jnp.bfloat16)
        return 0

    groups = per // GROUP
    for piece in range(pieces):
        copies[piece].wait()
        lax.fori_loop(piece * groups, (piece + 1) * groups, filter_group, 0)
    lax.fori_loop(frames // GROUP, frames // GROUP + 1, filter_group, 0)
    table_copy.wait()
    transform(filt, table, scale, stage, out_refs)
    later_copy.wait()


def transform_kernel(part, scale, filt, later, gains_ref, pick_ref, *refs):
    table = later.at[pl.ds((part - 1) * 2 * NCHAN, 2 * NCHAN)]
    if part == 1:
        columns, stage = refs[-2:]
        gains = jnp.concatenate([gains_ref[:, 0, :], gains_ref[:, 1, :]], axis=0)
        columns[...] = lax.dot_general(
            pick_ref[...],
            gains,
            (((1,), (1,)), ((), ())),
            precision=lax.Precision.HIGHEST,
            preferred_element_type=jnp.float32,
        )
        transform(filt, table, scale, stage, refs[:-2])
    else:
        transform(filt, table, scale, refs[-1], refs[:-1])


IN_VMEM = pl.BlockSpec(memory_space=pltpu.VMEM)
IN_HBM = pl.BlockSpec(memory_space=pl.ANY)


def filtered_and_first(voltages, owners, table):
    frames = voltages.shape[2] // NCHAN
    rows = (frames + GROUP) * SIG
    sent = (frames + TAPS - 1) * SIG
    pieces = 4
    across = table.shape[1]
    terms = table.shape[0] - PARTS * 2 * NCHAN
    lanes = 2 * CHANNELS // owners // PARTS
    *first, filt, later = pl.pallas_call(
        functools.partial(filter_kernel, frames, pieces, spectrum_scale()),
        out_shape=[jax.ShapeDtypeStruct((sent, lanes), jnp.bfloat16)] * owners
        + [
            jax.ShapeDtypeStruct((2, rows, NCHAN), jnp.bfloat16),
            jax.ShapeDtypeStruct(((PARTS - 1) * 2 * NCHAN, across), jnp.bfloat16),
        ],
        in_specs=[IN_HBM, IN_HBM],
        out_specs=[IN_VMEM] * (owners + 2),
        scratch_shapes=[
            pltpu.VMEM((2, SIG, (frames + GROUP + TAPS - 1) * NCHAN), jnp.int32),
            pltpu.VMEM((2 * NCHAN, across), jnp.bfloat16),
            pltpu.VMEM((terms, across), jnp.bfloat16),
            pltpu.VMEM((TAPS * NCHAN // across, across), jnp.float32),
            pltpu.VMEM((owners, sent, lanes), jnp.bfloat16),
            pltpu.SemaphoreType.DMA((pieces + 3,)),
        ],
        compiler_params=pltpu.CompilerParams(vmem_limit_bytes=FILTER_VMEM_BYTES),
        cost_estimate=pl.CostEstimate(flops=1 << 29, bytes_accessed=4 << 20, transcendentals=0),
        name="filter_and_transform",
    )(voltages, table)
    return filt, later, first


def pick_rows(channels):
    order = np.arange(channels).reshape(PARTS, BATCH, -1, 2)
    return np.eye(channels, dtype=np.float32)[np.transpose(order, (0, 3, 2, 1)).reshape(-1)]


def next_part(part, filt, later, gains, owners):
    rows = filt.shape[1] - (GROUP - TAPS + 1) * SIG
    lanes = 2 * CHANNELS // owners // PARTS
    channels = gains.shape[2]
    shapes = [jax.ShapeDtypeStruct((rows, lanes), jnp.bfloat16)] * owners
    if part == 1:
        shapes.append(jax.ShapeDtypeStruct((channels, 2 * SIG), jnp.float32))
    return pl.pallas_call(
        functools.partial(transform_kernel, part, spectrum_scale()),
        out_shape=shapes,
        in_specs=[IN_VMEM] * 4,
        out_specs=[IN_VMEM] * len(shapes),
        scratch_shapes=[pltpu.VMEM((owners, rows, lanes), jnp.bfloat16)],
        compiler_params=pltpu.CompilerParams(vmem_limit_bytes=VMEM_BYTES),
        cost_estimate=pl.CostEstimate(flops=1 << 29, bytes_accessed=2 << 20, transcendentals=0),
        name="transform",
    )(filt, later, gains, jnp.asarray(pick_rows(channels)))


def equalize_kernel(owners, frames, h, part, *refs):
    pieces = refs[owners - 1 :: -1]
    gains_ref, by_time, by_channel = refs[owners], refs[-2], refs[-1]
    out_ref = refs[owners + 1]
    width = 4 * h
    own_rows = frames * SIG
    over = (TAPS - 1) * SIG
    times = owners * frames
    tiles = times // LANES
    me = lax.axis_index("chan")
    for d in range(owners):
        source = jnp.bitwise_xor(me, d)
        start = pl.multiple_of(source * own_rows, own_rows)
        by_time[pl.ds(start, own_rows), :width] = pieces[d][:own_rows, :].astype(jnp.float32)
    for d in range(owners):
        source = jnp.bitwise_xor(me, d)

        @pl.when(source < owners - 1)
        def _():
            start = pl.multiple_of((source + 1) * own_rows, own_rows)
            by_time[pl.ds(start, over), :width] += pieces[d][own_rows:, :].astype(jnp.float32)

    gains = [gains_ref[(2 * part + r) * h : (2 * part + r + 1) * h, :] for r in range(2)]
    for s in range(SIG):
        x = by_time[pl.ds(s, times, stride=SIG), :][:, :width].T
        for r in range(2):
            real, imag = x[2 * r * h : (2 * r + 1) * h], x[(2 * r + 1) * h : (2 * r + 2) * h]
            gain_real, gain_imag = gains[r][:, s : s + 1], gains[r][:, SIG + s : SIG + s + 1]
            both = [real * gain_real - imag * gain_imag, real * gain_imag + imag * gain_real]
            for q in range(2):
                for tile in range(tiles):
                    by_channel[(2 * r + q) * tiles + tile, pl.ds(s, h, stride=SIG), :] = both[q][
                        :, tile * LANES : (tile + 1) * LANES
                    ]
    for r in range(2):
        for tile in range(2 * tiles):
            out_ref[r, :, tile * LANES : (tile + 1) * LANES] = by_channel[r * 2 * tiles + tile].astype(jnp.bfloat16)


def equalize(pieces, gains, part, frames):
    owners = len(pieces)
    h = gains.shape[0] // PARTS // 2
    times = owners * frames
    return pl.pallas_call(
        functools.partial(equalize_kernel, owners, frames, h, part),
        out_shape=jax.ShapeDtypeStruct((2, h * SIG, 2 * times), jnp.bfloat16),
        in_specs=[IN_VMEM] * (owners + 1),
        out_specs=IN_VMEM,
        scratch_shapes=[
            pltpu.VMEM((times * SIG, LANES), jnp.float32),
            pltpu.VMEM((4 * times // LANES, h * SIG, LANES), jnp.float32),
        ],
        compiler_params=pltpu.CompilerParams(vmem_limit_bytes=VMEM_BYTES),
        cost_estimate=pl.CostEstimate(flops=0, bytes_accessed=1 << 10, transcendentals=0),
        name="equalize",
    )(*pieces[::-1], gains)


def row_places(col, n_col):
    chips = n_col // 2
    chip, core = lax.div(col, 2), lax.rem(col, 2)
    places = [col] + [lax.rem(chip + chips - d, chips) * 2 + core for d in range(1, chips)]
    return places + [jnp.bitwise_xor(p, 1) for p in places]


def column_places(row, n_row):
    return [row] + [lax.rem(row + n_row - d, n_row) for d in range(1, n_row)]


def regroup(v):
    lane = lax.broadcasted_iota(jnp.int32, v[0].shape, 1)
    v = list(v)
    for bit in (2, 1):
        width = bit * LANES // 8
        low = (lane // width) % 2 == 0
        for i in range(4):
            if i & bit == 0:
                a, b = v[i], v[i + bit]
                v[i] = jnp.where(low, a, pltpu.roll(b, width, axis=1))
                v[i + bit] = jnp.where(low, pltpu.roll(a, LANES - width, axis=1), b)
    return v


def correlate_kernel(n_row, n_col, h, times, part, dense, *refs):
    row_blocks = refs[:n_col]
    col_blocks = (refs[0],) + refs[n_col : n_col + n_row - 1]
    last = part == PARTS - 1
    given = refs[n_col + n_row - 1 :]
    if part > 0:
        earlier, keeps = given[:2]
    if last:
        out_hbm, chosen, out_ref, sems = refs[-4:]
    else:
        out_ref, keeps_out, chosen = refs[-3:]
    me_row, me_col = lax.axis_index("brow"), lax.axis_index("bcol")
    row_at, col_at = row_places(me_col, n_col), column_places(me_row, n_row)
    rows = BATCH * SIG
    tiles = n_col * rows // LANES
    steps = 2 * h // BATCH
    if part == 0:
        owned = given[0][...]
        first, second = (lax.broadcasted_iota(jnp.int32, owned.shape, axis) for axis in range(2))
        for e in range(n_row):
            for d in range(n_col):
                here = (first == me_row * n_col + row_at[d]) & (second == col_at[e] * n_col + me_col)
                found = jnp.max(jnp.where(here, (owned == 1).astype(jnp.float32), 0.0), axis=(0, 1), keepdims=True)
                keeps_out[e, d] = jnp.broadcast_to(found * (1.0 / times), (SIG, LANES))
    elif not last:
        keeps_out[...] = keeps[...]
    index_in_batch = (lax.broadcasted_iota(jnp.int32, (SIG, LANES), 1) // SIG) % BATCH

    for step in range(steps):
        inner, parity = step // 2, step % 2
        here = slice(inner * rows, (inner + 1) * rows)
        a = jnp.concatenate([block[parity, here, :] for block in row_blocks], axis=0)
        b = jnp.concatenate([block[parity, here, :] for block in col_blocks], axis=0)
        turned = jnp.concatenate([-b[:, times:], b[:, :times]], axis=1)
        both = jnp.concatenate([b, turned], axis=0)
        result = lax.dot_general(both, a, (((1,), (1,)), ((), ())), preferred_element_type=jnp.float32)
        for k in range(2 * n_row):
            for tile in range(tiles):
                lanes = slice(tile * LANES, (tile + 1) * LANES)
                own = [result[k * rows + i * SIG : k * rows + (i + 1) * SIG, lanes] for i in range(BATCH)]
                kept = own[0]
                for i in range(1, BATCH):
                    kept = jnp.where(index_in_batch == i, own[i], kept)
                chosen[k * tiles + tile, pl.ds(step, SIG, stride=steps), :] = kept

    copies = []
    low = lax.broadcasted_iota(jnp.int32, (SIG, LANES), 1) < LANES // 2
    for q in range(2):
        for e in range(n_row):
            for d in range(n_col):
                if d % (LANES // rows) == 0:
                    x = chosen[(q * n_row + e) * tiles + d * rows // LANES].T
                start = d * rows % LANES
                v = [x[start + i * SIG : start + (i + 1) * SIG] for i in range(BATCH)]
                if last:
                    keep = keeps[e, d]
                a_at = pl.ds(pl.multiple_of(row_at[d] * SIG, SIG), SIG)
                mine = slice(d * SIG, (d + 1) * SIG)
                if dense:
                    for g, w in enumerate(regroup(v)):
                        if last:
                            before = earlier[q, e, g, mine, :]
                            pair = [
                                jnp.where(low, before, pltpu.roll(w, LANES // 2, axis=1)),
                                jnp.where(low, pltpu.roll(before, LANES // 2, axis=1), w),
                            ]
                            for half in range(2):
                                out_ref[q, col_at[e] * SIG + half * BATCH + g, a_at, :] = pair[half] * keep
                        else:
                            out_ref[q, e, g, mine, :] = w
                else:
                    for s2 in range(SIG):
                        w = jnp.concatenate([each[:, s2 * steps : (s2 + 1) * steps] for each in v], axis=1)
                        if part > 0:
                            w = jnp.concatenate([earlier[q, e, s2, mine, :], w], axis=1)
                        if last:
                            out_ref[q, col_at[e] * SIG + s2, a_at, :] = w * keep[:, : w.shape[1]]
                        else:
                            out_ref[q, e, s2, mine, :] = w
            if last:
                where = pl.ds(col_at[e] * SIG, SIG)
                copy = pltpu.make_async_copy(out_ref.at[q, where], out_hbm.at[q, where], sems.at[q * n_row + e])
                copy.start()
                copies.append(copy)
    for copy in copies:
        copy.wait()


def correlate(blocks, given, part, n_row, n_col):
    h = blocks[0].shape[1] // SIG
    times = blocks[0].shape[2] // 2
    channels = 2 * h
    dense = channels * 2 == LANES and PARTS == 2
    operands = list(blocks) + list(given)
    last = part == PARTS - 1
    if last:
        out_shape = (2, n_row * SIG, n_col * SIG, (part + 1) * channels)
    elif dense:
        out_shape = (2, n_row, SIG // 2, n_col * SIG, LANES)
    else:
        out_shape = (2, n_row, SIG, n_col * SIG, (part + 1) * channels)
    shapes = [out_shape] if last else [out_shape, (n_row, n_col, SIG, LANES)]
    in_last = [pltpu.VMEM(out_shape, jnp.float32), pltpu.SemaphoreType.DMA((2 * n_row,))]
    kept = pltpu.VMEM((2 * n_row * n_col * BATCH * SIG // LANES, SIG * channels // BATCH, LANES), jnp.float32)
    return pl.pallas_call(
        functools.partial(correlate_kernel, n_row, n_col, h, times, part, dense),
        out_shape=[jax.ShapeDtypeStruct(shape, jnp.float32) for shape in shapes],
        in_specs=[IN_VMEM] * len(operands),
        out_specs=[IN_HBM] if last else [IN_VMEM] * len(shapes),
        scratch_shapes=[kept] + (in_last if last else []),
        compiler_params=pltpu.CompilerParams(vmem_limit_bytes=VMEM_BYTES),
        cost_estimate=pl.CostEstimate(flops=0, bytes_accessed=1 << 10, transcendentals=0),
        name="correlate",
    )(*operands)


def to_owners(pieces):
    owners = len(pieces)
    arrived = [pieces[0]] + [None] * (owners - 1)
    for d in range(owners - 1, 0, -1):
        arrived[d] = lax.ppermute(pieces[d], "chan", [(i, i ^ d) for i in range(owners)])
    return arrived


def copied(kernel, out_like, operands, name):
    return pl.pallas_call(
        kernel,
        out_shape=[jax.ShapeDtypeStruct(block.shape, block.dtype) for block in out_like],
        in_specs=[IN_VMEM] * len(operands),
        out_specs=[IN_VMEM] * len(out_like),
        compiler_params=pltpu.CompilerParams(vmem_limit_bytes=VMEM_BYTES),
        cost_estimate=pl.CostEstimate(flops=0, bytes_accessed=1 << 10, transcendentals=0),
        name=name,
    )(*operands)


def held_back(blocks, after):
    def kernel(*refs):
        for i in range(len(blocks)):
            refs[len(blocks) + len(after) + i][...] = refs[i][...]

    return copied(kernel, blocks, list(blocks) + list(after), "held_back")


def sorted_by_core(first, second, after):
    count = len(first)

    def kernel(*refs):
        core = lax.rem(lax.axis_index("bcol"), 2)
        outs = refs[2 * count + len(after) :]
        for flip in range(2):

            @pl.when(core == flip)
            def _():
                for i in range(count):
                    outs[i][...] = refs[i + flip * count][...]
                    outs[count + i][...] = refs[i + (1 - flip) * count][...]

    both = copied(kernel, list(first) + list(second), list(first) + list(second) + list(after), "sorted_by_core")
    return list(both[:count]), list(both[count:])


def panel_permutes(block, n_row, n_col):
    chips = n_col // 2

    def x_step(row, col, d):
        return row * n_col + (col // 2 + d) % chips * 2 + col % 2

    def y_step(row, col, d):
        return (row + d) % n_row * n_col + col

    devices = [(row, col) for row in range(n_row) for col in range(n_col)]
    axes = ("brow", "bcol")
    first, second, far, column = [], [], [], []
    for d in range(1, max(chips, n_row)):
        if d < min(chips, n_row):
            for turn, results in ((0, first), (1, second)):
                route = [
                    (row * n_col + col, (x_step if col % 2 == turn else y_step)(row, col, d)) for row, col in devices
                ]
                results.append(lax.ppermute(block, axes, route))
        else:
            step, results = (x_step, far) if d < chips else (y_step, column)
            results.append(lax.ppermute(block, axes, [(row * n_col + col, step(row, col, d)) for row, col in devices]))
    return first, second, far, column


def shards(voltages, antenna_gains, tile_map):
    owners = lax.axis_size("chan")
    n_row = lax.axis_size("brow")
    n_col = lax.axis_size("bcol")
    frames = voltages.shape[2] // NCHAN
    table = jnp.asarray(constants(owners))
    other_core = [(i, i ^ 1) for i in range(n_col)]

    filt, tables, pieces = filtered_and_first(voltages, owners, table)
    own, panels = [], []
    arrived = to_owners(pieces)
    for part in range(PARTS):
        later = None
        if part < PARTS - 1:
            pieces = next_part(part + 1, filt, tables, antenna_gains, owners)
            if part == 0:
                *pieces, gains = pieces
            later = to_owners([pieces[0], *held_back(pieces[1:], arrived[-1:])])
        own.append(equalize(arrived, gains, part, frames))
        panels.append(panel_permutes(own[part], n_row, n_col))
        arrived = later
    beside = [lax.ppermute(block, "bcol", other_core) for block in own]
    result = [tile_map]
    for part in range(PARTS):
        first, second, far, column = panels[part]
        near_far, near_column = sorted_by_core(first, second, own[-1:] + far + column)
        far, column = near_far + far, near_column + column
        relayed = [lax.ppermute(block, "bcol", other_core) for block in far]
        blocks = [own[part]] + far + [beside[part]] + relayed + column
        result = correlate(blocks, result, part, n_row, n_col)
    return jnp.transpose(result[0], (3, 0, 1, 2))[None, None]


def solution(mesh):
    in_specs = (P(None, ("brow", "bcol"), "chan"), P(("brow", "bcol"), None, "chan"), P())
    out_specs = P("brow", "bcol", "chan", None, None, None)
    return jax.shard_map(shards, mesh=mesh, in_specs=in_specs, out_specs=out_specs, check_vma=False)
```

```python
import functools
import math

import jax
import jax.numpy as jnp
import ml_dtypes
import numpy as np
from jax import lax
from jax.experimental import pallas as pl
from jax.experimental.pallas import tpu as pltpu
from jax.sharding import PartitionSpec as P

NCHAN = 1024
HALF = NCHAN // 2
CHANNELS = 512
TAPS = 4
FIRST = 256
SIG = 8
LANES = 128
GROUP = 4
BATCH = 4
PARTS = 2
VMEM_BYTES = 16 * 1024 * 1024
FILTER_VMEM_BYTES = 101 * 512 * 1024
COEF_ROWS = 64


def fir_coefficients():
    position = np.arange(TAPS * NCHAN, dtype=np.float64) + 0.5
    offsets = position / NCHAN - TAPS / 2.0
    window = 0.5 - 0.5 * np.cos(2.0 * math.pi * position / (TAPS * NCHAN))
    return (np.sinc(offsets) * window).reshape(TAPS, NCHAN)


def spectrum_scale():
    return float(1.0 / (128.0 * np.sqrt(np.sum(fir_coefficients() ** 2))))


def dft_tables(owners):
    n = np.arange(HALF, dtype=np.int64).reshape(HALF, 1, 1, 1, 1, 1)
    k = FIRST + np.arange(CHANNELS, dtype=np.int64).reshape(owners, PARTS, BATCH, -1, 2)
    angles = (n * k % NCHAN) * (2.0 * math.pi / NCHAN)
    cosine, sine = np.cos(angles), np.sin(angles)
    first = np.stack([cosine, -sine], axis=2)
    second = np.stack([sine, cosine], axis=2)
    tables = np.stack([first, second])
    tables = np.transpose(tables, (4, 7, 0, 1, 2, 3, 6, 5))
    return tables.reshape(PARTS, 2 * NCHAN, -1).astype(np.float32).astype(ml_dtypes.bfloat16)


def constants(owners):
    tables = dft_tables(owners)
    lanes = tables.shape[2]
    left = fir_coefficients().astype(np.float32)
    terms = []
    for _ in range(3):
        terms.append(left.astype(ml_dtypes.bfloat16))
        left = left - terms[-1].astype(np.float32)
    terms = np.stack(terms).reshape(-1, lanes)
    pad = np.zeros((-terms.shape[0] % COEF_ROWS, lanes), ml_dtypes.bfloat16)
    return np.concatenate([tables.reshape(-1, lanes), terms, pad])


def transform(filt, table, scale, stage, out_refs):
    owners = len(out_refs)
    me = lax.axis_index("chan")
    spectra = [
        jnp.dot(filt[r], table[r * NCHAN : (r + 1) * NCHAN], preferred_element_type=jnp.float32) * scale
        for r in range(2)
    ]
    width = spectra[0].shape[1] // owners
    for owner in range(owners):
        here = slice(owner * width, (owner + 1) * width)
        piece = jnp.concatenate([spectra[0][:, here], spectra[1][:, here]], axis=1)
        stage[jnp.bitwise_xor(me, owner)] = piece[: stage.shape[1]].astype(jnp.bfloat16)
    for d in range(owners):
        out_refs[d][...] = stage[d]


def filter_kernel(frames, pieces, scale, volt_hbm, table_hbm, *refs):
    out_refs, (filt, later, volt, table, terms, coef, stage, sems) = refs[:-8], refs[-8:]
    per = frames // pieces
    lead = TAPS - 1
    copies = []
    for piece in range(pieces):
        copies.append(
            pltpu.make_async_copy(
                volt_hbm.at[:, :, pl.ds(piece * per * NCHAN, per * NCHAN)],
                volt.at[:, :, pl.ds((lead + piece * per) * NCHAN, per * NCHAN)],
                sems.at[piece],
            )
        )
    table_copy = pltpu.make_async_copy(table_hbm.at[pl.ds(0, 2 * NCHAN)], table, sems.at[pieces])
    coef_copy = pltpu.make_async_copy(
        table_hbm.at[pl.ds(PARTS * 2 * NCHAN, terms.shape[0])], terms, sems.at[pieces + 1]
    )
    coef_copy.start()
    for copy in copies:
        copy.start()
    later_copy = pltpu.make_async_copy(
        table_hbm.at[pl.ds(2 * NCHAN, (PARTS - 1) * 2 * NCHAN)], later, sems.at[pieces + 2]
    )
    table_copy.start()
    later_copy.start()
    tail = volt.shape[2] - (lead + frames) * NCHAN
    volt[:, :, : lead * NCHAN] = jnp.zeros((2, SIG, lead * NCHAN), jnp.int32)
    volt[:, :, (lead + frames) * NCHAN :] = jnp.zeros((2, SIG, tail), jnp.int32)
    coef_copy.wait()
    across = coef.shape[1]
    per_term = TAPS * NCHAN // across
    coef[...] = sum(terms[t * per_term : (t + 1) * per_term, :].astype(jnp.float32) for t in range(3))

    def filter_group(group, _):
        base = pl.multiple_of(group * (GROUP * NCHAN), GROUP * NCHAN)
        rows = pl.ds(pl.multiple_of(group * (GROUP * SIG), GROUP * SIG), GROUP * SIG)
        for column in range(HALF // LANES):
            for part in range(2):
                halves = []
                for half in range(2):
                    lane = half * HALF + column * LANES
                    at = [k * (NCHAN // across) + lane // across for k in range(TAPS)]
                    taps = [coef[i : i + 1, lane % across : lane % across + LANES] for i in at]
                    near = [
                        volt[part, :, pl.ds(base + f * NCHAN + lane, LANES)].astype(jnp.float32)
                        for f in range(GROUP + TAPS - 1)
                    ]
                    sums = []
                    for m in range(GROUP):
                        total = taps[0] * near[m]
                        for k in range(1, TAPS):
                            total = total + taps[k] * near[m + k]
                        sums.append(total)
                    halves.append(jnp.concatenate(sums, axis=0))
                where = pl.ds(part * HALF + column * LANES, LANES)
                filt[0, rows, where] = (halves[0] + halves[1]).astype(jnp.bfloat16)
                filt[1, rows, where] = (halves[0] - halves[1]).astype(jnp.bfloat16)
        return 0

    groups = per // GROUP
    for piece in range(pieces):
        copies[piece].wait()
        lax.fori_loop(piece * groups, (piece + 1) * groups, filter_group, 0)
    lax.fori_loop(frames // GROUP, frames // GROUP + 1, filter_group, 0)
    table_copy.wait()
    transform(filt, table, scale, stage, out_refs)
    later_copy.wait()


def transform_kernel(part, scale, filt, later, gains_ref, pick_ref, *refs):
    table = later.at[pl.ds((part - 1) * 2 * NCHAN, 2 * NCHAN)]
    if part == 1:
        columns, stage = refs[-2:]
        gains = jnp.concatenate([gains_ref[:, 0, :], gains_ref[:, 1, :]], axis=0)
        columns[...] = lax.dot_general(
            pick_ref[...],
            gains,
            (((1,), (1,)), ((), ())),
            precision=lax.Precision.HIGHEST,
            preferred_element_type=jnp.float32,
        )
        transform(filt, table, scale, stage, refs[:-2])
    else:
        transform(filt, table, scale, refs[-1], refs[:-1])


IN_VMEM = pl.BlockSpec(memory_space=pltpu.VMEM)
IN_HBM = pl.BlockSpec(memory_space=pl.ANY)


def filtered_and_first(voltages, owners, table):
    frames = voltages.shape[2] // NCHAN
    rows = (frames + GROUP) * SIG
    sent = (frames + TAPS - 1) * SIG
    pieces = 4
    across = table.shape[1]
    terms = table.shape[0] - PARTS * 2 * NCHAN
    lanes = 2 * CHANNELS // owners // PARTS
    *first, filt, later = pl.pallas_call(
        functools.partial(filter_kernel, frames, pieces, spectrum_scale()),
        out_shape=[jax.ShapeDtypeStruct((sent, lanes), jnp.bfloat16)] * owners
        + [
            jax.ShapeDtypeStruct((2, rows, NCHAN), jnp.bfloat16),
            jax.ShapeDtypeStruct(((PARTS - 1) * 2 * NCHAN, across), jnp.bfloat16),
        ],
        in_specs=[IN_HBM, IN_HBM],
        out_specs=[IN_VMEM] * (owners + 2),
        scratch_shapes=[
            pltpu.VMEM((2, SIG, (frames + GROUP + TAPS - 1) * NCHAN), jnp.int32),
            pltpu.VMEM((2 * NCHAN, across), jnp.bfloat16),
            pltpu.VMEM((terms, across), jnp.bfloat16),
            pltpu.VMEM((TAPS * NCHAN // across, across), jnp.float32),
            pltpu.VMEM((owners, sent, lanes), jnp.bfloat16),
            pltpu.SemaphoreType.DMA((pieces + 3,)),
        ],
        compiler_params=pltpu.CompilerParams(vmem_limit_bytes=FILTER_VMEM_BYTES),
        cost_estimate=pl.CostEstimate(flops=1 << 29, bytes_accessed=4 << 20, transcendentals=0),
        name="filter_and_transform",
    )(voltages, table)
    return filt, later, first


def pick_rows(channels):
    order = np.arange(channels).reshape(PARTS, BATCH, -1, 2)
    return np.eye(channels, dtype=np.float32)[np.transpose(order, (0, 3, 2, 1)).reshape(-1)]


def next_part(part, filt, later, gains, owners):
    rows = filt.shape[1] - (GROUP - TAPS + 1) * SIG
    lanes = 2 * CHANNELS // owners // PARTS
    channels = gains.shape[2]
    shapes = [jax.ShapeDtypeStruct((rows, lanes), jnp.bfloat16)] * owners
    if part == 1:
        shapes.append(jax.ShapeDtypeStruct((channels, 2 * SIG), jnp.float32))
    return pl.pallas_call(
        functools.partial(transform_kernel, part, spectrum_scale()),
        out_shape=shapes,
        in_specs=[IN_VMEM] * 4,
        out_specs=[IN_VMEM] * len(shapes),
        scratch_shapes=[pltpu.VMEM((owners, rows, lanes), jnp.bfloat16)],
        compiler_params=pltpu.CompilerParams(vmem_limit_bytes=VMEM_BYTES),
        cost_estimate=pl.CostEstimate(flops=1 << 29, bytes_accessed=2 << 20, transcendentals=0),
        name="transform",
    )(filt, later, gains, jnp.asarray(pick_rows(channels)))


def equalize_kernel(owners, frames, h, part, *refs):
    pieces = refs[owners - 1 :: -1]
    gains_ref, by_time, by_channel = refs[owners], refs[-2], refs[-1]
    out_ref = refs[owners + 1]
    width = 4 * h
    own_rows = frames * SIG
    over = (TAPS - 1) * SIG
    times = owners * frames
    tiles = times // LANES
    me = lax.axis_index("chan")
    for d in range(owners):
        source = jnp.bitwise_xor(me, d)
        start = pl.multiple_of(source * own_rows, own_rows)
        by_time[pl.ds(start, own_rows), :width] = pieces[d][:own_rows, :].astype(jnp.float32)
    for d in range(owners):
        source = jnp.bitwise_xor(me, d)

        @pl.when(source < owners - 1)
        def _():
            start = pl.multiple_of((source + 1) * own_rows, own_rows)
            by_time[pl.ds(start, over), :width] += pieces[d][own_rows:, :].astype(jnp.float32)

    gains = [gains_ref[(2 * part + r) * h : (2 * part + r + 1) * h, :] for r in range(2)]
    for s in range(SIG):
        x = by_time[pl.ds(s, times, stride=SIG), :][:, :width].T
        for r in range(2):
            real, imag = x[2 * r * h : (2 * r + 1) * h], x[(2 * r + 1) * h : (2 * r + 2) * h]
            gain_real, gain_imag = gains[r][:, s : s + 1], gains[r][:, SIG + s : SIG + s + 1]
            both = [real * gain_real - imag * gain_imag, real * gain_imag + imag * gain_real]
            for q in range(2):
                for tile in range(tiles):
                    by_channel[(2 * r + q) * tiles + tile, pl.ds(s, h, stride=SIG), :] = both[q][
                        :, tile * LANES : (tile + 1) * LANES
                    ]
    for r in range(2):
        for tile in range(2 * tiles):
            out_ref[r, :, tile * LANES : (tile + 1) * LANES] = by_channel[r * 2 * tiles + tile].astype(jnp.bfloat16)


def equalize(pieces, gains, part, frames):
    owners = len(pieces)
    h = gains.shape[0] // PARTS // 2
    times = owners * frames
    return pl.pallas_call(
        functools.partial(equalize_kernel, owners, frames, h, part),
        out_shape=jax.ShapeDtypeStruct((2, h * SIG, 2 * times), jnp.bfloat16),
        in_specs=[IN_VMEM] * (owners + 1),
        out_specs=IN_VMEM,
        scratch_shapes=[
            pltpu.VMEM((times * SIG, LANES), jnp.float32),
            pltpu.VMEM((4 * times // LANES, h * SIG, LANES), jnp.float32),
        ],
        compiler_params=pltpu.CompilerParams(vmem_limit_bytes=VMEM_BYTES),
        cost_estimate=pl.CostEstimate(flops=0, bytes_accessed=1 << 10, transcendentals=0),
        name="equalize",
    )(*pieces[::-1], gains)


def row_places(col, n_col):
    chips = n_col // 2
    chip, core = lax.div(col, 2), lax.rem(col, 2)
    places = [col] + [lax.rem(chip + chips - d, chips) * 2 + core for d in range(1, chips)]
    return places + [jnp.bitwise_xor(p, 1) for p in places]


def column_places(row, n_row):
    return [row] + [lax.rem(row + n_row - d, n_row) for d in range(1, n_row)]


def regroup(v):
    lane = lax.broadcasted_iota(jnp.int32, v[0].shape, 1)
    v = list(v)
    for bit in (2, 1):
        width = bit * LANES // 8
        low = (lane // width) % 2 == 0
        for i in range(4):
            if i & bit == 0:
                a, b = v[i], v[i + bit]
                v[i] = jnp.where(low, a, pltpu.roll(b, width, axis=1))
                v[i + bit] = jnp.where(low, pltpu.roll(a, LANES - width, axis=1), b)
    return v


def correlate_kernel(n_row, n_col, h, times, part, dense, *refs):
    row_blocks = refs[:n_col]
    col_blocks = (refs[0],) + refs[n_col : n_col + n_row - 1]
    last = part == PARTS - 1
    given = refs[n_col + n_row - 1 :]
    if part > 0:
        earlier, keeps = given[:2]
    if last:
        out_hbm, chosen, out_ref, sems = refs[-4:]
    else:
        out_ref, keeps_out, chosen = refs[-3:]
    me_row, me_col = lax.axis_index("brow"), lax.axis_index("bcol")
    row_at, col_at = row_places(me_col, n_col), column_places(me_row, n_row)
    rows = BATCH * SIG
    tiles = n_col * rows // LANES
    steps = 2 * h // BATCH
    if part == 0:
        owned = given[0][...]
        first, second = (lax.broadcasted_iota(jnp.int32, owned.shape, axis) for axis in range(2))
        for e in range(n_row):
            for d in range(n_col):
                here = (first == me_row * n_col + row_at[d]) & (second == col_at[e] * n_col + me_col)
                found = jnp.max(jnp.where(here, (owned == 1).astype(jnp.float32), 0.0), axis=(0, 1), keepdims=True)
                keeps_out[e, d] = jnp.broadcast_to(found * (1.0 / times), (SIG, LANES))
    elif not last:
        keeps_out[...] = keeps[...]
    index_in_batch = (lax.broadcasted_iota(jnp.int32, (SIG, LANES), 1) // SIG) % BATCH

    for step in range(steps):
        inner, parity = step // 2, step % 2
        here = slice(inner * rows, (inner + 1) * rows)
        a = jnp.concatenate([block[parity, here, :] for block in row_blocks], axis=0)
        b = jnp.concatenate([block[parity, here, :] for block in col_blocks], axis=0)
        turned = jnp.concatenate([-b[:, times:], b[:, :times]], axis=1)
        both = jnp.concatenate([b, turned], axis=0)
        result = lax.dot_general(both, a, (((1,), (1,)), ((), ())), preferred_element_type=jnp.float32)
        for k in range(2 * n_row):
            for tile in range(tiles):
                lanes = slice(tile * LANES, (tile + 1) * LANES)
                own = [result[k * rows + i * SIG : k * rows + (i + 1) * SIG, lanes] for i in range(BATCH)]
                kept = own[0]
                for i in range(1, BATCH):
                    kept = jnp.where(index_in_batch == i, own[i], kept)
                chosen[k * tiles + tile, pl.ds(step, SIG, stride=steps), :] = kept

    copies = []
    low = lax.broadcasted_iota(jnp.int32, (SIG, LANES), 1) < LANES // 2
    for q in range(2):
        for e in range(n_row):
            for d in range(n_col):
                if d % (LANES // rows) == 0:
                    x = chosen[(q * n_row + e) * tiles + d * rows // LANES].T
                start = d * rows % LANES
                v = [x[start + i * SIG : start + (i + 1) * SIG] for i in range(BATCH)]
                if last:
                    keep = keeps[e, d]
                a_at = pl.ds(pl.multiple_of(row_at[d] * SIG, SIG), SIG)
                mine = slice(d * SIG, (d + 1) * SIG)
                if dense:
                    for g, w in enumerate(regroup(v)):
                        if last:
                            before = earlier[q, e, g, mine, :]
                            pair = [
                                jnp.where(low, before, pltpu.roll(w, LANES // 2, axis=1)),
                                jnp.where(low, pltpu.roll(before, LANES // 2, axis=1), w),
                            ]
                            for half in range(2):
                                out_ref[q, col_at[e] * SIG + half * BATCH + g, a_at, :] = pair[half] * keep
                        else:
                            out_ref[q, e, g, mine, :] = w
                else:
                    for s2 in range(SIG):
                        w = jnp.concatenate([each[:, s2 * steps : (s2 + 1) * steps] for each in v], axis=1)
                        if part > 0:
                            w = jnp.concatenate([earlier[q, e, s2, mine, :], w], axis=1)
                        if last:
                            out_ref[q, col_at[e] * SIG + s2, a_at, :] = w * keep[:, : w.shape[1]]
                        else:
                            out_ref[q, e, s2, mine, :] = w
            if last:
                where = pl.ds(col_at[e] * SIG, SIG)
                copy = pltpu.make_async_copy(out_ref.at[q, where], out_hbm.at[q, where], sems.at[q * n_row + e])
                copy.start()
                copies.append(copy)
    for copy in copies:
        copy.wait()


def correlate(blocks, given, part, n_row, n_col):
    h = blocks[0].shape[1] // SIG
    times = blocks[0].shape[2] // 2
    channels = 2 * h
    dense = channels * 2 == LANES and PARTS == 2
    operands = list(blocks) + list(given)
    last = part == PARTS - 1
    if last:
        out_shape = (2, n_row * SIG, n_col * SIG, (part + 1) * channels)
    elif dense:
        out_shape = (2, n_row, SIG // 2, n_col * SIG, LANES)
    else:
        out_shape = (2, n_row, SIG, n_col * SIG, (part + 1) * channels)
    shapes = [out_shape] if last else [out_shape, (n_row, n_col, SIG, LANES)]
    in_last = [pltpu.VMEM(out_shape, jnp.float32), pltpu.SemaphoreType.DMA((2 * n_row,))]
    kept = pltpu.VMEM((2 * n_row * n_col * BATCH * SIG // LANES, SIG * channels // BATCH, LANES), jnp.float32)
    return pl.pallas_call(
        functools.partial(correlate_kernel, n_row, n_col, h, times, part, dense),
        out_shape=[jax.ShapeDtypeStruct(shape, jnp.float32) for shape in shapes],
        in_specs=[IN_VMEM] * len(operands),
        out_specs=[IN_HBM] if last else [IN_VMEM] * len(shapes),
        scratch_shapes=[kept] + (in_last if last else []),
        compiler_params=pltpu.CompilerParams(vmem_limit_bytes=VMEM_BYTES),
        cost_estimate=pl.CostEstimate(flops=0, bytes_accessed=1 << 10, transcendentals=0),
        name="correlate",
    )(*operands)


def to_owners(pieces):
    owners = len(pieces)
    arrived = [pieces[0]] + [None] * (owners - 1)
    for d in range(owners - 1, 0, -1):
        arrived[d] = lax.ppermute(pieces[d], "chan", [(i, i ^ d) for i in range(owners)])
    return arrived


def copied(kernel, out_like, operands, name):
    return pl.pallas_call(
        kernel,
        out_shape=[jax.ShapeDtypeStruct(block.shape, block.dtype) for block in out_like],
        in_specs=[IN_VMEM] * len(operands),
        out_specs=[IN_VMEM] * len(out_like),
        compiler_params=pltpu.CompilerParams(vmem_limit_bytes=VMEM_BYTES),
        cost_estimate=pl.CostEstimate(flops=0, bytes_accessed=1 << 10, transcendentals=0),
        name=name,
    )(*operands)


def sorted_by_core(first, second, after):
    count = len(first)

    def kernel(*refs):
        core = lax.rem(lax.axis_index("bcol"), 2)
        outs = refs[2 * count + len(after) :]
        for flip in range(2):

            @pl.when(core == flip)
            def _():
                for i in range(count):
                    outs[i][...] = refs[i + flip * count][...]
                    outs[count + i][...] = refs[i + (1 - flip) * count][...]

    both = copied(kernel, list(first) + list(second), list(first) + list(second) + list(after), "sorted_by_core")
    return list(both[:count]), list(both[count:])


def panel_permutes(block, n_row, n_col):
    chips = n_col // 2

    def x_step(row, col, d):
        return row * n_col + (col // 2 + d) % chips * 2 + col % 2

    def y_step(row, col, d):
        return (row + d) % n_row * n_col + col

    devices = [(row, col) for row in range(n_row) for col in range(n_col)]
    axes = ("brow", "bcol")
    first, second, far, column = [], [], [], []
    for d in range(1, max(chips, n_row)):
        if d < min(chips, n_row):
            for turn, results in ((0, first), (1, second)):
                route = [
                    (row * n_col + col, (x_step if col % 2 == turn else y_step)(row, col, d)) for row, col in devices
                ]
                results.append(lax.ppermute(block, axes, route))
        else:
            step, results = (x_step, far) if d < chips else (y_step, column)
            results.append(lax.ppermute(block, axes, [(row * n_col + col, step(row, col, d)) for row, col in devices]))
    return first, second, far, column


def shards(voltages, antenna_gains, tile_map):
    owners = lax.axis_size("chan")
    n_row = lax.axis_size("brow")
    n_col = lax.axis_size("bcol")
    frames = voltages.shape[2] // NCHAN
    table = jnp.asarray(constants(owners))
    other_core = [(i, i ^ 1) for i in range(n_col)]

    filt, tables, pieces = filtered_and_first(voltages, owners, table)
    own, panels = [], []
    arrived = to_owners(pieces)
    for part in range(PARTS):
        later = None
        if part < PARTS - 1:
            pieces = next_part(part + 1, filt, tables, antenna_gains, owners)
            if part == 0:
                *pieces, gains = pieces
            later = to_owners(pieces)
        own.append(equalize(arrived, gains, part, frames))
        panels.append(panel_permutes(own[part], n_row, n_col))
        arrived = later
    beside = [lax.ppermute(block, "bcol", other_core) for block in own]
    result = [tile_map]
    for part in range(PARTS):
        first, second, far, column = panels[part]
        near_far, near_column = sorted_by_core(first, second, own[-1:] + far + column)
        far, column = near_far + far, near_column + column
        relayed = [lax.ppermute(block, "bcol", other_core) for block in far]
        blocks = [own[part]] + far + [beside[part]] + relayed + column
        result = correlate(blocks, result, part, n_row, n_col)
    return jnp.transpose(result[0], (3, 0, 1, 2))[None, None]


def solution(mesh):
    in_specs = (P(None, ("brow", "bcol"), "chan"), P(("brow", "bcol"), None, "chan"), P())
    out_specs = P("brow", "bcol", "chan", None, None, None)
    return jax.shard_map(shards, mesh=mesh, in_specs=in_specs, out_specs=out_specs, check_vma=False)
```

```python
import functools
import math

import jax
import jax.numpy as jnp
import ml_dtypes
import numpy as np
from jax import lax
from jax.experimental import pallas as pl
from jax.experimental.pallas import tpu as pltpu
from jax.sharding import PartitionSpec as P

NCHAN = 1024
HALF = NCHAN // 2
CHANNELS = 512
TAPS = 4
FIRST = 256
SIG = 8
LANES = 128
GROUP = 4
BATCH = 4
PARTS = 2
VMEM_BYTES = 16 * 1024 * 1024
FILTER_VMEM_BYTES = 101 * 512 * 1024
COEF_ROWS = 64


def fir_coefficients():
    position = np.arange(TAPS * NCHAN, dtype=np.float64) + 0.5
    offsets = position / NCHAN - TAPS / 2.0
    window = 0.5 - 0.5 * np.cos(2.0 * math.pi * position / (TAPS * NCHAN))
    return (np.sinc(offsets) * window).reshape(TAPS, NCHAN)


def spectrum_scale():
    return float(1.0 / (128.0 * np.sqrt(np.sum(fir_coefficients() ** 2))))


def dft_tables(owners):
    n = np.arange(HALF, dtype=np.int64).reshape(HALF, 1, 1, 1, 1, 1)
    k = FIRST + np.arange(CHANNELS, dtype=np.int64).reshape(owners, PARTS, BATCH, -1, 2)
    angles = (n * k % NCHAN) * (2.0 * math.pi / NCHAN)
    cosine, sine = np.cos(angles), np.sin(angles)
    first = np.stack([cosine, -sine], axis=2)
    second = np.stack([sine, cosine], axis=2)
    tables = np.stack([first, second])
    tables = np.transpose(tables, (4, 7, 0, 1, 2, 3, 6, 5))
    return tables.reshape(PARTS, 2 * NCHAN, -1).astype(np.float32).astype(ml_dtypes.bfloat16)


def constants(owners):
    tables = dft_tables(owners)
    lanes = tables.shape[2]
    left = fir_coefficients().astype(np.float32)
    terms = []
    for _ in range(3):
        terms.append(left.astype(ml_dtypes.bfloat16))
        left = left - terms[-1].astype(np.float32)
    terms = np.stack(terms).reshape(-1, lanes)
    pad = np.zeros((-terms.shape[0] % COEF_ROWS, lanes), ml_dtypes.bfloat16)
    return np.concatenate([tables.reshape(-1, lanes), terms, pad])


def transform(filt, table, scale, stage, out_refs):
    owners = len(out_refs)
    me = lax.axis_index("chan")
    spectra = [
        jnp.dot(filt[r], table[r * NCHAN : (r + 1) * NCHAN], preferred_element_type=jnp.float32) * scale
        for r in range(2)
    ]
    width = spectra[0].shape[1] // owners
    for owner in range(owners):
        here = slice(owner * width, (owner + 1) * width)
        piece = jnp.concatenate([spectra[0][:, here], spectra[1][:, here]], axis=1)
        stage[jnp.bitwise_xor(me, owner)] = piece[: stage.shape[1]].astype(jnp.bfloat16)
    for d in range(owners):
        out_refs[d][...] = stage[d]


def filter_kernel(frames, pieces, scale, volt_hbm, table_hbm, *refs):
    out_refs, (filt, later, volt, table, terms, coef, stage, sems) = refs[:-8], refs[-8:]
    per = frames // pieces
    lead = TAPS - 1
    copies = []
    for piece in range(pieces):
        copies.append(
            pltpu.make_async_copy(
                volt_hbm.at[:, :, pl.ds(piece * per * NCHAN, per * NCHAN)],
                volt.at[:, :, pl.ds((lead + piece * per) * NCHAN, per * NCHAN)],
                sems.at[piece],
            )
        )
    table_copy = pltpu.make_async_copy(table_hbm.at[pl.ds(0, 2 * NCHAN)], table, sems.at[pieces])
    coef_copy = pltpu.make_async_copy(
        table_hbm.at[pl.ds(PARTS * 2 * NCHAN, terms.shape[0])], terms, sems.at[pieces + 1]
    )
    coef_copy.start()
    for copy in copies:
        copy.start()
    later_copy = pltpu.make_async_copy(
        table_hbm.at[pl.ds(2 * NCHAN, (PARTS - 1) * 2 * NCHAN)], later, sems.at[pieces + 2]
    )
    table_copy.start()
    later_copy.start()
    tail = volt.shape[2] - (lead + frames) * NCHAN
    volt[:, :, : lead * NCHAN] = jnp.zeros((2, SIG, lead * NCHAN), jnp.int32)
    volt[:, :, (lead + frames) * NCHAN :] = jnp.zeros((2, SIG, tail), jnp.int32)
    coef_copy.wait()
    across = coef.shape[1]
    per_term = TAPS * NCHAN // across
    coef[...] = sum(terms[t * per_term : (t + 1) * per_term, :].astype(jnp.float32) for t in range(3))

    def filter_group(group, _):
        base = pl.multiple_of(group * (GROUP * NCHAN), GROUP * NCHAN)
        rows = pl.ds(pl.multiple_of(group * (GROUP * SIG), GROUP * SIG), GROUP * SIG)
        for column in range(HALF // LANES):
            for part in range(2):
                halves = []
                for half in range(2):
                    lane = half * HALF + column * LANES
                    at = [k * (NCHAN // across) + lane // across for k in range(TAPS)]
                    taps = [coef[i : i + 1, lane % across : lane % across + LANES] for i in at]
                    near = [
                        volt[part, :, pl.ds(base + f * NCHAN + lane, LANES)].astype(jnp.float32)
                        for f in range(GROUP + TAPS - 1)
                    ]
                    sums = []
                    for m in range(GROUP):
                        total = taps[0] * near[m]
                        for k in range(1, TAPS):
                            total = total + taps[k] * near[m + k]
                        sums.append(total)
                    halves.append(jnp.concatenate(sums, axis=0))
                where = pl.ds(part * HALF + column * LANES, LANES)
                filt[0, rows, where] = (halves[0] + halves[1]).astype(jnp.bfloat16)
                filt[1, rows, where] = (halves[0] - halves[1]).astype(jnp.bfloat16)
        return 0

    groups = per // GROUP
    for piece in range(pieces):
        copies[piece].wait()
        lax.fori_loop(piece * groups, (piece + 1) * groups, filter_group, 0)
    lax.fori_loop(frames // GROUP, frames // GROUP + 1, filter_group, 0)
    table_copy.wait()
    transform(filt, table, scale, stage, out_refs)
    later_copy.wait()


def transform_kernel(part, scale, filt, later, gains_ref, pick_ref, *refs):
    table = later.at[pl.ds((part - 1) * 2 * NCHAN, 2 * NCHAN)]
    if part == 1:
        columns, stage = refs[-2:]
        gains = jnp.concatenate([gains_ref[:, 0, :], gains_ref[:, 1, :]], axis=0)
        columns[...] = lax.dot_general(
            pick_ref[...],
            gains,
            (((1,), (1,)), ((), ())),
            precision=lax.Precision.HIGHEST,
            preferred_element_type=jnp.float32,
        )
        transform(filt, table, scale, stage, refs[:-2])
    else:
        transform(filt, table, scale, refs[-1], refs[:-1])


IN_VMEM = pl.BlockSpec(memory_space=pltpu.VMEM)
IN_HBM = pl.BlockSpec(memory_space=pl.ANY)


def filtered_and_first(voltages, owners, table):
    frames = voltages.shape[2] // NCHAN
    rows = (frames + GROUP) * SIG
    sent = (frames + TAPS - 1) * SIG
    pieces = 4
    across = table.shape[1]
    terms = table.shape[0] - PARTS * 2 * NCHAN
    lanes = 2 * CHANNELS // owners // PARTS
    *first, filt, later = pl.pallas_call(
        functools.partial(filter_kernel, frames, pieces, spectrum_scale()),
        out_shape=[jax.ShapeDtypeStruct((sent, lanes), jnp.bfloat16)] * owners
        + [
            jax.ShapeDtypeStruct((2, rows, NCHAN), jnp.bfloat16),
            jax.ShapeDtypeStruct(((PARTS - 1) * 2 * NCHAN, across), jnp.bfloat16),
        ],
        in_specs=[IN_HBM, IN_HBM],
        out_specs=[IN_VMEM] * (owners + 2),
        scratch_shapes=[
            pltpu.VMEM((2, SIG, (frames + GROUP + TAPS - 1) * NCHAN), jnp.int32),
            pltpu.VMEM((2 * NCHAN, across), jnp.bfloat16),
            pltpu.VMEM((terms, across), jnp.bfloat16),
            pltpu.VMEM((TAPS * NCHAN // across, across), jnp.float32),
            pltpu.VMEM((owners, sent, lanes), jnp.bfloat16),
            pltpu.SemaphoreType.DMA((pieces + 3,)),
        ],
        compiler_params=pltpu.CompilerParams(vmem_limit_bytes=FILTER_VMEM_BYTES),
        cost_estimate=pl.CostEstimate(flops=1 << 29, bytes_accessed=4 << 20, transcendentals=0),
        name="filter_and_transform",
    )(voltages, table)
    return filt, later, first


def pick_rows(channels):
    order = np.arange(channels).reshape(PARTS, BATCH, -1, 2)
    return np.eye(channels, dtype=np.float32)[np.transpose(order, (0, 3, 2, 1)).reshape(-1)]


def next_part(part, filt, later, gains, owners):
    rows = filt.shape[1] - (GROUP - TAPS + 1) * SIG
    lanes = 2 * CHANNELS // owners // PARTS
    channels = gains.shape[2]
    shapes = [jax.ShapeDtypeStruct((rows, lanes), jnp.bfloat16)] * owners
    if part == 1:
        shapes.append(jax.ShapeDtypeStruct((channels, 2 * SIG), jnp.float32))
    return pl.pallas_call(
        functools.partial(transform_kernel, part, spectrum_scale()),
        out_shape=shapes,
        in_specs=[IN_VMEM] * 4,
        out_specs=[IN_VMEM] * len(shapes),
        scratch_shapes=[pltpu.VMEM((owners, rows, lanes), jnp.bfloat16)],
        compiler_params=pltpu.CompilerParams(vmem_limit_bytes=VMEM_BYTES),
        cost_estimate=pl.CostEstimate(flops=1 << 29, bytes_accessed=2 << 20, transcendentals=0),
        name="transform",
    )(filt, later, gains, jnp.asarray(pick_rows(channels)))


def equalize_kernel(owners, frames, h, part, *refs):
    pieces = refs[owners - 1 :: -1]
    gains_ref, by_time, by_channel = refs[owners], refs[-2], refs[-1]
    out_ref = refs[-3]
    width = 4 * h
    own_rows = frames * SIG
    over = (TAPS - 1) * SIG
    times = owners * frames
    tiles = times // LANES
    me = lax.axis_index("chan")
    for d in range(owners):
        source = jnp.bitwise_xor(me, d)
        start = pl.multiple_of(source * own_rows, own_rows)
        by_time[pl.ds(start, own_rows), :width] = pieces[d][:own_rows, :].astype(jnp.float32)
    for d in range(owners):
        source = jnp.bitwise_xor(me, d)

        @pl.when(source < owners - 1)
        def _():
            start = pl.multiple_of((source + 1) * own_rows, own_rows)
            by_time[pl.ds(start, over), :width] += pieces[d][own_rows:, :].astype(jnp.float32)

    gains = [gains_ref[(2 * part + r) * h : (2 * part + r + 1) * h, :] for r in range(2)]
    for s in range(SIG):
        x = by_time[pl.ds(s, times, stride=SIG), :][:, :width].T
        for r in range(2):
            real, imag = x[2 * r * h : (2 * r + 1) * h], x[(2 * r + 1) * h : (2 * r + 2) * h]
            gain_real, gain_imag = gains[r][:, s : s + 1], gains[r][:, SIG + s : SIG + s + 1]
            both = [real * gain_real - imag * gain_imag, real * gain_imag + imag * gain_real]
            for q in range(2):
                for tile in range(tiles):
                    by_channel[(2 * r + q) * tiles + tile, pl.ds(s, h, stride=SIG), :] = both[q][
                        :, tile * LANES : (tile + 1) * LANES
                    ]
    for r in range(2):
        for tile in range(2 * tiles):
            out_ref[r, :, tile * LANES : (tile + 1) * LANES] = by_channel[r * 2 * tiles + tile].astype(jnp.bfloat16)


def equalize(pieces, gains, part, frames, after):
    owners = len(pieces)
    h = gains.shape[0] // PARTS // 2
    times = owners * frames
    return pl.pallas_call(
        functools.partial(equalize_kernel, owners, frames, h, part),
        out_shape=jax.ShapeDtypeStruct((2, h * SIG, 2 * times), jnp.bfloat16),
        in_specs=[IN_VMEM] * (owners + 1 + len(after)),
        out_specs=IN_VMEM,
        scratch_shapes=[
            pltpu.VMEM((times * SIG, LANES), jnp.float32),
            pltpu.VMEM((4 * times // LANES, h * SIG, LANES), jnp.float32),
        ],
        compiler_params=pltpu.CompilerParams(vmem_limit_bytes=VMEM_BYTES),
        cost_estimate=pl.CostEstimate(flops=0, bytes_accessed=1 << 10, transcendentals=0),
        name="equalize",
    )(*pieces[::-1], gains, *after)


def row_places(col, n_col):
    chips = n_col // 2
    chip, core = lax.div(col, 2), lax.rem(col, 2)
    places = [col] + [lax.rem(chip + chips - d, chips) * 2 + core for d in range(1, chips)]
    return places + [jnp.bitwise_xor(p, 1) for p in places]


def column_places(row, n_row):
    return [row] + [lax.rem(row + n_row - d, n_row) for d in range(1, n_row)]


def regroup(v):
    lane = lax.broadcasted_iota(jnp.int32, v[0].shape, 1)
    v = list(v)
    for bit in (2, 1):
        width = bit * LANES // 8
        low = (lane // width) % 2 == 0
        for i in range(4):
            if i & bit == 0:
                a, b = v[i], v[i + bit]
                v[i] = jnp.where(low, a, pltpu.roll(b, width, axis=1))
                v[i + bit] = jnp.where(low, pltpu.roll(a, LANES - width, axis=1), b)
    return v


def correlate_kernel(n_row, n_col, h, times, part, dense, *refs):
    row_blocks = refs[:n_col]
    col_blocks = (refs[0],) + refs[n_col : n_col + n_row - 1]
    last = part == PARTS - 1
    given = refs[n_col + n_row - 1 :]
    if part > 0:
        earlier, keeps = given[:2]
    if last:
        out_hbm, chosen, out_ref, sems = refs[-4:]
    else:
        out_ref, keeps_out, chosen = refs[-3:]
    me_row, me_col = lax.axis_index("brow"), lax.axis_index("bcol")
    row_at, col_at = row_places(me_col, n_col), column_places(me_row, n_row)
    rows = BATCH * SIG
    tiles = n_col * rows // LANES
    steps = 2 * h // BATCH
    if part == 0:
        owned = given[0][...]
        first, second = (lax.broadcasted_iota(jnp.int32, owned.shape, axis) for axis in range(2))
        for e in range(n_row):
            for d in range(n_col):
                here = (first == me_row * n_col + row_at[d]) & (second == col_at[e] * n_col + me_col)
                found = jnp.max(jnp.where(here, (owned == 1).astype(jnp.float32), 0.0), axis=(0, 1), keepdims=True)
                keeps_out[e, d] = jnp.broadcast_to(found * (1.0 / times), (SIG, LANES))
    elif not last:
        keeps_out[...] = keeps[...]
    index_in_batch = (lax.broadcasted_iota(jnp.int32, (SIG, LANES), 1) // SIG) % BATCH

    for step in range(steps):
        inner, parity = step // 2, step % 2
        here = slice(inner * rows, (inner + 1) * rows)
        a = jnp.concatenate([block[parity, here, :] for block in row_blocks], axis=0)
        b = jnp.concatenate([block[parity, here, :] for block in col_blocks], axis=0)
        turned = jnp.concatenate([-b[:, times:], b[:, :times]], axis=1)
        both = jnp.concatenate([b, turned], axis=0)
        result = lax.dot_general(both, a, (((1,), (1,)), ((), ())), preferred_element_type=jnp.float32)
        for k in range(2 * n_row):
            for tile in range(tiles):
                lanes = slice(tile * LANES, (tile + 1) * LANES)
                own = [result[k * rows + i * SIG : k * rows + (i + 1) * SIG, lanes] for i in range(BATCH)]
                kept = own[0]
                for i in range(1, BATCH):
                    kept = jnp.where(index_in_batch == i, own[i], kept)
                chosen[k * tiles + tile, pl.ds(step, SIG, stride=steps), :] = kept

    copies = []
    low = lax.broadcasted_iota(jnp.int32, (SIG, LANES), 1) < LANES // 2
    for q in range(2):
        for e in range(n_row):
            for d in range(n_col):
                if d % (LANES // rows) == 0:
                    x = chosen[(q * n_row + e) * tiles + d * rows // LANES].T
                start = d * rows % LANES
                v = [x[start + i * SIG : start + (i + 1) * SIG] for i in range(BATCH)]
                if last:
                    keep = keeps[e, d]
                a_at = pl.ds(pl.multiple_of(row_at[d] * SIG, SIG), SIG)
                mine = slice(d * SIG, (d + 1) * SIG)
                if dense:
                    for g, w in enumerate(regroup(v)):
                        if last:
                            before = earlier[q, e, g, mine, :]
                            pair = [
                                jnp.where(low, before, pltpu.roll(w, LANES // 2, axis=1)),
                                jnp.where(low, pltpu.roll(before, LANES // 2, axis=1), w),
                            ]
                            for half in range(2):
                                out_ref[q, col_at[e] * SIG + half * BATCH + g, a_at, :] = pair[half] * keep
                        else:
                            out_ref[q, e, g, mine, :] = w
                else:
                    for s2 in range(SIG):
                        w = jnp.concatenate([each[:, s2 * steps : (s2 + 1) * steps] for each in v], axis=1)
                        if part > 0:
                            w = jnp.concatenate([earlier[q, e, s2, mine, :], w], axis=1)
                        if last:
                            out_ref[q, col_at[e] * SIG + s2, a_at, :] = w * keep[:, : w.shape[1]]
                        else:
                            out_ref[q, e, s2, mine, :] = w
            if last:
                where = pl.ds(col_at[e] * SIG, SIG)
                copy = pltpu.make_async_copy(out_ref.at[q, where], out_hbm.at[q, where], sems.at[q * n_row + e])
                copy.start()
                copies.append(copy)
    for copy in copies:
        copy.wait()


def correlate(blocks, given, part, n_row, n_col):
    h = blocks[0].shape[1] // SIG
    times = blocks[0].shape[2] // 2
    channels = 2 * h
    dense = channels * 2 == LANES and PARTS == 2
    operands = list(blocks) + list(given)
    last = part == PARTS - 1
    if last:
        out_shape = (2, n_row * SIG, n_col * SIG, (part + 1) * channels)
    elif dense:
        out_shape = (2, n_row, SIG // 2, n_col * SIG, LANES)
    else:
        out_shape = (2, n_row, SIG, n_col * SIG, (part + 1) * channels)
    shapes = [out_shape] if last else [out_shape, (n_row, n_col, SIG, LANES)]
    in_last = [pltpu.VMEM(out_shape, jnp.float32), pltpu.SemaphoreType.DMA((2 * n_row,))]
    kept = pltpu.VMEM((2 * n_row * n_col * BATCH * SIG // LANES, SIG * channels // BATCH, LANES), jnp.float32)
    return pl.pallas_call(
        functools.partial(correlate_kernel, n_row, n_col, h, times, part, dense),
        out_shape=[jax.ShapeDtypeStruct(shape, jnp.float32) for shape in shapes],
        in_specs=[IN_VMEM] * len(operands),
        out_specs=[IN_HBM] if last else [IN_VMEM] * len(shapes),
        scratch_shapes=[kept] + (in_last if last else []),
        compiler_params=pltpu.CompilerParams(vmem_limit_bytes=VMEM_BYTES),
        cost_estimate=pl.CostEstimate(flops=0, bytes_accessed=1 << 10, transcendentals=0),
        name="correlate",
    )(*operands)


def to_owners(pieces):
    owners = len(pieces)
    arrived = [pieces[0]] + [None] * (owners - 1)
    for d in range(owners - 1, 0, -1):
        arrived[d] = lax.ppermute(pieces[d], "chan", [(i, i ^ d) for i in range(owners)])
    return arrived


def copied(kernel, out_like, operands, name):
    return pl.pallas_call(
        kernel,
        out_shape=[jax.ShapeDtypeStruct(block.shape, block.dtype) for block in out_like],
        in_specs=[IN_VMEM] * len(operands),
        out_specs=[IN_VMEM] * len(out_like),
        compiler_params=pltpu.CompilerParams(vmem_limit_bytes=VMEM_BYTES),
        cost_estimate=pl.CostEstimate(flops=0, bytes_accessed=1 << 10, transcendentals=0),
        name=name,
    )(*operands)


def held_back(blocks, after):
    def kernel(*refs):
        for i in range(len(blocks)):
            refs[len(blocks) + len(after) + i][...] = refs[i][...]

    return copied(kernel, blocks, list(blocks) + list(after), "held_back")


def sorted_by_core(first, second, after):
    count = len(first)

    def kernel(*refs):
        core = lax.rem(lax.axis_index("bcol"), 2)
        outs = refs[2 * count + len(after) :]
        for flip in range(2):

            @pl.when(core == flip)
            def _():
                for i in range(count):
                    outs[i][...] = refs[i + flip * count][...]
                    outs[count + i][...] = refs[i + (1 - flip) * count][...]

    both = copied(kernel, list(first) + list(second), list(first) + list(second) + list(after), "sorted_by_core")
    return list(both[:count]), list(both[count:])


def panel_permutes(block, n_row, n_col):
    chips = n_col // 2

    def x_step(row, col, d):
        return row * n_col + (col // 2 + d) % chips * 2 + col % 2

    def y_step(row, col, d):
        return (row + d) % n_row * n_col + col

    devices = [(row, col) for row in range(n_row) for col in range(n_col)]
    axes = ("brow", "bcol")
    first, second, far, column = [], [], [], []
    for d in range(1, max(chips, n_row)):
        if d < min(chips, n_row):
            for turn, results in ((0, first), (1, second)):
                route = [
                    (row * n_col + col, (x_step if col % 2 == turn else y_step)(row, col, d)) for row, col in devices
                ]
                results.append(lax.ppermute(block, axes, route))
        else:
            step, results = (x_step, far) if d < chips else (y_step, column)
            results.append(lax.ppermute(block, axes, [(row * n_col + col, step(row, col, d)) for row, col in devices]))
    return first, second, far, column


def shards(voltages, antenna_gains, tile_map):
    owners = lax.axis_size("chan")
    n_row = lax.axis_size("brow")
    n_col = lax.axis_size("bcol")
    frames = voltages.shape[2] // NCHAN
    table = jnp.asarray(constants(owners))
    other_core = [(i, i ^ 1) for i in range(n_col)]

    filt, tables, pieces = filtered_and_first(voltages, owners, table)
    own, panels = [], []
    arrived = to_owners(pieces)
    for part in range(PARTS):
        if part < PARTS - 1:
            pieces = next_part(part + 1, filt, tables, antenna_gains, owners)
            if part == 0:
                *pieces, gains = pieces
        own.append(equalize(arrived, gains, part, frames, panels[-1][0] if part else []))
        first, second, far, column = panel_permutes(own[part], n_row, n_col)
        near_far, near_column = sorted_by_core(first, second, far + column)
        panels.append((near_far + far, near_column + column))
        if part < PARTS - 1:
            arrived = to_owners([pieces[0], *held_back(pieces[1:], own[part:])])
    beside = [lax.ppermute(block, "bcol", other_core) for block in own]
    result = [tile_map]
    for part in range(PARTS):
        far, column = panels[part]
        if part < PARTS - 1:
            far = list(held_back(far, own[-1:]))
        relayed = [lax.ppermute(block, "bcol", other_core) for block in far]
        blocks = [own[part]] + far + [beside[part]] + relayed + column
        result = correlate(blocks, result, part, n_row, n_col)
    return jnp.transpose(result[0], (3, 0, 1, 2))[None, None]


def solution(mesh):
    in_specs = (P(None, ("brow", "bcol"), "chan"), P(("brow", "bcol"), None, "chan"), P())
    out_specs = P("brow", "bcol", "chan", None, None, None)
    return jax.shard_map(shards, mesh=mesh, in_specs=in_specs, out_specs=out_specs, check_vma=False)
```

```python
import functools
import math

import jax
import jax.numpy as jnp
import ml_dtypes
import numpy as np
from jax import lax
from jax.experimental import pallas as pl
from jax.experimental.pallas import tpu as pltpu
from jax.sharding import PartitionSpec as P

NCHAN = 1024
HALF = NCHAN // 2
CHANNELS = 512
TAPS = 4
FIRST = 256
SIG = 8
LANES = 128
GROUP = 4
BATCH = 4
PARTS = 2
VMEM_BYTES = 16 * 1024 * 1024
FILTER_VMEM_BYTES = 101 * 512 * 1024
COEF_ROWS = 64


def fir_coefficients():
    position = np.arange(TAPS * NCHAN, dtype=np.float64) + 0.5
    offsets = position / NCHAN - TAPS / 2.0
    window = 0.5 - 0.5 * np.cos(2.0 * math.pi * position / (TAPS * NCHAN))
    return (np.sinc(offsets) * window).reshape(TAPS, NCHAN)


def spectrum_scale():
    return float(1.0 / (128.0 * np.sqrt(np.sum(fir_coefficients() ** 2))))


def dft_tables(owners):
    n = np.arange(HALF, dtype=np.int64).reshape(HALF, 1, 1, 1, 1, 1)
    k = FIRST + np.arange(CHANNELS, dtype=np.int64).reshape(owners, PARTS, BATCH, -1, 2)
    angles = (n * k % NCHAN) * (2.0 * math.pi / NCHAN)
    cosine, sine = np.cos(angles), np.sin(angles)
    first = np.stack([cosine, -sine], axis=2)
    second = np.stack([sine, cosine], axis=2)
    tables = np.stack([first, second])
    tables = np.transpose(tables, (4, 7, 0, 1, 2, 3, 6, 5))
    return tables.reshape(PARTS, 2 * NCHAN, -1).astype(np.float32).astype(ml_dtypes.bfloat16)


def constants(owners):
    tables = dft_tables(owners)
    lanes = tables.shape[2]
    left = fir_coefficients().astype(np.float32)
    terms = []
    for _ in range(3):
        terms.append(left.astype(ml_dtypes.bfloat16))
        left = left - terms[-1].astype(np.float32)
    terms = np.stack(terms).reshape(-1, lanes)
    pad = np.zeros((-terms.shape[0] % COEF_ROWS, lanes), ml_dtypes.bfloat16)
    return np.concatenate([tables.reshape(-1, lanes), terms, pad])


def transform(filt, table, scale, stage, out_refs):
    owners = len(out_refs)
    me = lax.axis_index("chan")
    spectra = [
        jnp.dot(filt[r], table[r * NCHAN : (r + 1) * NCHAN], preferred_element_type=jnp.float32) * scale
        for r in range(2)
    ]
    width = spectra[0].shape[1] // owners
    for owner in range(owners):
        here = slice(owner * width, (owner + 1) * width)
        piece = jnp.concatenate([spectra[0][:, here], spectra[1][:, here]], axis=1)
        stage[jnp.bitwise_xor(me, owner)] = piece[: stage.shape[1]].astype(jnp.bfloat16)
    for d in range(owners):
        out_refs[d][...] = stage[d]


def filter_kernel(frames, pieces, scale, volt_hbm, table_hbm, *refs):
    out_refs, (filt, later, volt, table, terms, coef, stage, sems) = refs[:-8], refs[-8:]
    per = frames // pieces
    lead = TAPS - 1
    copies = []
    for piece in range(pieces):
        copies.append(
            pltpu.make_async_copy(
                volt_hbm.at[:, :, pl.ds(piece * per * NCHAN, per * NCHAN)],
                volt.at[:, :, pl.ds((lead + piece * per) * NCHAN, per * NCHAN)],
                sems.at[piece],
            )
        )
    table_copy = pltpu.make_async_copy(table_hbm.at[pl.ds(0, 2 * NCHAN)], table, sems.at[pieces])
    coef_copy = pltpu.make_async_copy(
        table_hbm.at[pl.ds(PARTS * 2 * NCHAN, terms.shape[0])], terms, sems.at[pieces + 1]
    )
    coef_copy.start()
    for copy in copies:
        copy.start()
    later_copy = pltpu.make_async_copy(
        table_hbm.at[pl.ds(2 * NCHAN, (PARTS - 1) * 2 * NCHAN)], later, sems.at[pieces + 2]
    )
    table_copy.start()
    later_copy.start()
    tail = volt.shape[2] - (lead + frames) * NCHAN
    volt[:, :, : lead * NCHAN] = jnp.zeros((2, SIG, lead * NCHAN), jnp.int32)
    volt[:, :, (lead + frames) * NCHAN :] = jnp.zeros((2, SIG, tail), jnp.int32)
    coef_copy.wait()
    across = coef.shape[1]
    per_term = TAPS * NCHAN // across
    coef[...] = sum(terms[t * per_term : (t + 1) * per_term, :].astype(jnp.float32) for t in range(3))

    def filter_group(group, _):
        base = pl.multiple_of(group * (GROUP * NCHAN), GROUP * NCHAN)
        rows = pl.ds(pl.multiple_of(group * (GROUP * SIG), GROUP * SIG), GROUP * SIG)
        for column in range(HALF // LANES):
            for part in range(2):
                halves = []
                for half in range(2):
                    lane = half * HALF + column * LANES
                    at = [k * (NCHAN // across) + lane // across for k in range(TAPS)]
                    taps = [coef[i : i + 1, lane % across : lane % across + LANES] for i in at]
                    near = [
                        volt[part, :, pl.ds(base + f * NCHAN + lane, LANES)].astype(jnp.float32)
                        for f in range(GROUP + TAPS - 1)
                    ]
                    sums = []
                    for m in range(GROUP):
                        total = taps[0] * near[m]
                        for k in range(1, TAPS):
                            total = total + taps[k] * near[m + k]
                        sums.append(total)
                    halves.append(jnp.concatenate(sums, axis=0))
                where = pl.ds(part * HALF + column * LANES, LANES)
                filt[0, rows, where] = (halves[0] + halves[1]).astype(jnp.bfloat16)
                filt[1, rows, where] = (halves[0] - halves[1]).astype(jnp.bfloat16)
        return 0

    groups = per // GROUP
    for piece in range(pieces):
        copies[piece].wait()
        lax.fori_loop(piece * groups, (piece + 1) * groups, filter_group, 0)
    lax.fori_loop(frames // GROUP, frames // GROUP + 1, filter_group, 0)
    table_copy.wait()
    transform(filt, table, scale, stage, out_refs)
    later_copy.wait()


def transform_kernel(part, scale, filt, later, gains_ref, pick_ref, *refs):
    table = later.at[pl.ds((part - 1) * 2 * NCHAN, 2 * NCHAN)]
    if part == 1:
        columns, stage = refs[-2:]
        gains = jnp.concatenate([gains_ref[:, 0, :], gains_ref[:, 1, :]], axis=0)
        columns[...] = lax.dot_general(
            pick_ref[...],
            gains,
            (((1,), (1,)), ((), ())),
            precision=lax.Precision.HIGHEST,
            preferred_element_type=jnp.float32,
        )
        transform(filt, table, scale, stage, refs[:-2])
    else:
        transform(filt, table, scale, refs[-1], refs[:-1])


IN_VMEM = pl.BlockSpec(memory_space=pltpu.VMEM)
IN_HBM = pl.BlockSpec(memory_space=pl.ANY)


def filtered_and_first(voltages, owners, table):
    frames = voltages.shape[2] // NCHAN
    rows = (frames + GROUP) * SIG
    sent = (frames + TAPS - 1) * SIG
    pieces = 4
    across = table.shape[1]
    terms = table.shape[0] - PARTS * 2 * NCHAN
    lanes = 2 * CHANNELS // owners // PARTS
    *first, filt, later = pl.pallas_call(
        functools.partial(filter_kernel, frames, pieces, spectrum_scale()),
        out_shape=[jax.ShapeDtypeStruct((sent, lanes), jnp.bfloat16)] * owners
        + [
            jax.ShapeDtypeStruct((2, rows, NCHAN), jnp.bfloat16),
            jax.ShapeDtypeStruct(((PARTS - 1) * 2 * NCHAN, across), jnp.bfloat16),
        ],
        in_specs=[IN_HBM, IN_HBM],
        out_specs=[IN_VMEM] * (owners + 2),
        scratch_shapes=[
            pltpu.VMEM((2, SIG, (frames + GROUP + TAPS - 1) * NCHAN), jnp.int32),
            pltpu.VMEM((2 * NCHAN, across), jnp.bfloat16),
            pltpu.VMEM((terms, across), jnp.bfloat16),
            pltpu.VMEM((TAPS * NCHAN // across, across), jnp.float32),
            pltpu.VMEM((owners, sent, lanes), jnp.bfloat16),
            pltpu.SemaphoreType.DMA((pieces + 3,)),
        ],
        compiler_params=pltpu.CompilerParams(vmem_limit_bytes=FILTER_VMEM_BYTES),
        cost_estimate=pl.CostEstimate(flops=1 << 29, bytes_accessed=4 << 20, transcendentals=0),
        name="filter_and_transform",
    )(voltages, table)
    return filt, later, first


def pick_rows(channels):
    order = np.arange(channels).reshape(PARTS, BATCH, -1, 2)
    return np.eye(channels, dtype=np.float32)[np.transpose(order, (0, 3, 2, 1)).reshape(-1)]


def next_part(part, filt, later, gains, owners):
    rows = filt.shape[1] - (GROUP - TAPS + 1) * SIG
    lanes = 2 * CHANNELS // owners // PARTS
    channels = gains.shape[2]
    shapes = [jax.ShapeDtypeStruct((rows, lanes), jnp.bfloat16)] * owners
    if part == 1:
        shapes.append(jax.ShapeDtypeStruct((channels, 2 * SIG), jnp.float32))
    return pl.pallas_call(
        functools.partial(transform_kernel, part, spectrum_scale()),
        out_shape=shapes,
        in_specs=[IN_VMEM] * 4,
        out_specs=[IN_VMEM] * len(shapes),
        scratch_shapes=[pltpu.VMEM((owners, rows, lanes), jnp.bfloat16)],
        compiler_params=pltpu.CompilerParams(vmem_limit_bytes=VMEM_BYTES),
        cost_estimate=pl.CostEstimate(flops=1 << 29, bytes_accessed=2 << 20, transcendentals=0),
        name="transform",
    )(filt, later, gains, jnp.asarray(pick_rows(channels)))


def equalize_kernel(owners, frames, h, part, *refs):
    pieces = refs[owners - 1 :: -1]
    gains_ref, by_time, by_channel = refs[owners], refs[-2], refs[-1]
    out_ref = refs[owners + 1]
    width = 4 * h
    own_rows = frames * SIG
    over = (TAPS - 1) * SIG
    times = owners * frames
    tiles = times // LANES
    me = lax.axis_index("chan")
    for d in range(owners):
        source = jnp.bitwise_xor(me, d)
        start = pl.multiple_of(source * own_rows, own_rows)
        by_time[pl.ds(start, own_rows), :width] = pieces[d][:own_rows, :].astype(jnp.float32)
    for d in range(owners):
        source = jnp.bitwise_xor(me, d)

        @pl.when(source < owners - 1)
        def _():
            start = pl.multiple_of((source + 1) * own_rows, own_rows)
            by_time[pl.ds(start, over), :width] += pieces[d][own_rows:, :].astype(jnp.float32)

    gains = [gains_ref[(2 * part + r) * h : (2 * part + r + 1) * h, :] for r in range(2)]
    for s in range(SIG):
        x = by_time[pl.ds(s, times, stride=SIG), :][:, :width].T
        for r in range(2):
            real, imag = x[2 * r * h : (2 * r + 1) * h], x[(2 * r + 1) * h : (2 * r + 2) * h]
            gain_real, gain_imag = gains[r][:, s : s + 1], gains[r][:, SIG + s : SIG + s + 1]
            both = [real * gain_real - imag * gain_imag, real * gain_imag + imag * gain_real]
            for q in range(2):
                for tile in range(tiles):
                    by_channel[(2 * r + q) * tiles + tile, pl.ds(s, h, stride=SIG), :] = both[q][
                        :, tile * LANES : (tile + 1) * LANES
                    ]
    for r in range(2):
        for tile in range(2 * tiles):
            out_ref[r, :, tile * LANES : (tile + 1) * LANES] = by_channel[r * 2 * tiles + tile].astype(jnp.bfloat16)


def equalize(pieces, gains, part, frames):
    owners = len(pieces)
    h = gains.shape[0] // PARTS // 2
    times = owners * frames
    return pl.pallas_call(
        functools.partial(equalize_kernel, owners, frames, h, part),
        out_shape=jax.ShapeDtypeStruct((2, h * SIG, 2 * times), jnp.bfloat16),
        in_specs=[IN_VMEM] * (owners + 1),
        out_specs=IN_VMEM,
        scratch_shapes=[
            pltpu.VMEM((times * SIG, LANES), jnp.float32),
            pltpu.VMEM((4 * times // LANES, h * SIG, LANES), jnp.float32),
        ],
        compiler_params=pltpu.CompilerParams(vmem_limit_bytes=VMEM_BYTES),
        cost_estimate=pl.CostEstimate(flops=0, bytes_accessed=1 << 10, transcendentals=0),
        name="equalize",
    )(*pieces[::-1], gains)


def row_places(col, n_col):
    chips = n_col // 2
    chip, core = lax.div(col, 2), lax.rem(col, 2)
    places = [col] + [lax.rem(chip + chips - d, chips) * 2 + core for d in range(1, chips)]
    return places + [jnp.bitwise_xor(p, 1) for p in places]


def column_places(row, n_row):
    return [row] + [lax.rem(row + n_row - d, n_row) for d in range(1, n_row)]


def regroup(v):
    lane = lax.broadcasted_iota(jnp.int32, v[0].shape, 1)
    v = list(v)
    for bit in (2, 1):
        width = bit * LANES // 8
        low = (lane // width) % 2 == 0
        for i in range(4):
            if i & bit == 0:
                a, b = v[i], v[i + bit]
                v[i] = jnp.where(low, a, pltpu.roll(b, width, axis=1))
                v[i + bit] = jnp.where(low, pltpu.roll(a, LANES - width, axis=1), b)
    return v


def correlate_kernel(stage, slots, n_row, n_col, h, times, dense, *refs):
    row_blocks, col_blocks, refs = refs[: len(slots)], refs[len(slots) : len(slots) + n_row], refs[len(slots) + n_row :]
    if stage == "first":
        tile_map, out_ref, keeps, chosen = refs
    elif stage == "middle":
        earlier, keeps, out_ref, chosen = refs
    else:
        earlier, keeps, others, out_hbm, chosen, out_ref, sems = refs
    me_row, me_col = lax.axis_index("brow"), lax.axis_index("bcol")
    row_at, col_at = row_places(me_col, n_col), column_places(me_row, n_row)
    rows = BATCH * SIG
    width = len(slots) * rows
    tiles = -(-width // LANES)
    steps = 2 * h // BATCH
    copies = []
    if stage == "last":
        for d in range(n_col):
            if d not in slots:
                where = pl.ds(pl.multiple_of(row_at[d] * SIG, SIG), SIG)
                copies.append(pltpu.make_async_copy(others.at[:, :, where], out_hbm.at[:, :, where], sems.at[d]))
                copies[-1].start()
    if stage == "first":
        owned = tile_map[...]
        first, second = (lax.broadcasted_iota(jnp.int32, owned.shape, axis) for axis in range(2))
        for e in range(n_row):
            for d in range(n_col):
                here = (first == me_row * n_col + row_at[d]) & (second == col_at[e] * n_col + me_col)
                found = jnp.max(jnp.where(here, (owned == 1).astype(jnp.float32), 0.0), axis=(0, 1), keepdims=True)
                keeps[e, d] = jnp.broadcast_to(found * (1.0 / times), (SIG, LANES))
    index_in_batch = (lax.broadcasted_iota(jnp.int32, (SIG, LANES), 1) // SIG) % BATCH

    for step in range(steps):
        inner, parity = step // 2, step % 2
        here = slice(inner * rows, (inner + 1) * rows)
        a = jnp.concatenate([block[parity, here, :] for block in row_blocks], axis=0)
        b = jnp.concatenate([block[parity, here, :] for block in col_blocks], axis=0)
        turned = jnp.concatenate([-b[:, times:], b[:, :times]], axis=1)
        both = jnp.concatenate([b, turned], axis=0)
        result = lax.dot_general(both, a, (((1,), (1,)), ((), ())), preferred_element_type=jnp.float32)
        for k in range(2 * n_row):
            for tile in range(tiles):
                lanes = slice(tile * LANES, min((tile + 1) * LANES, width))
                count = lanes.stop - lanes.start
                own = [result[k * rows + i * SIG : k * rows + (i + 1) * SIG, lanes] for i in range(BATCH)]
                kept = own[0]
                for i in range(1, BATCH):
                    kept = jnp.where(index_in_batch[:, :count] == i, own[i], kept)
                chosen[k * tiles + tile, pl.ds(step, SIG, stride=steps), :count] = kept

    low = lax.broadcasted_iota(jnp.int32, (SIG, LANES), 1) < LANES // 2
    for q in range(2):
        for e in range(n_row):
            for slot, d in enumerate(slots):
                if slot % (LANES // rows) == 0:
                    x = chosen[(q * n_row + e) * tiles + slot * rows // LANES].T
                start = slot * rows % LANES
                v = [x[start + i * SIG : start + (i + 1) * SIG] for i in range(BATCH)]
                mine = slice(d * SIG, (d + 1) * SIG)
                if stage == "middle":
                    a_at = pl.ds(pl.multiple_of(row_at[d] * SIG, SIG), SIG)
                else:
                    a_at = slice(slot * SIG, (slot + 1) * SIG)
                if dense:
                    for g, w in enumerate(regroup(v)):
                        if stage == "first":
                            out_ref[q, e, g, mine, :] = w
                        else:
                            before = earlier[q, e, g, mine, :]
                            pair = [
                                jnp.where(low, before, pltpu.roll(w, LANES // 2, axis=1)),
                                jnp.where(low, pltpu.roll(before, LANES // 2, axis=1), w),
                            ]
                            for half in range(2):
                                out_ref[q, col_at[e] * SIG + half * BATCH + g, a_at, :] = pair[half] * keeps[e, d]
                else:
                    for s2 in range(SIG):
                        w = jnp.concatenate([each[:, s2 * steps : (s2 + 1) * steps] for each in v], axis=1)
                        if stage == "first":
                            out_ref[q, e, s2, mine, :] = w
                        else:
                            w = jnp.concatenate([earlier[q, e, s2, mine, :], w], axis=1)
                            out_ref[q, col_at[e] * SIG + s2, a_at, :] = w * keeps[e, d][:, : w.shape[1]]
            if stage == "last":
                there = pl.ds(col_at[e] * SIG, SIG)
                for slot, d in enumerate(slots):
                    copy = pltpu.make_async_copy(
                        out_ref.at[q, there, slice(slot * SIG, (slot + 1) * SIG)],
                        out_hbm.at[q, there, pl.ds(pl.multiple_of(row_at[d] * SIG, SIG), SIG)],
                        sems.at[n_col + (q * n_row + e) * len(slots) + slot],
                    )
                    copy.start()
                    copies.append(copy)
    for copy in copies:
        copy.wait()


def correlate(stage, slots, row_blocks, col_blocks, given, n_col):
    n_row = len(col_blocks)
    h = row_blocks[0].shape[1] // SIG
    times = row_blocks[0].shape[2] // 2
    channels = 2 * h
    dense = channels * 2 == LANES
    operands = [row_blocks[d] for d in slots] + list(col_blocks) + list(given)
    shapes = [(2, n_row * SIG, n_col * SIG, 2 * channels)]
    tiles = -(-len(slots) * BATCH * SIG // LANES)
    scratch = [pltpu.VMEM((2 * n_row * tiles, SIG * channels // BATCH, LANES), jnp.float32)]
    if stage == "first":
        shapes = [(2, n_row, SIG // 2, n_col * SIG, LANES) if dense else (2, n_row, SIG, n_col * SIG, channels)]
        shapes.append((n_row, n_col, SIG, LANES))
    if stage == "last":
        scratch.append(pltpu.VMEM((2, n_row * SIG, len(slots) * SIG, 2 * channels), jnp.float32))
        scratch.append(pltpu.SemaphoreType.DMA((n_col + 2 * n_row * len(slots),)))
    return pl.pallas_call(
        functools.partial(correlate_kernel, stage, slots, n_row, n_col, h, times, dense),
        out_shape=[jax.ShapeDtypeStruct(shape, jnp.float32) for shape in shapes],
        in_specs=[IN_VMEM] * len(operands),
        out_specs=[IN_HBM] if stage == "last" else [IN_VMEM] * len(shapes),
        scratch_shapes=scratch,
        compiler_params=pltpu.CompilerParams(vmem_limit_bytes=VMEM_BYTES),
        cost_estimate=pl.CostEstimate(flops=0, bytes_accessed=1 << 10, transcendentals=0),
        name="correlate_" + stage,
    )(*operands)


def to_owners(pieces):
    owners = len(pieces)
    arrived = [pieces[0]] + [None] * (owners - 1)
    for d in range(owners - 1, 0, -1):
        arrived[d] = lax.ppermute(pieces[d], "chan", [(i, i ^ d) for i in range(owners)])
    return arrived


def copied(kernel, out_like, operands, name):
    return pl.pallas_call(
        kernel,
        out_shape=[jax.ShapeDtypeStruct(block.shape, block.dtype) for block in out_like],
        in_specs=[IN_VMEM] * len(operands),
        out_specs=[IN_VMEM] * len(out_like),
        compiler_params=pltpu.CompilerParams(vmem_limit_bytes=VMEM_BYTES),
        cost_estimate=pl.CostEstimate(flops=0, bytes_accessed=1 << 10, transcendentals=0),
        name=name,
    )(*operands)


def held_back(blocks, after):
    def kernel(*refs):
        for i in range(len(blocks)):
            refs[len(blocks) + len(after) + i][...] = refs[i][...]

    return copied(kernel, blocks, list(blocks) + list(after), "held_back")


def sorted_by_core(first, second, after):
    count = len(first)

    def kernel(*refs):
        core = lax.rem(lax.axis_index("bcol"), 2)
        outs = refs[2 * count + len(after) :]
        for flip in range(2):

            @pl.when(core == flip)
            def _():
                for i in range(count):
                    outs[i][...] = refs[i + flip * count][...]
                    outs[count + i][...] = refs[i + (1 - flip) * count][...]

    both = copied(kernel, list(first) + list(second), list(first) + list(second) + list(after), "sorted_by_core")
    return list(both[:count]), list(both[count:])


def panel_permutes(block, n_row, n_col):
    chips = n_col // 2

    def x_step(row, col, d):
        return row * n_col + (col // 2 + d) % chips * 2 + col % 2

    def y_step(row, col, d):
        return (row + d) % n_row * n_col + col

    devices = [(row, col) for row in range(n_row) for col in range(n_col)]
    axes = ("brow", "bcol")
    first, second, far, column = [], [], [], []
    for d in range(1, max(chips, n_row)):
        if d < min(chips, n_row):
            for turn, results in ((0, first), (1, second)):
                route = [
                    (row * n_col + col, (x_step if col % 2 == turn else y_step)(row, col, d)) for row, col in devices
                ]
                results.append(lax.ppermute(block, axes, route))
        else:
            step, results = (x_step, far) if d < chips else (y_step, column)
            results.append(lax.ppermute(block, axes, [(row * n_col + col, step(row, col, d)) for row, col in devices]))
    return first, second, far, column


def shards(voltages, antenna_gains, tile_map):
    owners = lax.axis_size("chan")
    n_row = lax.axis_size("brow")
    n_col = lax.axis_size("bcol")
    frames = voltages.shape[2] // NCHAN
    table = jnp.asarray(constants(owners))
    other_core = [(i, i ^ 1) for i in range(n_col)]

    filt, tables, pieces = filtered_and_first(voltages, owners, table)
    own, panels = [], []
    arrived = to_owners(pieces)
    for part in range(PARTS):
        later = None
        if part < PARTS - 1:
            pieces = next_part(part + 1, filt, tables, antenna_gains, owners)
            if part == 0:
                *pieces, gains = pieces
            later = to_owners([pieces[0], *held_back(pieces[1:], arrived[-1:])])
        own.append(equalize(arrived, gains, part, frames))
        panels.append(panel_permutes(own[part], n_row, n_col))
        arrived = later
    beside = [lax.ppermute(block, "bcol", other_core) for block in own]
    all_slots = tuple(range(n_col))
    at_hand = tuple(range(n_col // 2 + 1))
    given = [tile_map]
    for part in range(PARTS):
        first, second, far, column = panels[part]
        near_far, near_column = sorted_by_core(first, second, own[-1:] + far + column)
        far, column = near_far + far, [own[part]] + near_column + column
        relayed = [lax.ppermute(block, "bcol", other_core) for block in far]
        rows = [own[part]] + far + [beside[part]] + relayed
        if part == 0:
            given = correlate("first", all_slots, rows, column, given, n_col)
        else:
            middle = correlate("middle", at_hand, rows, column, given, n_col)
            result = correlate("last", all_slots[len(at_hand) :], rows, column, list(given) + list(middle), n_col)
    return jnp.transpose(result[0], (3, 0, 1, 2))[None, None]


def solution(mesh):
    in_specs = (P(None, ("brow", "bcol"), "chan"), P(("brow", "bcol"), None, "chan"), P())
    out_specs = P("brow", "bcol", "chan", None, None, None)
    return jax.shard_map(shards, mesh=mesh, in_specs=in_specs, out_specs=out_specs, check_vma=False)
```

```python
import functools
import math

import jax
import jax.numpy as jnp
import ml_dtypes
import numpy as np
from jax import lax
from jax.experimental import pallas as pl
from jax.experimental.pallas import tpu as pltpu
from jax.sharding import PartitionSpec as P

NCHAN = 1024
HALF = NCHAN // 2
CHANNELS = 512
TAPS = 4
FIRST = 256
SIG = 8
LANES = 128
GROUP = 4
BATCH = 4
PARTS = 2
VMEM_BYTES = 16 * 1024 * 1024
FILTER_VMEM_BYTES = 101 * 512 * 1024
COEF_ROWS = 64


def fir_coefficients():
    position = np.arange(TAPS * NCHAN, dtype=np.float64) + 0.5
    offsets = position / NCHAN - TAPS / 2.0
    window = 0.5 - 0.5 * np.cos(2.0 * math.pi * position / (TAPS * NCHAN))
    return (np.sinc(offsets) * window).reshape(TAPS, NCHAN)


def spectrum_scale():
    return float(1.0 / (128.0 * np.sqrt(np.sum(fir_coefficients() ** 2))))


def dft_tables(owners):
    n = np.arange(HALF, dtype=np.int64).reshape(HALF, 1, 1, 1, 1, 1)
    k = FIRST + np.arange(CHANNELS, dtype=np.int64).reshape(owners, PARTS, BATCH, -1, 2)
    angles = (n * k % NCHAN) * (2.0 * math.pi / NCHAN)
    cosine, sine = np.cos(angles), np.sin(angles)
    first = np.stack([cosine, -sine], axis=2)
    second = np.stack([sine, cosine], axis=2)
    tables = np.stack([first, second])
    tables = np.transpose(tables, (4, 7, 0, 1, 2, 3, 6, 5))
    return tables.reshape(PARTS, 2 * NCHAN, -1).astype(np.float32).astype(ml_dtypes.bfloat16)


def constants(owners):
    tables = dft_tables(owners)
    lanes = tables.shape[2]
    left = fir_coefficients().astype(np.float32)
    terms = []
    for _ in range(3):
        terms.append(left.astype(ml_dtypes.bfloat16))
        left = left - terms[-1].astype(np.float32)
    terms = np.stack(terms).reshape(-1, lanes)
    pad = np.zeros((-terms.shape[0] % COEF_ROWS, lanes), ml_dtypes.bfloat16)
    return np.concatenate([tables.reshape(-1, lanes), terms, pad])


def transform(filt, table, scale, stage, out_refs):
    owners = len(out_refs)
    me = lax.axis_index("chan")
    spectra = [
        jnp.dot(filt[r], table[r * NCHAN : (r + 1) * NCHAN], preferred_element_type=jnp.float32) * scale
        for r in range(2)
    ]
    width = spectra[0].shape[1] // owners
    for owner in range(owners):
        here = slice(owner * width, (owner + 1) * width)
        piece = jnp.concatenate([spectra[0][:, here], spectra[1][:, here]], axis=1)
        stage[jnp.bitwise_xor(me, owner)] = piece[: stage.shape[1]].astype(jnp.bfloat16)
    for d in range(owners):
        out_refs[d][...] = stage[d]


def filter_kernel(frames, pieces, scale, volt_hbm, table_hbm, *refs):
    out_refs, (filt, later, volt, table, terms, coef, stage, sems) = refs[:-8], refs[-8:]
    per = frames // pieces
    lead = TAPS - 1
    copies = []
    for piece in range(pieces):
        copies.append(
            pltpu.make_async_copy(
                volt_hbm.at[:, :, pl.ds(piece * per * NCHAN, per * NCHAN)],
                volt.at[:, :, pl.ds((lead + piece * per) * NCHAN, per * NCHAN)],
                sems.at[piece],
            )
        )
    table_copy = pltpu.make_async_copy(table_hbm.at[pl.ds(0, 2 * NCHAN)], table, sems.at[pieces])
    coef_copy = pltpu.make_async_copy(
        table_hbm.at[pl.ds(PARTS * 2 * NCHAN, terms.shape[0])], terms, sems.at[pieces + 1]
    )
    coef_copy.start()
    for copy in copies:
        copy.start()
    later_copy = pltpu.make_async_copy(
        table_hbm.at[pl.ds(2 * NCHAN, (PARTS - 1) * 2 * NCHAN)], later, sems.at[pieces + 2]
    )
    table_copy.start()
    later_copy.start()
    tail = volt.shape[2] - (lead + frames) * NCHAN
    volt[:, :, : lead * NCHAN] = jnp.zeros((2, SIG, lead * NCHAN), jnp.int32)
    volt[:, :, (lead + frames) * NCHAN :] = jnp.zeros((2, SIG, tail), jnp.int32)
    coef_copy.wait()
    across = coef.shape[1]
    per_term = TAPS * NCHAN // across
    coef[...] = sum(terms[t * per_term : (t + 1) * per_term, :].astype(jnp.float32) for t in range(3))

    def filter_group(group, _):
        base = pl.multiple_of(group * (GROUP * NCHAN), GROUP * NCHAN)
        rows = pl.ds(pl.multiple_of(group * (GROUP * SIG), GROUP * SIG), GROUP * SIG)
        for column in range(HALF // LANES):
            for part in range(2):
                halves = []
                for half in range(2):
                    lane = half * HALF + column * LANES
                    at = [k * (NCHAN // across) + lane // across for k in range(TAPS)]
                    taps = [coef[i : i + 1, lane % across : lane % across + LANES] for i in at]
                    near = [
                        volt[part, :, pl.ds(base + f * NCHAN + lane, LANES)].astype(jnp.float32)
                        for f in range(GROUP + TAPS - 1)
                    ]
                    sums = []
                    for m in range(GROUP):
                        total = taps[0] * near[m]
                        for k in range(1, TAPS):
                            total = total + taps[k] * near[m + k]
                        sums.append(total)
                    halves.append(jnp.concatenate(sums, axis=0))
                where = pl.ds(part * HALF + column * LANES, LANES)
                filt[0, rows, where] = (halves[0] + halves[1]).astype(jnp.bfloat16)
                filt[1, rows, where] = (halves[0] - halves[1]).astype(jnp.bfloat16)
        return 0

    groups = per // GROUP
    for piece in range(pieces):
        copies[piece].wait()
        lax.fori_loop(piece * groups, (piece + 1) * groups, filter_group, 0)
    lax.fori_loop(frames // GROUP, frames // GROUP + 1, filter_group, 0)
    table_copy.wait()
    transform(filt, table, scale, stage, out_refs)
    later_copy.wait()


def transform_kernel(part, scale, filt, later, gains_ref, pick_ref, *refs):
    table = later.at[pl.ds((part - 1) * 2 * NCHAN, 2 * NCHAN)]
    if part == 1:
        columns, stage = refs[-2:]
        gains = jnp.concatenate([gains_ref[:, 0, :], gains_ref[:, 1, :]], axis=0)
        columns[...] = lax.dot_general(
            pick_ref[...],
            gains,
            (((1,), (1,)), ((), ())),
            precision=lax.Precision.HIGHEST,
            preferred_element_type=jnp.float32,
        )
        transform(filt, table, scale, stage, refs[:-2])
    else:
        transform(filt, table, scale, refs[-1], refs[:-1])


IN_VMEM = pl.BlockSpec(memory_space=pltpu.VMEM)
IN_HBM = pl.BlockSpec(memory_space=pl.ANY)


def filtered_and_first(voltages, owners, table):
    frames = voltages.shape[2] // NCHAN
    rows = (frames + GROUP) * SIG
    sent = (frames + TAPS - 1) * SIG
    pieces = 4
    across = table.shape[1]
    terms = table.shape[0] - PARTS * 2 * NCHAN
    lanes = 2 * CHANNELS // owners // PARTS
    *first, filt, later = pl.pallas_call(
        functools.partial(filter_kernel, frames, pieces, spectrum_scale()),
        out_shape=[jax.ShapeDtypeStruct((sent, lanes), jnp.bfloat16)] * owners
        + [
            jax.ShapeDtypeStruct((2, rows, NCHAN), jnp.bfloat16),
            jax.ShapeDtypeStruct(((PARTS - 1) * 2 * NCHAN, across), jnp.bfloat16),
        ],
        in_specs=[IN_HBM, IN_HBM],
        out_specs=[IN_VMEM] * (owners + 2),
        scratch_shapes=[
            pltpu.VMEM((2, SIG, (frames + GROUP + TAPS - 1) * NCHAN), jnp.int32),
            pltpu.VMEM((2 * NCHAN, across), jnp.bfloat16),
            pltpu.VMEM((terms, across), jnp.bfloat16),
            pltpu.VMEM((TAPS * NCHAN // across, across), jnp.float32),
            pltpu.VMEM((owners, sent, lanes), jnp.bfloat16),
            pltpu.SemaphoreType.DMA((pieces + 3,)),
        ],
        compiler_params=pltpu.CompilerParams(vmem_limit_bytes=FILTER_VMEM_BYTES),
        cost_estimate=pl.CostEstimate(flops=1 << 29, bytes_accessed=4 << 20, transcendentals=0),
        name="filter_and_transform",
    )(voltages, table)
    return filt, later, first


def pick_rows(channels):
    order = np.arange(channels).reshape(PARTS, BATCH, -1, 2)
    return np.eye(channels, dtype=np.float32)[np.transpose(order, (0, 3, 2, 1)).reshape(-1)]


def next_part(part, filt, later, gains, owners):
    rows = filt.shape[1] - (GROUP - TAPS + 1) * SIG
    lanes = 2 * CHANNELS // owners // PARTS
    channels = gains.shape[2]
    shapes = [jax.ShapeDtypeStruct((rows, lanes), jnp.bfloat16)] * owners
    if part == 1:
        shapes.append(jax.ShapeDtypeStruct((channels, 2 * SIG), jnp.float32))
    return pl.pallas_call(
        functools.partial(transform_kernel, part, spectrum_scale()),
        out_shape=shapes,
        in_specs=[IN_VMEM] * 4,
        out_specs=[IN_VMEM] * len(shapes),
        scratch_shapes=[pltpu.VMEM((owners, rows, lanes), jnp.bfloat16)],
        compiler_params=pltpu.CompilerParams(vmem_limit_bytes=VMEM_BYTES),
        cost_estimate=pl.CostEstimate(flops=1 << 29, bytes_accessed=2 << 20, transcendentals=0),
        name="transform",
    )(filt, later, gains, jnp.asarray(pick_rows(channels)))


def equalize_kernel(owners, frames, h, part, *refs):
    pieces = refs[owners - 1 :: -1]
    gains_ref, by_time, by_channel = refs[owners], refs[-2], refs[-1]
    out_ref = refs[owners + 1]
    width = 4 * h
    own_rows = frames * SIG
    over = (TAPS - 1) * SIG
    times = owners * frames
    tiles = times // LANES
    me = lax.axis_index("chan")
    for d in range(owners):
        source = jnp.bitwise_xor(me, d)
        start = pl.multiple_of(source * own_rows, own_rows)
        by_time[pl.ds(start, own_rows), :width] = pieces[d][:own_rows, :].astype(jnp.float32)
    for d in range(owners):
        source = jnp.bitwise_xor(me, d)

        @pl.when(source < owners - 1)
        def _():
            start = pl.multiple_of((source + 1) * own_rows, own_rows)
            by_time[pl.ds(start, over), :width] += pieces[d][own_rows:, :].astype(jnp.float32)

    gains = [gains_ref[(2 * part + r) * h : (2 * part + r + 1) * h, :] for r in range(2)]
    for s in range(SIG):
        x = by_time[pl.ds(s, times, stride=SIG), :][:, :width].T
        for r in range(2):
            real, imag = x[2 * r * h : (2 * r + 1) * h], x[(2 * r + 1) * h : (2 * r + 2) * h]
            gain_real, gain_imag = gains[r][:, s : s + 1], gains[r][:, SIG + s : SIG + s + 1]
            both = [real * gain_real - imag * gain_imag, real * gain_imag + imag * gain_real]
            for q in range(2):
                for tile in range(tiles):
                    by_channel[(2 * r + q) * tiles + tile, pl.ds(s, h, stride=SIG), :] = both[q][
                        :, tile * LANES : (tile + 1) * LANES
                    ]
    for r in range(2):
        for tile in range(2 * tiles):
            out_ref[r, :, tile * LANES : (tile + 1) * LANES] = by_channel[r * 2 * tiles + tile].astype(jnp.bfloat16)


def equalize(pieces, gains, part, frames):
    owners = len(pieces)
    h = gains.shape[0] // PARTS // 2
    times = owners * frames
    return pl.pallas_call(
        functools.partial(equalize_kernel, owners, frames, h, part),
        out_shape=jax.ShapeDtypeStruct((2, h * SIG, 2 * times), jnp.bfloat16),
        in_specs=[IN_VMEM] * (owners + 1),
        out_specs=IN_VMEM,
        scratch_shapes=[
            pltpu.VMEM((times * SIG, LANES), jnp.float32),
            pltpu.VMEM((4 * times // LANES, h * SIG, LANES), jnp.float32),
        ],
        compiler_params=pltpu.CompilerParams(vmem_limit_bytes=VMEM_BYTES),
        cost_estimate=pl.CostEstimate(flops=0, bytes_accessed=1 << 10, transcendentals=0),
        name="equalize",
    )(*pieces[::-1], gains)


def row_places(col, n_col):
    chips = n_col // 2
    chip, core = lax.div(col, 2), lax.rem(col, 2)
    places = [col] + [lax.rem(chip + chips - d, chips) * 2 + core for d in range(1, chips)]
    return places + [jnp.bitwise_xor(p, 1) for p in places]


def column_places(row, n_row):
    return [row] + [lax.rem(row + n_row - d, n_row) for d in range(1, n_row)]


def regroup(v):
    lane = lax.broadcasted_iota(jnp.int32, v[0].shape, 1)
    v = list(v)
    for bit in (2, 1):
        width = bit * LANES // 8
        low = (lane // width) % 2 == 0
        for i in range(4):
            if i & bit == 0:
                a, b = v[i], v[i + bit]
                v[i] = jnp.where(low, a, pltpu.roll(b, width, axis=1))
                v[i + bit] = jnp.where(low, pltpu.roll(a, LANES - width, axis=1), b)
    return v


def correlate_kernel(n_row, n_col, h, times, part, dense, *refs):
    row_blocks = refs[:n_col]
    col_blocks = (refs[0],) + refs[n_col : n_col + n_row - 1]
    last = part == PARTS - 1
    given = refs[n_col + n_row - 1 :]
    if part > 0:
        earlier, keeps = given[:2]
    if last:
        out_hbm, chosen, out_ref, sems = refs[-4:]
    else:
        out_ref, keeps_out, chosen = refs[-3:]
    me_row, me_col = lax.axis_index("brow"), lax.axis_index("bcol")
    row_at, col_at = row_places(me_col, n_col), column_places(me_row, n_row)
    rows = BATCH * SIG
    tiles = n_col * rows // LANES
    steps = 2 * h // BATCH
    if part == 0:
        owned = given[0][...]
        first, second = (lax.broadcasted_iota(jnp.int32, owned.shape, axis) for axis in range(2))
        for e in range(n_row):
            for d in range(n_col):
                here = (first == me_row * n_col + row_at[d]) & (second == col_at[e] * n_col + me_col)
                found = jnp.max(jnp.where(here, (owned == 1).astype(jnp.float32), 0.0), axis=(0, 1), keepdims=True)
                keeps_out[e, d] = jnp.broadcast_to(found * (1.0 / times), (SIG, LANES))
    elif not last:
        keeps_out[...] = keeps[...]
    index_in_batch = (lax.broadcasted_iota(jnp.int32, (SIG, LANES), 1) // SIG) % BATCH

    for step in range(steps):
        inner, parity = step // 2, step % 2
        here = slice(inner * rows, (inner + 1) * rows)
        a = jnp.concatenate([block[parity, here, :] for block in row_blocks], axis=0)
        b = jnp.concatenate([block[parity, here, :] for block in col_blocks], axis=0)
        turned = jnp.concatenate([-b[:, times:], b[:, :times]], axis=1)
        both = jnp.concatenate([b, turned], axis=0)
        result = lax.dot_general(both, a, (((1,), (1,)), ((), ())), preferred_element_type=jnp.float32)
        for k in range(2 * n_row):
            for tile in range(tiles):
                lanes = slice(tile * LANES, (tile + 1) * LANES)
                own = [result[k * rows + i * SIG : k * rows + (i + 1) * SIG, lanes] for i in range(BATCH)]
                kept = own[0]
                for i in range(1, BATCH):
                    kept = jnp.where(index_in_batch == i, own[i], kept)
                chosen[k * tiles + tile, pl.ds(step, SIG, stride=steps), :] = kept

    copies = []
    low = lax.broadcasted_iota(jnp.int32, (SIG, LANES), 1) < LANES // 2
    for q in range(2):
        for e in range(n_row):
            for d in range(n_col):
                if d % (LANES // rows) == 0:
                    x = chosen[(q * n_row + e) * tiles + d * rows // LANES].T
                start = d * rows % LANES
                v = [x[start + i * SIG : start + (i + 1) * SIG] for i in range(BATCH)]
                if last:
                    keep = keeps[e, d]
                a_at = pl.ds(pl.multiple_of(row_at[d] * SIG, SIG), SIG)
                mine = slice(d * SIG, (d + 1) * SIG)
                if dense:
                    for g, w in enumerate(regroup(v)):
                        if last:
                            before = earlier[q, e, g, mine, :]
                            pair = [
                                jnp.where(low, before, pltpu.roll(w, LANES // 2, axis=1)),
                                jnp.where(low, pltpu.roll(before, LANES // 2, axis=1), w),
                            ]
                            for half in range(2):
                                out_ref[q, col_at[e] * SIG + half * BATCH + g, a_at, :] = pair[half] * keep
                        else:
                            out_ref[q, e, g, mine, :] = w
                else:
                    for s2 in range(SIG):
                        w = jnp.concatenate([each[:, s2 * steps : (s2 + 1) * steps] for each in v], axis=1)
                        if part > 0:
                            w = jnp.concatenate([earlier[q, e, s2, mine, :], w], axis=1)
                        if last:
                            out_ref[q, col_at[e] * SIG + s2, a_at, :] = w * keep[:, : w.shape[1]]
                        else:
                            out_ref[q, e, s2, mine, :] = w
            if last:
                where = pl.ds(col_at[e] * SIG, SIG)
                copy = pltpu.make_async_copy(out_ref.at[q, where], out_hbm.at[q, where], sems.at[q * n_row + e])
                copy.start()
                copies.append(copy)
    for copy in copies:
        copy.wait()


def correlate(blocks, given, part, n_row, n_col):
    h = blocks[0].shape[1] // SIG
    times = blocks[0].shape[2] // 2
    channels = 2 * h
    dense = channels * 2 == LANES and PARTS == 2
    operands = list(blocks) + list(given)
    last = part == PARTS - 1
    if last:
        out_shape = (2, n_row * SIG, n_col * SIG, (part + 1) * channels)
    elif dense:
        out_shape = (2, n_row, SIG // 2, n_col * SIG, LANES)
    else:
        out_shape = (2, n_row, SIG, n_col * SIG, (part + 1) * channels)
    shapes = [out_shape] if last else [out_shape, (n_row, n_col, SIG, LANES)]
    in_last = [pltpu.VMEM(out_shape, jnp.float32), pltpu.SemaphoreType.DMA((2 * n_row,))]
    kept = pltpu.VMEM((2 * n_row * n_col * BATCH * SIG // LANES, SIG * channels // BATCH, LANES), jnp.float32)
    return pl.pallas_call(
        functools.partial(correlate_kernel, n_row, n_col, h, times, part, dense),
        out_shape=[jax.ShapeDtypeStruct(shape, jnp.float32) for shape in shapes],
        in_specs=[IN_VMEM] * len(operands),
        out_specs=[IN_HBM] if last else [IN_VMEM] * len(shapes),
        scratch_shapes=[kept] + (in_last if last else []),
        compiler_params=pltpu.CompilerParams(vmem_limit_bytes=VMEM_BYTES),
        cost_estimate=pl.CostEstimate(flops=0, bytes_accessed=1 << 10, transcendentals=0),
        name="correlate",
    )(*operands)


def to_owners(pieces):
    owners = len(pieces)
    arrived = [pieces[0]] + [None] * (owners - 1)
    for d in range(owners - 1, 0, -1):
        arrived[d] = lax.ppermute(pieces[d], "chan", [(i, i ^ d) for i in range(owners)])
    return arrived


def copied(kernel, out_like, operands, name):
    return pl.pallas_call(
        kernel,
        out_shape=[jax.ShapeDtypeStruct(block.shape, block.dtype) for block in out_like],
        in_specs=[IN_VMEM] * len(operands),
        out_specs=[IN_VMEM] * len(out_like),
        compiler_params=pltpu.CompilerParams(vmem_limit_bytes=VMEM_BYTES),
        cost_estimate=pl.CostEstimate(flops=0, bytes_accessed=1 << 10, transcendentals=0),
        name=name,
    )(*operands)


def held_back(blocks, after):
    def kernel(*refs):
        for i in range(len(blocks)):
            refs[len(blocks) + len(after) + i][...] = refs[i][...]

    return copied(kernel, blocks, list(blocks) + list(after), "held_back")


def sorted_by_core(first, second, after):
    count = len(first)

    def kernel(*refs):
        core = lax.rem(lax.axis_index("bcol"), 2)
        outs = refs[2 * count + len(after) :]
        for flip in range(2):

            @pl.when(core == flip)
            def _():
                for i in range(count):
                    outs[i][...] = refs[i + flip * count][...]
                    outs[count + i][...] = refs[i + (1 - flip) * count][...]

    both = copied(kernel, list(first) + list(second), list(first) + list(second) + list(after), "sorted_by_core")
    return list(both[:count]), list(both[count:])


def panel_permutes(block, n_row, n_col, crossed):
    chips = n_col // 2

    def x_step(row, col, d):
        return row * n_col + (col // 2 + d) % chips * 2 + col % 2

    def y_step(row, col, d):
        return (row + d) % n_row * n_col + col

    devices = [(row, col) for row in range(n_row) for col in range(n_col)]
    axes = ("brow", "bcol")
    first, second, far, column = [], [], [], []
    for d in range(1, max(chips, n_row)):
        if crossed and d < min(chips, n_row):
            for turn, results in ((0, first), (1, second)):
                route = [
                    (row * n_col + col, (x_step if col % 2 == turn else y_step)(row, col, d)) for row, col in devices
                ]
                results.append(lax.ppermute(block, axes, route))
        else:
            for step, results, steps in ((x_step, far, chips), (y_step, column, n_row)):
                if d < steps:
                    route = [(row * n_col + col, step(row, col, d)) for row, col in devices]
                    results.append(lax.ppermute(block, axes, route))
    return first, second, far, column


def shards(voltages, antenna_gains, tile_map):
    owners = lax.axis_size("chan")
    n_row = lax.axis_size("brow")
    n_col = lax.axis_size("bcol")
    frames = voltages.shape[2] // NCHAN
    table = jnp.asarray(constants(owners))
    other_core = [(i, i ^ 1) for i in range(n_col)]

    filt, tables, pieces = filtered_and_first(voltages, owners, table)
    own, panels = [], []
    arrived = to_owners(pieces)
    for part in range(PARTS):
        later = None
        if part < PARTS - 1:
            pieces = next_part(part + 1, filt, tables, antenna_gains, owners)
            if part == 0:
                *pieces, gains = pieces
            later = to_owners([pieces[0], *held_back(pieces[1:], arrived[-1:])])
        own.append(equalize(arrived, gains, part, frames))
        panels.append(panel_permutes(own[part], n_row, n_col, part < PARTS - 1))
        arrived = later
    result = [tile_map]
    for part in range(PARTS):
        first, second, far, column = panels[part]
        if first:
            near_far, near_column = sorted_by_core(first, second, own[-1:] + far + column)
            far, column = near_far + far, near_column + column
        mine = held_back(own[part : part + 1], far[:1])[0] if first else own[part]
        beside = lax.ppermute(mine, "bcol", other_core)
        relayed = [lax.ppermute(block, "bcol", other_core) for block in far]
        blocks = [own[part]] + far + [beside] + relayed + column
        after = panels[-1][3] if part == 0 else []
        result = correlate(blocks, list(result) + after, part, n_row, n_col)
    return jnp.transpose(result[0], (3, 0, 1, 2))[None, None]


def solution(mesh):
    in_specs = (P(None, ("brow", "bcol"), "chan"), P(("brow", "bcol"), None, "chan"), P())
    out_specs = P("brow", "bcol", "chan", None, None, None)
    return jax.shard_map(shards, mesh=mesh, in_specs=in_specs, out_specs=out_specs, check_vma=False)
```

```python
import functools
import math

import jax
import jax.numpy as jnp
import ml_dtypes
import numpy as np
from jax import lax
from jax.experimental import pallas as pl
from jax.experimental.pallas import tpu as pltpu
from jax.sharding import PartitionSpec as P

NCHAN = 1024
HALF = NCHAN // 2
CHANNELS = 512
TAPS = 4
FIRST = 256
SIG = 8
LANES = 128
GROUP = 4
BATCH = 4
PARTS = 2
VMEM_BYTES = 16 * 1024 * 1024
FILTER_VMEM_BYTES = 101 * 512 * 1024
COEF_ROWS = 64


def fir_coefficients():
    position = np.arange(TAPS * NCHAN, dtype=np.float64) + 0.5
    offsets = position / NCHAN - TAPS / 2.0
    window = 0.5 - 0.5 * np.cos(2.0 * math.pi * position / (TAPS * NCHAN))
    return (np.sinc(offsets) * window).reshape(TAPS, NCHAN)


def spectrum_scale():
    return float(1.0 / (128.0 * np.sqrt(np.sum(fir_coefficients() ** 2))))


def dft_tables(owners):
    n = np.arange(HALF, dtype=np.int64).reshape(HALF, 1, 1, 1, 1, 1)
    k = FIRST + np.arange(CHANNELS, dtype=np.int64).reshape(owners, PARTS, BATCH, -1, 2)
    angles = (n * k % NCHAN) * (2.0 * math.pi / NCHAN)
    cosine, sine = np.cos(angles), np.sin(angles)
    first = np.stack([cosine, -sine], axis=2)
    second = np.stack([sine, cosine], axis=2)
    tables = np.stack([first, second])
    tables = np.transpose(tables, (4, 7, 0, 1, 2, 3, 6, 5))
    return tables.reshape(PARTS, 2 * NCHAN, -1).astype(np.float32).astype(ml_dtypes.bfloat16)


def constants(owners):
    tables = dft_tables(owners)
    lanes = tables.shape[2]
    left = fir_coefficients().astype(np.float32)
    terms = []
    for _ in range(3):
        terms.append(left.astype(ml_dtypes.bfloat16))
        left = left - terms[-1].astype(np.float32)
    terms = np.stack(terms).reshape(-1, lanes)
    pad = np.zeros((-terms.shape[0] % COEF_ROWS, lanes), ml_dtypes.bfloat16)
    return np.concatenate([tables.reshape(-1, lanes), terms, pad])


def transform(filt, table, scale, stage, out_refs):
    owners = len(out_refs)
    me = lax.axis_index("chan")
    spectra = [
        jnp.dot(filt[r], table[r * NCHAN : (r + 1) * NCHAN], preferred_element_type=jnp.float32) * scale
        for r in range(2)
    ]
    width = spectra[0].shape[1] // owners
    for owner in range(owners):
        here = slice(owner * width, (owner + 1) * width)
        piece = jnp.concatenate([spectra[0][:, here], spectra[1][:, here]], axis=1)
        stage[jnp.bitwise_xor(me, owner)] = piece[: stage.shape[1]].astype(jnp.bfloat16)
    for d in range(owners):
        out_refs[d][...] = stage[d]


def filter_kernel(frames, pieces, scale, volt_hbm, table_hbm, *refs):
    out_refs, (filt, later, volt, table, terms, coef, stage, sems) = refs[:-8], refs[-8:]
    per = frames // pieces
    lead = TAPS - 1
    copies = []
    for piece in range(pieces):
        copies.append(
            pltpu.make_async_copy(
                volt_hbm.at[:, :, pl.ds(piece * per * NCHAN, per * NCHAN)],
                volt.at[:, :, pl.ds((lead + piece * per) * NCHAN, per * NCHAN)],
                sems.at[piece],
            )
        )
    table_copy = pltpu.make_async_copy(table_hbm.at[pl.ds(0, 2 * NCHAN)], table, sems.at[pieces])
    coef_copy = pltpu.make_async_copy(
        table_hbm.at[pl.ds(PARTS * 2 * NCHAN, terms.shape[0])], terms, sems.at[pieces + 1]
    )
    coef_copy.start()
    for copy in copies:
        copy.start()
    later_copy = pltpu.make_async_copy(
        table_hbm.at[pl.ds(2 * NCHAN, (PARTS - 1) * 2 * NCHAN)], later, sems.at[pieces + 2]
    )
    table_copy.start()
    later_copy.start()
    tail = volt.shape[2] - (lead + frames) * NCHAN
    volt[:, :, : lead * NCHAN] = jnp.zeros((2, SIG, lead * NCHAN), jnp.int32)
    volt[:, :, (lead + frames) * NCHAN :] = jnp.zeros((2, SIG, tail), jnp.int32)
    coef_copy.wait()
    across = coef.shape[1]
    per_term = TAPS * NCHAN // across
    coef[...] = sum(terms[t * per_term : (t + 1) * per_term, :].astype(jnp.float32) for t in range(3))

    def filter_group(group, _):
        base = pl.multiple_of(group * (GROUP * NCHAN), GROUP * NCHAN)
        rows = pl.ds(pl.multiple_of(group * (GROUP * SIG), GROUP * SIG), GROUP * SIG)
        for column in range(HALF // LANES):
            for part in range(2):
                halves = []
                for half in range(2):
                    lane = half * HALF + column * LANES
                    at = [k * (NCHAN // across) + lane // across for k in range(TAPS)]
                    taps = [coef[i : i + 1, lane % across : lane % across + LANES] for i in at]
                    near = [
                        volt[part, :, pl.ds(base + f * NCHAN + lane, LANES)].astype(jnp.float32)
                        for f in range(GROUP + TAPS - 1)
                    ]
                    sums = []
                    for m in range(GROUP):
                        total = taps[0] * near[m]
                        for k in range(1, TAPS):
                            total = total + taps[k] * near[m + k]
                        sums.append(total)
                    halves.append(jnp.concatenate(sums, axis=0))
                where = pl.ds(part * HALF + column * LANES, LANES)
                filt[0, rows, where] = (halves[0] + halves[1]).astype(jnp.bfloat16)
                filt[1, rows, where] = (halves[0] - halves[1]).astype(jnp.bfloat16)
        return 0

    groups = per // GROUP
    for piece in range(pieces):
        copies[piece].wait()
        lax.fori_loop(piece * groups, (piece + 1) * groups, filter_group, 0)
    lax.fori_loop(frames // GROUP, frames // GROUP + 1, filter_group, 0)
    table_copy.wait()
    transform(filt, table, scale, stage, out_refs)
    later_copy.wait()


def transform_kernel(part, scale, filt, later, gains_ref, pick_ref, *refs):
    table = later.at[pl.ds((part - 1) * 2 * NCHAN, 2 * NCHAN)]
    if part == 1:
        columns, stage = refs[-2:]
        gains = jnp.concatenate([gains_ref[:, 0, :], gains_ref[:, 1, :]], axis=0)
        columns[...] = lax.dot_general(
            pick_ref[...],
            gains,
            (((1,), (1,)), ((), ())),
            precision=lax.Precision.HIGHEST,
            preferred_element_type=jnp.float32,
        )
        transform(filt, table, scale, stage, refs[:-2])
    else:
        transform(filt, table, scale, refs[-1], refs[:-1])


IN_VMEM = pl.BlockSpec(memory_space=pltpu.VMEM)
IN_HBM = pl.BlockSpec(memory_space=pl.ANY)


def filtered_and_first(voltages, owners, table):
    frames = voltages.shape[2] // NCHAN
    rows = (frames + GROUP) * SIG
    sent = (frames + TAPS - 1) * SIG
    pieces = 4
    across = table.shape[1]
    terms = table.shape[0] - PARTS * 2 * NCHAN
    lanes = 2 * CHANNELS // owners // PARTS
    *first, filt, later = pl.pallas_call(
        functools.partial(filter_kernel, frames, pieces, spectrum_scale()),
        out_shape=[jax.ShapeDtypeStruct((sent, lanes), jnp.bfloat16)] * owners
        + [
            jax.ShapeDtypeStruct((2, rows, NCHAN), jnp.bfloat16),
            jax.ShapeDtypeStruct(((PARTS - 1) * 2 * NCHAN, across), jnp.bfloat16),
        ],
        in_specs=[IN_HBM, IN_HBM],
        out_specs=[IN_VMEM] * (owners + 2),
        scratch_shapes=[
            pltpu.VMEM((2, SIG, (frames + GROUP + TAPS - 1) * NCHAN), jnp.int32),
            pltpu.VMEM((2 * NCHAN, across), jnp.bfloat16),
            pltpu.VMEM((terms, across), jnp.bfloat16),
            pltpu.VMEM((TAPS * NCHAN // across, across), jnp.float32),
            pltpu.VMEM((owners, sent, lanes), jnp.bfloat16),
            pltpu.SemaphoreType.DMA((pieces + 3,)),
        ],
        compiler_params=pltpu.CompilerParams(vmem_limit_bytes=FILTER_VMEM_BYTES),
        cost_estimate=pl.CostEstimate(flops=1 << 29, bytes_accessed=4 << 20, transcendentals=0),
        name="filter_and_transform",
    )(voltages, table)
    return filt, later, first


def pick_rows(channels):
    order = np.arange(channels).reshape(PARTS, BATCH, -1, 2)
    return np.eye(channels, dtype=np.float32)[np.transpose(order, (0, 3, 2, 1)).reshape(-1)]


def next_part(part, filt, later, gains, owners):
    rows = filt.shape[1] - (GROUP - TAPS + 1) * SIG
    lanes = 2 * CHANNELS // owners // PARTS
    channels = gains.shape[2]
    shapes = [jax.ShapeDtypeStruct((rows, lanes), jnp.bfloat16)] * owners
    if part == 1:
        shapes.append(jax.ShapeDtypeStruct((channels, 2 * SIG), jnp.float32))
    return pl.pallas_call(
        functools.partial(transform_kernel, part, spectrum_scale()),
        out_shape=shapes,
        in_specs=[IN_VMEM] * 4,
        out_specs=[IN_VMEM] * len(shapes),
        scratch_shapes=[pltpu.VMEM((owners, rows, lanes), jnp.bfloat16)],
        compiler_params=pltpu.CompilerParams(vmem_limit_bytes=VMEM_BYTES),
        cost_estimate=pl.CostEstimate(flops=1 << 29, bytes_accessed=2 << 20, transcendentals=0),
        name="transform",
    )(filt, later, gains, jnp.asarray(pick_rows(channels)))


def equalize_kernel(owners, frames, h, part, *refs):
    pieces = refs[owners - 1 :: -1]
    gains_ref, by_time, by_channel = refs[owners], refs[-2], refs[-1]
    out_ref = refs[owners + 1]
    width = 4 * h
    own_rows = frames * SIG
    over = (TAPS - 1) * SIG
    times = owners * frames
    tiles = times // LANES
    me = lax.axis_index("chan")
    for d in range(owners):
        source = jnp.bitwise_xor(me, d)
        start = pl.multiple_of(source * own_rows, own_rows)
        by_time[pl.ds(start, own_rows), :width] = pieces[d][:own_rows, :].astype(jnp.float32)
    for d in range(owners):
        source = jnp.bitwise_xor(me, d)

        @pl.when(source < owners - 1)
        def _():
            start = pl.multiple_of((source + 1) * own_rows, own_rows)
            by_time[pl.ds(start, over), :width] += pieces[d][own_rows:, :].astype(jnp.float32)

    gains = [gains_ref[(2 * part + r) * h : (2 * part + r + 1) * h, :] for r in range(2)]
    for s in range(SIG):
        x = by_time[pl.ds(s, times, stride=SIG), :][:, :width].T
        for r in range(2):
            real, imag = x[2 * r * h : (2 * r + 1) * h], x[(2 * r + 1) * h : (2 * r + 2) * h]
            gain_real, gain_imag = gains[r][:, s : s + 1], gains[r][:, SIG + s : SIG + s + 1]
            both = [real * gain_real - imag * gain_imag, real * gain_imag + imag * gain_real]
            for q in range(2):
                for tile in range(tiles):
                    by_channel[(2 * r + q) * tiles + tile, pl.ds(s, h, stride=SIG), :] = both[q][
                        :, tile * LANES : (tile + 1) * LANES
                    ]
    for r in range(2):
        for tile in range(2 * tiles):
            out_ref[r, :, tile * LANES : (tile + 1) * LANES] = by_channel[r * 2 * tiles + tile].astype(jnp.bfloat16)


def equalize(pieces, gains, part, frames):
    owners = len(pieces)
    h = gains.shape[0] // PARTS // 2
    times = owners * frames
    return pl.pallas_call(
        functools.partial(equalize_kernel, owners, frames, h, part),
        out_shape=jax.ShapeDtypeStruct((2, h * SIG, 2 * times), jnp.bfloat16),
        in_specs=[IN_VMEM] * (owners + 1),
        out_specs=IN_VMEM,
        scratch_shapes=[
            pltpu.VMEM((times * SIG, LANES), jnp.float32),
            pltpu.VMEM((4 * times // LANES, h * SIG, LANES), jnp.float32),
        ],
        compiler_params=pltpu.CompilerParams(vmem_limit_bytes=VMEM_BYTES),
        cost_estimate=pl.CostEstimate(flops=0, bytes_accessed=1 << 10, transcendentals=0),
        name="equalize",
    )(*pieces[::-1], gains)


def row_places(col, n_col):
    chips = n_col // 2
    chip, core = lax.div(col, 2), lax.rem(col, 2)
    places = [col] + [lax.rem(chip + chips - d, chips) * 2 + core for d in range(1, chips)]
    return places + [jnp.bitwise_xor(p, 1) for p in places]


def column_places(row, n_row):
    return [row] + [lax.rem(row + n_row - d, n_row) for d in range(1, n_row)]


def regroup(v):
    lane = lax.broadcasted_iota(jnp.int32, v[0].shape, 1)
    v = list(v)
    for bit in (2, 1):
        width = bit * LANES // 8
        low = (lane // width) % 2 == 0
        for i in range(4):
            if i & bit == 0:
                a, b = v[i], v[i + bit]
                v[i] = jnp.where(low, a, pltpu.roll(b, width, axis=1))
                v[i + bit] = jnp.where(low, pltpu.roll(a, LANES - width, axis=1), b)
    return v


def correlate_kernel(n_row, n_col, h, times, part, dense, *refs):
    row_blocks = refs[:n_col]
    col_blocks = (refs[0],) + refs[n_col : n_col + n_row - 1]
    last = part == PARTS - 1
    given = refs[n_col + n_row - 1 :]
    if part > 0:
        earlier, keeps = given[:2]
    if last:
        out_hbm, chosen, out_ref, sems = refs[-4:]
    else:
        out_ref, keeps_out, chosen = refs[-3:]
    me_row, me_col = lax.axis_index("brow"), lax.axis_index("bcol")
    row_at, col_at = row_places(me_col, n_col), column_places(me_row, n_row)
    rows = BATCH * SIG
    tiles = n_col * rows // LANES
    steps = 2 * h // BATCH
    if part == 0:
        owned = given[0][...]
        first, second = (lax.broadcasted_iota(jnp.int32, owned.shape, axis) for axis in range(2))
        for e in range(n_row):
            for d in range(n_col):
                here = (first == me_row * n_col + row_at[d]) & (second == col_at[e] * n_col + me_col)
                found = jnp.max(jnp.where(here, (owned == 1).astype(jnp.float32), 0.0), axis=(0, 1), keepdims=True)
                keeps_out[e, d] = jnp.broadcast_to(found * (1.0 / times), (SIG, LANES))
    elif not last:
        keeps_out[...] = keeps[...]
    index_in_batch = (lax.broadcasted_iota(jnp.int32, (SIG, LANES), 1) // SIG) % BATCH

    for step in range(steps):
        inner, parity = step // 2, step % 2
        here = slice(inner * rows, (inner + 1) * rows)
        a = jnp.concatenate([block[parity, here, :] for block in row_blocks], axis=0)
        b = jnp.concatenate([block[parity, here, :] for block in col_blocks], axis=0)
        turned = jnp.concatenate([-b[:, times:], b[:, :times]], axis=1)
        both = jnp.concatenate([b, turned], axis=0)
        result = lax.dot_general(both, a, (((1,), (1,)), ((), ())), preferred_element_type=jnp.float32)
        for k in range(2 * n_row):
            for tile in range(tiles):
                lanes = slice(tile * LANES, (tile + 1) * LANES)
                own = [result[k * rows + i * SIG : k * rows + (i + 1) * SIG, lanes] for i in range(BATCH)]
                kept = own[0]
                for i in range(1, BATCH):
                    kept = jnp.where(index_in_batch == i, own[i], kept)
                chosen[k * tiles + tile, pl.ds(step, SIG, stride=steps), :] = kept

    copies = []
    low = lax.broadcasted_iota(jnp.int32, (SIG, LANES), 1) < LANES // 2
    for q in range(2):
        for e in range(n_row):
            for d in range(n_col):
                if d % (LANES // rows) == 0:
                    x = chosen[(q * n_row + e) * tiles + d * rows // LANES].T
                start = d * rows % LANES
                v = [x[start + i * SIG : start + (i + 1) * SIG] for i in range(BATCH)]
                if last:
                    keep = keeps[e, d]
                a_at = pl.ds(pl.multiple_of(row_at[d] * SIG, SIG), SIG)
                mine = slice(d * SIG, (d + 1) * SIG)
                if dense:
                    for g, w in enumerate(regroup(v)):
                        if last:
                            before = earlier[q, e, g, mine, :]
                            pair = [
                                jnp.where(low, before, pltpu.roll(w, LANES // 2, axis=1)),
                                jnp.where(low, pltpu.roll(before, LANES // 2, axis=1), w),
                            ]
                            for half in range(2):
                                out_ref[q, col_at[e] * SIG + half * BATCH + g, a_at, :] = pair[half] * keep
                        else:
                            out_ref[q, e, g, mine, :] = w
                else:
                    for s2 in range(SIG):
                        w = jnp.concatenate([each[:, s2 * steps : (s2 + 1) * steps] for each in v], axis=1)
                        if part > 0:
                            w = jnp.concatenate([earlier[q, e, s2, mine, :], w], axis=1)
                        if last:
                            out_ref[q, col_at[e] * SIG + s2, a_at, :] = w * keep[:, : w.shape[1]]
                        else:
                            out_ref[q, e, s2, mine, :] = w
            if last:
                where = pl.ds(col_at[e] * SIG, SIG)
                copy = pltpu.make_async_copy(out_ref.at[q, where], out_hbm.at[q, where], sems.at[q * n_row + e])
                copy.start()
                copies.append(copy)
    for copy in copies:
        copy.wait()


def correlate(blocks, given, part, n_row, n_col):
    h = blocks[0].shape[1] // SIG
    times = blocks[0].shape[2] // 2
    channels = 2 * h
    dense = channels * 2 == LANES and PARTS == 2
    operands = list(blocks) + list(given)
    last = part == PARTS - 1
    if last:
        out_shape = (2, n_row * SIG, n_col * SIG, (part + 1) * channels)
    elif dense:
        out_shape = (2, n_row, SIG // 2, n_col * SIG, LANES)
    else:
        out_shape = (2, n_row, SIG, n_col * SIG, (part + 1) * channels)
    shapes = [out_shape] if last else [out_shape, (n_row, n_col, SIG, LANES)]
    in_last = [pltpu.VMEM(out_shape, jnp.float32), pltpu.SemaphoreType.DMA((2 * n_row,))]
    kept = pltpu.VMEM((2 * n_row * n_col * BATCH * SIG // LANES, SIG * channels // BATCH, LANES), jnp.float32)
    return pl.pallas_call(
        functools.partial(correlate_kernel, n_row, n_col, h, times, part, dense),
        out_shape=[jax.ShapeDtypeStruct(shape, jnp.float32) for shape in shapes],
        in_specs=[IN_VMEM] * len(operands),
        out_specs=[IN_HBM] if last else [IN_VMEM] * len(shapes),
        scratch_shapes=[kept] + (in_last if last else []),
        compiler_params=pltpu.CompilerParams(vmem_limit_bytes=VMEM_BYTES),
        cost_estimate=pl.CostEstimate(flops=0, bytes_accessed=1 << 10, transcendentals=0),
        name="correlate",
    )(*operands)


def to_owners(pieces):
    owners = len(pieces)
    arrived = [pieces[0]] + [None] * (owners - 1)
    for d in range(owners - 1, 0, -1):
        arrived[d] = lax.ppermute(pieces[d], "chan", [(i, i ^ d) for i in range(owners)])
    return arrived


def held_back(blocks, after):
    def kernel(*refs):
        for i in range(len(blocks)):
            refs[len(blocks) + len(after) + i][...] = refs[i][...]

    return pl.pallas_call(
        kernel,
        out_shape=[jax.ShapeDtypeStruct(block.shape, block.dtype) for block in blocks],
        in_specs=[IN_VMEM] * (len(blocks) + len(after)),
        out_specs=[IN_VMEM] * len(blocks),
        compiler_params=pltpu.CompilerParams(vmem_limit_bytes=VMEM_BYTES),
        cost_estimate=pl.CostEstimate(flops=0, bytes_accessed=1 << 10, transcendentals=0),
        name="held_back",
    )(*blocks, *after)


def shards(voltages, antenna_gains, tile_map):
    owners = lax.axis_size("chan")
    n_row = lax.axis_size("brow")
    n_col = lax.axis_size("bcol")
    chips = n_col // 2
    frames = voltages.shape[2] // NCHAN
    across = [[(i, (i // 2 + d) % chips * 2 + i % 2) for i in range(n_col)] for d in range(chips)]
    along = [[(i, (i + d) % n_row) for i in range(n_row)] for d in range(n_row)]
    table = jnp.asarray(constants(owners))
    other_core = [(i, i ^ 1) for i in range(n_col)]

    filt, tables, pieces = filtered_and_first(voltages, owners, table)
    own, panels = [], []
    arrived = to_owners(pieces)
    for part in range(PARTS):
        later = None
        if part < PARTS - 1:
            pieces = next_part(part + 1, filt, tables, antenna_gains, owners)
            if part == 0:
                *pieces, gains = pieces
            later = to_owners([pieces[0], *held_back(pieces[1:], arrived[-1:])])
        own.append(equalize(arrived, gains, part, frames))
        far = [lax.ppermute(own[part], "bcol", across[d]) for d in range(1, chips)]
        column = [lax.ppermute(own[part], "brow", along[d]) for d in range(1, n_row)]
        panels.append((far, column))
        arrived = later
    result = [tile_map]
    for part in range(PARTS):
        far, column = panels[part]
        mine = own[part]
        if part < PARTS - 1:
            mine, *far = held_back([mine] + far, own[-1:])
        beside = lax.ppermute(mine, "bcol", other_core)
        relayed = [lax.ppermute(block, "bcol", other_core) for block in far]
        blocks = [own[part]] + far + [beside] + relayed + column
        after = panels[-1][1] if part == 0 else []
        result = correlate(blocks, list(result) + after, part, n_row, n_col)
    return jnp.transpose(result[0], (3, 0, 1, 2))[None, None]


def solution(mesh):
    in_specs = (P(None, ("brow", "bcol"), "chan"), P(("brow", "bcol"), None, "chan"), P())
    out_specs = P("brow", "bcol", "chan", None, None, None)
    return jax.shard_map(shards, mesh=mesh, in_specs=in_specs, out_specs=out_specs, check_vma=False)
```

```python
import functools
import math

import jax
import jax.numpy as jnp
import ml_dtypes
import numpy as np
from jax import lax
from jax.experimental import pallas as pl
from jax.experimental.pallas import tpu as pltpu
from jax.sharding import PartitionSpec as P

NCHAN = 1024
HALF = NCHAN // 2
CHANNELS = 512
TAPS = 4
FIRST = 256
SIG = 8
LANES = 128
GROUP = 4
BATCH = 4
PARTS = 2
VMEM_BYTES = 16 * 1024 * 1024
EXTRA_ROWS = 16
FILTER_VMEM_BYTES = 101 * 512 * 1024
COEF_ROWS = 64


def fir_coefficients():
    position = np.arange(TAPS * NCHAN, dtype=np.float64) + 0.5
    offsets = position / NCHAN - TAPS / 2.0
    window = 0.5 - 0.5 * np.cos(2.0 * math.pi * position / (TAPS * NCHAN))
    return (np.sinc(offsets) * window).reshape(TAPS, NCHAN)


def spectrum_scale():
    return float(1.0 / (128.0 * np.sqrt(np.sum(fir_coefficients() ** 2))))


def dft_tables(owners):
    n = np.arange(HALF, dtype=np.int64).reshape(HALF, 1, 1, 1, 1, 1)
    k = FIRST + np.arange(CHANNELS, dtype=np.int64).reshape(owners, PARTS, BATCH, -1, 2)
    angles = (n * k % NCHAN) * (2.0 * math.pi / NCHAN)
    cosine, sine = np.cos(angles), np.sin(angles)
    first = np.stack([cosine, -sine], axis=2)
    second = np.stack([sine, cosine], axis=2)
    tables = np.stack([first, second])
    tables = np.transpose(tables, (4, 7, 0, 1, 2, 3, 6, 5))
    return tables.reshape(PARTS, 2 * NCHAN, -1).astype(np.float32).astype(ml_dtypes.bfloat16)


def constants(owners):
    tables = dft_tables(owners)
    lanes = tables.shape[2]
    left = fir_coefficients().astype(np.float32)
    terms = []
    for _ in range(3):
        terms.append(left.astype(ml_dtypes.bfloat16))
        left = left - terms[-1].astype(np.float32)
    terms = np.stack(terms).reshape(-1, lanes)
    pad = np.zeros((-terms.shape[0] % COEF_ROWS, lanes), ml_dtypes.bfloat16)
    return np.concatenate([tables.reshape(-1, lanes), terms, pad])


def transform(filt, table, scale, stage, out_refs):
    owners = len(out_refs)
    me = lax.axis_index("chan")
    spectra = [
        jnp.dot(filt[r], table[r * NCHAN : (r + 1) * NCHAN], preferred_element_type=jnp.float32) * scale
        for r in range(2)
    ]
    width = spectra[0].shape[1] // owners
    for owner in range(owners):
        here = slice(owner * width, (owner + 1) * width)
        piece = jnp.concatenate([spectra[0][:, here], spectra[1][:, here]], axis=1)
        stage[jnp.bitwise_xor(me, owner)] = piece[: stage.shape[1]].astype(jnp.bfloat16)
    for d in range(owners):
        out_refs[d][...] = stage[d]


def filter_kernel(frames, pieces, scale, volt_hbm, table_hbm, *refs):
    out_refs, (filt, later, volt, table, terms, coef, stage, sems) = refs[:-8], refs[-8:]
    per = frames // pieces
    lead = TAPS - 1
    copies = []
    for piece in range(pieces):
        copies.append(
            pltpu.make_async_copy(
                volt_hbm.at[:, :, pl.ds(piece * per * NCHAN, per * NCHAN)],
                volt.at[:, :, pl.ds((lead + piece * per) * NCHAN, per * NCHAN)],
                sems.at[piece],
            )
        )
    table_copy = pltpu.make_async_copy(table_hbm.at[pl.ds(0, 2 * NCHAN)], table, sems.at[pieces])
    coef_copy = pltpu.make_async_copy(
        table_hbm.at[pl.ds(PARTS * 2 * NCHAN, terms.shape[0])], terms, sems.at[pieces + 1]
    )
    coef_copy.start()
    for copy in copies:
        copy.start()
    later_copy = pltpu.make_async_copy(
        table_hbm.at[pl.ds(2 * NCHAN, (PARTS - 1) * 2 * NCHAN)], later, sems.at[pieces + 2]
    )
    table_copy.start()
    later_copy.start()
    tail = volt.shape[2] - (lead + frames) * NCHAN
    volt[:, :, : lead * NCHAN] = jnp.zeros((2, SIG, lead * NCHAN), jnp.int32)
    volt[:, :, (lead + frames) * NCHAN :] = jnp.zeros((2, SIG, tail), jnp.int32)
    coef_copy.wait()
    across = coef.shape[1]
    per_term = TAPS * NCHAN // across
    coef[...] = sum(terms[t * per_term : (t + 1) * per_term, :].astype(jnp.float32) for t in range(3))

    def filter_group(group, _):
        base = pl.multiple_of(group * (GROUP * NCHAN), GROUP * NCHAN)
        rows = pl.ds(pl.multiple_of(group * (GROUP * SIG), GROUP * SIG), GROUP * SIG)
        for column in range(HALF // LANES):
            for part in range(2):
                halves = []
                for half in range(2):
                    lane = half * HALF + column * LANES
                    at = [k * (NCHAN // across) + lane // across for k in range(TAPS)]
                    taps = [coef[i : i + 1, lane % across : lane % across + LANES] for i in at]
                    near = [
                        volt[part, :, pl.ds(base + f * NCHAN + lane, LANES)].astype(jnp.float32)
                        for f in range(GROUP + TAPS - 1)
                    ]
                    sums = []
                    for m in range(GROUP):
                        total = taps[0] * near[m]
                        for k in range(1, TAPS):
                            total = total + taps[k] * near[m + k]
                        sums.append(total)
                    halves.append(jnp.concatenate(sums, axis=0))
                where = pl.ds(part * HALF + column * LANES, LANES)
                filt[0, rows, where] = (halves[0] + halves[1]).astype(jnp.bfloat16)
                filt[1, rows, where] = (halves[0] - halves[1]).astype(jnp.bfloat16)
        return 0

    groups = per // GROUP
    for piece in range(pieces):
        copies[piece].wait()
        lax.fori_loop(piece * groups, (piece + 1) * groups, filter_group, 0)
    lax.fori_loop(frames // GROUP, frames // GROUP + 1, filter_group, 0)
    table_copy.wait()
    transform(filt, table, scale, stage, out_refs)
    later_copy.wait()


def transform_kernel(part, scale, filt, later, gains_ref, pick_ref, *refs):
    table = later.at[pl.ds((part - 1) * 2 * NCHAN, 2 * NCHAN)]
    if part == 1:
        columns, stage = refs[-2:]
        gains = jnp.concatenate([gains_ref[:, 0, :], gains_ref[:, 1, :]], axis=0)
        columns[...] = lax.dot_general(
            pick_ref[...],
            gains,
            (((1,), (1,)), ((), ())),
            precision=lax.Precision.HIGHEST,
            preferred_element_type=jnp.float32,
        )
        transform(filt, table, scale, stage, refs[:-2])
    else:
        transform(filt, table, scale, refs[-1], refs[:-1])


IN_VMEM = pl.BlockSpec(memory_space=pltpu.VMEM)
IN_HBM = pl.BlockSpec(memory_space=pl.ANY)


def filtered_and_first(voltages, owners, table):
    frames = voltages.shape[2] // NCHAN
    rows = (frames + GROUP) * SIG
    sent = (frames + TAPS - 1) * SIG
    pieces = 4
    across = table.shape[1]
    terms = table.shape[0] - PARTS * 2 * NCHAN
    lanes = 2 * CHANNELS // owners // PARTS
    *first, filt, later = pl.pallas_call(
        functools.partial(filter_kernel, frames, pieces, spectrum_scale()),
        out_shape=[jax.ShapeDtypeStruct((sent, lanes), jnp.bfloat16)] * owners
        + [
            jax.ShapeDtypeStruct((2, rows, NCHAN), jnp.bfloat16),
            jax.ShapeDtypeStruct(((PARTS - 1) * 2 * NCHAN, across), jnp.bfloat16),
        ],
        in_specs=[IN_HBM, IN_HBM],
        out_specs=[IN_VMEM] * (owners + 2),
        scratch_shapes=[
            pltpu.VMEM((2, SIG, (frames + GROUP + TAPS - 1) * NCHAN), jnp.int32),
            pltpu.VMEM((2 * NCHAN, across), jnp.bfloat16),
            pltpu.VMEM((terms, across), jnp.bfloat16),
            pltpu.VMEM((TAPS * NCHAN // across, across), jnp.float32),
            pltpu.VMEM((owners, sent, lanes), jnp.bfloat16),
            pltpu.SemaphoreType.DMA((pieces + 3,)),
        ],
        compiler_params=pltpu.CompilerParams(vmem_limit_bytes=FILTER_VMEM_BYTES),
        cost_estimate=pl.CostEstimate(flops=1 << 29, bytes_accessed=4 << 20, transcendentals=0),
        name="filter_and_transform",
    )(voltages, table)
    return filt, later, first


def pick_rows(channels):
    order = np.arange(channels).reshape(PARTS, BATCH, -1, 2)
    return np.eye(channels, dtype=np.float32)[np.transpose(order, (0, 3, 2, 1)).reshape(-1)]


def next_part(part, filt, later, gains, owners):
    rows = filt.shape[1] - (GROUP - TAPS + 1) * SIG
    lanes = 2 * CHANNELS // owners // PARTS
    channels = gains.shape[2]
    shapes = [jax.ShapeDtypeStruct((rows, lanes), jnp.bfloat16)] * owners
    if part == 1:
        shapes.append(jax.ShapeDtypeStruct((channels, 2 * SIG), jnp.float32))
    return pl.pallas_call(
        functools.partial(transform_kernel, part, spectrum_scale()),
        out_shape=shapes,
        in_specs=[IN_VMEM] * 4,
        out_specs=[IN_VMEM] * len(shapes),
        scratch_shapes=[pltpu.VMEM((owners, rows, lanes), jnp.bfloat16)],
        compiler_params=pltpu.CompilerParams(vmem_limit_bytes=VMEM_BYTES),
        cost_estimate=pl.CostEstimate(flops=1 << 29, bytes_accessed=2 << 20, transcendentals=0),
        name="transform",
    )(filt, later, gains, jnp.asarray(pick_rows(channels)))


def equalize_kernel(owners, frames, h, part, *refs):
    pieces = refs[owners - 1 :: -1]
    gains_ref, by_time, by_channel = refs[owners], refs[-2], refs[-1]
    out_refs = refs[owners + 1 : -2]
    for out_ref in out_refs[1:]:
        out_ref[:, h * SIG :, :] = jnp.zeros((2, EXTRA_ROWS, out_ref.shape[2]), jnp.bfloat16)
    width = 4 * h
    own_rows = frames * SIG
    over = (TAPS - 1) * SIG
    times = owners * frames
    tiles = times // LANES
    me = lax.axis_index("chan")
    for d in range(owners):
        source = jnp.bitwise_xor(me, d)
        start = pl.multiple_of(source * own_rows, own_rows)
        by_time[pl.ds(start, own_rows), :width] = pieces[d][:own_rows, :].astype(jnp.float32)
    for d in range(owners):
        source = jnp.bitwise_xor(me, d)

        @pl.when(source < owners - 1)
        def _():
            start = pl.multiple_of((source + 1) * own_rows, own_rows)
            by_time[pl.ds(start, over), :width] += pieces[d][own_rows:, :].astype(jnp.float32)

    gains = [gains_ref[(2 * part + r) * h : (2 * part + r + 1) * h, :] for r in range(2)]
    for s in range(SIG):
        x = by_time[pl.ds(s, times, stride=SIG), :][:, :width].T
        for r in range(2):
            real, imag = x[2 * r * h : (2 * r + 1) * h], x[(2 * r + 1) * h : (2 * r + 2) * h]
            gain_real, gain_imag = gains[r][:, s : s + 1], gains[r][:, SIG + s : SIG + s + 1]
            both = [real * gain_real - imag * gain_imag, real * gain_imag + imag * gain_real]
            for q in range(2):
                for tile in range(tiles):
                    by_channel[(2 * r + q) * tiles + tile, pl.ds(s, h, stride=SIG), :] = both[q][
                        :, tile * LANES : (tile + 1) * LANES
                    ]
    for r in range(2):
        for tile in range(2 * tiles):
            for out_ref in out_refs:
                ready = by_channel[r * 2 * tiles + tile].astype(jnp.bfloat16)
                out_ref[r, : h * SIG, tile * LANES : (tile + 1) * LANES] = ready


def equalize(pieces, gains, part, frames):
    owners = len(pieces)
    h = gains.shape[0] // PARTS // 2
    times = owners * frames
    lengths = [h * SIG] + ([h * SIG + EXTRA_ROWS] if part == PARTS - 1 else [])
    return pl.pallas_call(
        functools.partial(equalize_kernel, owners, frames, h, part),
        out_shape=[jax.ShapeDtypeStruct((2, rows, 2 * times), jnp.bfloat16) for rows in lengths],
        in_specs=[IN_VMEM] * (owners + 1),
        out_specs=[IN_VMEM] * len(lengths),
        scratch_shapes=[
            pltpu.VMEM((times * SIG, LANES), jnp.float32),
            pltpu.VMEM((4 * times // LANES, h * SIG, LANES), jnp.float32),
        ],
        compiler_params=pltpu.CompilerParams(vmem_limit_bytes=VMEM_BYTES),
        cost_estimate=pl.CostEstimate(flops=0, bytes_accessed=1 << 10, transcendentals=0),
        name="equalize",
    )(*pieces[::-1], gains)


def row_places(col, n_col):
    chips = n_col // 2
    chip, core = lax.div(col, 2), lax.rem(col, 2)
    places = [col] + [lax.rem(chip + chips - d, chips) * 2 + core for d in range(1, chips)]
    return places + [jnp.bitwise_xor(p, 1) for p in places]


def column_places(row, n_row):
    return [row] + [lax.rem(row + n_row - d, n_row) for d in range(1, n_row)]


def regroup(v):
    lane = lax.broadcasted_iota(jnp.int32, v[0].shape, 1)
    v = list(v)
    for bit in (2, 1):
        width = bit * LANES // 8
        low = (lane // width) % 2 == 0
        for i in range(4):
            if i & bit == 0:
                a, b = v[i], v[i + bit]
                v[i] = jnp.where(low, a, pltpu.roll(b, width, axis=1))
                v[i + bit] = jnp.where(low, pltpu.roll(a, LANES - width, axis=1), b)
    return v


def correlate_kernel(n_row, n_col, h, times, part, dense, *refs):
    row_blocks = refs[:n_col]
    col_blocks = (refs[0],) + refs[n_col : n_col + n_row - 1]
    last = part == PARTS - 1
    given = refs[n_col + n_row - 1 :]
    if part > 0:
        earlier, keeps = given[:2]
    if last:
        out_hbm, chosen, out_ref, sems = refs[-4:]
    else:
        out_ref, keeps_out, chosen = refs[-3:]
    me_row, me_col = lax.axis_index("brow"), lax.axis_index("bcol")
    row_at, col_at = row_places(me_col, n_col), column_places(me_row, n_row)
    rows = BATCH * SIG
    tiles = n_col * rows // LANES
    steps = 2 * h // BATCH
    if part == 0:
        owned = given[0][...]
        first, second = (lax.broadcasted_iota(jnp.int32, owned.shape, axis) for axis in range(2))
        for e in range(n_row):
            for d in range(n_col):
                here = (first == me_row * n_col + row_at[d]) & (second == col_at[e] * n_col + me_col)
                found = jnp.max(jnp.where(here, (owned == 1).astype(jnp.float32), 0.0), axis=(0, 1), keepdims=True)
                keeps_out[e, d] = jnp.broadcast_to(found * (1.0 / times), (SIG, LANES))
    elif not last:
        keeps_out[...] = keeps[...]
    index_in_batch = (lax.broadcasted_iota(jnp.int32, (SIG, LANES), 1) // SIG) % BATCH

    for step in range(steps):
        inner, parity = step // 2, step % 2
        here = slice(inner * rows, (inner + 1) * rows)
        a = jnp.concatenate([block[parity, here, :] for block in row_blocks], axis=0)
        b = jnp.concatenate([block[parity, here, :] for block in col_blocks], axis=0)
        turned = jnp.concatenate([-b[:, times:], b[:, :times]], axis=1)
        both = jnp.concatenate([b, turned], axis=0)
        result = lax.dot_general(both, a, (((1,), (1,)), ((), ())), preferred_element_type=jnp.float32)
        for k in range(2 * n_row):
            for tile in range(tiles):
                lanes = slice(tile * LANES, (tile + 1) * LANES)
                own = [result[k * rows + i * SIG : k * rows + (i + 1) * SIG, lanes] for i in range(BATCH)]
                kept = own[0]
                for i in range(1, BATCH):
                    kept = jnp.where(index_in_batch == i, own[i], kept)
                chosen[k * tiles + tile, pl.ds(step, SIG, stride=steps), :] = kept

    copies = []
    low = lax.broadcasted_iota(jnp.int32, (SIG, LANES), 1) < LANES // 2
    for q in range(2):
        for e in range(n_row):
            for d in range(n_col):
                if d % (LANES // rows) == 0:
                    x = chosen[(q * n_row + e) * tiles + d * rows // LANES].T
                start = d * rows % LANES
                v = [x[start + i * SIG : start + (i + 1) * SIG] for i in range(BATCH)]
                if last:
                    keep = keeps[e, d]
                a_at = pl.ds(pl.multiple_of(row_at[d] * SIG, SIG), SIG)
                mine = slice(d * SIG, (d + 1) * SIG)
                if dense:
                    for g, w in enumerate(regroup(v)):
                        if last:
                            before = earlier[q, e, g, mine, :]
                            pair = [
                                jnp.where(low, before, pltpu.roll(w, LANES // 2, axis=1)),
                                jnp.where(low, pltpu.roll(before, LANES // 2, axis=1), w),
                            ]
                            for half in range(2):
                                out_ref[q, col_at[e] * SIG + half * BATCH + g, a_at, :] = pair[half] * keep
                        else:
                            out_ref[q, e, g, mine, :] = w
                else:
                    for s2 in range(SIG):
                        w = jnp.concatenate([each[:, s2 * steps : (s2 + 1) * steps] for each in v], axis=1)
                        if part > 0:
                            w = jnp.concatenate([earlier[q, e, s2, mine, :], w], axis=1)
                        if last:
                            out_ref[q, col_at[e] * SIG + s2, a_at, :] = w * keep[:, : w.shape[1]]
                        else:
                            out_ref[q, e, s2, mine, :] = w
            if last:
                where = pl.ds(col_at[e] * SIG, SIG)
                copy = pltpu.make_async_copy(out_ref.at[q, where], out_hbm.at[q, where], sems.at[q * n_row + e])
                copy.start()
                copies.append(copy)
    for copy in copies:
        copy.wait()


def correlate(blocks, given, part, n_row, n_col):
    h = blocks[0].shape[1] // SIG
    times = blocks[0].shape[2] // 2
    channels = 2 * h
    dense = channels * 2 == LANES and PARTS == 2
    operands = list(blocks) + list(given)
    last = part == PARTS - 1
    if last:
        out_shape = (2, n_row * SIG, n_col * SIG, (part + 1) * channels)
    elif dense:
        out_shape = (2, n_row, SIG // 2, n_col * SIG, LANES)
    else:
        out_shape = (2, n_row, SIG, n_col * SIG, (part + 1) * channels)
    shapes = [out_shape] if last else [out_shape, (n_row, n_col, SIG, LANES)]
    in_last = [pltpu.VMEM(out_shape, jnp.float32), pltpu.SemaphoreType.DMA((2 * n_row,))]
    kept = pltpu.VMEM((2 * n_row * n_col * BATCH * SIG // LANES, SIG * channels // BATCH, LANES), jnp.float32)
    return pl.pallas_call(
        functools.partial(correlate_kernel, n_row, n_col, h, times, part, dense),
        out_shape=[jax.ShapeDtypeStruct(shape, jnp.float32) for shape in shapes],
        in_specs=[IN_VMEM] * len(operands),
        out_specs=[IN_HBM] if last else [IN_VMEM] * len(shapes),
        scratch_shapes=[kept] + (in_last if last else []),
        compiler_params=pltpu.CompilerParams(vmem_limit_bytes=VMEM_BYTES),
        cost_estimate=pl.CostEstimate(flops=0, bytes_accessed=1 << 10, transcendentals=0),
        name="correlate",
    )(*operands)


def to_owners(pieces):
    owners = len(pieces)
    arrived = [pieces[0]] + [None] * (owners - 1)
    for d in range(owners - 1, 0, -1):
        arrived[d] = lax.ppermute(pieces[d], "chan", [(i, i ^ d) for i in range(owners)])
    return arrived


def held_back(blocks, after):
    def kernel(*refs):
        for i in range(len(blocks)):
            refs[len(blocks) + len(after) + i][...] = refs[i][...]

    return pl.pallas_call(
        kernel,
        out_shape=[jax.ShapeDtypeStruct(block.shape, block.dtype) for block in blocks],
        in_specs=[IN_VMEM] * (len(blocks) + len(after)),
        out_specs=[IN_VMEM] * len(blocks),
        compiler_params=pltpu.CompilerParams(vmem_limit_bytes=VMEM_BYTES),
        cost_estimate=pl.CostEstimate(flops=0, bytes_accessed=1 << 10, transcendentals=0),
        name="held_back",
    )(*blocks, *after)


def shards(voltages, antenna_gains, tile_map):
    owners = lax.axis_size("chan")
    n_row = lax.axis_size("brow")
    n_col = lax.axis_size("bcol")
    chips = n_col // 2
    frames = voltages.shape[2] // NCHAN
    across = [[(i, (i // 2 + d) % chips * 2 + i % 2) for i in range(n_col)] for d in range(chips)]
    along = [[(i, (i + d) % n_row) for i in range(n_row)] for d in range(n_row)]
    table = jnp.asarray(constants(owners))
    other_core = [(i, i ^ 1) for i in range(n_col)]

    filt, tables, pieces = filtered_and_first(voltages, owners, table)
    own, panels = [], []
    arrived = to_owners(pieces)
    for part in range(PARTS):
        later = None
        if part < PARTS - 1:
            pieces = next_part(part + 1, filt, tables, antenna_gains, owners)
            if part == 0:
                *pieces, gains = pieces
            later = to_owners([pieces[0], *held_back(pieces[1:], arrived[-1:])])
        block, *longer = equalize(arrived, gains, part, frames)
        own.append(block)
        far = [lax.ppermute(own[part], "bcol", across[d]) for d in range(1, chips)]
        column = [lax.ppermute((longer or own)[-1], "brow", along[d]) for d in range(1, n_row)]
        panels.append((far, column))
        arrived = later
    result = [tile_map]
    for part in range(PARTS):
        far, column = panels[part]
        mine = own[part]
        if part < PARTS - 1:
            mine, *far = held_back([mine] + far, own[-1:])
        beside = lax.ppermute(mine, "bcol", other_core)
        relayed = [lax.ppermute(block, "bcol", other_core) for block in far]
        if part > 0:
            column = list(held_back(column, result[1:]))
        blocks = [own[part]] + far + [beside] + relayed + column
        result = correlate(blocks, result, part, n_row, n_col)
    return jnp.transpose(result[0], (3, 0, 1, 2))[None, None]


def solution(mesh):
    in_specs = (P(None, ("brow", "bcol"), "chan"), P(("brow", "bcol"), None, "chan"), P())
    out_specs = P("brow", "bcol", "chan", None, None, None)
    return jax.shard_map(shards, mesh=mesh, in_specs=in_specs, out_specs=out_specs, check_vma=False)
```

```python
import functools
import math

import jax
import jax.numpy as jnp
import ml_dtypes
import numpy as np
from jax import lax
from jax.experimental import pallas as pl
from jax.experimental.pallas import tpu as pltpu
from jax.sharding import PartitionSpec as P

NCHAN = 1024
HALF = NCHAN // 2
CHANNELS = 512
TAPS = 4
FIRST = 256
SIG = 8
LANES = 128
GROUP = 4
BATCH = 4
PARTS = 2
VMEM_BYTES = 16 * 1024 * 1024
EXTRA_ROWS = 16
FILTER_VMEM_BYTES = 101 * 512 * 1024
COEF_ROWS = 64


def fir_coefficients():
    position = np.arange(TAPS * NCHAN, dtype=np.float64) + 0.5
    offsets = position / NCHAN - TAPS / 2.0
    window = 0.5 - 0.5 * np.cos(2.0 * math.pi * position / (TAPS * NCHAN))
    return (np.sinc(offsets) * window).reshape(TAPS, NCHAN)


def spectrum_scale():
    return float(1.0 / (128.0 * np.sqrt(np.sum(fir_coefficients() ** 2))))


def dft_tables(owners):
    n = np.arange(HALF, dtype=np.int64).reshape(HALF, 1, 1, 1, 1, 1)
    k = FIRST + np.arange(CHANNELS, dtype=np.int64).reshape(owners, PARTS, BATCH, -1, 2)
    angles = (n * k % NCHAN) * (2.0 * math.pi / NCHAN)
    cosine, sine = np.cos(angles), np.sin(angles)
    first = np.stack([cosine, -sine], axis=2)
    second = np.stack([sine, cosine], axis=2)
    tables = np.stack([first, second])
    tables = np.transpose(tables, (4, 7, 0, 1, 2, 3, 6, 5))
    return tables.reshape(PARTS, 2 * NCHAN, -1).astype(np.float32).astype(ml_dtypes.bfloat16)


def constants(owners):
    tables = dft_tables(owners)
    lanes = tables.shape[2]
    left = fir_coefficients().astype(np.float32)
    terms = []
    for _ in range(3):
        terms.append(left.astype(ml_dtypes.bfloat16))
        left = left - terms[-1].astype(np.float32)
    terms = np.stack(terms).reshape(-1, lanes)
    pad = np.zeros((-terms.shape[0] % COEF_ROWS, lanes), ml_dtypes.bfloat16)
    return np.concatenate([tables.reshape(-1, lanes), terms, pad])


def transform(filt, table, scale, stage, out_refs):
    owners = len(out_refs)
    me = lax.axis_index("chan")
    spectra = [
        jnp.dot(filt[r], table[r * NCHAN : (r + 1) * NCHAN], preferred_element_type=jnp.float32) * scale
        for r in range(2)
    ]
    width = spectra[0].shape[1] // owners
    for owner in range(owners):
        here = slice(owner * width, (owner + 1) * width)
        piece = jnp.concatenate([spectra[0][:, here], spectra[1][:, here]], axis=1)
        stage[jnp.bitwise_xor(me, owner)] = piece[: stage.shape[1]].astype(jnp.bfloat16)
    for d in range(owners):
        out_refs[d][...] = stage[d]


def filter_kernel(frames, pieces, scale, volt_hbm, table_hbm, *refs):
    out_refs, (filt, later, volt, table, terms, coef, stage, sems) = refs[:-8], refs[-8:]
    per = frames // pieces
    lead = TAPS - 1
    copies = []
    for piece in range(pieces):
        copies.append(
            pltpu.make_async_copy(
                volt_hbm.at[:, :, pl.ds(piece * per * NCHAN, per * NCHAN)],
                volt.at[:, :, pl.ds((lead + piece * per) * NCHAN, per * NCHAN)],
                sems.at[piece],
            )
        )
    table_copy = pltpu.make_async_copy(table_hbm.at[pl.ds(0, 2 * NCHAN)], table, sems.at[pieces])
    coef_copy = pltpu.make_async_copy(
        table_hbm.at[pl.ds(PARTS * 2 * NCHAN, terms.shape[0])], terms, sems.at[pieces + 1]
    )
    coef_copy.start()
    for copy in copies:
        copy.start()
    later_copy = pltpu.make_async_copy(
        table_hbm.at[pl.ds(2 * NCHAN, (PARTS - 1) * 2 * NCHAN)], later, sems.at[pieces + 2]
    )
    table_copy.start()
    later_copy.start()
    tail = volt.shape[2] - (lead + frames) * NCHAN
    volt[:, :, : lead * NCHAN] = jnp.zeros((2, SIG, lead * NCHAN), jnp.int32)
    volt[:, :, (lead + frames) * NCHAN :] = jnp.zeros((2, SIG, tail), jnp.int32)
    coef_copy.wait()
    across = coef.shape[1]
    per_term = TAPS * NCHAN // across
    coef[...] = sum(terms[t * per_term : (t + 1) * per_term, :].astype(jnp.float32) for t in range(3))

    def filter_group(start, count):
        base = start * NCHAN
        rows = slice(start * SIG, (start + count) * SIG)
        for column in range(HALF // LANES):
            for part in range(2):
                halves = []
                for half in range(2):
                    lane = half * HALF + column * LANES
                    at = [k * (NCHAN // across) + lane // across for k in range(TAPS)]
                    taps = [coef[i : i + 1, lane % across : lane % across + LANES] for i in at]
                    near = [
                        volt[part, :, pl.ds(base + f * NCHAN + lane, LANES)].astype(jnp.float32)
                        for f in range(count + TAPS - 1)
                    ]
                    sums = []
                    for m in range(count):
                        total = taps[0] * near[m]
                        for k in range(1, TAPS):
                            total = total + taps[k] * near[m + k]
                        sums.append(total)
                    halves.append(jnp.concatenate(sums, axis=0))
                where = pl.ds(part * HALF + column * LANES, LANES)
                filt[0, rows, where] = (halves[0] + halves[1]).astype(jnp.bfloat16)
                filt[1, rows, where] = (halves[0] - halves[1]).astype(jnp.bfloat16)

    for piece in range(pieces):
        copies[piece].wait()
        filter_group(piece * per, per)
    filter_group(frames, GROUP)
    table_copy.wait()
    transform(filt, table, scale, stage, out_refs)
    later_copy.wait()


def transform_kernel(part, scale, filt, later, gains_ref, pick_ref, *refs):
    table = later.at[pl.ds((part - 1) * 2 * NCHAN, 2 * NCHAN)]
    if part == 1:
        columns, stage = refs[-2:]
        gains = jnp.concatenate([gains_ref[:, 0, :], gains_ref[:, 1, :]], axis=0)
        columns[...] = lax.dot_general(
            pick_ref[...],
            gains,
            (((1,), (1,)), ((), ())),
            precision=lax.Precision.HIGHEST,
            preferred_element_type=jnp.float32,
        )
        transform(filt, table, scale, stage, refs[:-2])
    else:
        transform(filt, table, scale, refs[-1], refs[:-1])


IN_VMEM = pl.BlockSpec(memory_space=pltpu.VMEM)
IN_HBM = pl.BlockSpec(memory_space=pl.ANY)


def filtered_and_first(voltages, owners, table):
    frames = voltages.shape[2] // NCHAN
    rows = (frames + GROUP) * SIG
    sent = (frames + TAPS - 1) * SIG
    pieces = 4
    across = table.shape[1]
    terms = table.shape[0] - PARTS * 2 * NCHAN
    lanes = 2 * CHANNELS // owners // PARTS
    *first, filt, later = pl.pallas_call(
        functools.partial(filter_kernel, frames, pieces, spectrum_scale()),
        out_shape=[jax.ShapeDtypeStruct((sent, lanes), jnp.bfloat16)] * owners
        + [
            jax.ShapeDtypeStruct((2, rows, NCHAN), jnp.bfloat16),
            jax.ShapeDtypeStruct(((PARTS - 1) * 2 * NCHAN, across), jnp.bfloat16),
        ],
        in_specs=[IN_HBM, IN_HBM],
        out_specs=[IN_VMEM] * (owners + 2),
        scratch_shapes=[
            pltpu.VMEM((2, SIG, (frames + GROUP + TAPS - 1) * NCHAN), jnp.int32),
            pltpu.VMEM((2 * NCHAN, across), jnp.bfloat16),
            pltpu.VMEM((terms, across), jnp.bfloat16),
            pltpu.VMEM((TAPS * NCHAN // across, across), jnp.float32),
            pltpu.VMEM((owners, sent, lanes), jnp.bfloat16),
            pltpu.SemaphoreType.DMA((pieces + 3,)),
        ],
        compiler_params=pltpu.CompilerParams(vmem_limit_bytes=FILTER_VMEM_BYTES),
        cost_estimate=pl.CostEstimate(flops=1 << 29, bytes_accessed=4 << 20, transcendentals=0),
        name="filter_and_transform",
    )(voltages, table)
    return filt, later, first


def pick_rows(channels):
    order = np.arange(channels).reshape(PARTS, BATCH, -1, 2)
    return np.eye(channels, dtype=np.float32)[np.transpose(order, (0, 3, 2, 1)).reshape(-1)]


def next_part(part, filt, later, gains, owners):
    rows = filt.shape[1] - (GROUP - TAPS + 1) * SIG
    lanes = 2 * CHANNELS // owners // PARTS
    channels = gains.shape[2]
    shapes = [jax.ShapeDtypeStruct((rows, lanes), jnp.bfloat16)] * owners
    if part == 1:
        shapes.append(jax.ShapeDtypeStruct((channels, 2 * SIG), jnp.float32))
    return pl.pallas_call(
        functools.partial(transform_kernel, part, spectrum_scale()),
        out_shape=shapes,
        in_specs=[IN_VMEM] * 4,
        out_specs=[IN_VMEM] * len(shapes),
        scratch_shapes=[pltpu.VMEM((owners, rows, lanes), jnp.bfloat16)],
        compiler_params=pltpu.CompilerParams(vmem_limit_bytes=VMEM_BYTES),
        cost_estimate=pl.CostEstimate(flops=1 << 29, bytes_accessed=2 << 20, transcendentals=0),
        name="transform",
    )(filt, later, gains, jnp.asarray(pick_rows(channels)))


def equalize_kernel(owners, frames, h, part, *refs):
    pieces = refs[owners - 1 :: -1]
    gains_ref, by_time, by_channel = refs[owners], refs[-2], refs[-1]
    out_refs = refs[owners + 1 : -2]
    for out_ref in out_refs[1:]:
        out_ref[:, h * SIG :, :] = jnp.zeros((2, EXTRA_ROWS, out_ref.shape[2]), jnp.bfloat16)
    width = 4 * h
    own_rows = frames * SIG
    over = (TAPS - 1) * SIG
    times = owners * frames
    tiles = times // LANES
    me = lax.axis_index("chan")
    for d in range(owners):
        source = jnp.bitwise_xor(me, d)
        start = pl.multiple_of(source * own_rows, own_rows)
        by_time[pl.ds(start, own_rows), :width] = pieces[d][:own_rows, :].astype(jnp.float32)
    for d in range(owners):
        source = jnp.bitwise_xor(me, d)

        @pl.when(source < owners - 1)
        def _():
            start = pl.multiple_of((source + 1) * own_rows, own_rows)
            by_time[pl.ds(start, over), :width] += pieces[d][own_rows:, :].astype(jnp.float32)

    gains = [gains_ref[(2 * part + r) * h : (2 * part + r + 1) * h, :] for r in range(2)]
    for s in range(SIG):
        x = by_time[pl.ds(s, times, stride=SIG), :][:, :width].T
        for r in range(2):
            real, imag = x[2 * r * h : (2 * r + 1) * h], x[(2 * r + 1) * h : (2 * r + 2) * h]
            gain_real, gain_imag = gains[r][:, s : s + 1], gains[r][:, SIG + s : SIG + s + 1]
            both = [real * gain_real - imag * gain_imag, real * gain_imag + imag * gain_real]
            for q in range(2):
                for tile in range(tiles):
                    by_channel[(2 * r + q) * tiles + tile, pl.ds(s, h, stride=SIG), :] = both[q][
                        :, tile * LANES : (tile + 1) * LANES
                    ]
    for r in range(2):
        for tile in range(2 * tiles):
            for out_ref in out_refs:
                ready = by_channel[r * 2 * tiles + tile].astype(jnp.bfloat16)
                out_ref[r, : h * SIG, tile * LANES : (tile + 1) * LANES] = ready


def equalize(pieces, gains, part, frames):
    owners = len(pieces)
    h = gains.shape[0] // PARTS // 2
    times = owners * frames
    lengths = [h * SIG] + ([h * SIG + EXTRA_ROWS] if part == PARTS - 1 else [])
    return pl.pallas_call(
        functools.partial(equalize_kernel, owners, frames, h, part),
        out_shape=[jax.ShapeDtypeStruct((2, rows, 2 * times), jnp.bfloat16) for rows in lengths],
        in_specs=[IN_VMEM] * (owners + 1),
        out_specs=[IN_VMEM] * len(lengths),
        scratch_shapes=[
            pltpu.VMEM((times * SIG, LANES), jnp.float32),
            pltpu.VMEM((4 * times // LANES, h * SIG, LANES), jnp.float32),
        ],
        compiler_params=pltpu.CompilerParams(vmem_limit_bytes=VMEM_BYTES),
        cost_estimate=pl.CostEstimate(flops=0, bytes_accessed=1 << 10, transcendentals=0),
        name="equalize",
    )(*pieces[::-1], gains)


def row_places(col, n_col):
    chips = n_col // 2
    chip, core = lax.div(col, 2), lax.rem(col, 2)
    places = [col] + [lax.rem(chip + chips - d, chips) * 2 + core for d in range(1, chips)]
    return places + [jnp.bitwise_xor(p, 1) for p in places]


def column_places(row, n_row):
    return [row] + [lax.rem(row + n_row - d, n_row) for d in range(1, n_row)]


def regroup(v):
    lane = lax.broadcasted_iota(jnp.int32, v[0].shape, 1)
    v = list(v)
    for bit in (2, 1):
        width = bit * LANES // 8
        low = (lane // width) % 2 == 0
        for i in range(4):
            if i & bit == 0:
                a, b = v[i], v[i + bit]
                v[i] = jnp.where(low, a, pltpu.roll(b, width, axis=1))
                v[i + bit] = jnp.where(low, pltpu.roll(a, LANES - width, axis=1), b)
    return v


def correlate_kernel(n_row, n_col, h, times, part, dense, *refs):
    row_blocks = refs[:n_col]
    col_blocks = (refs[0],) + refs[n_col : n_col + n_row - 1]
    last = part == PARTS - 1
    given = refs[n_col + n_row - 1 :]
    if part > 0:
        earlier, keeps = given[:2]
    if last:
        out_hbm, chosen, out_ref, sems = refs[-4:]
    else:
        out_ref, keeps_out, chosen = refs[-3:]
    me_row, me_col = lax.axis_index("brow"), lax.axis_index("bcol")
    row_at, col_at = row_places(me_col, n_col), column_places(me_row, n_row)
    rows = BATCH * SIG
    tiles = n_col * rows // LANES
    steps = 2 * h // BATCH
    if part == 0:
        owned = given[0][...]
        first, second = (lax.broadcasted_iota(jnp.int32, owned.shape, axis) for axis in range(2))
        for e in range(n_row):
            for d in range(n_col):
                here = (first == me_row * n_col + row_at[d]) & (second == col_at[e] * n_col + me_col)
                found = jnp.max(jnp.where(here, (owned == 1).astype(jnp.float32), 0.0), axis=(0, 1), keepdims=True)
                keeps_out[e, d] = jnp.broadcast_to(found * (1.0 / times), (SIG, LANES))
    elif not last:
        keeps_out[...] = keeps[...]
    index_in_batch = (lax.broadcasted_iota(jnp.int32, (SIG, LANES), 1) // SIG) % BATCH

    for step in range(steps):
        inner, parity = step // 2, step % 2
        here = slice(inner * rows, (inner + 1) * rows)
        a = jnp.concatenate([block[parity, here, :] for block in row_blocks], axis=0)
        b = jnp.concatenate([block[parity, here, :] for block in col_blocks], axis=0)
        turned = jnp.concatenate([-b[:, times:], b[:, :times]], axis=1)
        both = jnp.concatenate([b, turned], axis=0)
        result = lax.dot_general(both, a, (((1,), (1,)), ((), ())), preferred_element_type=jnp.float32)
        for k in range(2 * n_row):
            for tile in range(tiles):
                lanes = slice(tile * LANES, (tile + 1) * LANES)
                own = [result[k * rows + i * SIG : k * rows + (i + 1) * SIG, lanes] for i in range(BATCH)]
                kept = own[0]
                for i in range(1, BATCH):
                    kept = jnp.where(index_in_batch == i, own[i], kept)
                chosen[k * tiles + tile, pl.ds(step, SIG, stride=steps), :] = kept

    copies = []
    low = lax.broadcasted_iota(jnp.int32, (SIG, LANES), 1) < LANES // 2
    for q in range(2):
        for e in range(n_row):
            for d in range(n_col):
                if d % (LANES // rows) == 0:
                    x = chosen[(q * n_row + e) * tiles + d * rows // LANES].T
                start = d * rows % LANES
                v = [x[start + i * SIG : start + (i + 1) * SIG] for i in range(BATCH)]
                if last:
                    keep = keeps[e, d]
                a_at = pl.ds(pl.multiple_of(row_at[d] * SIG, SIG), SIG)
                mine = slice(d * SIG, (d + 1) * SIG)
                if dense:
                    for g, w in enumerate(regroup(v)):
                        if last:
                            before = earlier[q, e, g, mine, :]
                            pair = [
                                jnp.where(low, before, pltpu.roll(w, LANES // 2, axis=1)),
                                jnp.where(low, pltpu.roll(before, LANES // 2, axis=1), w),
                            ]
                            for half in range(2):
                                out_ref[q, col_at[e] * SIG + half * BATCH + g, a_at, :] = pair[half] * keep
                        else:
                            out_ref[q, e, g, mine, :] = w
                else:
                    for s2 in range(SIG):
                        w = jnp.concatenate([each[:, s2 * steps : (s2 + 1) * steps] for each in v], axis=1)
                        if part > 0:
                            w = jnp.concatenate([earlier[q, e, s2, mine, :], w], axis=1)
                        if last:
                            out_ref[q, col_at[e] * SIG + s2, a_at, :] = w * keep[:, : w.shape[1]]
                        else:
                            out_ref[q, e, s2, mine, :] = w
            if last:
                where = pl.ds(col_at[e] * SIG, SIG)
                copy = pltpu.make_async_copy(out_ref.at[q, where], out_hbm.at[q, where], sems.at[q * n_row + e])
                copy.start()
                copies.append(copy)
    for copy in copies:
        copy.wait()


def correlate(blocks, given, part, n_row, n_col):
    h = blocks[0].shape[1] // SIG
    times = blocks[0].shape[2] // 2
    channels = 2 * h
    dense = channels * 2 == LANES and PARTS == 2
    operands = list(blocks) + list(given)
    last = part == PARTS - 1
    if last:
        out_shape = (2, n_row * SIG, n_col * SIG, (part + 1) * channels)
    elif dense:
        out_shape = (2, n_row, SIG // 2, n_col * SIG, LANES)
    else:
        out_shape = (2, n_row, SIG, n_col * SIG, (part + 1) * channels)
    shapes = [out_shape] if last else [out_shape, (n_row, n_col, SIG, LANES)]
    in_last = [pltpu.VMEM(out_shape, jnp.float32), pltpu.SemaphoreType.DMA((2 * n_row,))]
    kept = pltpu.VMEM((2 * n_row * n_col * BATCH * SIG // LANES, SIG * channels // BATCH, LANES), jnp.float32)
    return pl.pallas_call(
        functools.partial(correlate_kernel, n_row, n_col, h, times, part, dense),
        out_shape=[jax.ShapeDtypeStruct(shape, jnp.float32) for shape in shapes],
        in_specs=[IN_VMEM] * len(operands),
        out_specs=[IN_HBM] if last else [IN_VMEM] * len(shapes),
        scratch_shapes=[kept] + (in_last if last else []),
        compiler_params=pltpu.CompilerParams(vmem_limit_bytes=VMEM_BYTES),
        cost_estimate=pl.CostEstimate(flops=0, bytes_accessed=1 << 10, transcendentals=0),
        name="correlate",
    )(*operands)


def to_owners(pieces):
    owners = len(pieces)
    arrived = [pieces[0]] + [None] * (owners - 1)
    for d in range(owners - 1, 0, -1):
        arrived[d] = lax.ppermute(pieces[d], "chan", [(i, i ^ d) for i in range(owners)])
    return arrived


def held_back(blocks, after):
    def kernel(*refs):
        for i in range(len(blocks)):
            refs[len(blocks) + len(after) + i][...] = refs[i][...]

    return pl.pallas_call(
        kernel,
        out_shape=[jax.ShapeDtypeStruct(block.shape, block.dtype) for block in blocks],
        in_specs=[IN_VMEM] * (len(blocks) + len(after)),
        out_specs=[IN_VMEM] * len(blocks),
        compiler_params=pltpu.CompilerParams(vmem_limit_bytes=VMEM_BYTES),
        cost_estimate=pl.CostEstimate(flops=0, bytes_accessed=1 << 10, transcendentals=0),
        name="held_back",
    )(*blocks, *after)


def shards(voltages, antenna_gains, tile_map):
    owners = lax.axis_size("chan")
    n_row = lax.axis_size("brow")
    n_col = lax.axis_size("bcol")
    chips = n_col // 2
    frames = voltages.shape[2] // NCHAN
    across = [[(i, (i // 2 + d) % chips * 2 + i % 2) for i in range(n_col)] for d in range(chips)]
    along = [[(i, (i + d) % n_row) for i in range(n_row)] for d in range(n_row)]
    table = jnp.asarray(constants(owners))
    other_core = [(i, i ^ 1) for i in range(n_col)]

    filt, tables, pieces = filtered_and_first(voltages, owners, table)
    own, panels = [], []
    arrived = to_owners(pieces)
    for part in range(PARTS):
        later = None
        if part < PARTS - 1:
            pieces = next_part(part + 1, filt, tables, antenna_gains, owners)
            if part == 0:
                *pieces, gains = pieces
            later = to_owners([pieces[0], *held_back(pieces[1:], arrived[-1:])])
        block, *longer = equalize(arrived, gains, part, frames)
        own.append(block)
        far = [lax.ppermute(own[part], "bcol", across[d]) for d in range(1, chips)]
        column = [lax.ppermute((longer or own)[-1], "brow", along[d]) for d in range(1, n_row)]
        panels.append((far, column))
        arrived = later
    result = [tile_map]
    for part in range(PARTS):
        far, column = panels[part]
        mine = own[part]
        if part < PARTS - 1:
            mine, *far = held_back([mine] + far, own[-1:])
        beside = lax.ppermute(mine, "bcol", other_core)
        relayed = [lax.ppermute(block, "bcol", other_core) for block in far]
        if part > 0:
            column = list(held_back(column, result[1:]))
        blocks = [own[part]] + far + [beside] + relayed + column
        result = correlate(blocks, result, part, n_row, n_col)
    return jnp.transpose(result[0], (3, 0, 1, 2))[None, None]


def solution(mesh):
    in_specs = (P(None, ("brow", "bcol"), "chan"), P(("brow", "bcol"), None, "chan"), P())
    out_specs = P("brow", "bcol", "chan", None, None, None)
    return jax.shard_map(shards, mesh=mesh, in_specs=in_specs, out_specs=out_specs, check_vma=False)
```

```python
import functools
import math

import jax
import jax.numpy as jnp
import ml_dtypes
import numpy as np
from jax import lax
from jax.experimental import pallas as pl
from jax.experimental.pallas import tpu as pltpu
from jax.sharding import PartitionSpec as P

NCHAN = 1024
HALF = NCHAN // 2
CHANNELS = 512
TAPS = 4
FIRST = 256
SIG = 8
LANES = 128
GROUP = 4
BATCH = 4
PARTS = 2
VMEM_BYTES = 16 * 1024 * 1024
EXTRA_ROWS = 16
FILTER_VMEM_BYTES = 101 * 512 * 1024
COEF_ROWS = 64


def fir_coefficients():
    position = np.arange(TAPS * NCHAN, dtype=np.float64) + 0.5
    offsets = position / NCHAN - TAPS / 2.0
    window = 0.5 - 0.5 * np.cos(2.0 * math.pi * position / (TAPS * NCHAN))
    return (np.sinc(offsets) * window).reshape(TAPS, NCHAN)


def spectrum_scale():
    return float(1.0 / (128.0 * np.sqrt(np.sum(fir_coefficients() ** 2))))


def dft_tables(owners):
    n = np.arange(HALF, dtype=np.int64).reshape(HALF, 1, 1, 1, 1, 1)
    k = FIRST + np.arange(CHANNELS, dtype=np.int64).reshape(owners, PARTS, BATCH, -1, 2)
    angles = (n * k % NCHAN) * (2.0 * math.pi / NCHAN)
    cosine, sine = np.cos(angles), np.sin(angles)
    first = np.stack([cosine, -sine], axis=2)
    second = np.stack([sine, cosine], axis=2)
    tables = np.stack([first, second])
    tables = np.transpose(tables, (4, 7, 0, 1, 2, 3, 6, 5))
    return tables.reshape(PARTS, 2 * NCHAN, -1).astype(np.float32).astype(ml_dtypes.bfloat16)


def constants(owners):
    tables = dft_tables(owners)
    lanes = tables.shape[2]
    left = fir_coefficients().astype(np.float32)
    terms = []
    for _ in range(3):
        terms.append(left.astype(ml_dtypes.bfloat16))
        left = left - terms[-1].astype(np.float32)
    terms = np.stack(terms).reshape(-1, lanes)
    pad = np.zeros((-terms.shape[0] % COEF_ROWS, lanes), ml_dtypes.bfloat16)
    return np.concatenate([tables.reshape(-1, lanes), terms, pad])


def transform(filt, table, scale, stage, out_refs, table_copies=()):
    owners = len(out_refs)
    me = lax.axis_index("chan")
    spectra = []
    for r in range(2):
        for copy in table_copies[r : r + 1]:
            copy.wait()
        spectrum = jnp.dot(filt[r], table[r * NCHAN : (r + 1) * NCHAN], preferred_element_type=jnp.float32)
        spectra.append(spectrum * scale)
    width = spectra[0].shape[1] // owners
    for owner in range(owners):
        here = slice(owner * width, (owner + 1) * width)
        piece = jnp.concatenate([spectra[0][:, here], spectra[1][:, here]], axis=1)
        stage[jnp.bitwise_xor(me, owner)] = piece[: stage.shape[1]].astype(jnp.bfloat16)
    for d in range(owners):
        out_refs[d][...] = stage[d]


def filter_kernel(frames, pieces, scale, volt_hbm, table_hbm, *refs):
    out_refs, (filt, later, volt, table, terms, coef, stage, sems) = refs[:-8], refs[-8:]
    per = frames // pieces
    lead = TAPS - 1
    copies = []
    for piece in range(pieces):
        copies.append(
            pltpu.make_async_copy(
                volt_hbm.at[:, :, pl.ds(piece * per * NCHAN, per * NCHAN)],
                volt.at[:, :, pl.ds((lead + piece * per) * NCHAN, per * NCHAN)],
                sems.at[piece],
            )
        )
    table_copies = [
        pltpu.make_async_copy(
            table_hbm.at[pl.ds(r * NCHAN, NCHAN)], table.at[pl.ds(r * NCHAN, NCHAN)], sems.at[pieces + r]
        )
        for r in range(2)
    ]
    coef_copy = pltpu.make_async_copy(
        table_hbm.at[pl.ds(PARTS * 2 * NCHAN, terms.shape[0])], terms, sems.at[pieces + 2]
    )
    coef_copy.start()
    for copy in copies:
        copy.start()
    later_copy = pltpu.make_async_copy(
        table_hbm.at[pl.ds(2 * NCHAN, (PARTS - 1) * 2 * NCHAN)], later, sems.at[pieces + 3]
    )
    for copy in table_copies:
        copy.start()
    later_copy.start()
    tail = volt.shape[2] - (lead + frames) * NCHAN
    volt[:, :, : lead * NCHAN] = jnp.zeros((2, SIG, lead * NCHAN), jnp.int32)
    volt[:, :, (lead + frames) * NCHAN :] = jnp.zeros((2, SIG, tail), jnp.int32)
    coef_copy.wait()
    across = coef.shape[1]
    per_term = TAPS * NCHAN // across
    coef[...] = sum(terms[t * per_term : (t + 1) * per_term, :].astype(jnp.float32) for t in range(3))

    def filter_group(start, count):
        base = start * NCHAN
        rows = slice(start * SIG, (start + count) * SIG)
        for column in range(HALF // LANES):
            for part in range(2):
                halves = []
                for half in range(2):
                    lane = half * HALF + column * LANES
                    at = [k * (NCHAN // across) + lane // across for k in range(TAPS)]
                    taps = [coef[i : i + 1, lane % across : lane % across + LANES] for i in at]
                    near = [
                        volt[part, :, pl.ds(base + f * NCHAN + lane, LANES)].astype(jnp.float32)
                        for f in range(count + TAPS - 1)
                    ]
                    sums = []
                    for m in range(count):
                        total = taps[0] * near[m]
                        for k in range(1, TAPS):
                            total = total + taps[k] * near[m + k]
                        sums.append(total)
                    halves.append(jnp.concatenate(sums, axis=0))
                where = pl.ds(part * HALF + column * LANES, LANES)
                filt[0, rows, where] = (halves[0] + halves[1]).astype(jnp.bfloat16)
                filt[1, rows, where] = (halves[0] - halves[1]).astype(jnp.bfloat16)

    for piece in range(pieces):
        copies[piece].wait()
        filter_group(piece * per, per)
    filter_group(frames, GROUP)
    transform(filt, table, scale, stage, out_refs, table_copies)
    later_copy.wait()


def transform_kernel(part, scale, filt, later, gains_ref, pick_ref, *refs):
    table = later.at[pl.ds((part - 1) * 2 * NCHAN, 2 * NCHAN)]
    if part == 1:
        columns, stage = refs[-2:]
        gains = jnp.concatenate([gains_ref[:, 0, :], gains_ref[:, 1, :]], axis=0)
        columns[...] = lax.dot_general(
            pick_ref[...],
            gains,
            (((1,), (1,)), ((), ())),
            precision=lax.Precision.HIGHEST,
            preferred_element_type=jnp.float32,
        )
        transform(filt, table, scale, stage, refs[:-2])
    else:
        transform(filt, table, scale, refs[-1], refs[:-1])


IN_VMEM = pl.BlockSpec(memory_space=pltpu.VMEM)
IN_HBM = pl.BlockSpec(memory_space=pl.ANY)


def filtered_and_first(voltages, owners, table):
    frames = voltages.shape[2] // NCHAN
    rows = (frames + GROUP) * SIG
    sent = (frames + TAPS - 1) * SIG
    pieces = 4
    across = table.shape[1]
    terms = table.shape[0] - PARTS * 2 * NCHAN
    lanes = 2 * CHANNELS // owners // PARTS
    *first, filt, later = pl.pallas_call(
        functools.partial(filter_kernel, frames, pieces, spectrum_scale()),
        out_shape=[jax.ShapeDtypeStruct((sent, lanes), jnp.bfloat16)] * owners
        + [
            jax.ShapeDtypeStruct((2, rows, NCHAN), jnp.bfloat16),
            jax.ShapeDtypeStruct(((PARTS - 1) * 2 * NCHAN, across), jnp.bfloat16),
        ],
        in_specs=[IN_HBM, IN_HBM],
        out_specs=[IN_VMEM] * (owners + 2),
        scratch_shapes=[
            pltpu.VMEM((2, SIG, (frames + GROUP + TAPS - 1) * NCHAN), jnp.int32),
            pltpu.VMEM((2 * NCHAN, across), jnp.bfloat16),
            pltpu.VMEM((terms, across), jnp.bfloat16),
            pltpu.VMEM((TAPS * NCHAN // across, across), jnp.float32),
            pltpu.VMEM((owners, sent, lanes), jnp.bfloat16),
            pltpu.SemaphoreType.DMA((pieces + 4,)),
        ],
        compiler_params=pltpu.CompilerParams(vmem_limit_bytes=FILTER_VMEM_BYTES),
        cost_estimate=pl.CostEstimate(flops=1 << 29, bytes_accessed=4 << 20, transcendentals=0),
        name="filter_and_transform",
    )(voltages, table)
    return filt, later, first


def pick_rows(channels):
    order = np.arange(channels).reshape(PARTS, BATCH, -1, 2)
    return np.eye(channels, dtype=np.float32)[np.transpose(order, (0, 3, 2, 1)).reshape(-1)]


def next_part(part, filt, later, gains, owners):
    rows = filt.shape[1] - (GROUP - TAPS + 1) * SIG
    lanes = 2 * CHANNELS // owners // PARTS
    channels = gains.shape[2]
    shapes = [jax.ShapeDtypeStruct((rows, lanes), jnp.bfloat16)] * owners
    if part == 1:
        shapes.append(jax.ShapeDtypeStruct((channels, 2 * SIG), jnp.float32))
    return pl.pallas_call(
        functools.partial(transform_kernel, part, spectrum_scale()),
        out_shape=shapes,
        in_specs=[IN_VMEM] * 4,
        out_specs=[IN_VMEM] * len(shapes),
        scratch_shapes=[pltpu.VMEM((owners, rows, lanes), jnp.bfloat16)],
        compiler_params=pltpu.CompilerParams(vmem_limit_bytes=VMEM_BYTES),
        cost_estimate=pl.CostEstimate(flops=1 << 29, bytes_accessed=2 << 20, transcendentals=0),
        name="transform",
    )(filt, later, gains, jnp.asarray(pick_rows(channels)))


def equalize_kernel(owners, frames, h, part, *refs):
    pieces = refs[owners - 1 :: -1]
    gains_ref, by_time, by_channel = refs[owners], refs[-2], refs[-1]
    out_refs = refs[owners + 1 : -2]
    for out_ref in out_refs[1:]:
        out_ref[:, h * SIG :, :] = jnp.zeros((2, EXTRA_ROWS, out_ref.shape[2]), jnp.bfloat16)
    width = 4 * h
    own_rows = frames * SIG
    over = (TAPS - 1) * SIG
    times = owners * frames
    tiles = times // LANES
    me = lax.axis_index("chan")
    for d in range(owners):
        source = jnp.bitwise_xor(me, d)
        start = pl.multiple_of(source * own_rows, own_rows)
        by_time[pl.ds(start, own_rows), :width] = pieces[d][:own_rows, :].astype(jnp.float32)
    for d in range(owners):
        source = jnp.bitwise_xor(me, d)

        @pl.when(source < owners - 1)
        def _():
            start = pl.multiple_of((source + 1) * own_rows, own_rows)
            by_time[pl.ds(start, over), :width] += pieces[d][own_rows:, :].astype(jnp.float32)

    gains = [gains_ref[(2 * part + r) * h : (2 * part + r + 1) * h, :] for r in range(2)]
    for s in range(SIG):
        x = by_time[pl.ds(s, times, stride=SIG), :][:, :width].T
        for r in range(2):
            real, imag = x[2 * r * h : (2 * r + 1) * h], x[(2 * r + 1) * h : (2 * r + 2) * h]
            gain_real, gain_imag = gains[r][:, s : s + 1], gains[r][:, SIG + s : SIG + s + 1]
            both = [real * gain_real - imag * gain_imag, real * gain_imag + imag * gain_real]
            for q in range(2):
                for tile in range(tiles):
                    by_channel[(2 * r + q) * tiles + tile, pl.ds(s, h, stride=SIG), :] = both[q][
                        :, tile * LANES : (tile + 1) * LANES
                    ]
    for r in range(2):
        for tile in range(2 * tiles):
            for out_ref in out_refs:
                ready = by_channel[r * 2 * tiles + tile].astype(jnp.bfloat16)
                out_ref[r, : h * SIG, tile * LANES : (tile + 1) * LANES] = ready


def equalize(pieces, gains, part, frames):
    owners = len(pieces)
    h = gains.shape[0] // PARTS // 2
    times = owners * frames
    lengths = [h * SIG] + ([h * SIG + EXTRA_ROWS] if part == PARTS - 1 else [])
    return pl.pallas_call(
        functools.partial(equalize_kernel, owners, frames, h, part),
        out_shape=[jax.ShapeDtypeStruct((2, rows, 2 * times), jnp.bfloat16) for rows in lengths],
        in_specs=[IN_VMEM] * (owners + 1),
        out_specs=[IN_VMEM] * len(lengths),
        scratch_shapes=[
            pltpu.VMEM((times * SIG, LANES), jnp.float32),
            pltpu.VMEM((4 * times // LANES, h * SIG, LANES), jnp.float32),
        ],
        compiler_params=pltpu.CompilerParams(vmem_limit_bytes=VMEM_BYTES),
        cost_estimate=pl.CostEstimate(flops=0, bytes_accessed=1 << 10, transcendentals=0),
        name="equalize",
    )(*pieces[::-1], gains)


def row_places(col, n_col):
    chips = n_col // 2
    chip, core = lax.div(col, 2), lax.rem(col, 2)
    places = [col] + [lax.rem(chip + chips - d, chips) * 2 + core for d in range(1, chips)]
    return places + [jnp.bitwise_xor(p, 1) for p in places]


def column_places(row, n_row):
    return [row] + [lax.rem(row + n_row - d, n_row) for d in range(1, n_row)]


def regroup(v):
    lane = lax.broadcasted_iota(jnp.int32, v[0].shape, 1)
    v = list(v)
    for bit in (2, 1):
        width = bit * LANES // 8
        low = (lane // width) % 2 == 0
        for i in range(4):
            if i & bit == 0:
                a, b = v[i], v[i + bit]
                v[i] = jnp.where(low, a, pltpu.roll(b, width, axis=1))
                v[i + bit] = jnp.where(low, pltpu.roll(a, LANES - width, axis=1), b)
    return v


def correlate_kernel(n_row, n_col, h, times, part, dense, *refs):
    row_blocks = refs[:n_col]
    col_blocks = (refs[0],) + refs[n_col : n_col + n_row - 1]
    last = part == PARTS - 1
    given = refs[n_col + n_row - 1 :]
    if part > 0:
        earlier, keeps = given[:2]
    if last:
        out_hbm, chosen, out_ref, sems = refs[-4:]
    else:
        out_ref, keeps_out, chosen = refs[-3:]
    me_row, me_col = lax.axis_index("brow"), lax.axis_index("bcol")
    row_at, col_at = row_places(me_col, n_col), column_places(me_row, n_row)
    rows = BATCH * SIG
    tiles = n_col * rows // LANES
    steps = 2 * h // BATCH
    if part == 0:
        owned = given[0][...]
        first, second = (lax.broadcasted_iota(jnp.int32, owned.shape, axis) for axis in range(2))
        for e in range(n_row):
            for d in range(n_col):
                here = (first == me_row * n_col + row_at[d]) & (second == col_at[e] * n_col + me_col)
                found = jnp.max(jnp.where(here, (owned == 1).astype(jnp.float32), 0.0), axis=(0, 1), keepdims=True)
                keeps_out[e, d] = jnp.broadcast_to(found * (1.0 / times), (SIG, LANES))
    elif not last:
        keeps_out[...] = keeps[...]
    index_in_batch = (lax.broadcasted_iota(jnp.int32, (SIG, LANES), 1) // SIG) % BATCH

    for step in range(steps):
        inner, parity = step // 2, step % 2
        here = slice(inner * rows, (inner + 1) * rows)
        a = jnp.concatenate([block[parity, here, :] for block in row_blocks], axis=0)
        b = jnp.concatenate([block[parity, here, :] for block in col_blocks], axis=0)
        turned = jnp.concatenate([-b[:, times:], b[:, :times]], axis=1)
        both = jnp.concatenate([b, turned], axis=0)
        result = lax.dot_general(both, a, (((1,), (1,)), ((), ())), preferred_element_type=jnp.float32)
        for k in range(2 * n_row):
            for tile in range(tiles):
                lanes = slice(tile * LANES, (tile + 1) * LANES)
                own = [result[k * rows + i * SIG : k * rows + (i + 1) * SIG, lanes] for i in range(BATCH)]
                kept = own[0]
                for i in range(1, BATCH):
                    kept = jnp.where(index_in_batch == i, own[i], kept)
                chosen[k * tiles + tile, pl.ds(step, SIG, stride=steps), :] = kept

    copies = []
    low = lax.broadcasted_iota(jnp.int32, (SIG, LANES), 1) < LANES // 2
    for q in range(2):
        for e in range(n_row):
            for d in range(n_col):
                if d % (LANES // rows) == 0:
                    x = chosen[(q * n_row + e) * tiles + d * rows // LANES].T
                start = d * rows % LANES
                v = [x[start + i * SIG : start + (i + 1) * SIG] for i in range(BATCH)]
                if last:
                    keep = keeps[e, d]
                a_at = pl.ds(pl.multiple_of(row_at[d] * SIG, SIG), SIG)
                mine = slice(d * SIG, (d + 1) * SIG)
                if dense:
                    for g, w in enumerate(regroup(v)):
                        if last:
                            before = earlier[q, e, g, mine, :]
                            pair = [
                                jnp.where(low, before, pltpu.roll(w, LANES // 2, axis=1)),
                                jnp.where(low, pltpu.roll(before, LANES // 2, axis=1), w),
                            ]
                            for half in range(2):
                                out_ref[q, col_at[e] * SIG + half * BATCH + g, a_at, :] = pair[half] * keep
                        else:
                            out_ref[q, e, g, mine, :] = w
                else:
                    for s2 in range(SIG):
                        w = jnp.concatenate([each[:, s2 * steps : (s2 + 1) * steps] for each in v], axis=1)
                        if part > 0:
                            w = jnp.concatenate([earlier[q, e, s2, mine, :], w], axis=1)
                        if last:
                            out_ref[q, col_at[e] * SIG + s2, a_at, :] = w * keep[:, : w.shape[1]]
                        else:
                            out_ref[q, e, s2, mine, :] = w
            if last:
                where = pl.ds(col_at[e] * SIG, SIG)
                copy = pltpu.make_async_copy(out_ref.at[q, where], out_hbm.at[q, where], sems.at[q * n_row + e])
                copy.start()
                copies.append(copy)
    for copy in copies:
        copy.wait()


def correlate(blocks, given, part, n_row, n_col):
    h = blocks[0].shape[1] // SIG
    times = blocks[0].shape[2] // 2
    channels = 2 * h
    dense = channels * 2 == LANES and PARTS == 2
    operands = list(blocks) + list(given)
    last = part == PARTS - 1
    if last:
        out_shape = (2, n_row * SIG, n_col * SIG, (part + 1) * channels)
    elif dense:
        out_shape = (2, n_row, SIG // 2, n_col * SIG, LANES)
    else:
        out_shape = (2, n_row, SIG, n_col * SIG, (part + 1) * channels)
    shapes = [out_shape] if last else [out_shape, (n_row, n_col, SIG, LANES)]
    in_last = [pltpu.VMEM(out_shape, jnp.float32), pltpu.SemaphoreType.DMA((2 * n_row,))]
    kept = pltpu.VMEM((2 * n_row * n_col * BATCH * SIG // LANES, SIG * channels // BATCH, LANES), jnp.float32)
    return pl.pallas_call(
        functools.partial(correlate_kernel, n_row, n_col, h, times, part, dense),
        out_shape=[jax.ShapeDtypeStruct(shape, jnp.float32) for shape in shapes],
        in_specs=[IN_VMEM] * len(operands),
        out_specs=[IN_HBM] if last else [IN_VMEM] * len(shapes),
        scratch_shapes=[kept] + (in_last if last else []),
        compiler_params=pltpu.CompilerParams(vmem_limit_bytes=VMEM_BYTES),
        cost_estimate=pl.CostEstimate(flops=0, bytes_accessed=1 << 10, transcendentals=0),
        name="correlate",
    )(*operands)


def to_owners(pieces):
    owners = len(pieces)
    arrived = [pieces[0]] + [None] * (owners - 1)
    for d in range(owners - 1, 0, -1):
        arrived[d] = lax.ppermute(pieces[d], "chan", [(i, i ^ d) for i in range(owners)])
    return arrived


def held_back(blocks, after):
    def kernel(*refs):
        for i in range(len(blocks)):
            refs[len(blocks) + len(after) + i][...] = refs[i][...]

    return pl.pallas_call(
        kernel,
        out_shape=[jax.ShapeDtypeStruct(block.shape, block.dtype) for block in blocks],
        in_specs=[IN_VMEM] * (len(blocks) + len(after)),
        out_specs=[IN_VMEM] * len(blocks),
        compiler_params=pltpu.CompilerParams(vmem_limit_bytes=VMEM_BYTES),
        cost_estimate=pl.CostEstimate(flops=0, bytes_accessed=1 << 10, transcendentals=0),
        name="held_back",
    )(*blocks, *after)


def shards(voltages, antenna_gains, tile_map):
    owners = lax.axis_size("chan")
    n_row = lax.axis_size("brow")
    n_col = lax.axis_size("bcol")
    chips = n_col // 2
    frames = voltages.shape[2] // NCHAN
    across = [[(i, (i // 2 + d) % chips * 2 + i % 2) for i in range(n_col)] for d in range(chips)]
    along = [[(i, (i + d) % n_row) for i in range(n_row)] for d in range(n_row)]
    table = jnp.asarray(constants(owners))
    other_core = [(i, i ^ 1) for i in range(n_col)]

    filt, tables, pieces = filtered_and_first(voltages, owners, table)
    own, panels = [], []
    arrived = to_owners(pieces)
    for part in range(PARTS):
        later = None
        if part < PARTS - 1:
            pieces = next_part(part + 1, filt, tables, antenna_gains, owners)
            if part == 0:
                *pieces, gains = pieces
            later = to_owners([pieces[0], *held_back(pieces[1:], arrived[-1:])])
        block, *longer = equalize(arrived, gains, part, frames)
        own.append(block)
        far = [lax.ppermute(own[part], "bcol", across[d]) for d in range(1, chips)]
        column = [lax.ppermute((longer or own)[-1], "brow", along[d]) for d in range(1, n_row)]
        panels.append((far, column))
        arrived = later
    result = [tile_map]
    for part in range(PARTS):
        far, column = panels[part]
        mine = own[part]
        if part < PARTS - 1:
            mine, *far = held_back([mine] + far, own[-1:])
        beside = lax.ppermute(mine, "bcol", other_core)
        relayed = [lax.ppermute(block, "bcol", other_core) for block in far]
        if part > 0:
            column = list(held_back(column, result[1:]))
        blocks = [own[part]] + far + [beside] + relayed + column
        result = correlate(blocks, result, part, n_row, n_col)
    return jnp.transpose(result[0], (3, 0, 1, 2))[None, None]


def solution(mesh):
    in_specs = (P(None, ("brow", "bcol"), "chan"), P(("brow", "bcol"), None, "chan"), P())
    out_specs = P("brow", "bcol", "chan", None, None, None)
    return jax.shard_map(shards, mesh=mesh, in_specs=in_specs, out_specs=out_specs, check_vma=False)
```

```python
import functools
import math

import jax
import jax.numpy as jnp
import ml_dtypes
import numpy as np
from jax import lax
from jax.experimental import pallas as pl
from jax.experimental.pallas import tpu as pltpu
from jax.sharding import PartitionSpec as P

NCHAN = 1024
HALF = NCHAN // 2
CHANNELS = 512
TAPS = 4
FIRST = 256
SIG = 8
LANES = 128
GROUP = 4
BATCH = 4
PARTS = 2
VMEM_BYTES = 16 * 1024 * 1024
EXTRA_ROWS = 16
FILTER_VMEM_BYTES = 101 * 512 * 1024
COEF_ROWS = 64


def fir_coefficients():
    position = np.arange(TAPS * NCHAN, dtype=np.float64) + 0.5
    offsets = position / NCHAN - TAPS / 2.0
    window = 0.5 - 0.5 * np.cos(2.0 * math.pi * position / (TAPS * NCHAN))
    return (np.sinc(offsets) * window).reshape(TAPS, NCHAN)


def spectrum_scale():
    return float(1.0 / (128.0 * np.sqrt(np.sum(fir_coefficients() ** 2))))


def dft_tables(owners):
    n = np.arange(HALF, dtype=np.int64).reshape(HALF, 1, 1, 1, 1, 1)
    k = FIRST + np.arange(CHANNELS, dtype=np.int64).reshape(owners, PARTS, BATCH, -1, 2)
    angles = (n * k % NCHAN) * (2.0 * math.pi / NCHAN)
    cosine, sine = np.cos(angles), np.sin(angles)
    first = np.stack([cosine, -sine], axis=2)
    second = np.stack([sine, cosine], axis=2)
    tables = np.stack([first, second])
    tables = np.transpose(tables, (4, 7, 0, 1, 2, 3, 6, 5))
    return tables.reshape(PARTS, 2 * NCHAN, -1).astype(np.float32).astype(ml_dtypes.bfloat16)


def constants(owners):
    tables = dft_tables(owners)
    lanes = tables.shape[2]
    left = fir_coefficients().astype(np.float32)
    terms = []
    for _ in range(3):
        terms.append(left.astype(ml_dtypes.bfloat16))
        left = left - terms[-1].astype(np.float32)
    terms = np.stack(terms).reshape(-1, lanes)
    pad = np.zeros((-terms.shape[0] % COEF_ROWS, lanes), ml_dtypes.bfloat16)
    return np.concatenate([tables.reshape(-1, lanes), terms, pad])


def transform(filt, table, scale, stage, out_refs):
    owners = len(out_refs)
    me = lax.axis_index("chan")
    spectra = [
        jnp.dot(filt[r], table[r * NCHAN : (r + 1) * NCHAN], preferred_element_type=jnp.float32) * scale
        for r in range(2)
    ]
    width = spectra[0].shape[1] // owners
    for owner in range(owners):
        here = slice(owner * width, (owner + 1) * width)
        piece = jnp.concatenate([spectra[0][:, here], spectra[1][:, here]], axis=1)
        stage[jnp.bitwise_xor(me, owner)] = piece[: stage.shape[1]].astype(jnp.bfloat16)
    for d in range(owners):
        out_refs[d][...] = stage[d]


def filter_kernel(frames, pieces, scale, volt_hbm, table_hbm, *refs):
    out_refs, (filt, later, volt, table, terms, coef, stage, sems) = refs[:-8], refs[-8:]
    per = frames // pieces
    lead = TAPS - 1
    copies = []
    for piece in range(pieces):
        copies.append(
            pltpu.make_async_copy(
                volt_hbm.at[:, :, pl.ds(piece * per * NCHAN, per * NCHAN)],
                volt.at[:, :, pl.ds((lead + piece * per) * NCHAN, per * NCHAN)],
                sems.at[piece],
            )
        )
    table_copy = pltpu.make_async_copy(table_hbm.at[pl.ds(0, 2 * NCHAN)], table, sems.at[pieces])
    coef_copy = pltpu.make_async_copy(
        table_hbm.at[pl.ds(PARTS * 2 * NCHAN, terms.shape[0])], terms, sems.at[pieces + 1]
    )
    coef_copy.start()
    for copy in copies:
        copy.start()
    later_copy = pltpu.make_async_copy(
        table_hbm.at[pl.ds(2 * NCHAN, (PARTS - 1) * 2 * NCHAN)], later, sems.at[pieces + 2]
    )
    table_copy.start()
    later_copy.start()
    tail = volt.shape[2] - (lead + frames) * NCHAN
    volt[:, :, : lead * NCHAN] = jnp.zeros((2, SIG, lead * NCHAN), jnp.int32)
    volt[:, :, (lead + frames) * NCHAN :] = jnp.zeros((2, SIG, tail), jnp.int32)
    coef_copy.wait()
    across = coef.shape[1]
    per_term = TAPS * NCHAN // across
    coef[...] = sum(terms[t * per_term : (t + 1) * per_term, :].astype(jnp.float32) for t in range(3))

    def filter_group(start, count):
        base = start * NCHAN
        rows = slice(start * SIG, (start + count) * SIG)
        for column in range(HALF // LANES):
            for part in range(2):
                halves = []
                for half in range(2):
                    lane = half * HALF + column * LANES
                    at = [k * (NCHAN // across) + lane // across for k in range(TAPS)]
                    taps = [coef[i : i + 1, lane % across : lane % across + LANES] for i in at]
                    near = [
                        volt[part, :, pl.ds(base + f * NCHAN + lane, LANES)].astype(jnp.float32)
                        for f in range(count + TAPS - 1)
                    ]
                    sums = []
                    for m in range(count):
                        total = taps[0] * near[m]
                        for k in range(1, TAPS):
                            total = total + taps[k] * near[m + k]
                        sums.append(total)
                    halves.append(jnp.concatenate(sums, axis=0))
                where = pl.ds(part * HALF + column * LANES, LANES)
                filt[0, rows, where] = (halves[0] + halves[1]).astype(jnp.bfloat16)
                filt[1, rows, where] = (halves[0] - halves[1]).astype(jnp.bfloat16)

    for piece in range(pieces):
        copies[piece].wait()
        filter_group(piece * per, per)
    filter_group(frames, GROUP)
    table_copy.wait()
    transform(filt, table, scale, stage, out_refs)
    later_copy.wait()


def transform_kernel(part, scale, filt, later, gains_ref, pick_ref, *refs):
    table = later.at[pl.ds((part - 1) * 2 * NCHAN, 2 * NCHAN)]
    if part == 1:
        columns, stage = refs[-2:]
        gains = jnp.concatenate([gains_ref[:, 0, :], gains_ref[:, 1, :]], axis=0)
        columns[...] = lax.dot_general(
            pick_ref[...],
            gains,
            (((1,), (1,)), ((), ())),
            precision=lax.Precision.HIGHEST,
            preferred_element_type=jnp.float32,
        )
        transform(filt, table, scale, stage, refs[:-2])
    else:
        transform(filt, table, scale, refs[-1], refs[:-1])


IN_VMEM = pl.BlockSpec(memory_space=pltpu.VMEM)
IN_HBM = pl.BlockSpec(memory_space=pl.ANY)


def filtered_and_first(voltages, owners, table):
    frames = voltages.shape[2] // NCHAN
    rows = (frames + GROUP) * SIG
    sent = (frames + TAPS - 1) * SIG
    pieces = 2
    across = table.shape[1]
    terms = table.shape[0] - PARTS * 2 * NCHAN
    lanes = 2 * CHANNELS // owners // PARTS
    *first, filt, later = pl.pallas_call(
        functools.partial(filter_kernel, frames, pieces, spectrum_scale()),
        out_shape=[jax.ShapeDtypeStruct((sent, lanes), jnp.bfloat16)] * owners
        + [
            jax.ShapeDtypeStruct((2, rows, NCHAN), jnp.bfloat16),
            jax.ShapeDtypeStruct(((PARTS - 1) * 2 * NCHAN, across), jnp.bfloat16),
        ],
        in_specs=[IN_HBM, IN_HBM],
        out_specs=[IN_VMEM] * (owners + 2),
        scratch_shapes=[
            pltpu.VMEM((2, SIG, (frames + GROUP + TAPS - 1) * NCHAN), jnp.int32),
            pltpu.VMEM((2 * NCHAN, across), jnp.bfloat16),
            pltpu.VMEM((terms, across), jnp.bfloat16),
            pltpu.VMEM((TAPS * NCHAN // across, across), jnp.float32),
            pltpu.VMEM((owners, sent, lanes), jnp.bfloat16),
            pltpu.SemaphoreType.DMA((pieces + 3,)),
        ],
        compiler_params=pltpu.CompilerParams(vmem_limit_bytes=FILTER_VMEM_BYTES),
        cost_estimate=pl.CostEstimate(flops=1 << 29, bytes_accessed=4 << 20, transcendentals=0),
        name="filter_and_transform",
    )(voltages, table)
    return filt, later, first


def pick_rows(channels):
    order = np.arange(channels).reshape(PARTS, BATCH, -1, 2)
    return np.eye(channels, dtype=np.float32)[np.transpose(order, (0, 3, 2, 1)).reshape(-1)]


def next_part(part, filt, later, gains, owners):
    rows = filt.shape[1] - (GROUP - TAPS + 1) * SIG
    lanes = 2 * CHANNELS // owners // PARTS
    channels = gains.shape[2]
    shapes = [jax.ShapeDtypeStruct((rows, lanes), jnp.bfloat16)] * owners
    if part == 1:
        shapes.append(jax.ShapeDtypeStruct((channels, 2 * SIG), jnp.float32))
    return pl.pallas_call(
        functools.partial(transform_kernel, part, spectrum_scale()),
        out_shape=shapes,
        in_specs=[IN_VMEM] * 4,
        out_specs=[IN_VMEM] * len(shapes),
        scratch_shapes=[pltpu.VMEM((owners, rows, lanes), jnp.bfloat16)],
        compiler_params=pltpu.CompilerParams(vmem_limit_bytes=VMEM_BYTES),
        cost_estimate=pl.CostEstimate(flops=1 << 29, bytes_accessed=2 << 20, transcendentals=0),
        name="transform",
    )(filt, later, gains, jnp.asarray(pick_rows(channels)))


def equalize_kernel(owners, frames, h, part, *refs):
    pieces = refs[owners - 1 :: -1]
    gains_ref, by_time, by_channel = refs[owners], refs[-2], refs[-1]
    out_refs = refs[owners + 1 : -2]
    for out_ref in out_refs[1:]:
        out_ref[:, h * SIG :, :] = jnp.zeros((2, EXTRA_ROWS, out_ref.shape[2]), jnp.bfloat16)
    width = 4 * h
    own_rows = frames * SIG
    over = (TAPS - 1) * SIG
    times = owners * frames
    tiles = times // LANES
    me = lax.axis_index("chan")
    for d in range(owners):
        source = jnp.bitwise_xor(me, d)
        start = pl.multiple_of(source * own_rows, own_rows)
        by_time[pl.ds(start, own_rows), :width] = pieces[d][:own_rows, :].astype(jnp.float32)
    for d in range(owners):
        source = jnp.bitwise_xor(me, d)

        @pl.when(source < owners - 1)
        def _():
            start = pl.multiple_of((source + 1) * own_rows, own_rows)
            by_time[pl.ds(start, over), :width] += pieces[d][own_rows:, :].astype(jnp.float32)

    gains = [gains_ref[(2 * part + r) * h : (2 * part + r + 1) * h, :] for r in range(2)]
    for s in range(SIG):
        x = by_time[pl.ds(s, times, stride=SIG), :][:, :width].T
        for r in range(2):
            real, imag = x[2 * r * h : (2 * r + 1) * h], x[(2 * r + 1) * h : (2 * r + 2) * h]
            gain_real, gain_imag = gains[r][:, s : s + 1], gains[r][:, SIG + s : SIG + s + 1]
            both = [real * gain_real - imag * gain_imag, real * gain_imag + imag * gain_real]
            for q in range(2):
                for tile in range(tiles):
                    by_channel[(2 * r + q) * tiles + tile, pl.ds(s, h, stride=SIG), :] = both[q][
                        :, tile * LANES : (tile + 1) * LANES
                    ]
    for r in range(2):
        for tile in range(2 * tiles):
            for out_ref in out_refs:
                ready = by_channel[r * 2 * tiles + tile].astype(jnp.bfloat16)
                out_ref[r, : h * SIG, tile * LANES : (tile + 1) * LANES] = ready


def equalize(pieces, gains, part, frames):
    owners = len(pieces)
    h = gains.shape[0] // PARTS // 2
    times = owners * frames
    lengths = [h * SIG] + ([h * SIG + EXTRA_ROWS] if part == PARTS - 1 else [])
    return pl.pallas_call(
        functools.partial(equalize_kernel, owners, frames, h, part),
        out_shape=[jax.ShapeDtypeStruct((2, rows, 2 * times), jnp.bfloat16) for rows in lengths],
        in_specs=[IN_VMEM] * (owners + 1),
        out_specs=[IN_VMEM] * len(lengths),
        scratch_shapes=[
            pltpu.VMEM((times * SIG, LANES), jnp.float32),
            pltpu.VMEM((4 * times // LANES, h * SIG, LANES), jnp.float32),
        ],
        compiler_params=pltpu.CompilerParams(vmem_limit_bytes=VMEM_BYTES),
        cost_estimate=pl.CostEstimate(flops=0, bytes_accessed=1 << 10, transcendentals=0),
        name="equalize",
    )(*pieces[::-1], gains)


def row_places(col, n_col):
    chips = n_col // 2
    chip, core = lax.div(col, 2), lax.rem(col, 2)
    places = [col] + [lax.rem(chip + chips - d, chips) * 2 + core for d in range(1, chips)]
    return places + [jnp.bitwise_xor(p, 1) for p in places]


def column_places(row, n_row):
    return [row] + [lax.rem(row + n_row - d, n_row) for d in range(1, n_row)]


def regroup(v):
    lane = lax.broadcasted_iota(jnp.int32, v[0].shape, 1)
    v = list(v)
    for bit in (2, 1):
        width = bit * LANES // 8
        low = (lane // width) % 2 == 0
        for i in range(4):
            if i & bit == 0:
                a, b = v[i], v[i + bit]
                v[i] = jnp.where(low, a, pltpu.roll(b, width, axis=1))
                v[i + bit] = jnp.where(low, pltpu.roll(a, LANES - width, axis=1), b)
    return v


def correlate_kernel(n_row, n_col, h, times, part, dense, *refs):
    row_blocks = refs[:n_col]
    col_blocks = (refs[0],) + refs[n_col : n_col + n_row - 1]
    last = part == PARTS - 1
    given = refs[n_col + n_row - 1 :]
    if part > 0:
        earlier, keeps = given[:2]
    if last:
        out_hbm, chosen, out_ref, sems = refs[-4:]
    else:
        out_ref, keeps_out, chosen = refs[-3:]
    me_row, me_col = lax.axis_index("brow"), lax.axis_index("bcol")
    row_at, col_at = row_places(me_col, n_col), column_places(me_row, n_row)
    rows = BATCH * SIG
    tiles = n_col * rows // LANES
    steps = 2 * h // BATCH
    if part == 0:
        owned = given[0][...]
        first, second = (lax.broadcasted_iota(jnp.int32, owned.shape, axis) for axis in range(2))
        for e in range(n_row):
            for d in range(n_col):
                here = (first == me_row * n_col + row_at[d]) & (second == col_at[e] * n_col + me_col)
                found = jnp.max(jnp.where(here, (owned == 1).astype(jnp.float32), 0.0), axis=(0, 1), keepdims=True)
                keeps_out[e, d] = jnp.broadcast_to(found * (1.0 / times), (SIG, LANES))
    elif not last:
        keeps_out[...] = keeps[...]
    index_in_batch = (lax.broadcasted_iota(jnp.int32, (SIG, LANES), 1) // SIG) % BATCH

    for step in range(steps):
        inner, parity = step // 2, step % 2
        here = slice(inner * rows, (inner + 1) * rows)
        a = jnp.concatenate([block[parity, here, :] for block in row_blocks], axis=0)
        b = jnp.concatenate([block[parity, here, :] for block in col_blocks], axis=0)
        turned = jnp.concatenate([-b[:, times:], b[:, :times]], axis=1)
        both = jnp.concatenate([b, turned], axis=0)
        result = lax.dot_general(both, a, (((1,), (1,)), ((), ())), preferred_element_type=jnp.float32)
        for k in range(2 * n_row):
            for tile in range(tiles):
                lanes = slice(tile * LANES, (tile + 1) * LANES)
                own = [result[k * rows + i * SIG : k * rows + (i + 1) * SIG, lanes] for i in range(BATCH)]
                kept = own[0]
                for i in range(1, BATCH):
                    kept = jnp.where(index_in_batch == i, own[i], kept)
                chosen[k * tiles + tile, pl.ds(step, SIG, stride=steps), :] = kept

    copies = []
    low = lax.broadcasted_iota(jnp.int32, (SIG, LANES), 1) < LANES // 2
    for q in range(2):
        for e in range(n_row):
            for d in range(n_col):
                if d % (LANES // rows) == 0:
                    x = chosen[(q * n_row + e) * tiles + d * rows // LANES].T
                start = d * rows % LANES
                v = [x[start + i * SIG : start + (i + 1) * SIG] for i in range(BATCH)]
                if last:
                    keep = keeps[e, d]
                a_at = pl.ds(pl.multiple_of(row_at[d] * SIG, SIG), SIG)
                mine = slice(d * SIG, (d + 1) * SIG)
                if dense:
                    for g, w in enumerate(regroup(v)):
                        if last:
                            before = earlier[q, e, g, mine, :]
                            pair = [
                                jnp.where(low, before, pltpu.roll(w, LANES // 2, axis=1)),
                                jnp.where(low, pltpu.roll(before, LANES // 2, axis=1), w),
                            ]
                            for half in range(2):
                                out_ref[q, col_at[e] * SIG + half * BATCH + g, a_at, :] = pair[half] * keep
                        else:
                            out_ref[q, e, g, mine, :] = w
                else:
                    for s2 in range(SIG):
                        w = jnp.concatenate([each[:, s2 * steps : (s2 + 1) * steps] for each in v], axis=1)
                        if part > 0:
                            w = jnp.concatenate([earlier[q, e, s2, mine, :], w], axis=1)
                        if last:
                            out_ref[q, col_at[e] * SIG + s2, a_at, :] = w * keep[:, : w.shape[1]]
                        else:
                            out_ref[q, e, s2, mine, :] = w
            if last:
                where = pl.ds(col_at[e] * SIG, SIG)
                copy = pltpu.make_async_copy(out_ref.at[q, where], out_hbm.at[q, where], sems.at[q * n_row + e])
                copy.start()
                copies.append(copy)
    for copy in copies:
        copy.wait()


def correlate(blocks, given, part, n_row, n_col):
    h = blocks[0].shape[1] // SIG
    times = blocks[0].shape[2] // 2
    channels = 2 * h
    dense = channels * 2 == LANES and PARTS == 2
    operands = list(blocks) + list(given)
    last = part == PARTS - 1
    if last:
        out_shape = (2, n_row * SIG, n_col * SIG, (part + 1) * channels)
    elif dense:
        out_shape = (2, n_row, SIG // 2, n_col * SIG, LANES)
    else:
        out_shape = (2, n_row, SIG, n_col * SIG, (part + 1) * channels)
    shapes = [out_shape] if last else [out_shape, (n_row, n_col, SIG, LANES)]
    in_last = [pltpu.VMEM(out_shape, jnp.float32), pltpu.SemaphoreType.DMA((2 * n_row,))]
    kept = pltpu.VMEM((2 * n_row * n_col * BATCH * SIG // LANES, SIG * channels // BATCH, LANES), jnp.float32)
    return pl.pallas_call(
        functools.partial(correlate_kernel, n_row, n_col, h, times, part, dense),
        out_shape=[jax.ShapeDtypeStruct(shape, jnp.float32) for shape in shapes],
        in_specs=[IN_VMEM] * len(operands),
        out_specs=[IN_HBM] if last else [IN_VMEM] * len(shapes),
        scratch_shapes=[kept] + (in_last if last else []),
        compiler_params=pltpu.CompilerParams(vmem_limit_bytes=VMEM_BYTES),
        cost_estimate=pl.CostEstimate(flops=0, bytes_accessed=1 << 10, transcendentals=0),
        name="correlate",
    )(*operands)


def to_owners(pieces):
    owners = len(pieces)
    arrived = [pieces[0]] + [None] * (owners - 1)
    for d in range(owners - 1, 0, -1):
        arrived[d] = lax.ppermute(pieces[d], "chan", [(i, i ^ d) for i in range(owners)])
    return arrived


def held_back(blocks, after):
    def kernel(*refs):
        for i in range(len(blocks)):
            refs[len(blocks) + len(after) + i][...] = refs[i][...]

    return pl.pallas_call(
        kernel,
        out_shape=[jax.ShapeDtypeStruct(block.shape, block.dtype) for block in blocks],
        in_specs=[IN_VMEM] * (len(blocks) + len(after)),
        out_specs=[IN_VMEM] * len(blocks),
        compiler_params=pltpu.CompilerParams(vmem_limit_bytes=VMEM_BYTES),
        cost_estimate=pl.CostEstimate(flops=0, bytes_accessed=1 << 10, transcendentals=0),
        name="held_back",
    )(*blocks, *after)


def shards(voltages, antenna_gains, tile_map):
    owners = lax.axis_size("chan")
    n_row = lax.axis_size("brow")
    n_col = lax.axis_size("bcol")
    chips = n_col // 2
    frames = voltages.shape[2] // NCHAN
    across = [[(i, (i // 2 + d) % chips * 2 + i % 2) for i in range(n_col)] for d in range(chips)]
    along = [[(i, (i + d) % n_row) for i in range(n_row)] for d in range(n_row)]
    table = jnp.asarray(constants(owners))
    other_core = [(i, i ^ 1) for i in range(n_col)]

    filt, tables, pieces = filtered_and_first(voltages, owners, table)
    own, panels = [], []
    arrived = to_owners(pieces)
    for part in range(PARTS):
        later = None
        if part < PARTS - 1:
            pieces = next_part(part + 1, filt, tables, antenna_gains, owners)
            if part == 0:
                *pieces, gains = pieces
            later = to_owners([pieces[0], *held_back(pieces[1:], arrived[-1:])])
        block, *longer = equalize(arrived, gains, part, frames)
        own.append(block)
        far = [lax.ppermute(own[part], "bcol", across[d]) for d in range(1, chips)]
        column = [lax.ppermute((longer or own)[-1], "brow", along[d]) for d in range(1, n_row)]
        panels.append((far, column))
        arrived = later
    result = [tile_map]
    for part in range(PARTS):
        far, column = panels[part]
        mine = own[part]
        if part < PARTS - 1:
            mine, *far = held_back([mine] + far, own[-1:])
        beside = lax.ppermute(mine, "bcol", other_core)
        relayed = [lax.ppermute(block, "bcol", other_core) for block in far]
        if part > 0:
            column = list(held_back(column, result[1:]))
        blocks = [own[part]] + far + [beside] + relayed + column
        result = correlate(blocks, result, part, n_row, n_col)
    return jnp.transpose(result[0], (3, 0, 1, 2))[None, None]


def solution(mesh):
    in_specs = (P(None, ("brow", "bcol"), "chan"), P(("brow", "bcol"), None, "chan"), P())
    out_specs = P("brow", "bcol", "chan", None, None, None)
    return jax.shard_map(shards, mesh=mesh, in_specs=in_specs, out_specs=out_specs, check_vma=False)
```

```python
import functools
import math

import jax
import jax.numpy as jnp
import ml_dtypes
import numpy as np
from jax import lax
from jax.experimental import pallas as pl
from jax.experimental.pallas import tpu as pltpu
from jax.sharding import PartitionSpec as P

NCHAN = 1024
HALF = NCHAN // 2
CHANNELS = 512
TAPS = 4
FIRST = 256
SIG = 8
LANES = 128
GROUP = 4
BATCH = 4
PARTS = 2
VMEM_BYTES = 16 * 1024 * 1024
EXTRA_ROWS = 16
FILTER_VMEM_BYTES = 101 * 512 * 1024
COEF_ROWS = 64


def fir_coefficients():
    position = np.arange(TAPS * NCHAN, dtype=np.float64) + 0.5
    offsets = position / NCHAN - TAPS / 2.0
    window = 0.5 - 0.5 * np.cos(2.0 * math.pi * position / (TAPS * NCHAN))
    return (np.sinc(offsets) * window).reshape(TAPS, NCHAN)


def spectrum_scale():
    return float(1.0 / (128.0 * np.sqrt(np.sum(fir_coefficients() ** 2))))


def dft_tables(owners):
    n = np.arange(HALF, dtype=np.int64).reshape(HALF, 1, 1, 1, 1, 1)
    k = FIRST + np.arange(CHANNELS, dtype=np.int64).reshape(owners, PARTS, BATCH, -1, 2)
    angles = (n * k % NCHAN) * (2.0 * math.pi / NCHAN)
    cosine, sine = np.cos(angles), np.sin(angles)
    first = np.stack([cosine, -sine], axis=2)
    second = np.stack([sine, cosine], axis=2)
    tables = np.stack([first, second])
    tables = np.transpose(tables, (4, 7, 0, 1, 2, 3, 6, 5))
    return tables.reshape(PARTS, 2 * NCHAN, -1).astype(np.float32).astype(ml_dtypes.bfloat16)


def constants(owners):
    tables = dft_tables(owners)
    lanes = tables.shape[2]
    left = fir_coefficients().astype(np.float32)
    terms = []
    for _ in range(3):
        terms.append(left.astype(ml_dtypes.bfloat16))
        left = left - terms[-1].astype(np.float32)
    terms = np.stack(terms).reshape(-1, lanes)
    pad = np.zeros((-terms.shape[0] % COEF_ROWS, lanes), ml_dtypes.bfloat16)
    return np.concatenate([tables.reshape(-1, lanes), terms, pad])


def transform(filt, table, scale, stage, out_refs):
    owners = len(out_refs)
    me = lax.axis_index("chan")
    spectra = [
        jnp.dot(filt[r], table[r * NCHAN : (r + 1) * NCHAN], preferred_element_type=jnp.float32) * scale
        for r in range(2)
    ]
    width = spectra[0].shape[1] // owners
    for owner in range(owners):
        here = slice(owner * width, (owner + 1) * width)
        piece = jnp.concatenate([spectra[0][:, here], spectra[1][:, here]], axis=1)
        stage[jnp.bitwise_xor(me, owner)] = piece[: stage.shape[1]].astype(jnp.bfloat16)
    for d in range(owners):
        out_refs[d][...] = stage[d]


def filter_kernel(frames, pieces, scale, volt_hbm, table_hbm, *refs):
    out_refs, (filt, later, volt, table, terms, coef, stage, sems) = refs[:-8], refs[-8:]
    per = frames // pieces
    lead = TAPS - 1
    copies = []
    for piece in range(pieces):
        copies.append(
            pltpu.make_async_copy(
                volt_hbm.at[:, :, pl.ds(piece * per * NCHAN, per * NCHAN)],
                volt.at[:, :, pl.ds((lead + piece * per) * NCHAN, per * NCHAN)],
                sems.at[piece],
            )
        )
    table_copy = pltpu.make_async_copy(table_hbm.at[pl.ds(0, 2 * NCHAN)], table, sems.at[pieces])
    coef_copy = pltpu.make_async_copy(
        table_hbm.at[pl.ds(PARTS * 2 * NCHAN, terms.shape[0])], terms, sems.at[pieces + 1]
    )
    coef_copy.start()
    for copy in copies:
        copy.start()
    later_copy = pltpu.make_async_copy(
        table_hbm.at[pl.ds(2 * NCHAN, (PARTS - 1) * 2 * NCHAN)], later, sems.at[pieces + 2]
    )
    table_copy.start()
    later_copy.start()
    tail = volt.shape[2] - (lead + frames) * NCHAN
    volt[:, :, : lead * NCHAN] = jnp.zeros((2, SIG, lead * NCHAN), jnp.int32)
    volt[:, :, (lead + frames) * NCHAN :] = jnp.zeros((2, SIG, tail), jnp.int32)
    coef_copy.wait()
    across = coef.shape[1]
    per_term = TAPS * NCHAN // across
    coef[...] = sum(terms[t * per_term : (t + 1) * per_term, :].astype(jnp.float32) for t in range(3))

    def filter_group(start, count):
        base = start * NCHAN
        rows = slice(start * SIG, (start + count) * SIG)
        for column in range(HALF // LANES):
            for part in range(2):
                halves = []
                for half in range(2):
                    lane = half * HALF + column * LANES
                    at = [k * (NCHAN // across) + lane // across for k in range(TAPS)]
                    taps = [coef[i : i + 1, lane % across : lane % across + LANES] for i in at]
                    near = [
                        volt[part, :, pl.ds(base + f * NCHAN + lane, LANES)].astype(jnp.float32)
                        for f in range(count + TAPS - 1)
                    ]
                    sums = []
                    for m in range(count):
                        total = taps[0] * near[m]
                        for k in range(1, TAPS):
                            total = total + taps[k] * near[m + k]
                        sums.append(total)
                    halves.append(jnp.concatenate(sums, axis=0))
                where = pl.ds(part * HALF + column * LANES, LANES)
                filt[0, rows, where] = (halves[0] + halves[1]).astype(jnp.bfloat16)
                filt[1, rows, where] = (halves[0] - halves[1]).astype(jnp.bfloat16)

    for piece in range(pieces):
        copies[piece].wait()
        filter_group(piece * per, per)
    filter_group(frames, GROUP)
    table_copy.wait()
    transform(filt, table, scale, stage, out_refs)
    later_copy.wait()


def transform_kernel(part, scale, filt, later, gains_ref, pick_ref, *refs):
    table = later.at[pl.ds((part - 1) * 2 * NCHAN, 2 * NCHAN)]
    if part == 1:
        columns, stage = refs[-2:]
        gains = jnp.concatenate([gains_ref[:, 0, :], gains_ref[:, 1, :]], axis=0)
        columns[...] = lax.dot_general(
            pick_ref[...],
            gains,
            (((1,), (1,)), ((), ())),
            precision=lax.Precision.HIGHEST,
            preferred_element_type=jnp.float32,
        )
        transform(filt, table, scale, stage, refs[:-2])
    else:
        transform(filt, table, scale, refs[-1], refs[:-1])


IN_VMEM = pl.BlockSpec(memory_space=pltpu.VMEM)
IN_HBM = pl.BlockSpec(memory_space=pl.ANY)


def filtered_and_first(voltages, owners, table):
    frames = voltages.shape[2] // NCHAN
    rows = (frames + GROUP) * SIG
    sent = (frames + TAPS - 1) * SIG
    pieces = 4
    across = table.shape[1]
    terms = table.shape[0] - PARTS * 2 * NCHAN
    lanes = 2 * CHANNELS // owners // PARTS
    *first, filt, later = pl.pallas_call(
        functools.partial(filter_kernel, frames, pieces, spectrum_scale()),
        out_shape=[jax.ShapeDtypeStruct((sent, lanes), jnp.bfloat16)] * owners
        + [
            jax.ShapeDtypeStruct((2, rows, NCHAN), jnp.bfloat16),
            jax.ShapeDtypeStruct(((PARTS - 1) * 2 * NCHAN, across), jnp.bfloat16),
        ],
        in_specs=[IN_HBM, IN_HBM],
        out_specs=[IN_VMEM] * (owners + 2),
        scratch_shapes=[
            pltpu.VMEM((2, SIG, (frames + GROUP + TAPS - 1) * NCHAN), jnp.int32),
            pltpu.VMEM((2 * NCHAN, across), jnp.bfloat16),
            pltpu.VMEM((terms, across), jnp.bfloat16),
            pltpu.VMEM((TAPS * NCHAN // across, across), jnp.float32),
            pltpu.VMEM((owners, sent, lanes), jnp.bfloat16),
            pltpu.SemaphoreType.DMA((pieces + 3,)),
        ],
        compiler_params=pltpu.CompilerParams(vmem_limit_bytes=FILTER_VMEM_BYTES),
        cost_estimate=pl.CostEstimate(flops=1 << 29, bytes_accessed=4 << 20, transcendentals=0),
        name="filter_and_transform",
    )(voltages, table)
    return filt, later, first


def pick_rows(channels):
    order = np.arange(channels).reshape(PARTS, BATCH, -1, 2)
    return np.eye(channels, dtype=np.float32)[np.transpose(order, (0, 3, 2, 1)).reshape(-1)]


def next_part(part, filt, later, gains, owners):
    rows = filt.shape[1] - (GROUP - TAPS + 1) * SIG
    lanes = 2 * CHANNELS // owners // PARTS
    channels = gains.shape[2]
    shapes = [jax.ShapeDtypeStruct((rows, lanes), jnp.bfloat16)] * owners
    if part == 1:
        shapes.append(jax.ShapeDtypeStruct((channels, 2 * SIG), jnp.float32))
    return pl.pallas_call(
        functools.partial(transform_kernel, part, spectrum_scale()),
        out_shape=shapes,
        in_specs=[IN_VMEM] * 4,
        out_specs=[IN_VMEM] * len(shapes),
        scratch_shapes=[pltpu.VMEM((owners, rows, lanes), jnp.bfloat16)],
        compiler_params=pltpu.CompilerParams(vmem_limit_bytes=VMEM_BYTES),
        cost_estimate=pl.CostEstimate(flops=1 << 29, bytes_accessed=2 << 20, transcendentals=0),
        name="transform",
    )(filt, later, gains, jnp.asarray(pick_rows(channels)))


def equalize_kernel(owners, frames, h, part, *refs):
    pieces = refs[owners - 1 :: -1]
    gains_ref, by_time, by_channel = refs[owners], refs[-2], refs[-1]
    out_refs = refs[owners + 1 : -2]
    for out_ref in out_refs[1:]:
        out_ref[:, h * SIG :, :] = jnp.zeros((2, EXTRA_ROWS, out_ref.shape[2]), jnp.bfloat16)
    width = 4 * h
    own_rows = frames * SIG
    over = (TAPS - 1) * SIG
    times = owners * frames
    tiles = times // LANES
    me = lax.axis_index("chan")
    for d in range(owners):
        source = jnp.bitwise_xor(me, d)
        start = pl.multiple_of(source * own_rows, own_rows)
        by_time[pl.ds(start, own_rows), :width] = pieces[d][:own_rows, :].astype(jnp.float32)
    for d in range(owners):
        source = jnp.bitwise_xor(me, d)

        @pl.when(source < owners - 1)
        def _():
            start = pl.multiple_of((source + 1) * own_rows, own_rows)
            by_time[pl.ds(start, over), :width] += pieces[d][own_rows:, :].astype(jnp.float32)

    gains = [gains_ref[(2 * part + r) * h : (2 * part + r + 1) * h, :] for r in range(2)]
    for s in range(SIG):
        x = by_time[pl.ds(s, times, stride=SIG), :][:, :width].T
        for r in range(2):
            real, imag = x[2 * r * h : (2 * r + 1) * h], x[(2 * r + 1) * h : (2 * r + 2) * h]
            gain_real, gain_imag = gains[r][:, s : s + 1], gains[r][:, SIG + s : SIG + s + 1]
            both = [real * gain_real - imag * gain_imag, real * gain_imag + imag * gain_real]
            for q in range(2):
                for tile in range(tiles):
                    by_channel[(2 * r + q) * tiles + tile, pl.ds(s, h, stride=SIG), :] = both[q][
                        :, tile * LANES : (tile + 1) * LANES
                    ]
    for r in range(2):
        for tile in range(2 * tiles):
            for out_ref in out_refs:
                ready = by_channel[r * 2 * tiles + tile].astype(jnp.bfloat16)
                out_ref[r, : h * SIG, tile * LANES : (tile + 1) * LANES] = ready


def equalize(pieces, gains, part, frames):
    owners = len(pieces)
    h = gains.shape[0] // PARTS // 2
    times = owners * frames
    lengths = [h * SIG] + ([h * SIG + EXTRA_ROWS] if part == PARTS - 1 else [])
    return pl.pallas_call(
        functools.partial(equalize_kernel, owners, frames, h, part),
        out_shape=[jax.ShapeDtypeStruct((2, rows, 2 * times), jnp.bfloat16) for rows in lengths],
        in_specs=[IN_VMEM] * (owners + 1),
        out_specs=[IN_VMEM] * len(lengths),
        scratch_shapes=[
            pltpu.VMEM((times * SIG, LANES), jnp.float32),
            pltpu.VMEM((4 * times // LANES, h * SIG, LANES), jnp.float32),
        ],
        compiler_params=pltpu.CompilerParams(vmem_limit_bytes=VMEM_BYTES),
        cost_estimate=pl.CostEstimate(flops=0, bytes_accessed=1 << 10, transcendentals=0),
        name="equalize",
    )(*pieces[::-1], gains)


def row_places(col, n_col):
    chips = n_col // 2
    chip, core = lax.div(col, 2), lax.rem(col, 2)
    places = [col] + [lax.rem(chip + chips - d, chips) * 2 + core for d in range(1, chips)]
    return places + [jnp.bitwise_xor(p, 1) for p in places]


def column_places(row, n_row):
    return [row] + [lax.rem(row + n_row - d, n_row) for d in range(1, n_row)]


def regroup(v):
    lane = lax.broadcasted_iota(jnp.int32, v[0].shape, 1)
    v = list(v)
    for bit in (2, 1):
        width = bit * LANES // 8
        low = (lane // width) % 2 == 0
        for i in range(4):
            if i & bit == 0:
                a, b = v[i], v[i + bit]
                v[i] = jnp.where(low, a, pltpu.roll(b, width, axis=1))
                v[i + bit] = jnp.where(low, pltpu.roll(a, LANES - width, axis=1), b)
    return v


def correlate_kernel(n_row, n_col, h, times, part, dense, *refs):
    row_blocks = refs[:n_col]
    col_blocks = (refs[0],) + refs[n_col : n_col + n_row - 1]
    last = part == PARTS - 1
    given = refs[n_col + n_row - 1 :]
    if part > 0:
        earlier, keeps = given[:2]
    if last:
        out_hbm, chosen, out_ref, sems = refs[-4:]
    else:
        out_ref, keeps_out, chosen = refs[-3:]
    me_row, me_col = lax.axis_index("brow"), lax.axis_index("bcol")
    row_at, col_at = row_places(me_col, n_col), column_places(me_row, n_row)
    rows = BATCH * SIG
    tiles = n_col * rows // LANES
    steps = 2 * h // BATCH
    if part == 0:
        owned = given[0][...]
        first, second = (lax.broadcasted_iota(jnp.int32, owned.shape, axis) for axis in range(2))
        for e in range(n_row):
            for d in range(n_col):
                here = (first == me_row * n_col + row_at[d]) & (second == col_at[e] * n_col + me_col)
                found = jnp.max(jnp.where(here, (owned == 1).astype(jnp.float32), 0.0), axis=(0, 1), keepdims=True)
                keeps_out[e, d] = jnp.broadcast_to(found * (1.0 / times), (SIG, LANES))
    elif not last:
        keeps_out[...] = keeps[...]
    index_in_batch = (lax.broadcasted_iota(jnp.int32, (SIG, LANES), 1) // SIG) % BATCH

    for step in range(steps):
        inner, parity = step // 2, step % 2
        here = slice(inner * rows, (inner + 1) * rows)
        a = jnp.concatenate([block[parity, here, :] for block in row_blocks], axis=0)
        b = jnp.concatenate([block[parity, here, :] for block in col_blocks], axis=0)
        turned = jnp.concatenate([-b[:, times:], b[:, :times]], axis=1)
        both = jnp.concatenate([b, turned], axis=0)
        result = lax.dot_general(both, a, (((1,), (1,)), ((), ())), preferred_element_type=jnp.float32)
        for k in range(2 * n_row):
            for tile in range(tiles):
                lanes = slice(tile * LANES, (tile + 1) * LANES)
                own = [result[k * rows + i * SIG : k * rows + (i + 1) * SIG, lanes] for i in range(BATCH)]
                kept = own[0]
                for i in range(1, BATCH):
                    kept = jnp.where(index_in_batch == i, own[i], kept)
                chosen[k * tiles + tile, pl.ds(step, SIG, stride=steps), :] = kept

    copies = []
    low = lax.broadcasted_iota(jnp.int32, (SIG, LANES), 1) < LANES // 2
    for q in range(2):
        for e in range(n_row):
            for d in range(n_col):
                if d % (LANES // rows) == 0:
                    x = chosen[(q * n_row + e) * tiles + d * rows // LANES].T
                start = d * rows % LANES
                v = [x[start + i * SIG : start + (i + 1) * SIG] for i in range(BATCH)]
                if last:
                    keep = keeps[e, d]
                a_at = pl.ds(pl.multiple_of(row_at[d] * SIG, SIG), SIG)
                mine = slice(d * SIG, (d + 1) * SIG)
                if dense:
                    for g, w in enumerate(regroup(v)):
                        if last:
                            before = earlier[q, e, g, mine, :]
                            pair = [
                                jnp.where(low, before, pltpu.roll(w, LANES // 2, axis=1)),
                                jnp.where(low, pltpu.roll(before, LANES // 2, axis=1), w),
                            ]
                            for half in range(2):
                                out_ref[q, col_at[e] * SIG + half * BATCH + g, a_at, :] = pair[half] * keep
                        else:
                            out_ref[q, e, g, mine, :] = w
                else:
                    for s2 in range(SIG):
                        w = jnp.concatenate([each[:, s2 * steps : (s2 + 1) * steps] for each in v], axis=1)
                        if part > 0:
                            w = jnp.concatenate([earlier[q, e, s2, mine, :], w], axis=1)
                        if last:
                            out_ref[q, col_at[e] * SIG + s2, a_at, :] = w * keep[:, : w.shape[1]]
                        else:
                            out_ref[q, e, s2, mine, :] = w
            if last:
                where = pl.ds(col_at[e] * SIG, SIG)
                copy = pltpu.make_async_copy(out_ref.at[q, where], out_hbm.at[q, where], sems.at[q * n_row + e])
                copy.start()
                copies.append(copy)
    for copy in copies:
        copy.wait()


def correlate(blocks, given, part, n_row, n_col):
    h = blocks[0].shape[1] // SIG
    times = blocks[0].shape[2] // 2
    channels = 2 * h
    dense = channels * 2 == LANES and PARTS == 2
    operands = list(blocks) + list(given)
    last = part == PARTS - 1
    if last:
        out_shape = (2, n_row * SIG, n_col * SIG, (part + 1) * channels)
    elif dense:
        out_shape = (2, n_row, SIG // 2, n_col * SIG, LANES)
    else:
        out_shape = (2, n_row, SIG, n_col * SIG, (part + 1) * channels)
    shapes = [out_shape] if last else [out_shape, (n_row, n_col, SIG, LANES)]
    in_last = [pltpu.VMEM(out_shape, jnp.float32), pltpu.SemaphoreType.DMA((2 * n_row,))]
    kept = pltpu.VMEM((2 * n_row * n_col * BATCH * SIG // LANES, SIG * channels // BATCH, LANES), jnp.float32)
    return pl.pallas_call(
        functools.partial(correlate_kernel, n_row, n_col, h, times, part, dense),
        out_shape=[jax.ShapeDtypeStruct(shape, jnp.float32) for shape in shapes],
        in_specs=[IN_VMEM] * len(operands),
        out_specs=[IN_HBM] if last else [IN_VMEM] * len(shapes),
        scratch_shapes=[kept] + (in_last if last else []),
        compiler_params=pltpu.CompilerParams(vmem_limit_bytes=VMEM_BYTES),
        cost_estimate=pl.CostEstimate(flops=0, bytes_accessed=1 << 10, transcendentals=0),
        name="correlate",
    )(*operands)


def to_owners(pieces):
    owners = len(pieces)
    arrived = [pieces[0]] + [None] * (owners - 1)
    for d in range(owners - 1, 0, -1):
        arrived[d] = lax.ppermute(pieces[d], "chan", [(i, i ^ d) for i in range(owners)])
    return arrived


def held_back(blocks, after):
    def kernel(*refs):
        for i in range(len(blocks)):
            refs[len(blocks) + len(after) + i][...] = refs[i][...]

    return pl.pallas_call(
        kernel,
        out_shape=[jax.ShapeDtypeStruct(block.shape, block.dtype) for block in blocks],
        in_specs=[IN_VMEM] * (len(blocks) + len(after)),
        out_specs=[IN_VMEM] * len(blocks),
        compiler_params=pltpu.CompilerParams(vmem_limit_bytes=VMEM_BYTES),
        cost_estimate=pl.CostEstimate(flops=0, bytes_accessed=1 << 10, transcendentals=0),
        name="held_back",
    )(*blocks, *after)


def shards(voltages, antenna_gains, tile_map):
    owners = lax.axis_size("chan")
    n_row = lax.axis_size("brow")
    n_col = lax.axis_size("bcol")
    chips = n_col // 2
    frames = voltages.shape[2] // NCHAN
    across = [[(i, (i // 2 + d) % chips * 2 + i % 2) for i in range(n_col)] for d in range(chips)]
    along = [[(i, (i + d) % n_row) for i in range(n_row)] for d in range(n_row)]
    table = jnp.asarray(constants(owners))
    other_core = [(i, i ^ 1) for i in range(n_col)]

    filt, tables, pieces = filtered_and_first(voltages, owners, table)
    own, panels = [], []
    arrived = to_owners(pieces)
    for part in range(PARTS):
        later = None
        if part < PARTS - 1:
            pieces = next_part(part + 1, filt, tables, antenna_gains, owners)
            if part == 0:
                *pieces, gains = pieces
            later = to_owners([pieces[0], *held_back(pieces[1:], arrived[owners // 2 : owners // 2 + 1])])
        block, *longer = equalize(arrived, gains, part, frames)
        own.append(block)
        far = [lax.ppermute(own[part], "bcol", across[d]) for d in range(1, chips)]
        column = [lax.ppermute((longer or own)[-1], "brow", along[d]) for d in range(1, n_row)]
        panels.append((far, column))
        arrived = later
    result = [tile_map]
    for part in range(PARTS):
        far, column = panels[part]
        mine = own[part]
        if part < PARTS - 1:
            mine, *far = held_back([mine] + far, own[-1:])
        beside = lax.ppermute(mine, "bcol", other_core)
        relayed = [lax.ppermute(block, "bcol", other_core) for block in far]
        if part > 0:
            column = list(held_back(column, result[1:]))
        blocks = [own[part]] + far + [beside] + relayed + column
        result = correlate(blocks, result, part, n_row, n_col)
    return jnp.transpose(result[0], (3, 0, 1, 2))[None, None]


def solution(mesh):
    in_specs = (P(None, ("brow", "bcol"), "chan"), P(("brow", "bcol"), None, "chan"), P())
    out_specs = P("brow", "bcol", "chan", None, None, None)
    return jax.shard_map(shards, mesh=mesh, in_specs=in_specs, out_specs=out_specs, check_vma=False)
```

```python
import functools
import math

import jax
import jax.numpy as jnp
import ml_dtypes
import numpy as np
from jax import lax
from jax.experimental import pallas as pl
from jax.experimental.pallas import tpu as pltpu
from jax.sharding import PartitionSpec as P

NCHAN = 1024
HALF = NCHAN // 2
CHANNELS = 512
TAPS = 4
FIRST = 256
SIG = 8
LANES = 128
GROUP = 4
BATCH = 4
PARTS = 2
VMEM_BYTES = 16 * 1024 * 1024
EXTRA_ROWS = 16
FILTER_VMEM_BYTES = 101 * 512 * 1024
COEF_ROWS = 64


def fir_coefficients():
    position = np.arange(TAPS * NCHAN, dtype=np.float64) + 0.5
    offsets = position / NCHAN - TAPS / 2.0
    window = 0.5 - 0.5 * np.cos(2.0 * math.pi * position / (TAPS * NCHAN))
    return (np.sinc(offsets) * window).reshape(TAPS, NCHAN)


def spectrum_scale():
    return float(1.0 / (128.0 * np.sqrt(np.sum(fir_coefficients() ** 2))))


def dft_tables(owners):
    n = np.arange(HALF, dtype=np.int64).reshape(HALF, 1, 1, 1, 1, 1)
    k = FIRST + np.arange(CHANNELS, dtype=np.int64).reshape(owners, PARTS, BATCH, -1, 2)
    angles = (n * k % NCHAN) * (2.0 * math.pi / NCHAN)
    cosine, sine = np.cos(angles), np.sin(angles)
    first = np.stack([cosine, -sine], axis=2)
    second = np.stack([sine, cosine], axis=2)
    tables = np.stack([first, second])
    tables = np.transpose(tables, (4, 7, 0, 1, 2, 3, 6, 5))
    return tables.reshape(PARTS, 2 * NCHAN, -1).astype(np.float32).astype(ml_dtypes.bfloat16)


def constants(owners):
    tables = dft_tables(owners)
    lanes = tables.shape[2]
    left = fir_coefficients().astype(np.float32)
    terms = []
    for _ in range(3):
        terms.append(left.astype(ml_dtypes.bfloat16))
        left = left - terms[-1].astype(np.float32)
    terms = np.stack(terms).reshape(-1, lanes)
    pad = np.zeros((-terms.shape[0] % COEF_ROWS, lanes), ml_dtypes.bfloat16)
    return np.concatenate([tables.reshape(-1, lanes), terms, pad])


def transform(filt, table, scale, stage, out_refs):
    owners = len(out_refs)
    me = lax.axis_index("chan")
    spectra = [
        jnp.dot(filt[r], table[r * NCHAN : (r + 1) * NCHAN], preferred_element_type=jnp.float32) * scale
        for r in range(2)
    ]
    width = spectra[0].shape[1] // owners
    for owner in range(owners):
        here = slice(owner * width, (owner + 1) * width)
        piece = jnp.concatenate([spectra[0][:, here], spectra[1][:, here]], axis=1)
        stage[jnp.bitwise_xor(me, owner)] = piece[: stage.shape[1]].astype(jnp.bfloat16)
    for d in range(owners):
        out_refs[d][...] = stage[d]


def filter_kernel(frames, pieces, scale, volt_hbm, table_hbm, *refs):
    out_refs, (filt, later, volt, table, terms, coef, stage, sems) = refs[:-8], refs[-8:]
    per = frames // pieces
    lead = TAPS - 1
    copies = []
    for piece in range(pieces):
        copies.append(
            pltpu.make_async_copy(
                volt_hbm.at[:, :, pl.ds(piece * per * NCHAN, per * NCHAN)],
                volt.at[:, :, pl.ds((lead + piece * per) * NCHAN, per * NCHAN)],
                sems.at[piece],
            )
        )
    table_copy = pltpu.make_async_copy(table_hbm.at[pl.ds(0, 2 * NCHAN)], table, sems.at[pieces])
    coef_copy = pltpu.make_async_copy(
        table_hbm.at[pl.ds(PARTS * 2 * NCHAN, terms.shape[0])], terms, sems.at[pieces + 1]
    )
    copies[0].start()
    coef_copy.start()
    for copy in copies[1:]:
        copy.start()
    later_copy = pltpu.make_async_copy(
        table_hbm.at[pl.ds(2 * NCHAN, (PARTS - 1) * 2 * NCHAN)], later, sems.at[pieces + 2]
    )
    table_copy.start()
    later_copy.start()
    tail = volt.shape[2] - (lead + frames) * NCHAN
    volt[:, :, : lead * NCHAN] = jnp.zeros((2, SIG, lead * NCHAN), jnp.int32)
    volt[:, :, (lead + frames) * NCHAN :] = jnp.zeros((2, SIG, tail), jnp.int32)
    coef_copy.wait()
    across = coef.shape[1]
    per_term = TAPS * NCHAN // across
    coef[...] = sum(terms[t * per_term : (t + 1) * per_term, :].astype(jnp.float32) for t in range(3))

    def filter_group(start, count):
        base = start * NCHAN
        rows = slice(start * SIG, (start + count) * SIG)
        for column in range(HALF // LANES):
            for part in range(2):
                halves = []
                for half in range(2):
                    lane = half * HALF + column * LANES
                    at = [k * (NCHAN // across) + lane // across for k in range(TAPS)]
                    taps = [coef[i : i + 1, lane % across : lane % across + LANES] for i in at]
                    near = [
                        volt[part, :, pl.ds(base + f * NCHAN + lane, LANES)].astype(jnp.float32)
                        for f in range(count + TAPS - 1)
                    ]
                    sums = []
                    for m in range(count):
                        total = taps[0] * near[m]
                        for k in range(1, TAPS):
                            total = total + taps[k] * near[m + k]
                        sums.append(total)
                    halves.append(jnp.concatenate(sums, axis=0))
                where = pl.ds(part * HALF + column * LANES, LANES)
                filt[0, rows, where] = (halves[0] + halves[1]).astype(jnp.bfloat16)
                filt[1, rows, where] = (halves[0] - halves[1]).astype(jnp.bfloat16)

    for piece in range(pieces):
        copies[piece].wait()
        filter_group(piece * per, per)
    filter_group(frames, GROUP)
    table_copy.wait()
    transform(filt, table, scale, stage, out_refs)
    later_copy.wait()


def transform_kernel(part, scale, filt, later, gains_ref, pick_ref, *refs):
    table = later.at[pl.ds((part - 1) * 2 * NCHAN, 2 * NCHAN)]
    if part == 1:
        columns, stage = refs[-2:]
        gains = jnp.concatenate([gains_ref[:, 0, :], gains_ref[:, 1, :]], axis=0)
        columns[...] = lax.dot_general(
            pick_ref[...],
            gains,
            (((1,), (1,)), ((), ())),
            precision=lax.Precision.HIGHEST,
            preferred_element_type=jnp.float32,
        )
        transform(filt, table, scale, stage, refs[:-2])
    else:
        transform(filt, table, scale, refs[-1], refs[:-1])


IN_VMEM = pl.BlockSpec(memory_space=pltpu.VMEM)
IN_HBM = pl.BlockSpec(memory_space=pl.ANY)


def filtered_and_first(voltages, owners, table):
    frames = voltages.shape[2] // NCHAN
    rows = (frames + GROUP) * SIG
    sent = (frames + TAPS - 1) * SIG
    pieces = 4
    across = table.shape[1]
    terms = table.shape[0] - PARTS * 2 * NCHAN
    lanes = 2 * CHANNELS // owners // PARTS
    *first, filt, later = pl.pallas_call(
        functools.partial(filter_kernel, frames, pieces, spectrum_scale()),
        out_shape=[jax.ShapeDtypeStruct((sent, lanes), jnp.bfloat16)] * owners
        + [
            jax.ShapeDtypeStruct((2, rows, NCHAN), jnp.bfloat16),
            jax.ShapeDtypeStruct(((PARTS - 1) * 2 * NCHAN, across), jnp.bfloat16),
        ],
        in_specs=[IN_HBM, IN_HBM],
        out_specs=[IN_VMEM] * (owners + 2),
        scratch_shapes=[
            pltpu.VMEM((2, SIG, (frames + GROUP + TAPS - 1) * NCHAN), jnp.int32),
            pltpu.VMEM((2 * NCHAN, across), jnp.bfloat16),
            pltpu.VMEM((terms, across), jnp.bfloat16),
            pltpu.VMEM((TAPS * NCHAN // across, across), jnp.float32),
            pltpu.VMEM((owners, sent, lanes), jnp.bfloat16),
            pltpu.SemaphoreType.DMA((pieces + 3,)),
        ],
        compiler_params=pltpu.CompilerParams(vmem_limit_bytes=FILTER_VMEM_BYTES),
        cost_estimate=pl.CostEstimate(flops=1 << 29, bytes_accessed=4 << 20, transcendentals=0),
        name="filter_and_transform",
    )(voltages, table)
    return filt, later, first


def pick_rows(channels):
    order = np.arange(channels).reshape(PARTS, BATCH, -1, 2)
    return np.eye(channels, dtype=np.float32)[np.transpose(order, (0, 3, 2, 1)).reshape(-1)]


def next_part(part, filt, later, gains, owners):
    rows = filt.shape[1] - (GROUP - TAPS + 1) * SIG
    lanes = 2 * CHANNELS // owners // PARTS
    channels = gains.shape[2]
    shapes = [jax.ShapeDtypeStruct((rows, lanes), jnp.bfloat16)] * owners
    if part == 1:
        shapes.append(jax.ShapeDtypeStruct((channels, 2 * SIG), jnp.float32))
    return pl.pallas_call(
        functools.partial(transform_kernel, part, spectrum_scale()),
        out_shape=shapes,
        in_specs=[IN_VMEM] * 4,
        out_specs=[IN_VMEM] * len(shapes),
        scratch_shapes=[pltpu.VMEM((owners, rows, lanes), jnp.bfloat16)],
        compiler_params=pltpu.CompilerParams(vmem_limit_bytes=VMEM_BYTES),
        cost_estimate=pl.CostEstimate(flops=1 << 29, bytes_accessed=2 << 20, transcendentals=0),
        name="transform",
    )(filt, later, gains, jnp.asarray(pick_rows(channels)))


def equalize_kernel(owners, frames, h, part, *refs):
    pieces = refs[owners - 1 :: -1]
    gains_ref, by_time, by_channel = refs[owners], refs[-2], refs[-1]
    out_refs = refs[owners + 1 : -2]
    for out_ref in out_refs[1:]:
        out_ref[:, h * SIG :, :] = jnp.zeros((2, EXTRA_ROWS, out_ref.shape[2]), jnp.bfloat16)
    width = 4 * h
    own_rows = frames * SIG
    over = (TAPS - 1) * SIG
    times = owners * frames
    tiles = times // LANES
    me = lax.axis_index("chan")
    for d in range(owners):
        source = jnp.bitwise_xor(me, d)
        start = pl.multiple_of(source * own_rows, own_rows)
        by_time[pl.ds(start, own_rows), :width] = pieces[d][:own_rows, :].astype(jnp.float32)
    for d in range(owners):
        source = jnp.bitwise_xor(me, d)

        @pl.when(source < owners - 1)
        def _():
            start = pl.multiple_of((source + 1) * own_rows, own_rows)
            by_time[pl.ds(start, over), :width] += pieces[d][own_rows:, :].astype(jnp.float32)

    gains = [gains_ref[(2 * part + r) * h : (2 * part + r + 1) * h, :] for r in range(2)]
    for s in range(SIG):
        x = by_time[pl.ds(s, times, stride=SIG), :][:, :width].T
        for r in range(2):
            real, imag = x[2 * r * h : (2 * r + 1) * h], x[(2 * r + 1) * h : (2 * r + 2) * h]
            gain_real, gain_imag = gains[r][:, s : s + 1], gains[r][:, SIG + s : SIG + s + 1]
            both = [real * gain_real - imag * gain_imag, real * gain_imag + imag * gain_real]
            for q in range(2):
                for tile in range(tiles):
                    by_channel[(2 * r + q) * tiles + tile, pl.ds(s, h, stride=SIG), :] = both[q][
                        :, tile * LANES : (tile + 1) * LANES
                    ]
    for r in range(2):
        for tile in range(2 * tiles):
            for out_ref in out_refs:
                ready = by_channel[r * 2 * tiles + tile].astype(jnp.bfloat16)
                out_ref[r, : h * SIG, tile * LANES : (tile + 1) * LANES] = ready


def equalize(pieces, gains, part, frames):
    owners = len(pieces)
    h = gains.shape[0] // PARTS // 2
    times = owners * frames
    lengths = [h * SIG] + ([h * SIG + EXTRA_ROWS] if part == PARTS - 1 else [])
    return pl.pallas_call(
        functools.partial(equalize_kernel, owners, frames, h, part),
        out_shape=[jax.ShapeDtypeStruct((2, rows, 2 * times), jnp.bfloat16) for rows in lengths],
        in_specs=[IN_VMEM] * (owners + 1),
        out_specs=[IN_VMEM] * len(lengths),
        scratch_shapes=[
            pltpu.VMEM((times * SIG, LANES), jnp.float32),
            pltpu.VMEM((4 * times // LANES, h * SIG, LANES), jnp.float32),
        ],
        compiler_params=pltpu.CompilerParams(vmem_limit_bytes=VMEM_BYTES),
        cost_estimate=pl.CostEstimate(flops=0, bytes_accessed=1 << 10, transcendentals=0),
        name="equalize",
    )(*pieces[::-1], gains)


def row_places(col, n_col):
    chips = n_col // 2
    chip, core = lax.div(col, 2), lax.rem(col, 2)
    places = [col] + [lax.rem(chip + chips - d, chips) * 2 + core for d in range(1, chips)]
    return places + [jnp.bitwise_xor(p, 1) for p in places]


def column_places(row, n_row):
    return [row] + [lax.rem(row + n_row - d, n_row) for d in range(1, n_row)]


def regroup(v):
    lane = lax.broadcasted_iota(jnp.int32, v[0].shape, 1)
    v = list(v)
    for bit in (2, 1):
        width = bit * LANES // 8
        low = (lane // width) % 2 == 0
        for i in range(4):
            if i & bit == 0:
                a, b = v[i], v[i + bit]
                v[i] = jnp.where(low, a, pltpu.roll(b, width, axis=1))
                v[i + bit] = jnp.where(low, pltpu.roll(a, LANES - width, axis=1), b)
    return v


def correlate_kernel(n_row, n_col, h, times, part, dense, *refs):
    row_blocks = refs[:n_col]
    col_blocks = (refs[0],) + refs[n_col : n_col + n_row - 1]
    last = part == PARTS - 1
    given = refs[n_col + n_row - 1 :]
    if part > 0:
        earlier, keeps = given[:2]
    if last:
        out_hbm, chosen, out_ref, sems = refs[-4:]
    else:
        out_ref, keeps_out, chosen = refs[-3:]
    me_row, me_col = lax.axis_index("brow"), lax.axis_index("bcol")
    row_at, col_at = row_places(me_col, n_col), column_places(me_row, n_row)
    rows = BATCH * SIG
    tiles = n_col * rows // LANES
    steps = 2 * h // BATCH
    if part == 0:
        owned = given[0][...]
        first, second = (lax.broadcasted_iota(jnp.int32, owned.shape, axis) for axis in range(2))
        for e in range(n_row):
            for d in range(n_col):
                here = (first == me_row * n_col + row_at[d]) & (second == col_at[e] * n_col + me_col)
                found = jnp.max(jnp.where(here, (owned == 1).astype(jnp.float32), 0.0), axis=(0, 1), keepdims=True)
                keeps_out[e, d] = jnp.broadcast_to(found * (1.0 / times), (SIG, LANES))
    elif not last:
        keeps_out[...] = keeps[...]
    index_in_batch = (lax.broadcasted_iota(jnp.int32, (SIG, LANES), 1) // SIG) % BATCH

    for step in range(steps):
        inner, parity = step // 2, step % 2
        here = slice(inner * rows, (inner + 1) * rows)
        a = jnp.concatenate([block[parity, here, :] for block in row_blocks], axis=0)
        b = jnp.concatenate([block[parity, here, :] for block in col_blocks], axis=0)
        turned = jnp.concatenate([-b[:, times:], b[:, :times]], axis=1)
        both = jnp.concatenate([b, turned], axis=0)
        result = lax.dot_general(both, a, (((1,), (1,)), ((), ())), preferred_element_type=jnp.float32)
        for k in range(2 * n_row):
            for tile in range(tiles):
                lanes = slice(tile * LANES, (tile + 1) * LANES)
                own = [result[k * rows + i * SIG : k * rows + (i + 1) * SIG, lanes] for i in range(BATCH)]
                kept = own[0]
                for i in range(1, BATCH):
                    kept = jnp.where(index_in_batch == i, own[i], kept)
                chosen[k * tiles + tile, pl.ds(step, SIG, stride=steps), :] = kept

    copies = []
    low = lax.broadcasted_iota(jnp.int32, (SIG, LANES), 1) < LANES // 2
    for q in range(2):
        for e in range(n_row):
            for d in range(n_col):
                if d % (LANES // rows) == 0:
                    x = chosen[(q * n_row + e) * tiles + d * rows // LANES].T
                start = d * rows % LANES
                v = [x[start + i * SIG : start + (i + 1) * SIG] for i in range(BATCH)]
                if last:
                    keep = keeps[e, d]
                a_at = pl.ds(pl.multiple_of(row_at[d] * SIG, SIG), SIG)
                mine = slice(d * SIG, (d + 1) * SIG)
                if dense:
                    for g, w in enumerate(regroup(v)):
                        if last:
                            before = earlier[q, e, g, mine, :]
                            pair = [
                                jnp.where(low, before, pltpu.roll(w, LANES // 2, axis=1)),
                                jnp.where(low, pltpu.roll(before, LANES // 2, axis=1), w),
                            ]
                            for half in range(2):
                                out_ref[q, col_at[e] * SIG + half * BATCH + g, a_at, :] = pair[half] * keep
                        else:
                            out_ref[q, e, g, mine, :] = w
                else:
                    for s2 in range(SIG):
                        w = jnp.concatenate([each[:, s2 * steps : (s2 + 1) * steps] for each in v], axis=1)
                        if part > 0:
                            w = jnp.concatenate([earlier[q, e, s2, mine, :], w], axis=1)
                        if last:
                            out_ref[q, col_at[e] * SIG + s2, a_at, :] = w * keep[:, : w.shape[1]]
                        else:
                            out_ref[q, e, s2, mine, :] = w
            if last:
                where = pl.ds(col_at[e] * SIG, SIG)
                copy = pltpu.make_async_copy(out_ref.at[q, where], out_hbm.at[q, where], sems.at[q * n_row + e])
                copy.start()
                copies.append(copy)
    for copy in copies:
        copy.wait()


def correlate(blocks, given, part, n_row, n_col):
    h = blocks[0].shape[1] // SIG
    times = blocks[0].shape[2] // 2
    channels = 2 * h
    dense = channels * 2 == LANES and PARTS == 2
    operands = list(blocks) + list(given)
    last = part == PARTS - 1
    if last:
        out_shape = (2, n_row * SIG, n_col * SIG, (part + 1) * channels)
    elif dense:
        out_shape = (2, n_row, SIG // 2, n_col * SIG, LANES)
    else:
        out_shape = (2, n_row, SIG, n_col * SIG, (part + 1) * channels)
    shapes = [out_shape] if last else [out_shape, (n_row, n_col, SIG, LANES)]
    in_last = [pltpu.VMEM(out_shape, jnp.float32), pltpu.SemaphoreType.DMA((2 * n_row,))]
    kept = pltpu.VMEM((2 * n_row * n_col * BATCH * SIG // LANES, SIG * channels // BATCH, LANES), jnp.float32)
    return pl.pallas_call(
        functools.partial(correlate_kernel, n_row, n_col, h, times, part, dense),
        out_shape=[jax.ShapeDtypeStruct(shape, jnp.float32) for shape in shapes],
        in_specs=[IN_VMEM] * len(operands),
        out_specs=[IN_HBM] if last else [IN_VMEM] * len(shapes),
        scratch_shapes=[kept] + (in_last if last else []),
        compiler_params=pltpu.CompilerParams(vmem_limit_bytes=VMEM_BYTES),
        cost_estimate=pl.CostEstimate(flops=0, bytes_accessed=1 << 10, transcendentals=0),
        name="correlate",
    )(*operands)


def to_owners(pieces):
    owners = len(pieces)
    arrived = [pieces[0]] + [None] * (owners - 1)
    for d in range(owners - 1, 0, -1):
        arrived[d] = lax.ppermute(pieces[d], "chan", [(i, i ^ d) for i in range(owners)])
    return arrived


def held_back(blocks, after):
    def kernel(*refs):
        for i in range(len(blocks)):
            refs[len(blocks) + len(after) + i][...] = refs[i][...]

    return pl.pallas_call(
        kernel,
        out_shape=[jax.ShapeDtypeStruct(block.shape, block.dtype) for block in blocks],
        in_specs=[IN_VMEM] * (len(blocks) + len(after)),
        out_specs=[IN_VMEM] * len(blocks),
        compiler_params=pltpu.CompilerParams(vmem_limit_bytes=VMEM_BYTES),
        cost_estimate=pl.CostEstimate(flops=0, bytes_accessed=1 << 10, transcendentals=0),
        name="held_back",
    )(*blocks, *after)


def shards(voltages, antenna_gains, tile_map):
    owners = lax.axis_size("chan")
    n_row = lax.axis_size("brow")
    n_col = lax.axis_size("bcol")
    chips = n_col // 2
    frames = voltages.shape[2] // NCHAN
    across = [[(i, (i // 2 + d) % chips * 2 + i % 2) for i in range(n_col)] for d in range(chips)]
    along = [[(i, (i + d) % n_row) for i in range(n_row)] for d in range(n_row)]
    table = jnp.asarray(constants(owners))
    other_core = [(i, i ^ 1) for i in range(n_col)]

    filt, tables, pieces = filtered_and_first(voltages, owners, table)
    own, panels = [], []
    arrived = to_owners(pieces)
    for part in range(PARTS):
        later = None
        if part < PARTS - 1:
            pieces = next_part(part + 1, filt, tables, antenna_gains, owners)
            if part == 0:
                *pieces, gains = pieces
            later = to_owners([pieces[0], *held_back(pieces[1:], arrived[-1:])])
        block, *longer = equalize(arrived, gains, part, frames)
        own.append(block)
        far = [lax.ppermute(own[part], "bcol", across[d]) for d in range(1, chips)]
        column = [lax.ppermute((longer or own)[-1], "brow", along[d]) for d in range(1, n_row)]
        panels.append((far, column))
        arrived = later
    result = [tile_map]
    for part in range(PARTS):
        far, column = panels[part]
        mine = own[part]
        if part < PARTS - 1:
            mine, *far = held_back([mine] + far, own[-1:])
        beside = lax.ppermute(mine, "bcol", other_core)
        relayed = [lax.ppermute(block, "bcol", other_core) for block in far]
        if part > 0:
            column = list(held_back(column, result[1:]))
        blocks = [own[part]] + far + [beside] + relayed + column
        result = correlate(blocks, result, part, n_row, n_col)
    return jnp.transpose(result[0], (3, 0, 1, 2))[None, None]


def solution(mesh):
    in_specs = (P(None, ("brow", "bcol"), "chan"), P(("brow", "bcol"), None, "chan"), P())
    out_specs = P("brow", "bcol", "chan", None, None, None)
    return jax.shard_map(shards, mesh=mesh, in_specs=in_specs, out_specs=out_specs, check_vma=False)
```
